32 devices in a mesh: fsdp: 8 (over z, y), seq: 4 (over x, core).
Axes of the slice: x: 2, y: 2, z: 4, core: 2. Of those that a mesh axis runs over, the one named last changes fastest.
Arguments:
- image_tokens: bfloat16 [8, 1024, 1536], P('fsdp', 'seq'), may hold values from -6 to 6
- text_tokens: bfloat16 [8, 160, 1536], P('fsdp', 'seq'), may hold values from -6 to 6
- conditioning: float32 [8, 1536], P('fsdp'), may hold values from -6 to 6
- text_lengths: int32 [8], P('fsdp'), may hold values from 1 to 160, as said below
- mod_weight: bfloat16 [1, 2, 1536, 9216], P(None, None, 'fsdp'), may hold values from -0.15625 to 0.15625
- mod_bias: bfloat16 [1, 2, 9216], P(None, None, 'fsdp'), may hold values from -3 to 3
- qkv_weight: bfloat16 [1, 2, 1536, 4608], P(None, None, 'fsdp'), may hold values from -0.15625 to 0.15625
- qkv_bias: bfloat16 [1, 2, 3072], P(None, None, 'fsdp'), may hold values from -3 to 3
- proj_weight: bfloat16 [1, 2, 1536, 1536], P(None, None, 'fsdp'), may hold values from -0.625 to 0.625
- proj_bias: bfloat16 [1, 2, 1536], P(None, None, 'fsdp'), may hold values from -3 to 3
- hidden_weight: bfloat16 [1, 2, 1536, 6144], P(None, None, 'fsdp'), may hold values from -0.15625 to 0.15625
- hidden_bias: bfloat16 [1, 2, 6144], P(None, None, 'fsdp'), may hold values from -3 to 3
- output_weight: bfloat16 [1, 2, 6144, 1536], P(None, None, 'fsdp'), may hold values from -0.078125 to 0.078125
- output_bias: bfloat16 [1, 2, 1536], P(None, None, 'fsdp'), may hold values from -3 to 3
- image_cotangent: bfloat16 [8, 1024, 1536], P('fsdp', 'seq'), may hold values from -6 to 6
- text_cotangent: bfloat16 [8, 160, 1536], P('fsdp', 'seq'), may hold values from -6 to 6
Outputs:
- image_out: bfloat16 [8, 1024, 1536], P('fsdp', 'seq')
- text_out: bfloat16 [8, 160, 1536], P('fsdp', 'seq')
- image_grad: float32 [8, 1024, 1536], P('fsdp', 'seq')
- text_grad: float32 [8, 160, 1536], P('fsdp', 'seq')
- conditioning_grad: float32 [8, 1536], P('fsdp')
- mod_weight_grad: float32 [1, 2, 1536, 9216], P(None, None, 'fsdp')
- mod_bias_grad: float32 [1, 2, 9216], P(None, None, 'fsdp')
- qkv_weight_grad: float32 [1, 2, 1536, 4608], P(None, None, 'fsdp')
- qkv_bias_grad: float32 [1, 2, 3072], P(None, None, 'fsdp')
- proj_weight_grad: float32 [1, 2, 1536, 1536], P(None, None, 'fsdp')
- proj_bias_grad: float32 [1, 2, 1536], P(None, None, 'fsdp')
- hidden_weight_grad: float32 [1, 2, 1536, 6144], P(None, None, 'fsdp')
- hidden_bias_grad: float32 [1, 2, 6144], P(None, None, 'fsdp')
- output_weight_grad: float32 [1, 2, 6144, 1536], P(None, None, 'fsdp')
- output_bias_grad: float32 [1, 2, 1536], P(None, None, 'fsdp')
The draws below stay inside these ranges and needn't reach their ends.
Inputs may be any that keep to these rules, and one draw needn't show every extreme that they name: `text_lengths`: each sequence has from 1 to 160 valid text tokens, the first ones of its text slots; some sequence has all 160.
All inputs are finite; a program needn't handle non-finite values.
Results may differ from the reference program's by a relative error of at most 0.017.
Values may be sent and summed in bfloat16 or wider, within the bound.
A program may use at most 512 MiB of HBM per device.

```python
import jax
import jax.numpy as jnp
from jax import lax

D = 1536
HEADS = 24
HEAD_DIM = 64
FF = 6144
IMG = 1024
TXT = 160
LAYERS = 1
SEQS = 8


def draw_text_lengths(key, part):
    key = jax.random.fold_in(key, 7)
    first_key, second_key = jax.random.split(key)
    counts = jax.random.randint(first_key, (SEQS,), 1, TXT + 1)
    chosen = jax.random.randint(second_key, (), 0, SEQS)
    return jnp.where(jnp.arange(SEQS) == chosen, TXT, counts).astype(jnp.int32)


def steps_of(key, extent, cuts, low, top_value):
    level = 1.0
    for dim, blocks in cuts:
        steps = jax.random.uniform(jax.random.fold_in(jax.random.fold_in(key, 6), dim), (blocks,), jnp.float32, low / len(cuts), top_value / len(cuts))
        level = level * jnp.repeat(jnp.exp(steps), extent[dim] // blocks).reshape((-1,) + (1,) * (len(extent) - 1 - dim))
    return level


def bell_draw(key, dims, scale, bound, cuts=(), held_as=jnp.bfloat16):
    array = jax.random.normal(key, dims, jnp.float32) * scale
    if len(cuts) > 0:
        array = steps_of(key, dims, cuts, -0.22, 0.18) * array
    return jnp.clip(array, min=-bound, max=bound).astype(held_as)


def setup_inputs(seed: int = 0) -> dict:
    arg_keys = jax.random.split(jax.random.key(seed), 17)
    return {
        "image_tokens": bell_draw(arg_keys[0], (SEQS, IMG, D), 1.0, 6.0, ((0, 8), (1, 4))),
        "text_tokens": bell_draw(arg_keys[1], (SEQS, TXT, D), 1.0, 6.0, ((0, 8), (1, 4))),
        "conditioning": bell_draw(arg_keys[2], (SEQS, D), 1.0, 6.0, ((0, 8),), jnp.float32),
        "text_lengths": draw_text_lengths(jax.random.fold_in(arg_keys[16], 71), 0),
        "mod_weight": bell_draw(arg_keys[4], (LAYERS, 2, D, 6 * D), D ** -0.5, 0.15625, ((2, 8),)),
        "mod_bias": bell_draw(arg_keys[5], (LAYERS, 2, 6 * D), 0.5, 3.0, ((2, 8),)),
        "qkv_weight": bell_draw(arg_keys[6], (LAYERS, 2, D, 3 * D), D ** -0.5, 0.15625, ((2, 8),)),
        "qkv_bias": bell_draw(arg_keys[7], (LAYERS, 2, 2 * D), 0.5, 3.0, ((2, 8),)),
        "proj_weight": bell_draw(arg_keys[8], (LAYERS, 2, D, D), (D // 16) ** -0.5, 0.625, ((2, 8),)),
        "proj_bias": bell_draw(arg_keys[9], (LAYERS, 2, D), 0.5, 3.0, ((2, 8),)),
        "hidden_weight": bell_draw(arg_keys[10], (LAYERS, 2, D, FF), D ** -0.5, 0.15625, ((2, 8),)),
        "hidden_bias": bell_draw(arg_keys[11], (LAYERS, 2, FF), 0.5, 3.0, ((2, 8),)),
        "output_weight": bell_draw(arg_keys[12], (LAYERS, 2, FF, D), FF ** -0.5, 0.078125, ((2, 8),)),
        "output_bias": bell_draw(arg_keys[13], (LAYERS, 2, D), 0.5, 3.0, ((2, 8),)),
        "image_cotangent": bell_draw(arg_keys[14], (SEQS, IMG, D), 1.0, 6.0, ((0, 8), (1, 4))),
        "text_cotangent": bell_draw(arg_keys[15], (SEQS, TXT, D), 1.0, 6.0, ((0, 8), (1, 4))),
    }


@jax.custom_vjp
def low(v):
    return lax.optimization_barrier(v.astype(jnp.bfloat16)).astype(jnp.float32)

@jax.custom_vjp
def low_back(v):
    return v

def low_keep(v):
    return (low(v), None)

def low_pass(kept, grad):
    return (grad,)

def back_keep(v):
    return (v, None)

def back_low(kept, grad):
    return (low(grad),)
low.defvjp(low_keep, low_pass)
low_back.defvjp(back_keep, back_low)
NORM_EPS = 1e-06
MASKED_SCORE = -1e+30

def matmul_high(left, right):
    return jnp.matmul(left, right, precision=lax.Precision.HIGHEST)

def norm_rows(values):
    center = values - lax.optimization_barrier(jnp.mean(values, -1, keepdims=True))
    return center * lax.rsqrt(lax.optimization_barrier(jnp.mean(center * center, -1, keepdims=True)) + NORM_EPS)

def front_half(tokens, modulation, weight, bias):
    shift = modulation[:, None, 0:D]
    scale_up = modulation[:, None, D:2 * D]
    hidden = low(norm_rows(tokens) * (1.0 + scale_up) + shift)
    full_bias = jnp.concatenate([bias[:D], jnp.zeros((D,), bias.dtype), bias[D:]])
    return low(low_back(matmul_high(hidden, weight) + full_bias))

def attention(joint, valid):
    query = joint[:, 0]
    keys_all = joint[:, 1]
    values_all = joint[:, 2]
    scores = low_back(jnp.einsum('qhd,khd->hqk', query, keys_all, precision=lax.Precision.HIGHEST) * HEAD_DIM ** (-0.5))
    masked = jnp.where(valid[None, None, :], scores, MASKED_SCORE)
    probs = low(jax.nn.softmax(masked, axis=-1))
    return jnp.einsum('hqk,khd->qhd', probs, values_all, precision=lax.Precision.HIGHEST)

def rear_half(tokens, attended, modulation, proj_weight, proj_bias, hidden_weight, hidden_bias, output_weight, output_bias):
    branch = low_back(matmul_high(attended, proj_weight) + proj_bias)
    middle = tokens + modulation[:, None, 2 * D:3 * D] * branch
    hidden = low(norm_rows(middle) * (1.0 + modulation[:, None, 4 * D:5 * D]) + modulation[:, None, 3 * D:4 * D])
    before = low_back(matmul_high(hidden, hidden_weight) + hidden_bias)
    active = low(jax.nn.gelu(before, approximate=True))
    result = low_back(matmul_high(active, output_weight) + output_bias)
    return middle + modulation[:, None, 5 * D:6 * D] * result

def reference(image_tokens, text_tokens, conditioning, text_lengths, mod_weight, mod_bias, qkv_weight, qkv_bias, proj_weight, proj_bias, hidden_weight, hidden_bias, output_weight, output_bias, image_cotangent, text_cotangent):
    positions = jnp.arange(IMG + TXT, dtype=jnp.int32)
    valid = (positions[None, :] < IMG) | (positions[None, :] - IMG < text_lengths[:, None])
    attend_one = jax.checkpoint(lambda seq_pair: attention(seq_pair[0], seq_pair[1]))

    def forward_pass(image_now, text_now, cond_now, mod_weights, mod_biases, qkv_weights, qkv_biases, proj_weights, proj_biases, hidden_weights, hidden_biases, output_weights, output_biases):
        act_cond = low(jax.nn.silu(cond_now))
        current = [image_now, text_now]
        for layer_at in range(LAYERS):
            mods = [low_back(matmul_high(act_cond, mod_weights[layer_at, modality]) + mod_biases[layer_at, modality]) for modality in range(2)]
            joined = [front_half(current[modality], mods[modality], qkv_weights[layer_at, modality], qkv_biases[layer_at, modality]) for modality in range(2)]
            joint = jnp.concatenate(joined, 1).reshape(SEQS, IMG + TXT, 3, HEADS, HEAD_DIM)
            mixed = lax.map(attend_one, (joint, valid))
            mixed = low(low_back(mixed.reshape(SEQS, IMG + TXT, D)))
            pieces = [mixed[:, :IMG], mixed[:, IMG:]]
            current = [rear_half(current[modality], pieces[modality], mods[modality], proj_weights[layer_at, modality], proj_biases[layer_at, modality], hidden_weights[layer_at, modality], hidden_biases[layer_at, modality], output_weights[layer_at, modality], output_biases[layer_at, modality]) for modality in range(2)]
        return (current[0], current[1])
    floats = [value.astype(jnp.float32) for value in (image_tokens, text_tokens, conditioning, mod_weight, mod_bias, qkv_weight, qkv_bias, proj_weight, proj_bias, hidden_weight, hidden_bias, output_weight, output_bias)]
    outputs, pullback = jax.vjp(forward_pass, *floats)
    grads = pullback((image_cotangent.astype(jnp.float32), text_cotangent.astype(jnp.float32)))
    return (outputs[0].astype(jnp.bfloat16), outputs[1].astype(jnp.bfloat16), grads[0], grads[1], grads[2], grads[3], grads[4], grads[5], grads[6], grads[7], grads[8], grads[9], grads[10], grads[11], grads[12])
```

```python
import jax
import jax.numpy as jnp
from jax import lax
from jax.sharding import PartitionSpec as P

HEAD_DIM = 64
NORM_EPS = 1e-06
MASKED_SCORE = -1e30


def norm_rows(values):
    center = values - jnp.mean(values, -1, keepdims=True)
    return center * lax.rsqrt(jnp.mean(center * center, -1, keepdims=True) + NORM_EPS)


def modulated(values, shift, scale_up):
    return norm_rows(values) * (1.0 + scale_up) + shift


def gelu_tanh(values):
    return jax.nn.gelu(values, approximate=True)


def dot32(left, right, contract):
    return lax.dot_general(
        left, right, ((contract[0], contract[1]), ((), ())), preferred_element_type=jnp.float32
    )


def product(left, right):
    return dot32(left, right, ((1,), (0,)))


def rows_inner(left, right):
    return dot32(left, right, ((0,), (0,)))


def right_back(left, right):
    return dot32(left, right, ((1,), (1,)))


def seq_swap(values, mask):
    return lax.ppermute(values, "seq", [(at, at ^ mask) for at in range(4)])


def seq_gather(own):
    far = seq_swap(own, 2)
    near = seq_swap(jnp.stack([own, far]), 1)
    return [own, near[0], far, near[1]]


def seq_reduce(pieces):
    sent = jnp.stack([pieces[1], pieces[3]]).astype(jnp.bfloat16)
    got = seq_swap(sent, 1).astype(jnp.float32)
    far = (pieces[2].astype(jnp.float32) + got[1]).astype(jnp.bfloat16)
    back = seq_swap(far, 2).astype(jnp.float32)
    return pieces[0].astype(jnp.float32) + got[0] + back


def shards(
    image_tokens,
    text_tokens,
    conditioning,
    text_lengths,
    mod_weight,
    mod_bias,
    qkv_weight,
    qkv_bias,
    proj_weight,
    proj_bias,
    hidden_weight,
    hidden_bias,
    output_weight,
    output_bias,
    image_cotangent,
    text_cotangent,
):
    f32, b16 = jnp.float32, jnp.bfloat16
    width = image_tokens.shape[2]
    counts = (image_tokens.shape[1], text_tokens.shape[1])
    here = counts[0] + counts[1]
    parts = lax.axis_size("seq")
    owners = lax.axis_size("fsdp")
    ring = owners // parts
    head_part = width // parts
    heads_here = head_part // HEAD_DIM
    slab = width // owners
    units_slab = output_weight.shape[2]
    units_part = units_slab // parts
    units = units_slab * owners
    units_here = units // parts
    half = parts * slab
    score_scale = HEAD_DIM ** (-0.5)
    me = lax.axis_index("fsdp")
    s = lax.axis_index("seq")
    my_r = me % ring
    across = [[g * ring + r for g in range(parts)] for r in range(ring)]

    def cut(array, start, size, axis):
        return lax.dynamic_slice_in_dim(array, start, size, axis)

    def step_ring(values, k):
        return lax.ppermute(
            values,
            "fsdp",
            [(g * ring + r, g * ring + (r + k) % ring) for g in range(parts) for r in range(ring)],
        )

    def transpose_owners(values):
        pairs = [
            ((g * ring + r) * parts + q, (q * ring + r) * parts + g)
            for g in range(parts)
            for r in range(ring)
            for q in range(parts)
        ]
        return lax.ppermute(values, ("fsdp", "seq"), pairs)

    def gather_weight(rows):
        lined = lax.all_gather(rows, "fsdp", axis=0, tiled=True, axis_index_groups=across)
        return [lined] + [step_ring(lined, k) for k in range(1, ring)]

    def from_ring(stacked, k):
        return lax.dynamic_index_in_dim(stacked, (my_r - k) % ring, 0, keepdims=False)

    def natural(pieces):
        out = []
        for r in range(ring):
            value = pieces[0]
            for k in range(1, ring):
                value = jnp.where((my_r - r) % ring == k, pieces[k], value)
            out.append(value)
        return out

    def split_features(values):
        rows = values.shape[0]
        return values.reshape(rows, parts, ring, slab).transpose(2, 0, 1, 3).reshape(ring, rows, half)

    def join_features(pieces):
        rows = pieces[0].shape[0]
        return jnp.stack([p.reshape(rows, parts, slab) for p in pieces], 2).reshape(rows, width)

    def reduce_weight(stacked, right):
        total = None
        for k in range(1, ring):
            left = lax.dynamic_index_in_dim(stacked, (my_r + k) % ring, 0, keepdims=False)
            got = step_ring(rows_inner(left, right).astype(b16), k).astype(f32)
            total = got if total is None else total + got
        mine = rows_inner(from_ring(stacked, 0), right)
        total = mine if total is None else mine + total
        return lax.psum_scatter(
            total.astype(b16), "fsdp", scatter_dimension=0, tiled=True, axis_index_groups=across
        )

    bias_sizes = [b.shape[2] for b in (qkv_bias, proj_bias, hidden_bias, output_bias)]
    bias_local = jnp.concatenate(
        [b[0].astype(f32) for b in (qkv_bias, proj_bias, hidden_bias, output_bias)], 1
    )
    packed = jnp.concatenate([conditioning.reshape(-1), bias_local.reshape(-1)])
    everything = lax.all_gather(packed, "fsdp", axis=0)
    everyone = everything[:, :width]
    bias_all = everything[:, width:].reshape(owners, 2, sum(bias_sizes))
    offsets = [0]
    for size in bias_sizes:
        offsets.append(offsets[-1] + size)
    qkv_b, proj_b, hid_b_raw, out_b = [
        bias_all[:, :, offsets[i] : offsets[i + 1]].transpose(1, 0, 2) for i in range(4)
    ]
    qkv_b = qkv_b.reshape(2, 2, width)
    qkv_b = cut(qkv_b, s * head_part, head_part, 2)
    qkv_b = jnp.stack([qkv_b[:, 0], jnp.zeros_like(qkv_b[:, 0]), qkv_b[:, 1]], 1).reshape(
        2, 3 * head_part
    )
    proj_b = proj_b.reshape(2, width)
    out_b = out_b.reshape(2, width)
    hid_b = cut(hid_b_raw.reshape(2, parts, ring, parts, units_part), s, 1, 3)
    hid_b = hid_b.transpose(0, 2, 1, 3, 4).reshape(2, units_here)

    act_all = jax.nn.silu(everyone).astype(b16)
    act_cols = cut(act_all, me * slab, slab, 1)
    mod_part = mod_bias.shape[2]
    bias_spread = lax.dynamic_update_slice_in_dim(
        jnp.zeros((2, 6 * width), f32), mod_bias[0].astype(f32), me * mod_part, 1
    )
    term = jnp.einsum("sd,tde->ste", act_cols, mod_weight[0], preferred_element_type=f32)
    term = term + bias_spread[None]
    mods = jnp.sum(
        lax.all_to_all(term, "fsdp", split_axis=0, concat_axis=0, tiled=True), 0
    )
    shift1, scale1, gate1, shift2, scale2, gate2 = [
        [mods[m, i * width : (i + 1) * width] for m in range(2)] for i in range(6)
    ]

    qkv_mine = cut(qkv_weight[0].reshape(2, slab, 3, width), s * head_part, head_part, 3)
    qkv_mine = qkv_mine.reshape(2, slab, 3 * head_part)
    hid_mine = cut(
        hidden_weight[0].reshape(2, slab, parts, ring, parts, units_part), s, 1, 4
    )
    hid_mine = hid_mine.transpose(0, 1, 3, 2, 4, 5).reshape(2, slab, units_here)
    out_mine = cut(output_weight[0], s * units_part, units_part, 1)
    proj_cut = slab // parts
    proj_mine = transpose_owners(cut(proj_weight[0], s * proj_cut, proj_cut, 1))

    qkv_w = [gather_weight(qkv_mine[m]) for m in range(2)]
    proj_w = [gather_weight(proj_mine[m]) for m in range(2)]
    hid_w = [gather_weight(hid_mine[m]) for m in range(2)]
    out_w = [gather_weight(out_mine[m]) for m in range(2)]

    def pack(image, text):
        return jnp.concatenate([image, text], 0)

    def by_modality(pieces):
        return [
            jnp.concatenate([p[: counts[0]] for p in pieces], 0),
            jnp.concatenate([p[counts[0] :] for p in pieces], 0),
        ]

    def by_piece(image, text):
        return [
            pack(
                image[p * counts[0] : (p + 1) * counts[0]],
                text[p * counts[1] : (p + 1) * counts[1]],
            )
            for p in range(parts)
        ]

    def local_pair(values):
        return [values[: counts[0]], values[counts[0] :]]

    x_local = [image_tokens[0].astype(f32), text_tokens[0].astype(f32)]
    g_local = [image_cotangent[0].astype(f32), text_cotangent[0].astype(f32)]
    x_full = by_modality(seq_gather(pack(image_tokens[0], text_tokens[0])))
    g_full = by_modality(seq_gather(pack(image_cotangent[0], text_cotangent[0])))

    hidden1 = [
        split_features(modulated(x_full[m].astype(f32), shift1[m], scale1[m]).astype(b16))
        for m in range(2)
    ]

    def apply_rows(stacked, pieces):
        total = None
        for k in range(ring):
            term = product(from_ring(stacked, k), pieces[k])
            total = term if total is None else total + term
        return total

    qkv = [(apply_rows(hidden1[m], qkv_w[m]) + qkv_b[m]).astype(b16) for m in range(2)]
    all_rows = here * parts
    joint = jnp.concatenate(qkv, 0).reshape(all_rows, 3, heads_here, HEAD_DIM)
    text_slot = jnp.arange(counts[1] * parts)
    text_place = ((text_slot // counts[1]) ^ s) * counts[1] + text_slot % counts[1]
    valid = jnp.concatenate(
        [jnp.ones((counts[0] * parts,), bool), text_place < text_lengths[0]]
    )
    query, keys_all, values_all = joint[:, 0], joint[:, 1], joint[:, 2]

    def masked_scores():
        raw = jnp.einsum("qhd,khd->hqk", query, keys_all, preferred_element_type=f32) * score_scale
        return jnp.where(valid[None, None, :], raw, MASKED_SCORE)

    masked = masked_scores()
    row_max = jnp.max(masked, -1, keepdims=True)
    log_total = row_max + jnp.log(jnp.sum(jnp.exp(masked - row_max), -1, keepdims=True))
    probs = jnp.exp(masked - log_total).astype(b16)
    mixed = jnp.einsum("hqk,khd->qhd", probs, values_all, preferred_element_type=f32).astype(b16)
    mixed = mixed.reshape(all_rows, ring, slab).transpose(1, 0, 2)
    image_rows = counts[0] * parts
    attended = [mixed[:, :image_rows], mixed[:, image_rows:]]

    branch_part = [apply_rows(attended[m], proj_w[m]) for m in range(2)]
    branch = local_pair(seq_reduce(by_piece(*branch_part)))
    branch = [branch[m] + proj_b[m] for m in range(2)]
    middle = [x_local[m] + gate1[m] * branch[m] for m in range(2)]
    hidden2_local = [modulated(middle[m], shift2[m], scale2[m]).astype(b16) for m in range(2)]
    hidden2 = [split_features(v) for v in by_modality(seq_gather(pack(*hidden2_local)))]
    before = [apply_rows(hidden2[m], hid_w[m]) + hid_b[m] for m in range(2)]
    active = [
        gelu_tanh(before[m]).astype(b16).reshape(-1, ring, half * units_part // slab).transpose(1, 0, 2)
        for m in range(2)
    ]
    result_part = [apply_rows(active[m], out_w[m]) for m in range(2)]
    result = local_pair(seq_reduce(by_piece(*result_part)))
    result = [result[m] + out_b[m] for m in range(2)]
    image_out, text_out = [
        (middle[m] + gate2[m] * result[m]).astype(b16)[None] for m in range(2)
    ]

    def back_rows(right, pieces):
        return [right_back(right, pieces[k]) for k in range(ring)]

    d_gate2 = [jnp.sum(g_local[m] * result[m], 0) for m in range(2)]
    d_result = [(g_full[m].astype(f32) * gate2[m]).astype(b16) for m in range(2)]
    out_bt = [
        jnp.sum((g_local[m] * gate2[m]).astype(b16).astype(f32), 0) for m in range(2)
    ]
    out_g = [reduce_weight(active[m], d_result[m]) for m in range(2)]
    d_before = []
    for m in range(2):
        d_active = jnp.concatenate(natural(back_rows(d_result[m], out_w[m])), 1)
        d_before.append(jax.vjp(gelu_tanh, before[m])[1](d_active)[0].astype(b16))
    hid_bt = [jnp.sum(d_before[m].astype(f32), 0) for m in range(2)]
    hid_g = [reduce_weight(hidden2[m], d_before[m]) for m in range(2)]

    def back_features(right, weights):
        image, text = [back_rows(right[m], weights[m]) for m in range(2)]
        pieces = [
            by_piece(image[k].astype(b16), text[k].astype(b16)) for k in range(ring)
        ]
        joined = [jnp.concatenate([pieces[k][p] for k in range(ring)], 1) for p in range(parts)]
        summed = seq_reduce(joined)
        split = [summed[:, k * half : (k + 1) * half] for k in range(ring)]
        return local_pair(join_features(natural(split)))

    d_hidden2 = back_features(d_before, hid_w)
    d_middle, d_branch, d_gate1, d_shift2, d_scale2, proj_bt = [], [], [], [], [], []
    for m in range(2):
        pull = jax.vjp(modulated, middle[m], shift2[m], scale2[m])[1]
        d_norm, d_shift, d_scale = pull(d_hidden2[m])
        d_middle.append(g_local[m] + d_norm)
        d_branch.append((d_middle[m] * gate1[m]).astype(b16))
        d_gate1.append(jnp.sum(d_middle[m] * branch[m], 0))
        d_shift2.append(d_shift)
        d_scale2.append(d_scale)
        proj_bt.append(jnp.sum(d_branch[m].astype(f32), 0))
    d_branch_full = by_modality(seq_gather(pack(*d_branch)))
    proj_g = [reduce_weight(attended[m], d_branch_full[m]) for m in range(2)]
    d_attended = [
        jnp.concatenate(natural(back_rows(d_branch_full[m], proj_w[m])), 1).astype(b16)
        for m in range(2)
    ]
    d_heads = jnp.concatenate(d_attended, 0).reshape(all_rows, heads_here, HEAD_DIM)
    probs_full = jnp.exp(masked_scores() - log_total)
    probs = probs_full.astype(b16)
    d_values = jnp.einsum("hqk,qhd->khd", probs, d_heads, preferred_element_type=f32)
    d_probs = jnp.einsum("qhd,khd->hqk", d_heads, values_all, preferred_element_type=f32)
    d_scores = (
        probs_full * (d_probs - jnp.sum(d_probs * probs_full, -1, keepdims=True))
    ).astype(b16)
    d_query = (
        jnp.einsum("hqk,khd->qhd", d_scores, keys_all, preferred_element_type=f32) * score_scale
    )
    d_keys = jnp.einsum("hqk,qhd->khd", d_scores, query, preferred_element_type=f32) * score_scale
    d_joint = jnp.stack([d_query, d_keys, d_values], 1).astype(b16).reshape(all_rows, 3 * head_part)
    d_qkv = [d_joint[:image_rows], d_joint[image_rows:]]
    qkv_bt = [jnp.sum(d_qkv[m].astype(f32), 0).reshape(3, head_part) for m in range(2)]
    qkv_g = [reduce_weight(hidden1[m], d_qkv[m]) for m in range(2)]
    d_hidden1 = back_features(d_qkv, qkv_w)
    image_grad, d_shift1, d_scale1 = [], [], []
    for m in range(2):
        pull = jax.vjp(modulated, x_local[m], shift1[m], scale1[m])[1]
        d_norm, d_shift, d_scale = pull(d_hidden1[m])
        image_grad.append((d_middle[m] + d_norm)[None])
        d_shift1.append(d_shift)
        d_scale1.append(d_scale)

    qkv_bt = jnp.stack(qkv_bt)[:, ::2]
    qkv_bt = lax.dynamic_update_slice_in_dim(
        jnp.zeros((2, 2, width), f32), qkv_bt, s * head_part, 2
    ).reshape(2, 2 * width)
    hid_bt = jnp.stack(hid_bt).reshape(2, ring, parts, 1, units_part).transpose(0, 2, 1, 3, 4)
    hid_bt = lax.dynamic_update_slice_in_dim(
        jnp.zeros((2, parts, ring, parts, units_part), f32), hid_bt, s, 3
    ).reshape(2, units)
    sums = jnp.concatenate(
        [
            jnp.stack(v)
            for v in (d_shift1, d_scale1, d_gate1, d_shift2, d_scale2, d_gate2)
        ]
        + [qkv_bt, jnp.stack(proj_bt), hid_bt, jnp.stack(out_bt)],
        1,
    )
    sums = sums + seq_swap(sums, 2)
    sums = sums + seq_swap(sums, 1)
    sums_all = lax.all_gather(sums.astype(b16), "fsdp", axis=0)
    d_mods = sums_all[:, :, : 6 * width]
    bias_sum = jnp.sum(sums_all[:, :, 6 * width :].astype(f32), 0)
    bias_at = [0, 2 * width, 3 * width, 3 * width + units, 4 * width + units]
    bias_grads = [
        cut(bias_sum[:, bias_at[i] : bias_at[i + 1]], me * bias_sizes[i], bias_sizes[i], 1)[None]
        for i in range(4)
    ]
    mod_grad_w = jnp.einsum("sd,ste->tde", act_cols, d_mods, preferred_element_type=f32)[None]
    mod_grad_b = jnp.sum(cut(d_mods, me * mod_part, mod_part, 2).astype(f32), 0)[None]
    d_act_cols = jnp.einsum("ste,tde->sd", d_mods, mod_weight[0], preferred_element_type=f32)
    d_act = lax.all_to_all(d_act_cols, "fsdp", split_axis=0, concat_axis=1, tiled=True)
    conditioning_grad = jax.vjp(jax.nn.silu, conditioning)[1](d_act)[0]

    def share(values):
        return lax.all_gather(jnp.stack(values), "seq", axis=0).astype(f32)

    out_grad = share(out_g).transpose(1, 0, 2, 3).reshape(1, 2, units_slab, width)
    hid_grad = (
        share(hid_g)
        .reshape(parts, 2, slab, ring, parts, units_part)
        .transpose(1, 2, 4, 3, 0, 5)
        .reshape(1, 2, slab, units)
    )
    proj_grad = share([transpose_owners(v) for v in proj_g])
    proj_grad = proj_grad.transpose(1, 0, 2, 3).reshape(1, 2, slab, width)
    qkv_grad = (
        share(qkv_g)
        .reshape(parts, 2, slab, 3, head_part)
        .transpose(1, 2, 3, 0, 4)
        .reshape(1, 2, slab, 3 * width)
    )
    return (
        image_out,
        text_out,
        image_grad[0],
        image_grad[1],
        conditioning_grad,
        mod_grad_w,
        mod_grad_b,
        qkv_grad,
        bias_grads[0],
        proj_grad,
        bias_grads[1],
        hid_grad,
        bias_grads[2],
        out_grad,
        bias_grads[3],
    )


def solution(mesh):
    tokens = P("fsdp", "seq", None)
    weight = P(None, None, "fsdp", None)
    bias = P(None, None, "fsdp")
    pairs = (weight, bias) * 5
    return jax.shard_map(
        shards,
        mesh=mesh,
        in_specs=(tokens, tokens, P("fsdp", None), P("fsdp")) + pairs + (tokens, tokens),
        out_specs=(tokens, tokens, tokens, tokens, P("fsdp", None)) + pairs,
        check_vma=False,
    )
```

```python
import jax
import jax.numpy as jnp
from jax import lax
from jax.sharding import PartitionSpec as P

HEAD_DIM = 64
NORM_EPS = 1e-06
MASKED_SCORE = -1e30


def norm_rows(values):
    center = values - jnp.mean(values, -1, keepdims=True)
    return center * lax.rsqrt(jnp.mean(center * center, -1, keepdims=True) + NORM_EPS)


def modulated(values, shift, scale_up):
    return norm_rows(values) * (1.0 + scale_up) + shift


def gelu_tanh(values):
    return jax.nn.gelu(values, approximate=True)


def dot32(left, right, contract):
    return lax.dot_general(
        left, right, ((contract[0], contract[1]), ((), ())), preferred_element_type=jnp.float32
    )


def product(left, right):
    return dot32(left, right, ((1,), (0,)))


def rows_inner(left, right):
    return dot32(left, right, ((0,), (0,)))


def right_back(left, right):
    return dot32(left, right, ((1,), (1,)))


def swap_r(values):
    count = lax.axis_size("fsdp")
    return lax.ppermute(values, "fsdp", [(at, at ^ 1) for at in range(count)])


def swap_x(values):
    return lax.ppermute(values, "seq", [(at, at ^ 2) for at in range(4)])


def swap_c(values):
    return lax.ppermute(values, "seq", [(at, at ^ 1) for at in range(4)])


def group_gather(own):
    cut = own.shape[1] // 2
    a0, b0 = own[:, :cut], own[:, cut:]
    near0 = swap_c(own)
    a1 = swap_r(a0)
    b1 = swap_x(b0)
    near1 = swap_c(jnp.stack([a1, b1]))
    a2 = swap_x(jnp.stack([a0, a1]))
    b2 = swap_r(jnp.stack([b0, b1]))
    near2 = swap_c(jnp.concatenate([a2, b2], 0))

    def joined(left, right):
        return jnp.concatenate([left, right], 1)

    return {
        (0, 0, 0): own,
        (0, 0, 1): near0,
        (1, 0, 0): joined(a1, b2[0]),
        (0, 1, 0): joined(a2[0], b1),
        (1, 1, 0): joined(a2[1], b2[1]),
        (1, 0, 1): joined(near1[0], near2[2]),
        (0, 1, 1): joined(near2[0], near1[1]),
        (1, 1, 1): joined(near2[1], near2[3]),
    }


def group_reduce(pieces):
    f32, b16 = jnp.float32, jnp.bfloat16
    corners = [(0, 0), (0, 1), (1, 0), (1, 1)]
    got = swap_c(jnp.stack([pieces[at + (1,)].astype(b16) for at in corners]))
    acc = {
        at: (pieces[at + (0,)].astype(f32) + got[i].astype(f32)).astype(b16)
        for i, at in enumerate(corners)
    }
    cut = pieces[(0, 0, 0)].shape[1] // 2
    a = {at: v[:, :cut] for at, v in acc.items()}
    b = {at: v[:, cut:] for at, v in acc.items()}
    got_a = swap_x(jnp.stack([a[(0, 1)], a[(1, 1)]]))
    got_b = swap_r(jnp.stack([b[(1, 0)], b[(1, 1)]]))
    a = [(a[(dr, 0)].astype(f32) + got_a[dr].astype(f32)).astype(b16) for dr in range(2)]
    b = [(b[(0, dx)].astype(f32) + got_b[dx].astype(f32)).astype(b16) for dx in range(2)]
    last_a, last_b = swap_r(a[1]), swap_x(b[1])
    return jnp.concatenate(
        [a[0].astype(f32) + last_a.astype(f32), b[0].astype(f32) + last_b.astype(f32)], 1
    )


def shards(
    image_tokens,
    text_tokens,
    conditioning,
    text_lengths,
    mod_weight,
    mod_bias,
    qkv_weight,
    qkv_bias,
    proj_weight,
    proj_bias,
    hidden_weight,
    hidden_bias,
    output_weight,
    output_bias,
    image_cotangent,
    text_cotangent,
):
    f32, b16 = jnp.float32, jnp.bfloat16
    width = image_tokens.shape[2]
    counts = (image_tokens.shape[1], text_tokens.shape[1])
    parts = lax.axis_size("seq")
    owners = lax.axis_size("fsdp")
    line = owners // 2
    head_part = width // (2 * parts)
    heads_here = head_part // HEAD_DIM
    slab = width // owners
    units_slab = output_weight.shape[2]
    units_part = units_slab // parts
    units = units_slab * owners
    units_here = line * units_part
    score_scale = HEAD_DIM ** (-0.5)
    me = lax.axis_index("fsdp")
    s = lax.axis_index("seq")
    r = me % 2
    along = [[z * 2 + q for z in range(line)] for q in range(2)]
    direct_proj = line == parts
    image_rows, text_rows = counts[0] * parts, counts[1] * parts

    def cut(array, start, size, axis):
        return lax.dynamic_slice_in_dim(array, start, size, axis)

    def transpose_owners(values):
        pairs = [
            ((z * 2 + q) * parts + t, (t * 2 + q) * parts + z)
            for z in range(line)
            for q in range(2)
            for t in range(parts)
        ]
        return lax.ppermute(values, ("fsdp", "seq"), pairs)

    def line_gather(rows):
        return lax.all_gather(rows, "fsdp", axis=0, tiled=True, axis_index_groups=along)

    def line_reduce(term):
        return lax.psum_scatter(
            term.astype(b16), "fsdp", scatter_dimension=0, tiled=True, axis_index_groups=along
        )

    def by_r(own, other, axis):
        return jnp.where(r == 0, jnp.stack([own, other], axis), jnp.stack([other, own], axis))

    def pick(array, index, axis):
        return lax.dynamic_index_in_dim(array, index, axis, keepdims=False)

    bias_sizes = [b.shape[2] for b in (qkv_bias, proj_bias, hidden_bias, output_bias)]
    bias_local = jnp.concatenate(
        [b[0].astype(f32) for b in (qkv_bias, proj_bias, hidden_bias, output_bias)], 1
    )
    packed = jnp.concatenate(
        [conditioning.reshape(-1), bias_local.reshape(-1), jnp.tile(text_lengths.astype(f32), 128)]
    )
    everything = lax.all_gather(packed, "fsdp", axis=0)
    everyone = everything[:, :width]
    lengths = [pick(everything[:, -1], me ^ dr, 0) for dr in range(2)]
    bias_all = everything[:, width:-128].reshape(owners, 2, sum(bias_sizes))
    offsets = [0]
    for size in bias_sizes:
        offsets.append(offsets[-1] + size)
    qkv_b, proj_b, hid_b, out_b = [
        bias_all[:, :, offsets[i] : offsets[i + 1]].transpose(1, 0, 2) for i in range(4)
    ]
    group = s * 2 + r
    qkv_b = cut(qkv_b.reshape(2, 2, width), group * head_part, head_part, 2)
    qkv_b = jnp.stack([qkv_b[:, 0], jnp.zeros_like(qkv_b[:, 0]), qkv_b[:, 1]], 1).reshape(
        2, 3 * head_part
    )
    proj_b = proj_b.reshape(2, width)
    out_b = out_b.reshape(2, width)
    hid_b = pick(pick(hid_b.reshape(2, line, 2, parts, units_part), s, 3), r, 2).reshape(
        2, units_here
    )

    act_all = jax.nn.silu(everyone).astype(b16)
    act_cols = cut(act_all, me * slab, slab, 1)
    mod_part = mod_bias.shape[2]
    bias_spread = lax.dynamic_update_slice_in_dim(
        jnp.zeros((2, 6 * width), f32), mod_bias[0].astype(f32), me * mod_part, 1
    )
    term = jnp.einsum("sd,tde->ste", act_cols, mod_weight[0], preferred_element_type=f32)
    term = term + bias_spread[None]
    mods = jnp.sum(lax.all_to_all(term, "fsdp", split_axis=0, concat_axis=0, tiled=True), 0)
    mods_pair = jnp.stack([mods, swap_r(mods)], 1)

    def mod_at(index, m):
        at = slice(index * width, (index + 1) * width)
        return mods[m, None, at], mods_pair[m, :, None, at]

    shift1, scale1, gate1, shift2, scale2, gate2 = [
        [mod_at(i, m) for m in range(2)] for i in range(6)
    ]

    qkv_view = qkv_weight[0].reshape(2, slab, 3, 2 * parts, head_part)
    qkv_got = swap_r(pick(qkv_view, s * 2 + 1 - r, 3))
    qkv_mine = by_r(pick(qkv_view, group, 3), qkv_got, 1).reshape(2, 2 * slab, 3 * head_part)
    hid_view = pick(hidden_weight[0].reshape(2, slab, line, 2, parts, units_part), s, 4)
    hid_got = swap_r(pick(hid_view, 1 - r, 3))
    hid_mine = by_r(pick(hid_view, r, 3), hid_got, 1).reshape(2, 2 * slab, units_here)
    out_mine = cut(output_weight[0], s * units_part, units_part, 1)
    qkv_w = [line_gather(qkv_mine[m]) for m in range(2)]
    if direct_proj:
        chunk = slab // parts
        proj_mine = transpose_owners(cut(proj_weight[0], s * chunk, chunk, 1))
        proj_w = [line_gather(proj_mine[m]) for m in range(2)]
    else:
        proj_all = lax.all_gather(proj_weight[0], "fsdp", axis=1, tiled=True)
        proj_w = [cut(proj_all[m], group * head_part, head_part, 0) for m in range(2)]
    hid_w = [line_gather(hid_mine[m]) for m in range(2)]
    out_w = [line_gather(out_mine[m]) for m in range(2)]

    def pack(image, text):
        return jnp.concatenate([image, text], 0)

    def local_pair(values):
        return [values[: counts[0]], values[counts[0] :]]

    inner = [(0, 0), (0, 1), (1, 0), (1, 1)]

    def by_modality(pieces):
        cuts = (slice(None, counts[0]), slice(counts[0], None))
        return [
            jnp.stack(
                [
                    jnp.concatenate([pieces[(dr,) + at][c] for at in inner], 0)
                    for dr in range(2)
                ]
            )
            for c in cuts
        ]

    def by_piece(image, text):
        image = image.reshape(2, parts, counts[0], -1)
        text = text.reshape(2, parts, counts[1], -1)
        return {
            (dr,) + at: pack(image[dr, i], text[dr, i])
            for dr in range(2)
            for i, at in enumerate(inner)
        }

    def flat(values):
        return values.reshape(-1, values.shape[-1])

    x_local = [image_tokens[0].astype(f32), text_tokens[0].astype(f32)]
    g_local = [image_cotangent[0].astype(f32), text_cotangent[0].astype(f32)]
    x_full = by_modality(group_gather(pack(image_tokens[0], text_tokens[0])))
    g_full = by_modality(group_gather(pack(image_cotangent[0], text_cotangent[0])))

    hidden1 = [
        flat(modulated(x_full[m].astype(f32), shift1[m][1], scale1[m][1]).astype(b16))
        for m in range(2)
    ]
    qkv = [(product(hidden1[m], qkv_w[m]) + qkv_b[m]).astype(b16) for m in range(2)]
    all_rows = image_rows + text_rows
    joint = jnp.concatenate(
        [qkv[0].reshape(2, image_rows, -1), qkv[1].reshape(2, text_rows, -1)], 1
    ).reshape(2, all_rows, 3, heads_here, HEAD_DIM)
    text_slot = jnp.arange(text_rows)
    text_place = ((text_slot // counts[1]) ^ s) * counts[1] + text_slot % counts[1]
    valid = jnp.stack(
        [
            jnp.concatenate(
                [jnp.ones((image_rows,), bool), text_place.astype(f32) < lengths[dr]]
            )
            for dr in range(2)
        ]
    )
    query, keys_all, values_all = joint[:, :, 0], joint[:, :, 1], joint[:, :, 2]

    def masked_scores():
        raw = jnp.einsum("bqhd,bkhd->bhqk", query, keys_all, preferred_element_type=f32)
        return jnp.where(valid[:, None, None, :], raw * score_scale, MASKED_SCORE)

    masked = masked_scores()
    row_max = jnp.max(masked, -1, keepdims=True)
    log_total = row_max + jnp.log(jnp.sum(jnp.exp(masked - row_max), -1, keepdims=True))
    probs = jnp.exp(masked - log_total).astype(b16)
    mixed = jnp.einsum("bhqk,bkhd->bqhd", probs, values_all, preferred_element_type=f32)
    mixed = mixed.astype(b16).reshape(2, all_rows, head_part)
    attended = [flat(mixed[:, :image_rows]), flat(mixed[:, image_rows:])]

    def reduce_pair(image, text):
        return local_pair(group_reduce(by_piece(image, text)))

    branch = reduce_pair(*[product(attended[m], proj_w[m]).astype(b16) for m in range(2)])
    branch = [branch[m] + proj_b[m] for m in range(2)]
    middle = [x_local[m] + gate1[m][0] * branch[m] for m in range(2)]
    hidden2_local = [
        modulated(middle[m], shift2[m][0], scale2[m][0]).astype(b16) for m in range(2)
    ]
    hidden2 = [flat(v) for v in by_modality(group_gather(pack(*hidden2_local)))]
    before = [product(hidden2[m], hid_w[m]) + hid_b[m] for m in range(2)]
    active = [gelu_tanh(before[m]).astype(b16) for m in range(2)]
    result = reduce_pair(*[product(active[m], out_w[m]).astype(b16) for m in range(2)])
    result = [result[m] + out_b[m] for m in range(2)]
    image_out, text_out = [
        (middle[m] + gate2[m][0] * result[m]).astype(b16)[None] for m in range(2)
    ]

    d_gate2 = [jnp.sum(g_local[m] * result[m], 0) for m in range(2)]
    d_result = [flat((g_full[m].astype(f32) * gate2[m][1]).astype(b16)) for m in range(2)]
    out_bt = [jnp.sum((g_local[m] * gate2[m][0]).astype(b16).astype(f32), 0) for m in range(2)]
    out_g = [line_reduce(rows_inner(active[m], d_result[m])) for m in range(2)]
    d_before = []
    for m in range(2):
        d_active = right_back(d_result[m], out_w[m])
        d_before.append(jax.vjp(gelu_tanh, before[m])[1](d_active)[0].astype(b16))
    hid_bt = [jnp.sum(d_before[m].astype(f32), 0) for m in range(2)]
    hid_g = [line_reduce(rows_inner(hidden2[m], d_before[m])) for m in range(2)]
    d_hidden2 = reduce_pair(*[right_back(d_before[m], hid_w[m]).astype(b16) for m in range(2)])
    d_middle, d_branch, d_gate1, d_shift2, d_scale2, proj_bt = [], [], [], [], [], []
    for m in range(2):
        pull = jax.vjp(modulated, middle[m], shift2[m][0], scale2[m][0])[1]
        d_norm, d_shift, d_scale = pull(d_hidden2[m])
        d_middle.append(g_local[m] + d_norm)
        d_branch.append((d_middle[m] * gate1[m][0]).astype(b16))
        d_gate1.append(jnp.sum(d_middle[m] * branch[m], 0))
        d_shift2.append(d_shift[0])
        d_scale2.append(d_scale[0])
        proj_bt.append(jnp.sum(d_branch[m].astype(f32), 0))
    d_branch_full = [flat(v) for v in by_modality(group_gather(pack(*d_branch)))]
    proj_t = [rows_inner(attended[m], d_branch_full[m]) for m in range(2)]
    if direct_proj:
        proj_g = [line_reduce(v) for v in proj_t]
    d_attended = [right_back(d_branch_full[m], proj_w[m]).astype(b16) for m in range(2)]
    d_heads = jnp.concatenate(
        [d_attended[0].reshape(2, image_rows, -1), d_attended[1].reshape(2, text_rows, -1)], 1
    ).reshape(2, all_rows, heads_here, HEAD_DIM)
    probs_full = jnp.exp(masked_scores() - log_total)
    probs = probs_full.astype(b16)
    d_values = jnp.einsum("bhqk,bqhd->bkhd", probs, d_heads, preferred_element_type=f32)
    d_probs = jnp.einsum("bqhd,bkhd->bhqk", d_heads, values_all, preferred_element_type=f32)
    d_scores = (
        probs_full * (d_probs - jnp.sum(d_probs * probs_full, -1, keepdims=True))
    ).astype(b16)
    d_query = score_scale * jnp.einsum(
        "bhqk,bkhd->bqhd", d_scores, keys_all, preferred_element_type=f32
    )
    d_keys = score_scale * jnp.einsum(
        "bhqk,bqhd->bkhd", d_scores, query, preferred_element_type=f32
    )
    d_joint = jnp.stack([d_query, d_keys, d_values], 2).astype(b16)
    d_joint = d_joint.reshape(2, all_rows, 3 * head_part)
    d_qkv = [flat(d_joint[:, :image_rows]), flat(d_joint[:, image_rows:])]
    qkv_bt = [jnp.sum(d_qkv[m].astype(f32), 0).reshape(3, head_part) for m in range(2)]
    qkv_g = [line_reduce(rows_inner(hidden1[m], d_qkv[m])) for m in range(2)]
    d_hidden1 = reduce_pair(*[right_back(d_qkv[m], qkv_w[m]).astype(b16) for m in range(2)])
    token_grads, d_shift1, d_scale1 = [], [], []
    for m in range(2):
        pull = jax.vjp(modulated, x_local[m], shift1[m][0], scale1[m][0])[1]
        d_norm, d_shift, d_scale = pull(d_hidden1[m])
        token_grads.append((d_middle[m] + d_norm)[None])
        d_shift1.append(d_shift[0])
        d_scale1.append(d_scale[0])

    qkv_bt = jnp.stack(qkv_bt)[:, ::2]
    qkv_bt = lax.dynamic_update_slice_in_dim(
        jnp.zeros((2, 2, width), f32), qkv_bt, group * head_part, 2
    ).reshape(2, 2 * width)
    hid_bt = jnp.stack(hid_bt).reshape(2, line, 1, 1, units_part)
    hid_bt = lax.dynamic_update_slice(
        jnp.zeros((2, line, 2, parts, units_part), f32), hid_bt, (0, 0, r, s, 0)
    ).reshape(2, units)
    sums = jnp.concatenate(
        [
            jnp.stack(v)
            for v in (d_shift1, d_scale1, d_gate1, d_shift2, d_scale2, d_gate2)
        ]
        + [qkv_bt, jnp.stack(proj_bt), hid_bt, jnp.stack(out_bt)],
        1,
    )
    sums = sums + swap_x(sums)
    sums = sums + swap_c(sums)
    sums_all = lax.all_gather(sums.astype(b16), "fsdp", axis=0)
    d_mods = sums_all[:, :, : 6 * width]
    bias_sum = jnp.sum(sums_all[:, :, 6 * width :].astype(f32), 0)
    bias_at = [0, 2 * width, 3 * width, 3 * width + units, 4 * width + units]
    bias_grads = [
        cut(bias_sum[:, bias_at[i] : bias_at[i + 1]], me * bias_sizes[i], bias_sizes[i], 1)[None]
        for i in range(4)
    ]
    mod_grad_w = jnp.einsum("sd,ste->tde", act_cols, d_mods, preferred_element_type=f32)[None]
    mod_grad_b = jnp.sum(cut(d_mods, me * mod_part, mod_part, 2).astype(f32), 0)[None]
    d_act_cols = jnp.einsum("ste,tde->sd", d_mods, mod_weight[0], preferred_element_type=f32)
    d_act = lax.all_to_all(d_act_cols, "fsdp", split_axis=0, concat_axis=1, tiled=True)
    conditioning_grad = jax.vjp(jax.nn.silu, conditioning)[1](d_act)[0]

    def share(values):
        return lax.all_gather(jnp.stack(values), "seq", axis=0).astype(f32)

    def both_r(values):
        rows = values.reshape(2, slab, -1)
        return by_r(pick(rows, r, 0), swap_r(pick(rows, 1 - r, 0)), 0)

    out_grad = share(out_g).transpose(1, 0, 2, 3).reshape(1, 2, units_slab, width)
    hid_grad = (
        share([both_r(v) for v in hid_g])
        .reshape(parts, 2, 2, slab, line, units_part)
        .transpose(1, 3, 4, 2, 0, 5)
        .reshape(1, 2, slab, units)
    )
    if direct_proj:
        proj_grad = share([transpose_owners(v) for v in proj_g])
        proj_grad = proj_grad.transpose(1, 0, 2, 3).reshape(1, 2, slab, width)
    else:
        proj_grad = []
        for m in range(2):
            spread = lax.dynamic_update_slice_in_dim(
                jnp.zeros((width, width), f32), proj_t[m], group * head_part, 0
            ).astype(b16)
            own = lax.psum_scatter(spread, "fsdp", scatter_dimension=0, tiled=True)
            proj_grad.append(lax.psum(own, "seq").astype(f32))
        proj_grad = jnp.stack(proj_grad)[None]
    qkv_grad = (
        share([both_r(v) for v in qkv_g])
        .reshape(parts, 2, 2, slab, 3, head_part)
        .transpose(1, 3, 4, 0, 2, 5)
        .reshape(1, 2, slab, 3 * width)
    )
    return (
        image_out,
        text_out,
        token_grads[0],
        token_grads[1],
        conditioning_grad,
        mod_grad_w,
        mod_grad_b,
        qkv_grad,
        bias_grads[0],
        proj_grad,
        bias_grads[1],
        hid_grad,
        bias_grads[2],
        out_grad,
        bias_grads[3],
    )


def solution(mesh):
    tokens = P("fsdp", "seq", None)
    weight = P(None, None, "fsdp", None)
    bias = P(None, None, "fsdp")
    pairs = (weight, bias) * 5
    return jax.shard_map(
        shards,
        mesh=mesh,
        in_specs=(tokens, tokens, P("fsdp", None), P("fsdp")) + pairs + (tokens, tokens),
        out_specs=(tokens, tokens, tokens, tokens, P("fsdp", None)) + pairs,
        check_vma=False,
    )
```

```python
import functools

import jax
import jax.numpy as jnp
from jax import lax
from jax.experimental import pallas as pl
from jax.experimental.pallas import tpu as pltpu
from jax.sharding import PartitionSpec as P

HEAD_DIM = 64
NORM_EPS = 1e-06
MASKED_SCORE = -1e30
VMEM_LIMIT = 60 * 2**20


def mm(left, right):
    return lax.dot_general(left, right, (((1,), (0,)), ((), ())), preferred_element_type=jnp.float32)


def key_scores(key_image, key_text, query_t, open_text, scale):
    image = mm(key_image, query_t) * scale
    text = jnp.where(open_text > 0.0, mm(key_text, query_t) * scale, MASKED_SCORE)
    return image, text


def attention_kernel(part, scale, image_ref, text_ref, open_ref, out_image, out_text, lse_image, lse_text):
    heads = part // HEAD_DIM
    b16 = jnp.bfloat16
    open_text = open_ref[0, :, :1]

    def columns(ref, kind, head):
        return ref[0, :, kind * part + head * HEAD_DIM : kind * part + (head + 1) * HEAD_DIM]

    keys = [(columns(image_ref, 1, h), columns(text_ref, 1, h)) for h in range(heads)]
    values_t = (image_ref[0, :, 2 * part :].T, text_ref[0, :, 2 * part :].T)

    def block(queries, width):
        queries_t = queries.T
        mixed, lse = [], []
        for h in range(heads):
            at = slice(h * HEAD_DIM, (h + 1) * HEAD_DIM)
            image, text = key_scores(*keys[h], queries_t[at], open_text, scale)
            top = jnp.maximum(
                jnp.max(image, 0, keepdims=True), jnp.max(text, 0, keepdims=True)
            )
            image, text = jnp.exp(image - top), jnp.exp(text - top)
            total = jnp.sum(image, 0, keepdims=True) + jnp.sum(text, 0, keepdims=True)
            out_t = mm(values_t[0][at], image.astype(b16)) + mm(values_t[1][at], text.astype(b16))
            mixed.append(out_t / total)
            lse.append(top + jnp.log(total))
        lse.append(jnp.zeros((8 - heads, width), jnp.float32))
        return jnp.concatenate(mixed, 0).T.astype(b16), jnp.concatenate(lse, 0)

    step = 256

    def body(i, carry):
        rows = pl.ds(pl.multiple_of(i * step, step), step)
        mixed, lse = block(image_ref[0, rows, :part], step)
        out_image[0, rows, :] = mixed
        lse_image[0, :, rows] = lse
        return carry

    lax.fori_loop(0, image_ref.shape[1] // step, body, 0)
    mixed, lse = block(text_ref[0, :, :part], text_ref.shape[1])
    out_text[0] = mixed
    lse_text[0] = lse


def attention(image_qkv, text_qkv, open_text, scale):
    two, image_rows, columns = image_qkv.shape
    text_rows, part = text_qkv.shape[1], columns // 3

    def spec(*dims):
        return pl.BlockSpec((1,) + dims, lambda i: (i, 0, 0))

    return pl.pallas_call(
        functools.partial(attention_kernel, part, scale),
        grid=(two,),
        in_specs=[spec(image_rows, columns), spec(text_rows, columns), spec(text_rows, 128)],
        out_specs=[
            spec(image_rows, part),
            spec(text_rows, part),
            spec(8, image_rows),
            spec(8, text_rows),
        ],
        out_shape=[
            jax.ShapeDtypeStruct((two, image_rows, part), jnp.bfloat16),
            jax.ShapeDtypeStruct((two, text_rows, part), jnp.bfloat16),
            jax.ShapeDtypeStruct((two, 8, image_rows), jnp.float32),
            jax.ShapeDtypeStruct((two, 8, text_rows), jnp.float32),
        ],
        compiler_params=pltpu.CompilerParams(vmem_limit_bytes=VMEM_LIMIT),
        name="attention",
    )(image_qkv, text_qkv, open_text)


def attention_back_kernel(
    part, scale, image_ref, text_ref, open_ref, lse_image, lse_text, up_image, up_text,
    out_image, out_text, d_keys, d_values,
):
    heads = part // HEAD_DIM
    b16 = jnp.bfloat16
    open_text = open_ref[0, :, :1]
    image_rows = image_ref.shape[1]

    def columns(ref, kind, head):
        return ref[0, :, kind * part + head * HEAD_DIM : kind * part + (head + 1) * HEAD_DIM]

    keys = [(columns(image_ref, 1, h), columns(text_ref, 1, h)) for h in range(heads)]
    values = [(columns(image_ref, 2, h), columns(text_ref, 2, h)) for h in range(heads)]
    keys_t = (image_ref[0, :, part : 2 * part].T, text_ref[0, :, part : 2 * part].T)

    def block(queries, ups, lse, first):
        queries_t, ups_t = queries.T, ups.T
        d_queries = []
        for h in range(heads):
            at = slice(h * HEAD_DIM, (h + 1) * HEAD_DIM)
            image, text = key_scores(*keys[h], queries_t[at], open_text, scale)
            row = lse[h : h + 1]
            image, text = jnp.exp(image - row), jnp.exp(text - row)
            up_rows = ups[:, at]
            terms = (mm(image.astype(b16), up_rows), mm(text.astype(b16), up_rows))
            d_image = mm(values[h][0], ups_t[at]) * image
            d_text = mm(values[h][1], ups_t[at]) * text
            row = jnp.sum(d_image, 0, keepdims=True) + jnp.sum(d_text, 0, keepdims=True)
            d_image = (d_image - row * image).astype(b16)
            d_text = (d_text - row * text).astype(b16)
            query_rows = queries[:, at]
            more = (mm(d_image, query_rows), mm(d_text, query_rows))
            d_queries.append((mm(keys_t[0][at], d_image) + mm(keys_t[1][at], d_text)) * scale)
            for ref, (a, b) in ((d_values, terms), (d_keys, more)):
                if first:
                    ref[h, :image_rows] = a
                    ref[h, image_rows:] = b
                else:
                    ref[h, :image_rows] += a
                    ref[h, image_rows:] += b
        return jnp.concatenate(d_queries, 0).T.astype(b16)

    step = 256
    out_text[0, :, :part] = block(text_ref[0, :, :part], up_text[0], lse_text[0], True)

    def body(i, carry):
        rows = pl.ds(pl.multiple_of(i * step, step), step)
        out_image[0, rows, :part] = block(
            image_ref[0, rows, :part], up_image[0, rows, :], lse_image[0, :, rows], False
        )
        return carry

    lax.fori_loop(0, image_rows // step, body, 0)
    for h in range(heads):
        for kind, ref, factor in ((1, d_keys, scale), (2, d_values, 1.0)):
            at = slice(kind * part + h * HEAD_DIM, kind * part + (h + 1) * HEAD_DIM)
            out_image[0, :, at] = (ref[h, :image_rows] * factor).astype(b16)
            out_text[0, :, at] = (ref[h, image_rows:] * factor).astype(b16)


def attention_back(image_qkv, text_qkv, open_text, lse_image, lse_text, up_image, up_text, scale):
    two, image_rows, columns = image_qkv.shape
    text_rows, part = text_qkv.shape[1], columns // 3
    heads = part // HEAD_DIM

    def spec(*dims):
        return pl.BlockSpec((1,) + dims, lambda i: (i, 0, 0))

    return pl.pallas_call(
        functools.partial(attention_back_kernel, part, scale),
        grid=(two,),
        in_specs=[
            spec(image_rows, columns),
            spec(text_rows, columns),
            spec(text_rows, 128),
            spec(8, image_rows),
            spec(8, text_rows),
            spec(image_rows, part),
            spec(text_rows, part),
        ],
        out_specs=[spec(image_rows, columns), spec(text_rows, columns)],
        out_shape=[
            jax.ShapeDtypeStruct(image_qkv.shape, jnp.bfloat16),
            jax.ShapeDtypeStruct(text_qkv.shape, jnp.bfloat16),
        ],
        scratch_shapes=[
            pltpu.VMEM((heads, image_rows + text_rows, HEAD_DIM), jnp.float32),
            pltpu.VMEM((heads, image_rows + text_rows, HEAD_DIM), jnp.float32),
        ],
        compiler_params=pltpu.CompilerParams(vmem_limit_bytes=VMEM_LIMIT),
        name="attention_back",
    )(image_qkv, text_qkv, open_text, lse_image, lse_text, up_image, up_text)


MESH = pl.DeviceIdType.MESH


def modulation_kernel(
    owners, parts, slab, send, weight, small_out, act_out, mods_out,
    small, piece, term, got, mods, load_sem, sems,
):
    f, s = lax.axis_index("fsdp"), lax.axis_index("seq")
    quarter = piece.shape[2]
    columns = pl.ds(pl.multiple_of(s * quarter, 128), quarter)
    load = pltpu.make_async_copy(weight.at[:, :, columns], piece, load_sem)
    load.start()
    barrier = pltpu.get_barrier_semaphore()
    for k in range(1, owners):
        pl.semaphore_signal(
            barrier, inc=1, device_id=(lax.rem(f + k, owners), s), device_id_type=MESH
        )
    for q in range(1, parts):
        pl.semaphore_signal(barrier, inc=1, device_id=(f, s ^ q), device_id_type=MESH)
    pl.semaphore_wait(barrier, owners + parts - 2)

    def exchange(source, target, stage):
        copies = []
        for k in range(1, owners):
            peer = lax.rem(f + k, owners)
            copy = pltpu.make_async_remote_copy(
                src_ref=source.at[peer],
                dst_ref=target.at[f],
                send_sem=sems.at[stage, 0, k],
                recv_sem=sems.at[stage, 1, k],
                device_id=(peer, s),
                device_id_type=MESH,
            )
            copy.start()
            copies.append(copy)
        target[f] = source[f]
        for copy in copies:
            copy.wait()

    exchange(send, small, 0)
    small_out[...] = small[...]
    act = jnp.concatenate([small[k, :, :slab] for k in range(owners)], 0)
    act = (act / (1.0 + jnp.exp(-act))).astype(jnp.bfloat16)
    act_out[...] = act
    load.wait()
    for m in range(2):
        full = mm(act, piece[m])
        for k in range(owners):
            for dr in range(2):
                term[k, dr * 2 + m : dr * 2 + m + 1, :] = full[k ^ dr : (k ^ dr) + 1]
    exchange(term, got, 1)
    total = got[0]
    for k in range(1, owners):
        total = total + got[k]
    mods[s] = total
    copies = []
    for q in range(1, parts):
        copy = pltpu.make_async_remote_copy(
            src_ref=mods.at[s],
            dst_ref=mods.at[s],
            send_sem=sems.at[2, 0, q],
            recv_sem=sems.at[2, 1, q],
            device_id=(f, s ^ q),
            device_id_type=MESH,
        )
        copy.start()
        copies.append(copy)
    for copy in copies:
        copy.wait()
    mods_out[...] = mods[...]


def modulation(send, weight, owners, parts):
    slab, columns = weight.shape[1], weight.shape[2]
    quarter = columns // parts
    f32 = jnp.float32
    return pl.pallas_call(
        functools.partial(modulation_kernel, owners, parts, slab),
        in_specs=[
            pl.BlockSpec(memory_space=pltpu.VMEM),
            pl.BlockSpec(memory_space=pl.ANY),
        ],
        out_specs=[pl.BlockSpec(memory_space=pltpu.VMEM)] * 3,
        out_shape=[
            jax.ShapeDtypeStruct(send.shape, f32),
            jax.ShapeDtypeStruct((owners, slab), jnp.bfloat16),
            jax.ShapeDtypeStruct((parts, 4, quarter), f32),
        ],
        scratch_shapes=[
            pltpu.VMEM(send.shape, f32),
            pltpu.VMEM((2, slab, quarter), jnp.bfloat16),
            pltpu.VMEM((owners, 4, quarter), f32),
            pltpu.VMEM((owners, 4, quarter), f32),
            pltpu.VMEM((parts, 4, quarter), f32),
            pltpu.SemaphoreType.DMA,
            pltpu.SemaphoreType.DMA((3, 2, owners)),
        ],
        compiler_params=pltpu.CompilerParams(
            collective_id=1, has_side_effects=True, vmem_limit_bytes=VMEM_LIMIT
        ),
        cost_estimate=pl.CostEstimate(
            flops=4 * owners * slab * quarter, bytes_accessed=60_000_000, transcendentals=0
        ),
        name="modulation",
    )(send, weight)


def pick_kernel(part, line, place, *refs):
    qkv, hid = refs[:3], refs[3 : 3 + 2 * line]
    qkv_own, qkv_other, hid_own, hid_other = refs[3 + 2 * line :]
    high, odd = place[1] == 1, place[2] == 1
    for kind in range(3):
        at = slice(kind * part, (kind + 1) * part)
        low, up = qkv[kind][:, :, :part], qkv[kind][:, :, part:]
        qkv_own[:, :, at] = jnp.where(high, up, low)
        qkv_other[:, :, at] = jnp.where(high, low, up)
    for z in range(line):
        chosen = []
        for q in range(2):
            block = hid[z * 2 + q]
            cut = block.shape[2] // 2
            chosen.append(jnp.where(odd, block[:, :, cut:], block[:, :, :cut]))
        at = slice(z * cut, (z + 1) * cut)
        hid_own[:, :, at] = jnp.where(high, chosen[1], chosen[0])
        hid_other[:, :, at] = jnp.where(high, chosen[0], chosen[1])


def pick_parts(qkv_weight, hidden_weight, s, r, part, line):
    slab, width = qkv_weight.shape[1], qkv_weight.shape[2] // 3
    units = hidden_weight.shape[2] // (2 * line)
    place = jnp.stack([s, r, s % 2]).astype(jnp.int32)
    per_kind = width // (2 * part)

    def qkv_spec(kind):
        return pl.BlockSpec((2, slab, 2 * part), lambda i, at: (0, 0, kind * per_kind + at[0]))

    def hid_spec(f):
        return pl.BlockSpec((2, slab, units // 2), lambda i, at: (0, 0, 2 * f + at[0] // 2))

    shapes = [(2, slab, 3 * part)] * 2 + [(2, slab, line * units // 4)] * 2
    return pl.pallas_call(
        functools.partial(pick_kernel, part, line),
        grid_spec=pltpu.PrefetchScalarGridSpec(
            num_scalar_prefetch=1,
            grid=(1,),
            in_specs=[qkv_spec(k) for k in range(3)] + [hid_spec(f) for f in range(2 * line)],
            out_specs=[pl.BlockSpec(dims, lambda i, at: (0, 0, 0)) for dims in shapes],
        ),
        out_shape=[jax.ShapeDtypeStruct(dims, jnp.bfloat16) for dims in shapes],
        compiler_params=pltpu.CompilerParams(vmem_limit_bytes=VMEM_LIMIT),
        name="pick_parts",
    )(place, *([qkv_weight] * 3), *([hidden_weight] * (2 * line)))


def chosen_piece(pieces, x, c, q):
    near = [jnp.where(c == q % 2, pieces[2 * dx], pieces[2 * dx + 1]) for dx in range(2)]
    return jnp.where(x == q // 2, near[0], near[1])


def columns_kernel(chunk, kinds, inner_first, place, *refs):
    out = refs[8]
    r, x, c = place[0], place[1], place[2]
    for kind in range(kinds):
        at = slice(kind * chunk, (kind + 1) * chunk)
        by_dr = [
            [chosen_piece([refs[dr * 4 + p][0, :, at] for p in range(4)], x, c, q) for q in range(4)]
            for dr in range(2)
        ]
        for q in range(4):
            for natural in range(2):
                value = jnp.where(r == natural, by_dr[0][q], by_dr[1][q])
                spot = q * 2 + natural if inner_first else natural * 4 + q
                start = (kind * 8 + spot) * chunk
                out[0, 0, :, start : start + chunk] = value.astype(jnp.float32)


def join_columns(pieces, place, chunk, kinds, inner_first):
    rows, columns = pieces[0].shape[1:]
    step = 64 if rows % 64 == 0 else rows
    return pl.pallas_call(
        functools.partial(columns_kernel, chunk, kinds, inner_first),
        grid_spec=pltpu.PrefetchScalarGridSpec(
            num_scalar_prefetch=1,
            grid=(2, rows // step),
            in_specs=[pl.BlockSpec((1, step, columns), lambda m, i, at: (m, i, 0))] * 8,
            out_specs=pl.BlockSpec((1, 1, step, 8 * columns), lambda m, i, at: (0, m, i, 0)),
        ),
        out_shape=jax.ShapeDtypeStruct((1, 2, rows, 8 * columns), jnp.float32),
        compiler_params=pltpu.CompilerParams(vmem_limit_bytes=VMEM_LIMIT),
        name="join_columns",
    )(place, *pieces)


def rows_kernel(place, *refs):
    out = refs[4]
    rows = refs[0].shape[1]
    for q in range(4):
        value = chosen_piece([refs[p][0] for p in range(4)], place[1], place[2], q)
        out[0, 0, q * rows : (q + 1) * rows, :] = value.astype(jnp.float32)


def join_rows(pieces, place):
    rows, columns = pieces[0].shape[1:]
    step = columns // 2
    return pl.pallas_call(
        rows_kernel,
        grid_spec=pltpu.PrefetchScalarGridSpec(
            num_scalar_prefetch=1,
            grid=(2, 2),
            in_specs=[pl.BlockSpec((1, rows, step), lambda m, i, at: (m, 0, i))] * 4,
            out_specs=pl.BlockSpec((1, 1, 4 * rows, step), lambda m, i, at: (0, m, 0, i)),
        ),
        out_shape=jax.ShapeDtypeStruct((1, 2, 4 * rows, columns), jnp.float32),
        compiler_params=pltpu.CompilerParams(vmem_limit_bytes=VMEM_LIMIT),
        name="join_rows",
    )(place, *pieces)


def together(*values):
    return lax.optimization_barrier(values)


def norm_rows(values):
    center = values - jnp.mean(values, -1, keepdims=True)
    return center * lax.rsqrt(jnp.mean(center * center, -1, keepdims=True) + NORM_EPS)


def modulated(values, shift, scale_up):
    return norm_rows(values) * (1.0 + scale_up) + shift


def gelu_tanh(values):
    return jax.nn.gelu(values, approximate=True)


def dot32(left, right, contract):
    return lax.dot_general(
        left, right, ((contract[0], contract[1]), ((), ())), preferred_element_type=jnp.float32
    )


def product(left, right):
    return dot32(left, right, ((1,), (0,)))


def rows_inner(left, right):
    return dot32(left, right, ((0,), (0,)))


def right_back(left, right):
    return dot32(left, right, ((1,), (1,)))


def swap_r(values):
    count = lax.axis_size("fsdp")
    return lax.ppermute(values, "fsdp", [(at, at ^ 1) for at in range(count)])


def swap_x(values):
    return lax.ppermute(values, "seq", [(at, at ^ 2) for at in range(4)])


def swap_c(values):
    return lax.ppermute(values, "seq", [(at, at ^ 1) for at in range(4)])


def group_gather(own):
    cut = own.shape[1] // 2
    a0, b0 = own[:, :cut], own[:, cut:]
    near0 = swap_c(own)
    a1 = swap_r(a0)
    b1 = swap_x(b0)
    near1 = swap_c(jnp.stack([a1, b1]))
    a2 = swap_x(jnp.stack([a0, a1]))
    b2 = swap_r(jnp.stack([b0, b1]))
    near2 = swap_c(jnp.concatenate([a2, b2], 0))

    def joined(left, right):
        return jnp.concatenate([left, right], 1)

    return {
        (0, 0, 0): own,
        (0, 0, 1): near0,
        (1, 0, 0): joined(a1, b2[0]),
        (0, 1, 0): joined(a2[0], b1),
        (1, 1, 0): joined(a2[1], b2[1]),
        (1, 0, 1): joined(near1[0], near2[2]),
        (0, 1, 1): joined(near2[0], near1[1]),
        (1, 1, 1): joined(near2[1], near2[3]),
    }


def group_reduce(pieces, meanwhile=None):
    f32, b16 = jnp.float32, jnp.bfloat16
    corners = [(0, 0), (0, 1), (1, 0), (1, 1)]
    got = swap_c(jnp.stack([pieces[at + (1,)].astype(b16) for at in corners]))
    acc = {
        at: (pieces[at + (0,)].astype(f32) + got[i].astype(f32)).astype(b16)
        for i, at in enumerate(corners)
    }
    cut = pieces[(0, 0, 0)].shape[1] // 2
    a = {at: v[:, :cut] for at, v in acc.items()}
    b = {at: v[:, cut:] for at, v in acc.items()}
    got_a = swap_x(jnp.stack([a[(0, 1)], a[(1, 1)]]))
    got_b = swap_r(jnp.stack([b[(1, 0)], b[(1, 1)]]))
    if meanwhile is not None:
        got_a, got_b, meanwhile = together(got_a, got_b, meanwhile)
    a = [(a[(dr, 0)].astype(f32) + got_a[dr].astype(f32)).astype(b16) for dr in range(2)]
    b = [(b[(0, dx)].astype(f32) + got_b[dx].astype(f32)).astype(b16) for dx in range(2)]
    last_a, last_b = swap_r(a[1]), swap_x(b[1])
    total = jnp.concatenate(
        [a[0].astype(f32) + last_a.astype(f32), b[0].astype(f32) + last_b.astype(f32)], 1
    )
    return total if meanwhile is None else (total, meanwhile)


def shards(
    image_tokens,
    text_tokens,
    conditioning,
    text_lengths,
    mod_weight,
    mod_bias,
    qkv_weight,
    qkv_bias,
    proj_weight,
    proj_bias,
    hidden_weight,
    hidden_bias,
    output_weight,
    output_bias,
    image_cotangent,
    text_cotangent,
):
    f32, b16 = jnp.float32, jnp.bfloat16
    width = image_tokens.shape[2]
    counts = (image_tokens.shape[1], text_tokens.shape[1])
    parts = lax.axis_size("seq")
    owners = lax.axis_size("fsdp")
    line = owners // 2
    head_part = width // (2 * parts)
    heads_here = head_part // HEAD_DIM
    slab = width // owners
    units_slab = output_weight.shape[2]
    units_part = units_slab // parts
    units = units_slab * owners
    units_here = line * units_part
    score_scale = HEAD_DIM ** (-0.5)
    me = lax.axis_index("fsdp")
    s = lax.axis_index("seq")
    r = me % 2
    along = [[z * 2 + q for z in range(line)] for q in range(2)]
    direct_proj = line == parts
    image_rows, text_rows = counts[0] * parts, counts[1] * parts

    def cut(array, start, size, axis):
        return lax.dynamic_slice_in_dim(array, start, size, axis)

    def transpose_owners(values):
        pairs = [
            ((z * 2 + q) * parts + t, (t * 2 + q) * parts + z)
            for z in range(line)
            for q in range(2)
            for t in range(parts)
        ]
        return lax.ppermute(values, ("fsdp", "seq"), pairs)

    def line_gather(rows):
        return lax.all_gather(rows, "fsdp", axis=1, tiled=True, axis_index_groups=along)

    def line_reduce(term):
        return lax.psum_scatter(
            term, "fsdp", scatter_dimension=1, tiled=True, axis_index_groups=along
        )

    def weight_terms(left, right):
        return jnp.stack([rows_inner(left[m], right[m]).astype(b16) for m in range(2)])

    def by_r(own, other, axis):
        return jnp.where(r == 0, jnp.stack([own, other], axis), jnp.stack([other, own], axis))

    def pick(array, index, axis):
        return lax.dynamic_index_in_dim(array, index, axis, keepdims=False)

    biases = (mod_bias, qkv_bias, proj_bias, hidden_bias, output_bias)
    bias_sizes = [v.shape[2] for v in biases]
    bias_local = jnp.concatenate([v[0].astype(f32) for v in biases], 1)
    padded = -(-slab // 128) * 128
    common = jnp.concatenate([bias_local.reshape(-1), jnp.tile(text_lengths.astype(f32), 128)])
    send = jnp.concatenate(
        [
            conditioning.reshape(owners, slab),
            jnp.zeros((owners, padded - slab), f32),
            jnp.broadcast_to(common, (owners, common.shape[0])),
        ],
        1,
    )
    small, act_cols, mods = modulation(send[:, None], mod_weight[0], owners, parts)
    small = small[:, 0, padded:]
    lengths = [pick(small[:, -1], me ^ dr, 0) for dr in range(2)]
    bias_all = small[:, :-128].reshape(owners, 2, sum(bias_sizes))
    offsets = [0]
    for size in bias_sizes:
        offsets.append(offsets[-1] + size)
    mod_b, qkv_b, proj_b, hid_b, out_b = [
        bias_all[:, :, offsets[i] : offsets[i + 1]].transpose(1, 0, 2) for i in range(5)
    ]
    group = s * 2 + r
    qkv_b = cut(qkv_b.reshape(2, 2, width), group * head_part, head_part, 2)
    qkv_b = jnp.stack([qkv_b[:, 0], jnp.zeros_like(qkv_b[:, 0]), qkv_b[:, 1]], 1).reshape(
        2, 3 * head_part
    )
    proj_b = proj_b.reshape(2, width)
    out_b = out_b.reshape(2, width)
    hid_b = pick(pick(hid_b.reshape(2, line, 2, parts, units_part), s, 3), r, 2).reshape(
        2, units_here
    )
    mods = mods.reshape(parts, 2, 2, -1).transpose(1, 2, 0, 3).reshape(2, 2, 6 * width)
    mods = mods + mod_b.reshape(2, 6 * width)
    mod_part = mod_bias.shape[2]

    def mod_at(index, m):
        at = slice(index * width, (index + 1) * width)
        return mods[0, m, None, at], mods[:, m, None, at]

    shift1, scale1, gate1, shift2, scale2, gate2 = [
        [mod_at(i, m) for m in range(2)] for i in range(6)
    ]

    if direct_proj:
        chunk = slab // parts
        proj_mine = transpose_owners(cut(proj_weight[0], s * chunk, chunk, 1))
        proj_w = line_gather(proj_mine)
    else:
        proj_all = lax.all_gather(proj_weight[0], "fsdp", axis=1, tiled=True)
        proj_w = cut(proj_all, group * head_part, head_part, 1)
    if (2 * head_part) % 128 == 0 and (2 * units_part) % 128 == 0:
        qkv_own, qkv_other, hid_own, hid_other = pick_parts(
            qkv_weight[0], hidden_weight[0], s, r, head_part, line
        )
    else:
        qkv_view = qkv_weight[0].reshape(2, slab, 3, 2 * parts, head_part)
        qkv_own, qkv_other = [
            pick(qkv_view, s * 2 + at, 3).reshape(2, slab, 3 * head_part) for at in (r, 1 - r)
        ]
        hid_view = pick(hidden_weight[0].reshape(2, slab, line, 2, parts, units_part), s, 4)
        hid_own, hid_other = [
            pick(hid_view, at, 3).reshape(2, slab, units_here) for at in (r, 1 - r)
        ]
    qkv_mine = by_r(qkv_own, swap_r(qkv_other), 1).reshape(2, 2 * slab, 3 * head_part)
    qkv_w = line_gather(qkv_mine)
    hid_mine = by_r(hid_own, swap_r(hid_other), 1).reshape(2, 2 * slab, units_here)
    hid_w = line_gather(hid_mine)
    out_w = line_gather(cut(output_weight[0], s * units_part, units_part, 1))

    def pack(image, text):
        return jnp.concatenate([image, text], 0)

    def local_pair(values):
        return [values[: counts[0]], values[counts[0] :]]

    inner = [(0, 0), (0, 1), (1, 0), (1, 1)]

    def by_modality(pieces):
        cuts = (slice(None, counts[0]), slice(counts[0], None))
        return [
            jnp.stack(
                [
                    jnp.concatenate([pieces[(dr,) + at][c] for at in inner], 0)
                    for dr in range(2)
                ]
            )
            for c in cuts
        ]

    def by_piece(image, text):
        image = image.reshape(2, parts, counts[0], -1)
        text = text.reshape(2, parts, counts[1], -1)
        return {
            (dr,) + at: pack(image[dr, i], text[dr, i])
            for dr in range(2)
            for i, at in enumerate(inner)
        }

    def flat(values):
        return values.reshape(-1, values.shape[-1])

    x_local = [image_tokens[0].astype(f32), text_tokens[0].astype(f32)]
    g_local = [image_cotangent[0].astype(f32), text_cotangent[0].astype(f32)]
    x_full = by_modality(group_gather(pack(image_tokens[0], text_tokens[0])))
    g_full = by_modality(group_gather(pack(image_cotangent[0], text_cotangent[0])))

    hidden1 = [
        flat(modulated(x_full[m].astype(f32), shift1[m][1], scale1[m][1]).astype(b16))
        for m in range(2)
    ]
    qkv = [(product(hidden1[m], qkv_w[m]) + qkv_b[m]).astype(b16) for m in range(2)]
    qkv = [v.reshape(2, -1, 3 * head_part) for v in qkv]
    text_slot = jnp.arange(text_rows)
    text_place = ((text_slot // counts[1]) ^ s) * counts[1] + text_slot % counts[1]
    open_text = jnp.stack([(text_place.astype(f32) < n).astype(f32) for n in lengths])
    open_text = jnp.broadcast_to(open_text[:, :, None], (2, text_rows, 128))
    mixed_image, mixed_text, lse_image, lse_text = attention(*qkv, open_text, score_scale)
    attended = [flat(mixed_image), flat(mixed_text)]

    def reduce_pair(image, text, meanwhile=None):
        total = group_reduce(by_piece(image, text), meanwhile)
        if meanwhile is None:
            return local_pair(total)
        return local_pair(total[0]), total[1]

    branch = reduce_pair(*[product(attended[m], proj_w[m]).astype(b16) for m in range(2)])
    branch = [branch[m] + proj_b[m] for m in range(2)]
    middle = [x_local[m] + gate1[m][0] * branch[m] for m in range(2)]
    hidden2_local = [
        modulated(middle[m], shift2[m][0], scale2[m][0]).astype(b16) for m in range(2)
    ]
    hidden2 = [flat(v) for v in by_modality(group_gather(pack(*hidden2_local)))]
    before = [product(hidden2[m], hid_w[m]) + hid_b[m] for m in range(2)]
    active = [gelu_tanh(before[m]).astype(b16) for m in range(2)]

    d_result = [flat((g_full[m].astype(f32) * gate2[m][1]).astype(b16)) for m in range(2)]
    out_bt = [jnp.sum((g_local[m] * gate2[m][0]).astype(b16).astype(f32), 0) for m in range(2)]
    out_t = weight_terms(active, d_result)
    out_g = line_reduce(out_t)
    d_result[0], d_result[1], _ = together(*d_result, out_t)
    d_before = []
    for m in range(2):
        d_active = right_back(d_result[m], out_w[m])
        d_before.append(jax.vjp(gelu_tanh, before[m])[1](d_active)[0].astype(b16))
    hid_bt = [jnp.sum(d_before[m].astype(f32), 0) for m in range(2)]
    hid_t = weight_terms(hidden2, d_before)
    d_hidden2, hid_t = reduce_pair(
        *[right_back(d_before[m], hid_w[m]).astype(b16) for m in range(2)], meanwhile=hid_t
    )
    hid_g = line_reduce(hid_t)
    d_middle, d_branch, d_gate1, d_shift2, d_scale2, proj_bt = [], [], [], [], [], []
    for m in range(2):
        pull = jax.vjp(modulated, middle[m], shift2[m][0], scale2[m][0])[1]
        d_norm, d_shift, d_scale = pull(d_hidden2[m])
        d_middle.append(g_local[m] + d_norm)
        d_branch.append((d_middle[m] * gate1[m][0]).astype(b16))
        d_gate1.append(jnp.sum(d_middle[m] * branch[m], 0))
        d_shift2.append(d_shift[0])
        d_scale2.append(d_scale[0])
        proj_bt.append(jnp.sum(d_branch[m].astype(f32), 0))
    d_branch_full = [flat(v) for v in by_modality(group_gather(pack(*d_branch)))]
    result_part = [product(active[m], out_w[m]).astype(b16) for m in range(2)]
    proj_t = weight_terms(attended, d_branch_full)
    if direct_proj:
        proj_g = line_reduce(proj_t)
    d_attended = [
        right_back(d_branch_full[m], proj_w[m]).astype(b16).reshape(2, -1, head_part)
        for m in range(2)
    ]
    d_attended[0], d_attended[1], proj_t, result_part = together(
        *d_attended, proj_t, result_part
    )
    d_qkv = attention_back(*qkv, open_text, lse_image, lse_text, *d_attended, score_scale)
    d_qkv = [flat(v) for v in d_qkv]
    qkv_t = weight_terms(hidden1, d_qkv)
    qkv_g = line_reduce(qkv_t)
    d_qkv[0], d_qkv[1], qkv_t = together(*d_qkv, qkv_t)
    qkv_bt = [jnp.sum(d_qkv[m].astype(f32), 0).reshape(3, head_part) for m in range(2)]
    d_hidden1 = reduce_pair(*[right_back(d_qkv[m], qkv_w[m]).astype(b16) for m in range(2)])
    result = reduce_pair(*result_part)
    result = [result[m] + out_b[m] for m in range(2)]
    image_out, text_out = [
        (middle[m] + gate2[m][0] * result[m]).astype(b16)[None] for m in range(2)
    ]
    d_gate2 = [jnp.sum(g_local[m] * result[m], 0) for m in range(2)]
    token_grads, d_shift1, d_scale1 = [], [], []
    for m in range(2):
        pull = jax.vjp(modulated, x_local[m], shift1[m][0], scale1[m][0])[1]
        d_norm, d_shift, d_scale = pull(d_hidden1[m])
        token_grads.append((d_middle[m] + d_norm)[None])
        d_shift1.append(d_shift[0])
        d_scale1.append(d_scale[0])

    qkv_bt = jnp.stack(qkv_bt)[:, ::2]
    qkv_bt = lax.dynamic_update_slice_in_dim(
        jnp.zeros((2, 2, width), f32), qkv_bt, group * head_part, 2
    ).reshape(2, 2 * width)
    hid_bt = jnp.stack(hid_bt).reshape(2, line, 1, 1, units_part)
    hid_bt = lax.dynamic_update_slice(
        jnp.zeros((2, line, 2, parts, units_part), f32), hid_bt, (0, 0, r, s, 0)
    ).reshape(2, units)
    sums = jnp.concatenate(
        [
            jnp.stack(v)
            for v in (d_shift1, d_scale1, d_gate1, d_shift2, d_scale2, d_gate2)
        ]
        + [qkv_bt, jnp.stack(proj_bt), hid_bt, jnp.stack(out_bt)],
        1,
    )
    sums = sums + swap_x(sums)
    sums = sums + swap_c(sums)
    sums_all = lax.all_gather(sums.astype(b16), "fsdp", axis=0)
    d_mods = sums_all[:, :, : 6 * width]
    bias_sum = jnp.sum(sums_all[:, :, 6 * width :].astype(f32), 0)
    bias_at = [0, 2 * width, 3 * width, 3 * width + units, 4 * width + units]
    bias_grads = [
        cut(bias_sum[:, bias_at[i] : bias_at[i + 1]], me * size, size, 1)[None]
        for i, size in enumerate(bias_sizes[1:])
    ]
    mod_grad_w = jnp.einsum("sd,ste->tde", act_cols, d_mods, preferred_element_type=f32)[None]
    mod_grad_b = jnp.sum(cut(d_mods, me * mod_part, mod_part, 2).astype(f32), 0)[None]
    d_act_cols = jnp.einsum("ste,tde->sd", d_mods, mod_weight[0], preferred_element_type=f32)
    d_act = lax.all_to_all(d_act_cols, "fsdp", split_axis=0, concat_axis=1, tiled=True)
    conditioning_grad = jax.vjp(jax.nn.silu, conditioning)[1](d_act)[0]

    place = jnp.stack([r, s // 2, s % 2]).astype(jnp.int32)

    def share(own):
        far = swap_x(own)
        return [own, swap_c(own), far, swap_c(far)]

    def both_r(values):
        rows = values.reshape(2, 2, slab, -1)
        return pick(rows, r, 1), swap_r(pick(rows, 1 - r, 1))

    out_grad = join_rows(share(out_g), place)
    hid_parts = [p for part in both_r(hid_g) for p in share(part)]
    hid_grad = join_columns(hid_parts, place, units_part, line, False)
    if direct_proj:
        proj_grad = join_rows(share(transpose_owners(proj_g)), place)
    else:
        proj_grad = []
        for m in range(2):
            spread = lax.dynamic_update_slice_in_dim(
                jnp.zeros((width, width), b16), proj_t[m], group * head_part, 0
            )
            own = lax.psum_scatter(spread, "fsdp", scatter_dimension=0, tiled=True)
            proj_grad.append(lax.psum(own, "seq").astype(f32))
        proj_grad = jnp.stack(proj_grad)[None]
    qkv_parts = [p for part in both_r(qkv_g) for p in share(part)]
    qkv_grad = join_columns(qkv_parts, place, head_part, 3, True)
    return (
        image_out,
        text_out,
        token_grads[0],
        token_grads[1],
        conditioning_grad,
        mod_grad_w,
        mod_grad_b,
        qkv_grad,
        bias_grads[0],
        proj_grad,
        bias_grads[1],
        hid_grad,
        bias_grads[2],
        out_grad,
        bias_grads[3],
    )


def solution(mesh):
    tokens = P("fsdp", "seq", None)
    weight = P(None, None, "fsdp", None)
    bias = P(None, None, "fsdp")
    pairs = (weight, bias) * 5
    return jax.shard_map(
        shards,
        mesh=mesh,
        in_specs=(tokens, tokens, P("fsdp", None), P("fsdp")) + pairs + (tokens, tokens),
        out_specs=(tokens, tokens, tokens, tokens, P("fsdp", None)) + pairs,
        check_vma=False,
    )
```

```python
import functools

import jax
import jax.numpy as jnp
from jax import lax
from jax.experimental import pallas as pl
from jax.experimental.layout import Layout, with_layout_constraint
from jax.experimental.pallas import tpu as pltpu
from jax.sharding import PartitionSpec as P

HEAD_DIM = 64
NORM_EPS = 1e-06
MASKED_SCORE = -1e30
VMEM_LIMIT = 60 * 2**20


def mm(left, right):
    return lax.dot_general(left, right, (((1,), (0,)), ((), ())), preferred_element_type=jnp.float32)


def key_scores(key_image, key_text, query_t, open_text, scale):
    image = mm(key_image, query_t) * scale
    text = jnp.where(open_text > 0.0, mm(key_text, query_t) * scale, MASKED_SCORE)
    return image, text


def attention_kernel(part, scale, image_ref, text_ref, open_ref, out_image, out_text, lse_image, lse_text):
    heads = part // HEAD_DIM
    b16 = jnp.bfloat16
    open_text = open_ref[0, :, :1]

    def columns(ref, kind, head):
        return ref[0, :, kind * part + head * HEAD_DIM : kind * part + (head + 1) * HEAD_DIM]

    keys = [(columns(image_ref, 1, h), columns(text_ref, 1, h)) for h in range(heads)]
    values_t = (image_ref[0, :, 2 * part :].T, text_ref[0, :, 2 * part :].T)

    def block(queries, width):
        queries_t = queries.T
        mixed, lse = [], []
        for h in range(heads):
            at = slice(h * HEAD_DIM, (h + 1) * HEAD_DIM)
            image, text = key_scores(*keys[h], queries_t[at], open_text, scale)
            top = jnp.maximum(
                jnp.max(image, 0, keepdims=True), jnp.max(text, 0, keepdims=True)
            )
            image, text = jnp.exp(image - top), jnp.exp(text - top)
            total = jnp.sum(image, 0, keepdims=True) + jnp.sum(text, 0, keepdims=True)
            out_t = mm(values_t[0][at], image.astype(b16)) + mm(values_t[1][at], text.astype(b16))
            mixed.append(out_t / total)
            lse.append(top + jnp.log(total))
        lse.append(jnp.zeros((8 - heads, width), jnp.float32))
        return jnp.concatenate(mixed, 0).T.astype(b16), jnp.concatenate(lse, 0)

    step = 256

    def body(i, carry):
        rows = pl.ds(pl.multiple_of(i * step, step), step)
        mixed, lse = block(image_ref[0, rows, :part], step)
        out_image[0, rows, :] = mixed
        lse_image[0, :, rows] = lse
        return carry

    lax.fori_loop(0, image_ref.shape[1] // step, body, 0)
    mixed, lse = block(text_ref[0, :, :part], text_ref.shape[1])
    out_text[0] = mixed
    lse_text[0] = lse


def attention(image_qkv, text_qkv, open_text, scale):
    two, image_rows, columns = image_qkv.shape
    text_rows, part = text_qkv.shape[1], columns // 3

    def spec(*dims):
        return pl.BlockSpec((1,) + dims, lambda i: (i, 0, 0))

    return pl.pallas_call(
        functools.partial(attention_kernel, part, scale),
        grid=(two,),
        in_specs=[spec(image_rows, columns), spec(text_rows, columns), spec(text_rows, 128)],
        out_specs=[
            spec(image_rows, part),
            spec(text_rows, part),
            spec(8, image_rows),
            spec(8, text_rows),
        ],
        out_shape=[
            jax.ShapeDtypeStruct((two, image_rows, part), jnp.bfloat16),
            jax.ShapeDtypeStruct((two, text_rows, part), jnp.bfloat16),
            jax.ShapeDtypeStruct((two, 8, image_rows), jnp.float32),
            jax.ShapeDtypeStruct((two, 8, text_rows), jnp.float32),
        ],
        compiler_params=pltpu.CompilerParams(vmem_limit_bytes=VMEM_LIMIT),
        cost_estimate=pl.CostEstimate(flops=0, bytes_accessed=90_000_000, transcendentals=0),
        name="attention",
    )(image_qkv, text_qkv, open_text)


def attention_back_kernel(
    part, scale, image_ref, text_ref, open_ref, lse_image, lse_text, up_image, up_text,
    out_image, out_text, d_keys, d_values,
):
    heads = part // HEAD_DIM
    b16 = jnp.bfloat16
    open_text = open_ref[0, :, :1]
    image_rows = image_ref.shape[1]

    def columns(ref, kind, head):
        return ref[0, :, kind * part + head * HEAD_DIM : kind * part + (head + 1) * HEAD_DIM]

    keys = [(columns(image_ref, 1, h), columns(text_ref, 1, h)) for h in range(heads)]
    values = [(columns(image_ref, 2, h), columns(text_ref, 2, h)) for h in range(heads)]
    keys_t = (image_ref[0, :, part : 2 * part].T, text_ref[0, :, part : 2 * part].T)

    def block(queries, ups, lse, first):
        queries_t, ups_t = queries.T, ups.T
        d_queries = []
        for h in range(heads):
            at = slice(h * HEAD_DIM, (h + 1) * HEAD_DIM)
            image, text = key_scores(*keys[h], queries_t[at], open_text, scale)
            row = lse[h : h + 1]
            image, text = jnp.exp(image - row), jnp.exp(text - row)
            up_rows = ups[:, at]
            terms = (mm(image.astype(b16), up_rows), mm(text.astype(b16), up_rows))
            d_image = mm(values[h][0], ups_t[at]) * image
            d_text = mm(values[h][1], ups_t[at]) * text
            row = jnp.sum(d_image, 0, keepdims=True) + jnp.sum(d_text, 0, keepdims=True)
            d_image = (d_image - row * image).astype(b16)
            d_text = (d_text - row * text).astype(b16)
            query_rows = queries[:, at]
            more = (mm(d_image, query_rows), mm(d_text, query_rows))
            d_queries.append((mm(keys_t[0][at], d_image) + mm(keys_t[1][at], d_text)) * scale)
            for ref, (a, b) in ((d_values, terms), (d_keys, more)):
                if first:
                    ref[h, :image_rows] = a
                    ref[h, image_rows:] = b
                else:
                    ref[h, :image_rows] += a
                    ref[h, image_rows:] += b
        return jnp.concatenate(d_queries, 0).T.astype(b16)

    step = 256
    out_text[0, :, :part] = block(text_ref[0, :, :part], up_text[0], lse_text[0], True)

    def body(i, carry):
        rows = pl.ds(pl.multiple_of(i * step, step), step)
        out_image[0, rows, :part] = block(
            image_ref[0, rows, :part], up_image[0, rows, :], lse_image[0, :, rows], False
        )
        return carry

    lax.fori_loop(0, image_rows // step, body, 0)
    for h in range(heads):
        for kind, ref, factor in ((1, d_keys, scale), (2, d_values, 1.0)):
            at = slice(kind * part + h * HEAD_DIM, kind * part + (h + 1) * HEAD_DIM)
            out_image[0, :, at] = (ref[h, :image_rows] * factor).astype(b16)
            out_text[0, :, at] = (ref[h, image_rows:] * factor).astype(b16)


def attention_back(image_qkv, text_qkv, open_text, lse_image, lse_text, up_image, up_text, scale):
    two, image_rows, columns = image_qkv.shape
    text_rows, part = text_qkv.shape[1], columns // 3
    heads = part // HEAD_DIM

    def spec(*dims):
        return pl.BlockSpec((1,) + dims, lambda i: (i, 0, 0))

    return pl.pallas_call(
        functools.partial(attention_back_kernel, part, scale),
        grid=(two,),
        in_specs=[
            spec(image_rows, columns),
            spec(text_rows, columns),
            spec(text_rows, 128),
            spec(8, image_rows),
            spec(8, text_rows),
            spec(image_rows, part),
            spec(text_rows, part),
        ],
        out_specs=[spec(image_rows, columns), spec(text_rows, columns)],
        out_shape=[
            jax.ShapeDtypeStruct(image_qkv.shape, jnp.bfloat16),
            jax.ShapeDtypeStruct(text_qkv.shape, jnp.bfloat16),
        ],
        scratch_shapes=[
            pltpu.VMEM((heads, image_rows + text_rows, HEAD_DIM), jnp.float32),
            pltpu.VMEM((heads, image_rows + text_rows, HEAD_DIM), jnp.float32),
        ],
        compiler_params=pltpu.CompilerParams(vmem_limit_bytes=VMEM_LIMIT),
        cost_estimate=pl.CostEstimate(flops=0, bytes_accessed=200_000_000, transcendentals=0),
        name="attention_back",
    )(image_qkv, text_qkv, open_text, lse_image, lse_text, up_image, up_text)


MESH = pl.DeviceIdType.MESH


def group_peers():
    f, s = lax.axis_index("fsdp"), lax.axis_index("seq")
    return {"r": (f ^ 1, s), "x": (f, s ^ 2), "c": (f, s ^ 1)}


def greet(peers):
    barrier = pltpu.get_barrier_semaphore()
    for peer in peers.values():
        pl.semaphore_signal(barrier, inc=1, device_id=peer, device_id_type=MESH)
    pl.semaphore_wait(barrier, len(peers))


def gather_kernel(own_image, own_text, image, text, local_sem, send_sem, recv_sem):
    peers = group_peers()
    cut = own_image.shape[1] // 2
    halves = {"a": pl.ds(0, cut), "b": pl.ds(cut, cut), "all": pl.ds(0, 2 * cut)}
    own, full = (own_image, own_text), (image, text)
    greet(peers)
    count = [0]

    def send(peer, source, piece, columns):
        copies = []
        for m in range(2):
            at = own[m].at[:, halves[columns]]
            if source is not None:
                at = full[m].at[source[0], source[1], :, halves[columns]]
            copy = pltpu.make_async_remote_copy(
                src_ref=at,
                dst_ref=full[m].at[piece[0], piece[1], :, halves[columns]],
                send_sem=send_sem.at[count[0]],
                recv_sem=recv_sem.at[count[0]],
                device_id=peers[peer],
                device_id_type=MESH,
            )
            copy.start()
            count[0] += 1
            copies.append(copy)
        return copies

    def landed(copies):
        for copy in copies:
            copy.wait_recv()

    a_r = send("r", None, (1, 0), "a")
    b_x = send("x", None, (0, 2), "b")
    a_x = send("x", None, (0, 2), "a")
    b_r = send("r", None, (1, 0), "b")
    all_c = send("c", None, (0, 1), "all")
    local = []
    for m in range(2):
        copy = pltpu.make_async_copy(own[m], full[m].at[0, 0], local_sem.at[m])
        copy.start()
        local.append(copy)
    landed(a_r)
    a_rx = send("x", (1, 0), (1, 2), "a")
    a_rc = send("c", (1, 0), (1, 1), "a")
    landed(b_x)
    b_xr = send("r", (0, 2), (1, 2), "b")
    b_xc = send("c", (0, 2), (0, 3), "b")
    landed(a_x)
    a_xc = send("c", (0, 2), (0, 3), "a")
    landed(b_r)
    b_rc = send("c", (1, 0), (1, 1), "b")
    landed(a_rx)
    a_rxc = send("c", (1, 2), (1, 3), "a")
    landed(b_xr)
    b_xrc = send("c", (1, 2), (1, 3), "b")
    for copies in (all_c, a_rc, b_xc, a_xc, b_rc, a_rxc, b_xrc):
        landed(copies)
    for copies in (a_r, b_x, a_x, b_r, all_c, a_rx, a_rc, b_xr, b_xc, a_xc, b_rc, a_rxc, b_xrc):
        for copy in copies:
            copy.wait_send()
    for copy in local:
        copy.wait()


def gather_group(image, text, collective_id):
    outs = [jax.ShapeDtypeStruct((2, 4) + v.shape, v.dtype) for v in (image, text)]
    anywhere = pl.BlockSpec(memory_space=pl.ANY)
    return pl.pallas_call(
        gather_kernel,
        in_specs=[anywhere] * 2,
        out_specs=[anywhere] * 2,
        out_shape=outs,
        scratch_shapes=[
            pltpu.SemaphoreType.DMA((2,)),
            pltpu.SemaphoreType.DMA((26,)),
            pltpu.SemaphoreType.DMA((26,)),
        ],
        compiler_params=pltpu.CompilerParams(
            collective_id=collective_id, has_side_effects=True, vmem_limit_bytes=VMEM_LIMIT
        ),
        cost_estimate=pl.CostEstimate(flops=0, bytes_accessed=120_000_000, transcendentals=0),
        name="gather_group",
    )(image, text)


def reduce_kernel(epilogue, extra, outs, image, text, *refs):
    extra_refs, out_refs = refs[:extra], refs[extra : extra + outs]
    (
        mine, near, acc, got_a, got_b, acc_a, acc_b, last_a, last_b, total,
        load_sem, send_sem, recv_sem,
    ) = refs[extra + outs :]
    f32, b16 = jnp.float32, jnp.bfloat16
    peers = group_peers()
    t_image = image.shape[2]
    cut = image.shape[3] // 2
    spans = (pl.ds(0, t_image), pl.ds(t_image, text.shape[2]))
    sources = (image, text)
    corners = [(1, 1), (0, 1), (1, 0), (0, 0)]
    loads = {}
    for i, (dr, dx) in enumerate(corners):
        loads[dr, dx] = []
        for m in range(2):
            copy = pltpu.make_async_copy(
                sources[m].at[dr, dx * 2], mine.at[dr * 2 + dx, spans[m]], load_sem.at[2 * i + m]
            )
            copy.start()
            loads[dr, dx].append(copy)
    greet(peers)
    started = []

    def send(peer, source, target):
        copy = pltpu.make_async_remote_copy(
            src_ref=source,
            dst_ref=target,
            send_sem=send_sem.at[len(started)],
            recv_sem=recv_sem.at[len(started)],
            device_id=peers[peer],
            device_id_type=MESH,
        )
        copy.start()
        started.append(copy)
        return copy

    near_copies = {
        (dr, dx): [
            send("c", sources[m].at[dr, dx * 2 + 1], near.at[dr * 2 + dx, spans[m]])
            for m in range(2)
        ]
        for dr, dx in corners
    }
    a, b = slice(None, cut), slice(cut, None)

    def plus(left, right):
        return (left.astype(f32) + right.astype(f32)).astype(b16)

    far = {}
    for dr, dx in corners:
        at = dr * 2 + dx
        for copy in loads[dr, dx]:
            copy.wait()
        for copy in near_copies[dr, dx]:
            copy.wait_recv()
        acc[at] = plus(mine[at], near[at])
        if dx == 1:
            far["a", dr] = send("x", acc.at[at, :, pl.ds(0, cut)], got_a.at[dr])
        if dr == 1:
            far["b", dx] = send("r", acc.at[at, :, pl.ds(cut, cut)], got_b.at[dx])
    far["a", 1].wait_recv()
    acc_a[1] = plus(acc[2, :, a], got_a[1])
    to_a = send("r", acc_a.at[1], last_a)
    far["b", 1].wait_recv()
    acc_b[1] = plus(acc[1, :, b], got_b[1])
    to_b = send("x", acc_b.at[1], last_b)
    far["a", 0].wait_recv()
    acc_a[0] = plus(acc[0, :, a], got_a[0])
    far["b", 0].wait_recv()
    acc_b[0] = plus(acc[0, :, b], got_b[0])
    to_a.wait_recv()
    total[:, a] = acc_a[0].astype(f32) + last_a[...].astype(f32)
    to_b.wait_recv()
    total[:, b] = acc_b[0].astype(f32) + last_b[...].astype(f32)
    epilogue(total, t_image, extra_refs, out_refs)
    for copy in started:
        copy.wait_send()


def reduce_group(image, text, collective_id, epilogue, extra, outs):
    rows, width = image.shape[2] + text.shape[2], image.shape[3]
    b16 = jnp.bfloat16
    half = (rows, width // 2)
    return pl.pallas_call(
        functools.partial(reduce_kernel, epilogue, len(extra), len(outs)),
        in_specs=[pl.BlockSpec(memory_space=pl.ANY)] * 2
        + [pl.BlockSpec(memory_space=pltpu.VMEM)] * len(extra),
        out_specs=[pl.BlockSpec(memory_space=pltpu.VMEM)] * len(outs),
        out_shape=outs,
        scratch_shapes=[
            pltpu.VMEM((4, rows, width), b16),
            pltpu.VMEM((4, rows, width), b16),
            pltpu.VMEM((4, rows, width), b16),
            pltpu.VMEM((2,) + half, b16),
            pltpu.VMEM((2,) + half, b16),
            pltpu.VMEM((2,) + half, b16),
            pltpu.VMEM((2,) + half, b16),
            pltpu.VMEM(half, b16),
            pltpu.VMEM(half, b16),
            pltpu.VMEM((rows, width), jnp.float32),
            pltpu.SemaphoreType.DMA((8,)),
            pltpu.SemaphoreType.DMA((14,)),
            pltpu.SemaphoreType.DMA((14,)),
        ],
        compiler_params=pltpu.CompilerParams(
            collective_id=collective_id, has_side_effects=True, vmem_limit_bytes=VMEM_LIMIT
        ),
        cost_estimate=pl.CostEstimate(flops=0, bytes_accessed=150_000_000, transcendentals=0),
        name="reduce_group",
    )(image, text, *extra)


def row_norm(values):
    center = values - jnp.mean(values, -1, keepdims=True)
    inverse = lax.rsqrt(jnp.mean(center * center, -1, keepdims=True) + NORM_EPS)
    return center * inverse, inverse


def row_sums(values):
    return jnp.sum(values, 0, keepdims=True)


def middle_epilogue(total, t_image, extra, outs):
    vectors = extra[2]
    for m, rows in ((0, slice(None, t_image)), (1, slice(t_image, None))):
        bias, gate, shift, scale = [vectors[4 * m + i : 4 * m + i + 1] for i in range(4)]
        branch = total[rows] + bias
        middle = extra[m][...].astype(jnp.float32) + gate * branch
        normal, _ = row_norm(middle)
        outs[m][...] = branch
        outs[2 + m][...] = middle
        outs[4 + m][...] = (normal * (1.0 + scale) + shift).astype(jnp.bfloat16)


def norm_back(d_hidden, values, scale):
    normal, inverse = row_norm(values)
    e = d_hidden * (1.0 + scale)
    mean = jnp.mean(e, -1, keepdims=True)
    along = jnp.mean(e * normal, -1, keepdims=True)
    return (e - mean - normal * along) * inverse, row_sums(d_hidden), row_sums(d_hidden * normal)


def middle_back_epilogue(total, t_image, extra, outs):
    f32 = jnp.float32
    vectors, sums = extra[6], outs[4]
    for m, rows in ((0, slice(None, t_image)), (1, slice(t_image, None))):
        scale, gate = [vectors[2 * m + i : 2 * m + i + 1] for i in range(2)]
        d_norm, d_shift, d_scale = norm_back(total[rows], extra[m][...], scale)
        d_middle = extra[2 + m][...].astype(f32) + d_norm
        d_branch = (d_middle * gate).astype(jnp.bfloat16)
        outs[m][...] = d_middle
        outs[2 + m][...] = d_branch
        parts = (d_shift, d_scale, row_sums(d_middle * extra[4 + m][...]), row_sums(d_branch.astype(f32)))
        for i, part in enumerate(parts):
            sums[4 * m + i : 4 * m + i + 1] = part


def input_back_epilogue(total, t_image, extra, outs):
    vectors, sums = extra[4], outs[2]
    sums[...] = jnp.zeros(sums.shape, jnp.float32)
    for m, rows in ((0, slice(None, t_image)), (1, slice(t_image, None))):
        d_norm, d_shift, d_scale = norm_back(
            total[rows], extra[m][...].astype(jnp.float32), vectors[m : m + 1]
        )
        outs[m][...] = extra[2 + m][...] + d_norm
        sums[2 * m : 2 * m + 1] = d_shift
        sums[2 * m + 1 : 2 * m + 2] = d_scale


def modulation_kernel(
    owners, parts, slab, send, weight, small_out, act_out, mods_out,
    small, piece, term, got, mods, load_sem, sems,
):
    f, s = lax.axis_index("fsdp"), lax.axis_index("seq")
    quarter = piece.shape[2]
    columns = pl.ds(pl.multiple_of(s * quarter, 128), quarter)
    load = pltpu.make_async_copy(weight.at[:, :, columns], piece, load_sem)
    load.start()
    barrier = pltpu.get_barrier_semaphore()
    for k in range(1, owners):
        pl.semaphore_signal(
            barrier, inc=1, device_id=(lax.rem(f + k, owners), s), device_id_type=MESH
        )
    for q in range(1, parts):
        pl.semaphore_signal(barrier, inc=1, device_id=(f, s ^ q), device_id_type=MESH)
    pl.semaphore_wait(barrier, owners + parts - 2)

    def exchange(source, target, stage):
        copies = []
        for k in range(1, owners):
            peer = lax.rem(f + k, owners)
            copy = pltpu.make_async_remote_copy(
                src_ref=source.at[peer],
                dst_ref=target.at[f],
                send_sem=sems.at[stage, 0, k],
                recv_sem=sems.at[stage, 1, k],
                device_id=(peer, s),
                device_id_type=MESH,
            )
            copy.start()
            copies.append(copy)
        target[f] = source[f]
        for copy in copies:
            copy.wait()

    exchange(send, small, 0)
    small_out[...] = small[...]
    act = jnp.concatenate([small[k, :, :slab] for k in range(owners)], 0)
    act = (act / (1.0 + jnp.exp(-act))).astype(jnp.bfloat16)
    act_out[...] = act
    load.wait()
    for m in range(2):
        full = mm(act, piece[m])
        for k in range(owners):
            for dr in range(2):
                term[k, dr * 2 + m : dr * 2 + m + 1, :] = full[k ^ dr : (k ^ dr) + 1]
    exchange(term, got, 1)
    total = got[0]
    for k in range(1, owners):
        total = total + got[k]
    mods[s] = total
    copies = []
    for q in range(1, parts):
        copy = pltpu.make_async_remote_copy(
            src_ref=mods.at[s],
            dst_ref=mods.at[s],
            send_sem=sems.at[2, 0, q],
            recv_sem=sems.at[2, 1, q],
            device_id=(f, s ^ q),
            device_id_type=MESH,
        )
        copy.start()
        copies.append(copy)
    for copy in copies:
        copy.wait()
    mods_out[...] = mods[...]


def modulation(send, weight, owners, parts):
    slab, columns = weight.shape[1], weight.shape[2]
    quarter = columns // parts
    f32 = jnp.float32
    return pl.pallas_call(
        functools.partial(modulation_kernel, owners, parts, slab),
        in_specs=[
            pl.BlockSpec(memory_space=pltpu.VMEM),
            pl.BlockSpec(memory_space=pl.ANY),
        ],
        out_specs=[pl.BlockSpec(memory_space=pltpu.VMEM)] * 3,
        out_shape=[
            jax.ShapeDtypeStruct(send.shape, f32),
            jax.ShapeDtypeStruct((owners, slab), jnp.bfloat16),
            jax.ShapeDtypeStruct((parts, 4, quarter), f32),
        ],
        scratch_shapes=[
            pltpu.VMEM(send.shape, f32),
            pltpu.VMEM((2, slab, quarter), jnp.bfloat16),
            pltpu.VMEM((owners, 4, quarter), f32),
            pltpu.VMEM((owners, 4, quarter), f32),
            pltpu.VMEM((parts, 4, quarter), f32),
            pltpu.SemaphoreType.DMA,
            pltpu.SemaphoreType.DMA((3, 2, owners)),
        ],
        compiler_params=pltpu.CompilerParams(
            collective_id=1, has_side_effects=True, vmem_limit_bytes=VMEM_LIMIT
        ),
        cost_estimate=pl.CostEstimate(
            flops=4 * owners * slab * quarter, bytes_accessed=60_000_000, transcendentals=0
        ),
        name="modulation",
    )(send, weight)


def spread_kernel(owners, sums, out, mine, first, second, rounded, got, sems):
    f, s = lax.axis_index("fsdp"), lax.axis_index("seq")
    barrier = pltpu.get_barrier_semaphore()
    for k in range(1, owners):
        pl.semaphore_signal(
            barrier, inc=1, device_id=(lax.rem(f + k, owners), s), device_id_type=MESH
        )
    for q in range(1, 3):
        pl.semaphore_signal(barrier, inc=1, device_id=(f, s ^ q), device_id_type=MESH)
    pl.semaphore_wait(barrier, owners + 1)

    def swap(source, target, q):
        copy = pltpu.make_async_remote_copy(
            src_ref=source,
            dst_ref=target,
            send_sem=sems.at[0, owners - 1 + q],
            recv_sem=sems.at[1, owners - 1 + q],
            device_id=(f, s ^ q),
            device_id_type=MESH,
        )
        copy.start()
        copy.wait()

    swap(sums, first, 2)
    mine[...] = sums[...] + first[...]
    swap(mine, second, 1)
    rounded[...] = (mine[...] + second[...]).astype(jnp.bfloat16)
    copies = []
    for k in range(1, owners):
        copy = pltpu.make_async_remote_copy(
            src_ref=rounded,
            dst_ref=got.at[f],
            send_sem=sems.at[0, k],
            recv_sem=sems.at[1, k],
            device_id=(lax.rem(f + k, owners), s),
            device_id_type=MESH,
        )
        copy.start()
        copies.append(copy)
    got[f] = rounded[...]
    for copy in copies:
        copy.wait()
    out[...] = got[...]


def spread_sums(sums, owners):
    shape = sums.shape
    b16 = jnp.bfloat16
    return pl.pallas_call(
        functools.partial(spread_kernel, owners),
        in_specs=[pl.BlockSpec(memory_space=pltpu.VMEM)],
        out_specs=pl.BlockSpec(memory_space=pltpu.VMEM),
        out_shape=jax.ShapeDtypeStruct((owners,) + shape, b16),
        scratch_shapes=[
            pltpu.VMEM(shape, jnp.float32),
            pltpu.VMEM(shape, jnp.float32),
            pltpu.VMEM(shape, jnp.float32),
            pltpu.VMEM(shape, b16),
            pltpu.VMEM((owners,) + shape, b16),
            pltpu.SemaphoreType.DMA((2, owners + 2)),
        ],
        compiler_params=pltpu.CompilerParams(
            collective_id=2, has_side_effects=True, vmem_limit_bytes=VMEM_LIMIT
        ),
        cost_estimate=pl.CostEstimate(flops=0, bytes_accessed=80_000_000, transcendentals=0),
        name="spread_sums",
    )(sums)


def pick_kernel(part, line, place, *refs):
    qkv, hid = refs[:3], refs[3 : 3 + 2 * line]
    qkv_own, qkv_other, hid_own, hid_other = refs[3 + 2 * line :]
    high, odd = place[1] == 1, place[2] == 1
    for kind in range(3):
        for m in range(2):
            at = slice((m * 3 + kind) * part, (m * 3 + kind + 1) * part)
            low, up = qkv[kind][m, :, :part], qkv[kind][m, :, part:]
            qkv_own[:, at] = jnp.where(high, up, low)
            qkv_other[:, at] = jnp.where(high, low, up)
    for z in range(line):
        chosen = []
        for q in range(2):
            block = hid[z * 2 + q]
            cut = block.shape[2] // 2
            chosen.append(jnp.where(odd, block[:, :, cut:], block[:, :, :cut]))
        at = slice(z * cut, (z + 1) * cut)
        hid_own[:, :, at] = jnp.where(high, chosen[1], chosen[0])
        hid_other[:, :, at] = jnp.where(high, chosen[0], chosen[1])


def pick_parts(qkv_weight, hidden_weight, s, r, part, line):
    slab, width = qkv_weight.shape[1], qkv_weight.shape[2] // 3
    units = hidden_weight.shape[2] // (2 * line)
    place = jnp.stack([s, r, s % 2]).astype(jnp.int32)
    per_kind = width // (2 * part)

    def qkv_spec(kind):
        return pl.BlockSpec((2, slab, 2 * part), lambda i, at: (0, 0, kind * per_kind + at[0]))

    def hid_spec(f):
        return pl.BlockSpec((2, slab, units // 2), lambda i, at: (0, 0, 2 * f + at[0] // 2))

    shapes = [(slab, 6 * part)] * 2 + [(2, slab, line * units // 4)] * 2
    return pl.pallas_call(
        functools.partial(pick_kernel, part, line),
        grid_spec=pltpu.PrefetchScalarGridSpec(
            num_scalar_prefetch=1,
            grid=(1,),
            in_specs=[qkv_spec(k) for k in range(3)] + [hid_spec(f) for f in range(2 * line)],
            out_specs=[
                pl.BlockSpec(dims, lambda i, at, n=len(dims): (0,) * n) for dims in shapes
            ],
        ),
        out_shape=[jax.ShapeDtypeStruct(dims, jnp.bfloat16) for dims in shapes],
        compiler_params=pltpu.CompilerParams(vmem_limit_bytes=VMEM_LIMIT),
        name="pick_parts",
    )(place, *([qkv_weight] * 3), *([hidden_weight] * (2 * line)))


def chosen_piece(pieces, x, c, q):
    near = [jnp.where(c == q % 2, pieces[2 * dx], pieces[2 * dx + 1]) for dx in range(2)]
    return jnp.where(x == q // 2, near[0], near[1])


def stacked_kernel(image, text, up_image, up_text, out):
    part = up_image.shape[1]

    def inner(left, right):
        return lax.dot_general(
            left[...], right[...], (((0,), (0,)), ((), ())), preferred_element_type=jnp.float32
        ).astype(jnp.bfloat16)

    out[:, :part] = inner(image, up_image)
    out[:, part:] = inner(text, up_text)


def stacked_terms(hidden, ups):
    width, part = hidden[0].shape[1], ups[0].shape[1]
    rows = width // 4
    return pl.pallas_call(
        stacked_kernel,
        grid=(4,),
        in_specs=[pl.BlockSpec((v.shape[0], rows), lambda z: (0, z)) for v in hidden]
        + [pl.BlockSpec(v.shape, lambda z: (0, 0)) for v in ups],
        out_specs=pl.BlockSpec((rows, 2 * part), lambda z: (z, 0)),
        out_shape=jax.ShapeDtypeStruct((width, 2 * part), jnp.bfloat16),
        compiler_params=pltpu.CompilerParams(vmem_limit_bytes=VMEM_LIMIT),
        cost_estimate=pl.CostEstimate(flops=0, bytes_accessed=35_000_000, transcendentals=0),
        name="stacked_terms",
    )(*hidden, *ups)


def columns_kernel(chunk, kinds, inner_first, place, *refs):
    out = refs[8]
    r, x, c = place[0], place[1], place[2]
    for m in range(out.shape[1]):
        for kind in range(kinds):
            at = slice((m * kinds + kind) * chunk, (m * kinds + kind + 1) * chunk)
            by_dr = [
                [chosen_piece([refs[dr * 4 + p][:, at] for p in range(4)], x, c, q) for q in range(4)]
                for dr in range(2)
            ]
            for q in range(4):
                for natural in range(2):
                    value = jnp.where(r == natural, by_dr[0][q], by_dr[1][q])
                    spot = q * 2 + natural if inner_first else natural * 4 + q
                    start = (kind * 8 + spot) * chunk
                    out[0, m, :, start : start + chunk] = value.astype(jnp.float32)


def join_columns(pieces, place, chunk, kinds, inner_first):
    rows = pieces[0].shape[-2]
    columns = 8 * kinds * chunk
    step = 64 if rows % 64 == 0 else rows
    if pieces[0].ndim == 3:
        grid = (rows // step, 2)
        piece = pl.BlockSpec((None, step, columns // 8), lambda i, m, at: (m, i, 0))
        out = pl.BlockSpec((1, 1, step, columns), lambda i, m, at: (0, m, i, 0))
    else:
        grid = (rows // step,)
        piece = pl.BlockSpec((step, columns // 4), lambda i, at: (i, 0))
        out = pl.BlockSpec((1, 2, step, columns), lambda i, at: (0, 0, i, 0))
    return pl.pallas_call(
        functools.partial(columns_kernel, chunk, kinds, inner_first),
        grid_spec=pltpu.PrefetchScalarGridSpec(
            num_scalar_prefetch=1, grid=grid, in_specs=[piece] * 8, out_specs=out
        ),
        out_shape=jax.ShapeDtypeStruct((1, 2, rows, columns), jnp.float32),
        compiler_params=pltpu.CompilerParams(vmem_limit_bytes=VMEM_LIMIT),
        name="join_columns",
    )(place, *pieces)


def rows_kernel(place, *refs):
    out = refs[4]
    rows = refs[0].shape[1]
    for q in range(4):
        value = chosen_piece([refs[p][0] for p in range(4)], place[1], place[2], q)
        out[0, 0, q * rows : (q + 1) * rows, :] = value.astype(jnp.float32)


def join_rows(pieces, place):
    rows, columns = pieces[0].shape[1:]
    step = columns // 2
    return pl.pallas_call(
        rows_kernel,
        grid_spec=pltpu.PrefetchScalarGridSpec(
            num_scalar_prefetch=1,
            grid=(2, 2),
            in_specs=[pl.BlockSpec((1, rows, step), lambda m, i, at: (m, 0, i))] * 4,
            out_specs=pl.BlockSpec((1, 1, 4 * rows, step), lambda m, i, at: (0, m, 0, i)),
        ),
        out_shape=jax.ShapeDtypeStruct((1, 2, 4 * rows, columns), jnp.float32),
        compiler_params=pltpu.CompilerParams(vmem_limit_bytes=VMEM_LIMIT),
        name="join_rows",
    )(place, *pieces)


def rows_major(values):
    return with_layout_constraint(values, Layout(major_to_minor=(0, 1)))


def together(*values):
    return lax.optimization_barrier(values)


def norm_rows(values):
    center = values - jnp.mean(values, -1, keepdims=True)
    return center * lax.rsqrt(jnp.mean(center * center, -1, keepdims=True) + NORM_EPS)


def modulated(values, shift, scale_up):
    return norm_rows(values) * (1.0 + scale_up) + shift


def gelu_tanh(values):
    return jax.nn.gelu(values, approximate=True)


def dot32(left, right, contract):
    return lax.dot_general(
        left, right, ((contract[0], contract[1]), ((), ())), preferred_element_type=jnp.float32
    )


def product(left, right):
    return dot32(left, right, ((1,), (0,)))


def rows_inner(left, right):
    return dot32(left, right, ((0,), (0,)))


def right_back(left, right):
    return dot32(left, right, ((1,), (1,)))


def swap_r(values):
    count = lax.axis_size("fsdp")
    return lax.ppermute(values, "fsdp", [(at, at ^ 1) for at in range(count)])


def swap_x(values):
    return lax.ppermute(values, "seq", [(at, at ^ 2) for at in range(4)])


def swap_c(values):
    return lax.ppermute(values, "seq", [(at, at ^ 1) for at in range(4)])


CORNERS = [(0, 0), (0, 1), (1, 0), (1, 1)]


def reduce_near(pieces):
    f32, b16 = jnp.float32, jnp.bfloat16
    got = swap_c(jnp.stack([pieces[at + (1,)].astype(b16) for at in CORNERS]))
    return [
        (pieces[at + (0,)].astype(f32) + got[i].astype(f32)).astype(b16)
        for i, at in enumerate(CORNERS)
    ]


def reduce_far(near):
    cut = near[0].shape[1] // 2
    a = {at: v[:, :cut] for at, v in zip(CORNERS, near)}
    b = {at: v[:, cut:] for at, v in zip(CORNERS, near)}
    got_a = swap_x(jnp.stack([a[(0, 1)], a[(1, 1)]]))
    got_b = swap_r(jnp.stack([b[(1, 0)], b[(1, 1)]]))
    return [a[(0, 0)], a[(1, 0)], b[(0, 0)], b[(0, 1)], got_a, got_b]


def reduce_last(parts):
    f32, b16 = jnp.float32, jnp.bfloat16
    got_a, got_b = parts[4], parts[5]
    a = [(parts[dr].astype(f32) + got_a[dr].astype(f32)).astype(b16) for dr in range(2)]
    b = [(parts[2 + dx].astype(f32) + got_b[dx].astype(f32)).astype(b16) for dx in range(2)]
    last_a, last_b = swap_r(a[1]), swap_x(b[1])
    return jnp.concatenate(
        [a[0].astype(f32) + last_a.astype(f32), b[0].astype(f32) + last_b.astype(f32)], 1
    )


def shards(
    image_tokens,
    text_tokens,
    conditioning,
    text_lengths,
    mod_weight,
    mod_bias,
    qkv_weight,
    qkv_bias,
    proj_weight,
    proj_bias,
    hidden_weight,
    hidden_bias,
    output_weight,
    output_bias,
    image_cotangent,
    text_cotangent,
):
    f32, b16 = jnp.float32, jnp.bfloat16
    width = image_tokens.shape[2]
    counts = (image_tokens.shape[1], text_tokens.shape[1])
    parts = lax.axis_size("seq")
    owners = lax.axis_size("fsdp")
    line = owners // 2
    head_part = width // (2 * parts)
    heads_here = head_part // HEAD_DIM
    slab = width // owners
    units_slab = output_weight.shape[2]
    units_part = units_slab // parts
    units = units_slab * owners
    units_here = line * units_part
    score_scale = HEAD_DIM ** (-0.5)
    me = lax.axis_index("fsdp")
    s = lax.axis_index("seq")
    r = me % 2
    along = [[z * 2 + q for z in range(line)] for q in range(2)]
    direct_proj = line == parts
    image_rows, text_rows = counts[0] * parts, counts[1] * parts

    def cut(array, start, size, axis):
        return lax.dynamic_slice_in_dim(array, start, size, axis)

    def transpose_owners(values):
        pairs = [
            ((z * 2 + q) * parts + t, (t * 2 + q) * parts + z)
            for z in range(line)
            for q in range(2)
            for t in range(parts)
        ]
        return lax.ppermute(values, ("fsdp", "seq"), pairs)

    def line_gather(rows):
        return lax.all_gather(rows, "fsdp", axis=rows.ndim - 2, tiled=True, axis_index_groups=along)

    def line_reduce(term):
        return lax.psum_scatter(
            term, "fsdp", scatter_dimension=term.ndim - 2, tiled=True, axis_index_groups=along
        )

    def weight_terms(left, right):
        return jnp.stack([rows_inner(left[m], right[m]).astype(b16) for m in range(2)])

    def both_r(values):
        rows = values.reshape(values.shape[:-2] + (2, slab, -1))
        return pick(rows, r, values.ndim - 2), swap_r(pick(rows, 1 - r, values.ndim - 2))

    def by_r(own, other, axis):
        return jnp.where(r == 0, jnp.stack([own, other], axis), jnp.stack([other, own], axis))

    def pick(array, index, axis):
        return lax.dynamic_index_in_dim(array, index, axis, keepdims=False)

    biases = (mod_bias, qkv_bias, proj_bias, hidden_bias, output_bias)
    bias_sizes = [v.shape[2] for v in biases]
    bias_local = jnp.concatenate([v[0].astype(f32) for v in biases], 1)
    padded = -(-slab // 128) * 128
    common = jnp.concatenate([bias_local.reshape(-1), jnp.tile(text_lengths.astype(f32), 128)])
    if (2 * head_part) % 128 == 0 and (2 * units_part) % 128 == 0:
        qkv_own, qkv_other, hid_own, hid_other = pick_parts(
            qkv_weight[0], hidden_weight[0], s, r, head_part, line
        )
    else:
        qkv_view = qkv_weight[0].reshape(2, slab, 3, 2 * parts, head_part)
        qkv_own, qkv_other = [
            pick(qkv_view, s * 2 + at, 3).transpose(1, 0, 2, 3).reshape(slab, 6 * head_part)
            for at in (r, 1 - r)
        ]
        hid_view = pick(hidden_weight[0].reshape(2, slab, line, 2, parts, units_part), s, 4)
        hid_own, hid_other = [
            pick(hid_view, at, 3).reshape(2, slab, units_here) for at in (r, 1 - r)
        ]
    qkv_got = swap_r(qkv_other)
    proj_mine = proj_weight[0]
    if direct_proj:
        chunk = slab // parts
        proj_mine = transpose_owners(cut(proj_weight[0], s * chunk, chunk, 1))
    qkv_mine = by_r(qkv_own, qkv_got, 0).reshape(2 * slab, 6 * head_part)
    hid_got = swap_r(hid_other)
    image_in, text_in, qkv_mine = together(image_tokens[0], text_tokens[0], qkv_mine)
    x_full = [v.reshape(2, -1, width) for v in gather_group(image_in, text_in, 3)]
    cond_in, proj_mine, x_full[0] = together(conditioning, proj_mine, x_full[0])
    send = jnp.concatenate(
        [
            cond_in.reshape(owners, slab),
            jnp.zeros((owners, padded - slab), f32),
            jnp.broadcast_to(common, (owners, common.shape[0])),
        ],
        1,
    )
    small, act_cols, mods = modulation(send[:, None], mod_weight[0], owners, parts)
    small = small[:, 0, padded:]
    lengths = [pick(small[:, -1], me ^ dr, 0) for dr in range(2)]
    bias_all = small[:, :-128].reshape(owners, 2, sum(bias_sizes))
    offsets = [0]
    for size in bias_sizes:
        offsets.append(offsets[-1] + size)
    mod_b, qkv_b, proj_b, hid_b, out_b = [
        bias_all[:, :, offsets[i] : offsets[i + 1]].transpose(1, 0, 2) for i in range(5)
    ]
    group = s * 2 + r
    qkv_b = cut(qkv_b.reshape(2, 2, width), group * head_part, head_part, 2)
    qkv_b = jnp.stack([qkv_b[:, 0], jnp.zeros_like(qkv_b[:, 0]), qkv_b[:, 1]], 1).reshape(
        2, 3 * head_part
    )
    proj_b = proj_b.reshape(2, width)
    out_b = out_b.reshape(2, width)
    hid_b = pick(pick(hid_b.reshape(2, line, 2, parts, units_part), s, 3), r, 2).reshape(
        2, units_here
    )
    mods = mods.reshape(parts, 2, 2, -1).transpose(1, 2, 0, 3).reshape(2, 2, 6 * width)
    mods = mods + mod_b.reshape(2, 6 * width)
    mod_part = mod_bias.shape[2]

    qkv_w = line_gather(qkv_mine)
    qkv_w = [qkv_w[:, m * 3 * head_part : (m + 1) * 3 * head_part] for m in range(2)]
    if direct_proj:
        proj_w = line_gather(proj_mine)
    else:
        proj_all = lax.all_gather(proj_mine, "fsdp", axis=1, tiled=True)
        proj_w = cut(proj_all, group * head_part, head_part, 1)
    mods, hid_got = together(mods, hid_got)
    hid_w = line_gather(by_r(hid_own, hid_got, 1).reshape(2, 2 * slab, units_here))
    out_w = line_gather(cut(output_weight[0], s * units_part, units_part, 1))

    def mod_at(index, m):
        at = slice(index * width, (index + 1) * width)
        return mods[0, m, None, at], mods[:, m, None, at]

    shift1, scale1, gate1, shift2, scale2, gate2 = [
        [mod_at(i, m) for m in range(2)] for i in range(6)
    ]

    def joined(pieces):
        return [v.reshape(2, -1, v.shape[-1]) for v in pieces]

    def apart(values, m):
        return values.reshape(2, parts, counts[m], -1)

    def flat(values):
        return values.reshape(-1, values.shape[-1])


    hidden1 = [
        flat(modulated(x_full[m].astype(f32), shift1[m][1], scale1[m][1]).astype(b16))
        for m in range(2)
    ]
    qkv = [rows_major((product(hidden1[m], qkv_w[m]) + qkv_b[m]).astype(b16)) for m in range(2)]
    qkv = [v.reshape(2, -1, 3 * head_part) for v in qkv]
    text_slot = jnp.arange(text_rows)
    text_place = ((text_slot // counts[1]) ^ s) * counts[1] + text_slot % counts[1]
    open_text = jnp.stack([(text_place.astype(f32) < n).astype(f32) for n in lengths])
    open_text = jnp.broadcast_to(open_text[:, :, None], (2, text_rows, 128))
    mixed_image, mixed_text, lse_image, lse_text = attention(*qkv, open_text, score_scale)
    attended = [flat(mixed_image), flat(mixed_text)]

    def like(pair, kind):
        return [jax.ShapeDtypeStruct(v.shape, kind) for v in pair]

    own = [image_tokens[0], text_tokens[0]]
    own_up = [image_cotangent[0], text_cotangent[0]]

    def summed(terms, collective_id, epilogue, extra, outs):
        pieces = [apart(terms[m], m) for m in range(2)]
        return list(reduce_group(*pieces, collective_id, epilogue, extra, outs))

    vectors = [v for m in range(2) for v in (proj_b[m, None], gate1[m][0], shift2[m][0], scale2[m][0])]
    reduced = summed(
        [product(attended[m], proj_w[m]).astype(b16) for m in range(2)],
        5,
        middle_epilogue,
        own + [jnp.concatenate(vectors, 0)],
        like(own, f32) + like(own, f32) + like(own, b16),
    )
    branch, middle = reduced[:2], reduced[2:4]
    hidden2 = [flat(v) for v in gather_group(*reduced[4:], 6)]
    before = [product(hidden2[m], hid_w[m]) + hid_b[m] for m in range(2)]
    active = [gelu_tanh(before[m]).astype(b16) for m in range(2)]

    image_up, text_up, _ = together(*own_up, active[0])
    g_full = joined(gather_group(image_up, text_up, 4))
    d_result = [flat((g_full[m].astype(f32) * gate2[m][1]).astype(b16)) for m in range(2)]
    out_t = weight_terms(active, d_result)
    out_g = line_reduce(out_t)
    d_result[0], d_result[1], out_t = together(*d_result, out_t)
    d_before = []
    for m in range(2):
        d_active = right_back(d_result[m], out_w[m])
        d_before.append(jax.vjp(gelu_tanh, before[m])[1](d_active)[0].astype(b16))
    d_hidden2 = [right_back(d_before[m], hid_w[m]).astype(b16) for m in range(2)]

    def by_corner(values):
        return {
            (dr,) + at: values[dr, i] for dr in range(2) for i, at in enumerate(CORNERS)
        }

    vectors = [v for m in range(2) for v in (scale2[m][0], gate1[m][0])]
    reduced = summed(
        d_hidden2,
        7,
        middle_back_epilogue,
        list(middle) + own_up + list(branch) + [jnp.concatenate(vectors, 0)],
        like(own, f32) + like(own, b16) + [jax.ShapeDtypeStruct((8, width), f32)],
    )
    d_middle, d_branch, sums2 = reduced[:2], reduced[2:4], reduced[4]
    d_branch[0], *late = together(d_branch[0], *active, *d_before)
    hid_t = weight_terms(hidden2, late[2:])
    hid_g = line_reduce(hid_t)
    result_parts = [product(late[m], out_w[m]).astype(b16) for m in range(2)]
    result_near = reduce_near(by_corner(jnp.concatenate(
        [apart(result_parts[m], m) for m in range(2)], 2
    )))
    d_branch[0], d_branch[1], hid_t, out_g, *result_parts = together(
        *d_branch, hid_t, out_g, *result_parts
    )
    d_branch_full = [flat(v) for v in gather_group(*d_branch, 8)]
    proj_t = weight_terms(attended, d_branch_full)
    d_attended = [
        rows_major(right_back(d_branch_full[m], proj_w[m]).astype(b16)).reshape(2, -1, head_part)
        for m in range(2)
    ]
    out_far = swap_x(out_g)
    d_attended[0], d_attended[1], proj_t, *result_near = together(
        *d_attended, proj_t, *result_near
    )
    result_far = reduce_far(result_near)
    d_qkv = attention_back(*qkv, open_text, lse_image, lse_text, *d_attended, score_scale)
    d_qkv = [flat(v) for v in d_qkv]
    d_qkv[0], d_qkv[1], hid_g, *result_far = together(*d_qkv, hid_g, *result_far)
    if slab % 96 == 0:
        qkv_t = stacked_terms(hidden1, d_qkv)
    else:
        qkv_t = [rows_inner(hidden1[m], d_qkv[m]).astype(b16) for m in range(2)]
        qkv_t = jnp.concatenate(qkv_t, 1)
    qkv_g = line_reduce(qkv_t)
    result_last = reduce_last(result_far)
    hid_keep, hid_got = both_r(hid_g)
    d_qkv[0], d_qkv[1], qkv_t, out_far, hid_keep = together(*d_qkv, qkv_t, out_far, hid_keep)
    d_hidden1 = [right_back(d_qkv[m], qkv_w[m]).astype(b16) for m in range(2)]
    d_hidden1[0], d_hidden1[1], result_last, hid_got, proj_t = together(
        *d_hidden1, result_last, hid_got, proj_t
    )
    if direct_proj:
        proj_g = line_reduce(proj_t)
    reduced = summed(
        d_hidden1,
        9,
        input_back_epilogue,
        own + list(d_middle) + [jnp.concatenate([scale1[m][0] for m in range(2)], 0)],
        like(own, f32) + [jax.ShapeDtypeStruct((8, width), f32)],
    )
    token_grads, sums1 = [v[None] for v in reduced[:2]], reduced[2]
    hid_far, hid_got_far = swap_x(hid_keep), swap_x(hid_got)
    sums1, result_last, *late = together(sums1, result_last, *d_before, *d_qkv)
    result = [result_last[: counts[0]] + out_b[0], result_last[counts[0] :] + out_b[1]]
    image_out, text_out = [
        (middle[m] + gate2[m][0] * result[m]).astype(b16)[None] for m in range(2)
    ]

    all_rows = []
    for m in range(2):
        columns = row_sums(late[2 + m].astype(f32)).reshape(3, head_part)
        qkv_bt = lax.dynamic_update_slice_in_dim(
            jnp.zeros((2, width), f32), columns[::2], group * head_part, 1
        )
        units_bt = row_sums(late[m].astype(f32)).reshape(line, units_part)
        hid_bt = lax.dynamic_update_slice_in_dim(
            jnp.zeros((line, 2 * units_slab), f32), units_bt, r * units_slab + s * units_part, 1
        )
        up = own_up[m].astype(f32)
        all_rows += [
            sums1[2 * m : 2 * m + 2],
            sums2[4 * m + 2 : 4 * m + 3],
            sums2[4 * m : 4 * m + 2],
            row_sums(up * result[m]),
            qkv_bt,
            sums2[4 * m + 3 : 4 * m + 4],
            hid_bt.reshape(-1, width),
            row_sums((up * gate2[m][0]).astype(b16).astype(f32)),
        ]
    sums = jnp.concatenate(all_rows, 0)
    length = sums.shape[0]
    place = jnp.stack([r, s // 2, s % 2]).astype(jnp.int32)

    def share(own, far=None):
        far = swap_x(own) if far is None else far
        return [own, swap_c(own), far, swap_c(far)]

    out_grad = join_rows(share(out_g, out_far), place)
    sums, out_grad = together(sums, out_grad)
    sums = jnp.pad(sums, ((0, -length % 16), (0, 0)))
    sums_all = spread_sums(sums, owners)[:, :length].reshape(owners, 2, -1)
    sums_all, qkv_g, hid_far, hid_got_far = together(sums_all, qkv_g, hid_far, hid_got_far)
    qkv_keep, qkv_got = both_r(qkv_g)
    qkv_far = swap_x(qkv_keep)
    if direct_proj:
        proj_g = transpose_owners(proj_g)
    d_mods = sums_all[:, :, : 6 * width]
    bias_sum = jnp.sum(sums_all[:, :, 6 * width :].astype(f32), 0)
    bias_at = [0, 2 * width, 3 * width, 3 * width + units, 4 * width + units]
    bias_grads = [
        cut(bias_sum[:, bias_at[i] : bias_at[i + 1]], me * size, size, 1)[None]
        for i, size in enumerate(bias_sizes[1:])
    ]
    mod_grad_w = jnp.einsum("sd,ste->tde", act_cols, d_mods, preferred_element_type=f32)[None]
    mod_grad_b = jnp.sum(cut(d_mods, me * mod_part, mod_part, 2).astype(f32), 0)[None]
    d_act_cols = jnp.einsum("ste,tde->sd", d_mods, mod_weight[0], preferred_element_type=f32)
    d_act = lax.all_to_all(d_act_cols, "fsdp", split_axis=0, concat_axis=1, tiled=True)
    conditioning_grad = jax.vjp(jax.nn.silu, conditioning)[1](d_act)[0]

    hid_parts = share(hid_keep, hid_far) + share(hid_got, hid_got_far)
    hid_grad = join_columns(hid_parts, place, units_part, line, False)
    if direct_proj:
        proj_grad = join_rows(share(proj_g), place)
    else:
        proj_grad = []
        for m in range(2):
            spread = lax.dynamic_update_slice_in_dim(
                jnp.zeros((width, width), b16), proj_t[m], group * head_part, 0
            )
            own = lax.psum_scatter(spread, "fsdp", scatter_dimension=0, tiled=True)
            proj_grad.append(lax.psum(own, "seq").astype(f32))
        proj_grad = jnp.stack(proj_grad)[None]
    qkv_parts = share(qkv_keep, qkv_far) + share(qkv_got)
    qkv_grad = join_columns(qkv_parts, place, head_part, 3, True)
    return (
        image_out,
        text_out,
        token_grads[0],
        token_grads[1],
        conditioning_grad,
        mod_grad_w,
        mod_grad_b,
        qkv_grad,
        bias_grads[0],
        proj_grad,
        bias_grads[1],
        hid_grad,
        bias_grads[2],
        out_grad,
        bias_grads[3],
    )


def solution(mesh):
    tokens = P("fsdp", "seq", None)
    weight = P(None, None, "fsdp", None)
    bias = P(None, None, "fsdp")
    pairs = (weight, bias) * 5
    return jax.shard_map(
        shards,
        mesh=mesh,
        in_specs=(tokens, tokens, P("fsdp", None), P("fsdp")) + pairs + (tokens, tokens),
        out_specs=(tokens, tokens, tokens, tokens, P("fsdp", None)) + pairs,
        check_vma=False,
    )
```

```python
import functools

import jax
import jax.numpy as jnp
from jax import lax
from jax.experimental import pallas as pl
from jax.experimental.layout import Layout, with_layout_constraint
from jax.experimental.pallas import tpu as pltpu
from jax.sharding import PartitionSpec as P

HEAD_DIM = 64
NORM_EPS = 1e-06
MASKED_SCORE = -1e30
VMEM_LIMIT = 60 * 2**20


def mm(left, right):
    return lax.dot_general(left, right, (((1,), (0,)), ((), ())), preferred_element_type=jnp.float32)


def key_scores(key_image, key_text, query_t, open_text, scale):
    image = mm(key_image, query_t) * scale
    text = jnp.where(open_text > 0.0, mm(key_text, query_t) * scale, MASKED_SCORE)
    return image, text


def attention_kernel(part, scale, image_ref, text_ref, open_ref, out_image, out_text, lse_image, lse_text):
    heads = part // HEAD_DIM
    b16 = jnp.bfloat16
    open_text = open_ref[0, :, :1]

    def columns(ref, kind, head):
        return ref[0, :, kind * part + head * HEAD_DIM : kind * part + (head + 1) * HEAD_DIM]

    keys = [(columns(image_ref, 1, h), columns(text_ref, 1, h)) for h in range(heads)]
    values_t = (image_ref[0, :, 2 * part :].T, text_ref[0, :, 2 * part :].T)

    def block(queries, width):
        queries_t = queries.T
        mixed, lse = [], []
        for h in range(heads):
            at = slice(h * HEAD_DIM, (h + 1) * HEAD_DIM)
            image, text = key_scores(*keys[h], queries_t[at], open_text, scale)
            top = jnp.maximum(
                jnp.max(image, 0, keepdims=True), jnp.max(text, 0, keepdims=True)
            )
            image, text = jnp.exp(image - top), jnp.exp(text - top)
            total = jnp.sum(image, 0, keepdims=True) + jnp.sum(text, 0, keepdims=True)
            out_t = mm(values_t[0][at], image.astype(b16)) + mm(values_t[1][at], text.astype(b16))
            mixed.append(out_t / total)
            lse.append(top + jnp.log(total))
        lse.append(jnp.zeros((8 - heads, width), jnp.float32))
        return jnp.concatenate(mixed, 0).T.astype(b16), jnp.concatenate(lse, 0)

    step = 256

    def body(i, carry):
        rows = pl.ds(pl.multiple_of(i * step, step), step)
        mixed, lse = block(image_ref[0, rows, :part], step)
        out_image[0, rows, :] = mixed
        lse_image[0, :, rows] = lse
        return carry

    lax.fori_loop(0, image_ref.shape[1] // step, body, 0)
    mixed, lse = block(text_ref[0, :, :part], text_ref.shape[1])
    out_text[0] = mixed
    lse_text[0] = lse


def attention(image_qkv, text_qkv, open_text, scale):
    two, image_rows, columns = image_qkv.shape
    text_rows, part = text_qkv.shape[1], columns // 3

    def spec(*dims):
        return pl.BlockSpec((1,) + dims, lambda i: (i, 0, 0))

    return pl.pallas_call(
        functools.partial(attention_kernel, part, scale),
        grid=(two,),
        in_specs=[spec(image_rows, columns), spec(text_rows, columns), spec(text_rows, 128)],
        out_specs=[
            spec(image_rows, part),
            spec(text_rows, part),
            spec(8, image_rows),
            spec(8, text_rows),
        ],
        out_shape=[
            jax.ShapeDtypeStruct((two, image_rows, part), jnp.bfloat16),
            jax.ShapeDtypeStruct((two, text_rows, part), jnp.bfloat16),
            jax.ShapeDtypeStruct((two, 8, image_rows), jnp.float32),
            jax.ShapeDtypeStruct((two, 8, text_rows), jnp.float32),
        ],
        compiler_params=pltpu.CompilerParams(vmem_limit_bytes=VMEM_LIMIT),
        cost_estimate=pl.CostEstimate(flops=0, bytes_accessed=90_000_000, transcendentals=0),
        name="attention",
    )(image_qkv, text_qkv, open_text)


def attention_back_kernel(
    part, scale, image_ref, text_ref, open_ref, lse_image, lse_text, up_image, up_text,
    out_image, out_text, d_keys, d_values,
):
    heads = part // HEAD_DIM
    b16 = jnp.bfloat16
    open_text = open_ref[0, :, :1]
    image_rows = image_ref.shape[1]

    def columns(ref, kind, head):
        return ref[0, :, kind * part + head * HEAD_DIM : kind * part + (head + 1) * HEAD_DIM]

    keys = [(columns(image_ref, 1, h), columns(text_ref, 1, h)) for h in range(heads)]
    values = [(columns(image_ref, 2, h), columns(text_ref, 2, h)) for h in range(heads)]
    keys_t = (image_ref[0, :, part : 2 * part].T, text_ref[0, :, part : 2 * part].T)

    def block(queries, ups, lse, first):
        queries_t, ups_t = queries.T, ups.T
        d_queries = []
        for h in range(heads):
            at = slice(h * HEAD_DIM, (h + 1) * HEAD_DIM)
            image, text = key_scores(*keys[h], queries_t[at], open_text, scale)
            row = lse[h : h + 1]
            image, text = jnp.exp(image - row), jnp.exp(text - row)
            up_rows = ups[:, at]
            terms = (mm(image.astype(b16), up_rows), mm(text.astype(b16), up_rows))
            d_image = mm(values[h][0], ups_t[at]) * image
            d_text = mm(values[h][1], ups_t[at]) * text
            row = jnp.sum(d_image, 0, keepdims=True) + jnp.sum(d_text, 0, keepdims=True)
            d_image = (d_image - row * image).astype(b16)
            d_text = (d_text - row * text).astype(b16)
            query_rows = queries[:, at]
            more = (mm(d_image, query_rows), mm(d_text, query_rows))
            d_queries.append((mm(keys_t[0][at], d_image) + mm(keys_t[1][at], d_text)) * scale)
            for ref, (a, b) in ((d_values, terms), (d_keys, more)):
                if first:
                    ref[h, :image_rows] = a
                    ref[h, image_rows:] = b
                else:
                    ref[h, :image_rows] += a
                    ref[h, image_rows:] += b
        return jnp.concatenate(d_queries, 0).T.astype(b16)

    step = 256
    out_text[0, :, :part] = block(text_ref[0, :, :part], up_text[0], lse_text[0], True)

    def body(i, carry):
        rows = pl.ds(pl.multiple_of(i * step, step), step)
        out_image[0, rows, :part] = block(
            image_ref[0, rows, :part], up_image[0, rows, :], lse_image[0, :, rows], False
        )
        return carry

    lax.fori_loop(0, image_rows // step, body, 0)
    for h in range(heads):
        for kind, ref, factor in ((1, d_keys, scale), (2, d_values, 1.0)):
            at = slice(kind * part + h * HEAD_DIM, kind * part + (h + 1) * HEAD_DIM)
            out_image[0, :, at] = (ref[h, :image_rows] * factor).astype(b16)
            out_text[0, :, at] = (ref[h, image_rows:] * factor).astype(b16)


def attention_back(image_qkv, text_qkv, open_text, lse_image, lse_text, up_image, up_text, scale):
    two, image_rows, columns = image_qkv.shape
    text_rows, part = text_qkv.shape[1], columns // 3
    heads = part // HEAD_DIM

    def spec(*dims):
        return pl.BlockSpec((1,) + dims, lambda i: (i, 0, 0))

    return pl.pallas_call(
        functools.partial(attention_back_kernel, part, scale),
        grid=(two,),
        in_specs=[
            spec(image_rows, columns),
            spec(text_rows, columns),
            spec(text_rows, 128),
            spec(8, image_rows),
            spec(8, text_rows),
            spec(image_rows, part),
            spec(text_rows, part),
        ],
        out_specs=[spec(image_rows, columns), spec(text_rows, columns)],
        out_shape=[
            jax.ShapeDtypeStruct(image_qkv.shape, jnp.bfloat16),
            jax.ShapeDtypeStruct(text_qkv.shape, jnp.bfloat16),
        ],
        scratch_shapes=[
            pltpu.VMEM((heads, image_rows + text_rows, HEAD_DIM), jnp.float32),
            pltpu.VMEM((heads, image_rows + text_rows, HEAD_DIM), jnp.float32),
        ],
        compiler_params=pltpu.CompilerParams(vmem_limit_bytes=VMEM_LIMIT),
        cost_estimate=pl.CostEstimate(flops=0, bytes_accessed=200_000_000, transcendentals=0),
        name="attention_back",
    )(image_qkv, text_qkv, open_text, lse_image, lse_text, up_image, up_text)


MESH = pl.DeviceIdType.MESH


def group_peers():
    f, s = lax.axis_index("fsdp"), lax.axis_index("seq")
    return {"r": (f ^ 1, s), "x": (f, s ^ 2), "c": (f, s ^ 1)}


def greet(peers):
    barrier = pltpu.get_barrier_semaphore()
    for peer in peers.values():
        pl.semaphore_signal(barrier, inc=1, device_id=peer, device_id_type=MESH)
    pl.semaphore_wait(barrier, len(peers))


def gather_kernel(work, extra, outs, own_image, own_text, *refs):
    extra_refs, (image, text) = refs[:extra], refs[extra : extra + 2]
    out_refs = refs[extra + 2 : extra + 2 + outs]
    local_sem, send_sem, recv_sem, *scratch = refs[extra + 2 + outs :]
    peers = group_peers()
    begin, run, finish = work(extra_refs, out_refs, scratch, peers)
    begin()
    cut = own_image.shape[1] // 2
    halves = {"a": pl.ds(0, cut), "b": pl.ds(cut, cut), "all": pl.ds(0, 2 * cut)}
    own, full = (own_image, own_text), (image, text)
    greet(peers)
    count = [0]

    def send(peer, source, piece, columns):
        copies = []
        for m in range(2):
            at = own[m].at[:, halves[columns]]
            if source is not None:
                at = full[m].at[source[0], source[1], :, halves[columns]]
            copy = pltpu.make_async_remote_copy(
                src_ref=at,
                dst_ref=full[m].at[piece[0], piece[1], :, halves[columns]],
                send_sem=send_sem.at[count[0]],
                recv_sem=recv_sem.at[count[0]],
                device_id=peers[peer],
                device_id_type=MESH,
            )
            copy.start()
            count[0] += 1
            copies.append(copy)
        return copies

    def landed(copies):
        for copy in copies:
            copy.wait_recv()

    a_r = send("r", None, (1, 0), "a")
    b_x = send("x", None, (0, 2), "b")
    a_x = send("x", None, (0, 2), "a")
    b_r = send("r", None, (1, 0), "b")
    all_c = send("c", None, (0, 1), "all")
    local = []
    for m in range(2):
        copy = pltpu.make_async_copy(own[m], full[m].at[0, 0], local_sem.at[m])
        copy.start()
        local.append(copy)
    landed(a_r)
    a_rx = send("x", (1, 0), (1, 2), "a")
    a_rc = send("c", (1, 0), (1, 1), "a")
    landed(b_x)
    b_xr = send("r", (0, 2), (1, 2), "b")
    b_xc = send("c", (0, 2), (0, 3), "b")
    run()
    landed(a_x)
    a_xc = send("c", (0, 2), (0, 3), "a")
    landed(b_r)
    b_rc = send("c", (1, 0), (1, 1), "b")
    landed(a_rx)
    a_rxc = send("c", (1, 2), (1, 3), "a")
    landed(b_xr)
    b_xrc = send("c", (1, 2), (1, 3), "b")
    for copies in (all_c, a_rc, b_xc, a_xc, b_rc, a_rxc, b_xrc):
        landed(copies)
    for copies in (a_r, b_x, a_x, b_r, all_c, a_rx, a_rc, b_xr, b_xc, a_xc, b_rc, a_rxc, b_xrc):
        for copy in copies:
            copy.wait_send()
    for copy in local:
        copy.wait()
    finish()


def no_work(extra, outs, scratch, peers):
    return (lambda: None,) * 3


def gather_group(
    image, text, collective_id, work=no_work, extra=(), outs=(), scratch=(), micros=35
):
    full = [jax.ShapeDtypeStruct((2, 4) + v.shape, v.dtype) for v in (image, text)]
    anywhere = pl.BlockSpec(memory_space=pl.ANY)
    return pl.pallas_call(
        functools.partial(gather_kernel, work, len(extra), len(outs)),
        in_specs=[anywhere] * (2 + len(extra)),
        out_specs=[anywhere] * (2 + len(outs)),
        out_shape=full + list(outs),
        scratch_shapes=[
            pltpu.SemaphoreType.DMA((2,)),
            pltpu.SemaphoreType.DMA((26,)),
            pltpu.SemaphoreType.DMA((26,)),
        ]
        + list(scratch),
        compiler_params=pltpu.CompilerParams(
            collective_id=collective_id, has_side_effects=True, vmem_limit_bytes=VMEM_LIMIT
        ),
        cost_estimate=pl.CostEstimate(
            flops=0, bytes_accessed=micros * 3_700_000, transcendentals=0
        ),
        name="gather_group",
    )(image, text, *extra)


def copies_of(sources, targets, sems, first):
    return [
        pltpu.make_async_copy(source, target, sems.at[first + i])
        for i, (source, target) in enumerate(zip(sources, targets))
    ]


def start_all(copies):
    for copy in copies:
        copy.start()


def wait_all(copies):
    for copy in copies:
        copy.wait()


def first_layer_work(extra, outs, scratch, peers):
    *held, before_image, before_text, active_image, active_text, sems = scratch
    results = (before_image, before_text, active_image, active_text)
    loads = copies_of(extra, held, sems, 0)
    stores = copies_of(results, outs, sems, 4)
    hidden_image, hidden_text, weight, bias = held

    def layer(rows, m):
        before = mm(rows, weight[m]) + bias[m : m + 1]
        inner = 0.7978845608028654 * (before + 0.044715 * before * before * before)
        return before, (0.5 * before * (1.0 + jnp.tanh(inner))).astype(jnp.bfloat16)

    def run():
        wait_all(loads)

        def body(i, carry):
            rows = pl.ds(pl.multiple_of(i * 256, 256), 256)
            before_image[rows, :], active_image[rows, :] = layer(hidden_image[rows, :], 0)
            return carry

        lax.fori_loop(0, hidden_image.shape[0] // 256, body, 0)
        before_text[...], active_text[...] = layer(hidden_text[...], 1)
        start_all(stores)

    return functools.partial(start_all, loads), run, functools.partial(wait_all, stores)


def second_layer_work(extra, outs, scratch, peers):
    active_image, active_text, weight, terms, got, sems, send_sem, recv_sem = scratch
    f32, b16 = jnp.float32, jnp.bfloat16
    loads = copies_of(extra, scratch[:3], sems, 0)
    pieces = 8
    cut = terms.shape[3] // 2
    first, last = pl.ds(0, cut), pl.ds(cut, cut)
    sources, targets = [], []
    for at in range(2):
        for i in range(2):
            sources += [terms.at[0, 2 * i + at, :, first], terms.at[0, 2 * at + i, :, last]]
            targets += [outs[at].at[i], outs[2 + at].at[i]]
    stores = copies_of(sources, targets, sems, 3)
    image_rows, text_rows = active_image.shape[0] // pieces, active_text.shape[0] // pieces
    swap = pltpu.make_async_remote_copy(
        src_ref=terms.at[1],
        dst_ref=got,
        send_sem=send_sem,
        recv_sem=recv_sem,
        device_id=peers["c"],
        device_id_type=MESH,
    )

    def run():
        wait_all(loads)

        def body(i, carry):
            rows = pl.ds(pl.multiple_of(i * image_rows, image_rows), image_rows)
            product = mm(active_image[rows, :], weight[0]).astype(b16)
            terms[i % 2, i // 2, :image_rows, :] = product
            return carry

        lax.fori_loop(0, pieces, body, 0)
        product = mm(active_text[...], weight[1])
        for i in range(pieces):
            rows = product[i * text_rows : (i + 1) * text_rows].astype(b16)
            terms[i % 2, i // 2, image_rows:, :] = rows
        swap.start()

    def finish():
        swap.wait()
        for i in range(pieces // 2):
            terms[0, i] = (terms[0, i].astype(f32) + got[i].astype(f32)).astype(b16)
        start_all(stores)
        wait_all(stores)

    return functools.partial(start_all, loads), run, finish


def weight_terms_work(extra, outs, scratch, peers):
    left_image, left_text, right_image, right_text, terms, sems = scratch
    loads = copies_of(extra, scratch[:4], sems, 0)
    stores = copies_of([terms], outs, sems, 4)
    block = 256

    def inner(left, right):
        return lax.dot_general(
            left, right, (((0,), (0,)), ((), ())), preferred_element_type=jnp.float32
        ).astype(jnp.bfloat16)

    def run():
        wait_all(loads)

        def body(i, carry):
            columns = pl.ds(pl.multiple_of(i * block, block), block)
            terms[0, columns, :] = inner(left_image[:, columns], right_image[...])
            terms[1, columns, :] = inner(left_text[:, columns], right_text[...])
            return carry

        lax.fori_loop(0, terms.shape[1] // block, body, 0)
        start_all(stores)

    return functools.partial(start_all, loads), run, functools.partial(wait_all, stores)


def held(arrays):
    return [pltpu.VMEM(v.shape, v.dtype) for v in arrays]


def reduce_kernel(epilogue, extra, outs, work, work_extra, work_outs, image, text, *refs):
    extra_refs, refs = refs[:extra], refs[extra:]
    work_refs, refs = refs[:work_extra], refs[work_extra:]
    out_refs, refs = refs[:outs], refs[outs:]
    work_out_refs, refs = refs[:work_outs], refs[work_outs:]
    (
        mine, near, acc, got_a, got_b, acc_a, acc_b, last_a, last_b, total,
        load_sem, send_sem, recv_sem, *scratch,
    ) = refs
    f32, b16 = jnp.float32, jnp.bfloat16
    peers = group_peers()
    begin, run, finish = work(work_refs, work_out_refs, scratch, peers)
    t_image = image.shape[2]
    cut = image.shape[3] // 2
    spans = (pl.ds(0, t_image), pl.ds(t_image, text.shape[2]))
    sources = (image, text)
    corners = [(1, 1), (0, 1), (1, 0), (0, 0)]
    loads = {}
    for i, (dr, dx) in enumerate(corners):
        loads[dr, dx] = []
        for m in range(2):
            copy = pltpu.make_async_copy(
                sources[m].at[dr, dx * 2], mine.at[dr * 2 + dx, spans[m]], load_sem.at[2 * i + m]
            )
            copy.start()
            loads[dr, dx].append(copy)
    begin()
    greet(peers)
    started = []

    def send(peer, source, target):
        copy = pltpu.make_async_remote_copy(
            src_ref=source,
            dst_ref=target,
            send_sem=send_sem.at[len(started)],
            recv_sem=recv_sem.at[len(started)],
            device_id=peers[peer],
            device_id_type=MESH,
        )
        copy.start()
        started.append(copy)
        return copy

    near_copies = {
        (dr, dx): [
            send("c", sources[m].at[dr, dx * 2 + 1], near.at[dr * 2 + dx, spans[m]])
            for m in range(2)
        ]
        for dr, dx in corners
    }
    a, b = slice(None, cut), slice(cut, None)

    def plus(left, right):
        return (left.astype(f32) + right.astype(f32)).astype(b16)

    far = {}
    for dr, dx in corners:
        at = dr * 2 + dx
        for copy in loads[dr, dx]:
            copy.wait()
        for copy in near_copies[dr, dx]:
            copy.wait_recv()
        acc[at] = plus(mine[at], near[at])
        if dx == 1:
            far["a", dr] = send("x", acc.at[at, :, pl.ds(0, cut)], got_a.at[dr])
        if dr == 1:
            far["b", dx] = send("r", acc.at[at, :, pl.ds(cut, cut)], got_b.at[dx])
    run()
    far["a", 1].wait_recv()
    acc_a[1] = plus(acc[2, :, a], got_a[1])
    to_a = send("r", acc_a.at[1], last_a)
    far["b", 1].wait_recv()
    acc_b[1] = plus(acc[1, :, b], got_b[1])
    to_b = send("x", acc_b.at[1], last_b)
    far["a", 0].wait_recv()
    acc_a[0] = plus(acc[0, :, a], got_a[0])
    far["b", 0].wait_recv()
    acc_b[0] = plus(acc[0, :, b], got_b[0])
    to_a.wait_recv()
    total[:, a] = acc_a[0].astype(f32) + last_a[...].astype(f32)
    to_b.wait_recv()
    total[:, b] = acc_b[0].astype(f32) + last_b[...].astype(f32)
    epilogue(total, t_image, extra_refs, out_refs)
    for copy in started:
        copy.wait_send()
    finish()


def reduce_group(
    image, text, collective_id, epilogue, extra, outs,
    work=no_work, work_extra=(), work_outs=(), scratch=(), micros=40,
):
    anywhere = pl.BlockSpec(memory_space=pl.ANY)
    rows, width = image.shape[2] + text.shape[2], image.shape[3]
    b16 = jnp.bfloat16
    half = (rows, width // 2)
    return pl.pallas_call(
        functools.partial(
            reduce_kernel, epilogue, len(extra), len(outs), work, len(work_extra), len(work_outs)
        ),
        in_specs=[anywhere] * 2
        + [pl.BlockSpec(memory_space=pltpu.VMEM)] * len(extra)
        + [anywhere] * len(work_extra),
        out_specs=[pl.BlockSpec(memory_space=pltpu.VMEM)] * len(outs)
        + [anywhere] * len(work_outs),
        out_shape=list(outs) + list(work_outs),
        scratch_shapes=[
            pltpu.VMEM((4, rows, width), b16),
            pltpu.VMEM((4, rows, width), b16),
            pltpu.VMEM((4, rows, width), b16),
            pltpu.VMEM((2,) + half, b16),
            pltpu.VMEM((2,) + half, b16),
            pltpu.VMEM((2,) + half, b16),
            pltpu.VMEM((2,) + half, b16),
            pltpu.VMEM(half, b16),
            pltpu.VMEM(half, b16),
            pltpu.VMEM((rows, width), jnp.float32),
            pltpu.SemaphoreType.DMA((8,)),
            pltpu.SemaphoreType.DMA((14,)),
            pltpu.SemaphoreType.DMA((14,)),
        ]
        + list(scratch),
        compiler_params=pltpu.CompilerParams(
            collective_id=collective_id, has_side_effects=True, vmem_limit_bytes=VMEM_LIMIT
        ),
        cost_estimate=pl.CostEstimate(
            flops=0, bytes_accessed=micros * 3_700_000, transcendentals=0
        ),
        name="reduce_group",
    )(image, text, *extra, *work_extra)


def row_norm(values):
    center = values - jnp.mean(values, -1, keepdims=True)
    inverse = lax.rsqrt(jnp.mean(center * center, -1, keepdims=True) + NORM_EPS)
    return center * inverse, inverse


def row_sums(values):
    return jnp.sum(values, 0, keepdims=True)


def middle_epilogue(total, t_image, extra, outs):
    vectors = extra[2]
    for m, rows in ((0, slice(None, t_image)), (1, slice(t_image, None))):
        bias, gate, shift, scale = [vectors[4 * m + i : 4 * m + i + 1] for i in range(4)]
        branch = total[rows] + bias
        middle = extra[m][...].astype(jnp.float32) + gate * branch
        normal, _ = row_norm(middle)
        outs[m][...] = branch
        outs[2 + m][...] = middle
        outs[4 + m][...] = (normal * (1.0 + scale) + shift).astype(jnp.bfloat16)


def norm_back(d_hidden, values, scale):
    normal, inverse = row_norm(values)
    e = d_hidden * (1.0 + scale)
    mean = jnp.mean(e, -1, keepdims=True)
    along = jnp.mean(e * normal, -1, keepdims=True)
    return (e - mean - normal * along) * inverse, row_sums(d_hidden), row_sums(d_hidden * normal)


def middle_back_epilogue(total, t_image, extra, outs):
    f32 = jnp.float32
    vectors, sums = extra[6], outs[4]
    for m, rows in ((0, slice(None, t_image)), (1, slice(t_image, None))):
        scale, gate = [vectors[2 * m + i : 2 * m + i + 1] for i in range(2)]
        d_norm, d_shift, d_scale = norm_back(total[rows], extra[m][...], scale)
        d_middle = extra[2 + m][...].astype(f32) + d_norm
        d_branch = (d_middle * gate).astype(jnp.bfloat16)
        outs[m][...] = d_middle
        outs[2 + m][...] = d_branch
        parts = (d_shift, d_scale, row_sums(d_middle * extra[4 + m][...]), row_sums(d_branch.astype(f32)))
        for i, part in enumerate(parts):
            sums[4 * m + i : 4 * m + i + 1] = part


def input_back_epilogue(total, t_image, extra, outs):
    vectors, sums = extra[4], outs[2]
    sums[...] = jnp.zeros(sums.shape, jnp.float32)
    for m, rows in ((0, slice(None, t_image)), (1, slice(t_image, None))):
        d_norm, d_shift, d_scale = norm_back(
            total[rows], extra[m][...].astype(jnp.float32), vectors[m : m + 1]
        )
        outs[m][...] = extra[2 + m][...] + d_norm
        sums[2 * m : 2 * m + 1] = d_shift
        sums[2 * m + 1 : 2 * m + 2] = d_scale


def modulation_kernel(
    owners, parts, slab, send, weight, small_out, act_out, mods_out,
    small, piece, term, got, mods, load_sem, sems,
):
    f, s = lax.axis_index("fsdp"), lax.axis_index("seq")
    quarter = piece.shape[2]
    columns = pl.ds(pl.multiple_of(s * quarter, 128), quarter)
    load = pltpu.make_async_copy(weight.at[:, :, columns], piece, load_sem)
    load.start()
    barrier = pltpu.get_barrier_semaphore()
    for k in range(1, owners):
        pl.semaphore_signal(
            barrier, inc=1, device_id=(lax.rem(f + k, owners), s), device_id_type=MESH
        )
    for q in range(1, parts):
        pl.semaphore_signal(barrier, inc=1, device_id=(f, s ^ q), device_id_type=MESH)
    pl.semaphore_wait(barrier, owners + parts - 2)

    def exchange(source, target, stage):
        copies = []
        for k in range(1, owners):
            peer = lax.rem(f + k, owners)
            copy = pltpu.make_async_remote_copy(
                src_ref=source.at[peer],
                dst_ref=target.at[f],
                send_sem=sems.at[stage, 0, k],
                recv_sem=sems.at[stage, 1, k],
                device_id=(peer, s),
                device_id_type=MESH,
            )
            copy.start()
            copies.append(copy)
        target[f] = source[f]
        for copy in copies:
            copy.wait()

    exchange(send, small, 0)
    small_out[...] = small[...]
    act = jnp.concatenate([small[k, :, :slab] for k in range(owners)], 0)
    act = (act / (1.0 + jnp.exp(-act))).astype(jnp.bfloat16)
    act_out[...] = act
    load.wait()
    for m in range(2):
        full = mm(act, piece[m])
        for k in range(owners):
            for dr in range(2):
                term[k, dr * 2 + m : dr * 2 + m + 1, :] = full[k ^ dr : (k ^ dr) + 1]
    exchange(term, got, 1)
    total = got[0]
    for k in range(1, owners):
        total = total + got[k]
    mods[s] = total
    copies = []
    for q in range(1, parts):
        copy = pltpu.make_async_remote_copy(
            src_ref=mods.at[s],
            dst_ref=mods.at[s],
            send_sem=sems.at[2, 0, q],
            recv_sem=sems.at[2, 1, q],
            device_id=(f, s ^ q),
            device_id_type=MESH,
        )
        copy.start()
        copies.append(copy)
    for copy in copies:
        copy.wait()
    mods_out[...] = mods[...]


def modulation(send, weight, owners, parts):
    slab, columns = weight.shape[1], weight.shape[2]
    quarter = columns // parts
    f32 = jnp.float32
    return pl.pallas_call(
        functools.partial(modulation_kernel, owners, parts, slab),
        in_specs=[
            pl.BlockSpec(memory_space=pltpu.VMEM),
            pl.BlockSpec(memory_space=pl.ANY),
        ],
        out_specs=[pl.BlockSpec(memory_space=pltpu.VMEM)] * 3,
        out_shape=[
            jax.ShapeDtypeStruct(send.shape, f32),
            jax.ShapeDtypeStruct((owners, slab), jnp.bfloat16),
            jax.ShapeDtypeStruct((parts, 4, quarter), f32),
        ],
        scratch_shapes=[
            pltpu.VMEM(send.shape, f32),
            pltpu.VMEM((2, slab, quarter), jnp.bfloat16),
            pltpu.VMEM((owners, 4, quarter), f32),
            pltpu.VMEM((owners, 4, quarter), f32),
            pltpu.VMEM((parts, 4, quarter), f32),
            pltpu.SemaphoreType.DMA,
            pltpu.SemaphoreType.DMA((3, 2, owners)),
        ],
        compiler_params=pltpu.CompilerParams(
            collective_id=1, has_side_effects=True, vmem_limit_bytes=VMEM_LIMIT
        ),
        cost_estimate=pl.CostEstimate(
            flops=4 * owners * slab * quarter, bytes_accessed=60_000_000, transcendentals=0
        ),
        name="modulation",
    )(send, weight)


def finish_kernel(
    owners, with_proj, sums, qkv, proj, weight, sums_out, act_out, qkv_out, proj_out,
    mine, first, second, rounded, got, act, act_got, held_weight, local_sem, sems, far_sem,
):
    f, s = lax.axis_index("fsdp"), lax.axis_index("seq")
    r, z = f % 2, f // 2
    f32, b16 = jnp.float32, jnp.bfloat16
    load = pltpu.make_async_copy(weight, held_weight, local_sem.at[0])
    load.start()
    peers = {"y": (f ^ 1, s), "x": (f, s ^ 2), "c": (f, s ^ 1)}
    turned = (s * 2 + r, z)
    barrier = pltpu.get_barrier_semaphore()
    for k in range(1, owners):
        pl.semaphore_signal(
            barrier, inc=1, device_id=(lax.rem(f + k, owners), s), device_id_type=MESH
        )
    for peer in ("x", "c"):
        pl.semaphore_signal(barrier, inc=1, device_id=peers[peer], device_id_type=MESH)
    if with_proj:

        @pl.when(z != s)
        def _():
            pl.semaphore_signal(barrier, inc=1, device_id=turned, device_id_type=MESH)
            pl.semaphore_wait(barrier, owners + 2)

        @pl.when(z == s)
        def _():
            pl.semaphore_wait(barrier, owners + 1)

    else:
        pl.semaphore_wait(barrier, owners + 1)

    started = []

    def send(peer, source, target):
        copy = pltpu.make_async_remote_copy(
            src_ref=source,
            dst_ref=target,
            send_sem=sems.at[0, len(started)],
            recv_sem=sems.at[1, len(started)],
            device_id=peers[peer] if isinstance(peer, str) else peer,
            device_id_type=MESH,
        )
        copy.start()
        started.append(copy)
        return copy

    near_sums = send("x", sums, first)
    y_other = send("y", qkv.at[1 - r], qkv_out.at[r, s])
    x_keep = send("x", qkv.at[r], qkv_out.at[r, s])
    c_keep = send("c", qkv.at[r], qkv_out.at[r, s])
    own = pltpu.make_async_copy(qkv.at[r], qkv_out.at[r, s], local_sem.at[1])
    own.start()
    if with_proj:
        turn = pltpu.make_async_remote_copy(
            src_ref=proj,
            dst_ref=proj_out.at[z],
            send_sem=far_sem.at[0],
            recv_sem=far_sem.at[1],
            device_id=turned,
            device_id_type=MESH,
        )
        stay = pltpu.make_async_copy(proj, proj_out.at[s], far_sem.at[0])

        @pl.when(z != s)
        def _():
            turn.start()

        @pl.when(z == s)
        def _():
            stay.start()

    near_sums.wait_recv()
    mine[...] = sums[...] + first[...]
    send("c", mine, second).wait_recv()
    rounded[...] = (mine[...] + second[...]).astype(b16)
    spread = [
        send((lax.rem(f + k, owners), s), rounded, got.at[f]) for k in range(1, owners)
    ]
    got[f] = rounded[...]
    y_other.wait_recv()
    x_got = send("x", qkv_out.at[1 - r, s], qkv_out.at[1 - r, s])
    last = [c_keep, send("c", qkv_out.at[1 - r, s], qkv_out.at[1 - r, s])]
    x_keep.wait_recv()
    last.append(send("c", qkv_out.at[r, s ^ 2], qkv_out.at[r, s ^ 2]))
    if with_proj:

        @pl.when(z != s)
        def _():
            turn.wait()

        @pl.when(z == s)
        def _():
            stay.wait()

        x_proj = send("x", proj_out.at[s], proj_out.at[s])
        last.append(send("c", proj_out.at[s], proj_out.at[s]))
    for copy in spread:
        copy.wait_recv()
    load.wait()
    everyone = got[...].reshape(owners * sums.shape[0], sums.shape[1])
    rows, width = sums.shape
    per = 14
    total = [None] * owners
    for m in range(2):
        for i in range(6):
            part = lax.dot_general(
                everyone,
                held_weight[m, :, i * width : (i + 1) * width],
                (((1,), (1,)), ((), ())),
                preferred_element_type=f32,
            )
            for k in range(owners):
                row = part[k * rows + m * per + i : k * rows + m * per + i + 1]
                total[k] = row if total[k] is None else total[k] + row
    slab = held_weight.shape[1]
    act[...] = jnp.zeros(act.shape, f32)
    for k in range(owners):
        act[k, :, :slab] = total[k]
    act_got[f] = act[f]
    for k in range(1, owners):
        peer = lax.rem(f + k, owners)
        last.append(send((peer, s), act.at[peer], act_got.at[f]))
    sums_out[...] = got[...]
    x_got.wait_recv()
    last.append(send("c", qkv_out.at[1 - r, s ^ 2], qkv_out.at[1 - r, s ^ 2]))
    if with_proj:
        x_proj.wait_recv()
        last.append(send("c", proj_out.at[s ^ 2], proj_out.at[s ^ 2]))
    for copy in last:
        copy.wait_recv()
    act_out[...] = act_got[...]
    own.wait()
    for copy in started:
        copy.wait_send()


def finish(sums, qkv, proj, weight, owners, with_proj):
    f32, b16 = jnp.float32, jnp.bfloat16
    slab = weight.shape[1]
    anywhere = pl.BlockSpec(memory_space=pl.ANY)
    inside = pl.BlockSpec(memory_space=pltpu.VMEM)
    all_sums = (owners,) + sums.shape
    all_act = (owners, 1, -(-slab // 128) * 128)
    count = 2 * owners + 12
    return pl.pallas_call(
        functools.partial(finish_kernel, owners, with_proj),
        in_specs=[inside, anywhere, anywhere, anywhere],
        out_specs=[inside, inside, anywhere, anywhere],
        out_shape=[
            jax.ShapeDtypeStruct(all_sums, b16),
            jax.ShapeDtypeStruct(all_act, f32),
            jax.ShapeDtypeStruct((2, 4) + qkv.shape[1:], b16),
            jax.ShapeDtypeStruct((4,) + proj.shape, b16),
        ],
        scratch_shapes=[
            pltpu.VMEM(sums.shape, f32),
            pltpu.VMEM(sums.shape, f32),
            pltpu.VMEM(sums.shape, f32),
            pltpu.VMEM(sums.shape, b16),
            pltpu.VMEM(all_sums, b16),
            pltpu.VMEM(all_act, f32),
            pltpu.VMEM(all_act, f32),
            pltpu.VMEM(weight.shape, b16),
            pltpu.SemaphoreType.DMA((2,)),
            pltpu.SemaphoreType.DMA((2, count)),
            pltpu.SemaphoreType.DMA((2,)),
        ],
        compiler_params=pltpu.CompilerParams(
            collective_id=2, has_side_effects=True, vmem_limit_bytes=VMEM_LIMIT
        ),
        cost_estimate=pl.CostEstimate(flops=0, bytes_accessed=130_000_000, transcendentals=0),
        name="finish",
    )(sums, qkv, proj, weight)


def pick_kernel(part, line, place, *refs):
    qkv, hid = refs[:3], refs[3 : 3 + 2 * line]
    qkv_own, qkv_other, hid_own, hid_other = refs[3 + 2 * line :]
    high, odd = place[1] == 1, place[2] == 1
    for kind in range(3):
        for m in range(2):
            at = slice((m * 3 + kind) * part, (m * 3 + kind + 1) * part)
            low, up = qkv[kind][m, :, :part], qkv[kind][m, :, part:]
            qkv_own[:, at] = jnp.where(high, up, low)
            qkv_other[:, at] = jnp.where(high, low, up)
    for z in range(line):
        chosen = []
        for q in range(2):
            block = hid[z * 2 + q]
            cut = block.shape[2] // 2
            chosen.append(jnp.where(odd, block[:, :, cut:], block[:, :, :cut]))
        at = slice(z * cut, (z + 1) * cut)
        hid_own[:, :, at] = jnp.where(high, chosen[1], chosen[0])
        hid_other[:, :, at] = jnp.where(high, chosen[0], chosen[1])


def pick_parts(qkv_weight, hidden_weight, s, r, part, line):
    slab, width = qkv_weight.shape[1], qkv_weight.shape[2] // 3
    units = hidden_weight.shape[2] // (2 * line)
    place = jnp.stack([s, r, s % 2]).astype(jnp.int32)
    per_kind = width // (2 * part)

    def qkv_spec(kind):
        return pl.BlockSpec((2, slab, 2 * part), lambda i, at: (0, 0, kind * per_kind + at[0]))

    def hid_spec(f):
        return pl.BlockSpec((2, slab, units // 2), lambda i, at: (0, 0, 2 * f + at[0] // 2))

    shapes = [(slab, 6 * part)] * 2 + [(2, slab, line * units // 4)] * 2
    return pl.pallas_call(
        functools.partial(pick_kernel, part, line),
        grid_spec=pltpu.PrefetchScalarGridSpec(
            num_scalar_prefetch=1,
            grid=(1,),
            in_specs=[qkv_spec(k) for k in range(3)] + [hid_spec(f) for f in range(2 * line)],
            out_specs=[
                pl.BlockSpec(dims, lambda i, at, n=len(dims): (0,) * n) for dims in shapes
            ],
        ),
        out_shape=[jax.ShapeDtypeStruct(dims, jnp.bfloat16) for dims in shapes],
        compiler_params=pltpu.CompilerParams(vmem_limit_bytes=VMEM_LIMIT),
        name="pick_parts",
    )(place, *([qkv_weight] * 3), *([hidden_weight] * (2 * line)))


def chosen_piece(pieces, x, c, q):
    near = [jnp.where(c == q % 2, pieces[2 * dx], pieces[2 * dx + 1]) for dx in range(2)]
    return jnp.where(x == q // 2, near[0], near[1])


def stacked_kernel(image, text, up_image, up_text, proj, out):
    b16 = jnp.bfloat16
    rows, part = image.shape[1], up_image.shape[1]
    wide = 2 * part

    def inner(left, right):
        return lax.dot_general(
            left[...], right[...], (((0,), (0,)), ((), ())), preferred_element_type=jnp.float32
        ).astype(b16)

    out[0, :rows, :part] = inner(image, up_image)
    out[0, :rows, part:] = inner(text, up_text)
    more = jnp.concatenate([proj[0], proj[1]], 0)
    count = more.shape[0]
    out[0, rows : rows + count, :] = more[:, :wide]
    third, left = count // 3, wide // 3
    for i in range(3):
        out[0, rows + count :, i * left : (i + 1) * left] = more[i * third : (i + 1) * third, wide:]


def stacked_terms(hidden, ups, proj, line):
    rows = hidden[0].shape[1] // line
    part, chunk, width = ups[0].shape[1], proj.shape[1] // line, proj.shape[2]
    more = 2 * chunk * width // (2 * part)
    return pl.pallas_call(
        stacked_kernel,
        grid=(line,),
        in_specs=[pl.BlockSpec((v.shape[0], rows), lambda z: (0, z)) for v in hidden]
        + [pl.BlockSpec(v.shape, lambda z: (0, 0)) for v in ups]
        + [pl.BlockSpec((2, chunk, width), lambda z: (0, z, 0))],
        out_specs=pl.BlockSpec((1, rows + more, 2 * part), lambda z: (z, 0, 0)),
        out_shape=jax.ShapeDtypeStruct((line, rows + more, 2 * part), jnp.bfloat16),
        compiler_params=pltpu.CompilerParams(vmem_limit_bytes=VMEM_LIMIT),
        cost_estimate=pl.CostEstimate(flops=0, bytes_accessed=35_000_000, transcendentals=0),
        name="stacked_terms",
    )(*hidden, *ups, proj)


def columns_kernel(chunk, kinds, inner_first, place, *refs):
    out = refs[8]
    r, x, c = place[0], place[1], place[2]
    for m in range(out.shape[1]):
        for kind in range(kinds):
            at = slice((m * kinds + kind) * chunk, (m * kinds + kind + 1) * chunk)
            by_dr = [
                [chosen_piece([refs[dr * 4 + p][:, at] for p in range(4)], x, c, q) for q in range(4)]
                for dr in range(2)
            ]
            for q in range(4):
                for natural in range(2):
                    value = jnp.where(r == natural, by_dr[0][q], by_dr[1][q])
                    spot = q * 2 + natural if inner_first else natural * 4 + q
                    start = (kind * 8 + spot) * chunk
                    out[0, m, :, start : start + chunk] = value.astype(jnp.float32)


def natural_columns_kernel(chunk, kinds, pieces, out):
    for m in range(2):
        for kind in range(kinds):
            at = slice((m * kinds + kind) * chunk, (m * kinds + kind + 1) * chunk)
            for q in range(4):
                for p in range(2):
                    start = (kind * 8 + q * 2 + p) * chunk
                    out[0, m, :, start : start + chunk] = pieces[p, q, :, at].astype(jnp.float32)


def join_natural_columns(pieces, chunk, kinds):
    rows, columns = pieces.shape[2], 8 * kinds * chunk
    step = 48 if rows % 48 == 0 else rows
    return pl.pallas_call(
        functools.partial(natural_columns_kernel, chunk, kinds),
        grid=(rows // step,),
        in_specs=[pl.BlockSpec((2, 4, step, pieces.shape[3]), lambda i: (0, 0, i, 0))],
        out_specs=pl.BlockSpec((1, 2, step, columns), lambda i: (0, 0, i, 0)),
        out_shape=jax.ShapeDtypeStruct((1, 2, rows, columns), jnp.float32),
        compiler_params=pltpu.CompilerParams(vmem_limit_bytes=VMEM_LIMIT),
        name="join_natural_columns",
    )(pieces)


def join_columns(pieces, place, chunk, kinds, inner_first):
    rows = pieces[0].shape[-2]
    columns = 8 * kinds * chunk
    step = 64 if rows % 64 == 0 else rows
    if pieces[0].ndim == 3:
        grid = (rows // step, 2)
        piece = pl.BlockSpec((None, step, columns // 8), lambda i, m, at: (m, i, 0))
        out = pl.BlockSpec((1, 1, step, columns), lambda i, m, at: (0, m, i, 0))
    else:
        grid = (rows // step,)
        piece = pl.BlockSpec((step, columns // 4), lambda i, at: (i, 0))
        out = pl.BlockSpec((1, 2, step, columns), lambda i, at: (0, 0, i, 0))
    return pl.pallas_call(
        functools.partial(columns_kernel, chunk, kinds, inner_first),
        grid_spec=pltpu.PrefetchScalarGridSpec(
            num_scalar_prefetch=1, grid=grid, in_specs=[piece] * 8, out_specs=out
        ),
        out_shape=jax.ShapeDtypeStruct((1, 2, rows, columns), jnp.float32),
        compiler_params=pltpu.CompilerParams(vmem_limit_bytes=VMEM_LIMIT),
        name="join_columns",
    )(place, *pieces)


def rows_kernel(place, *refs):
    out = refs[4]
    rows = refs[0].shape[1]
    for q in range(4):
        value = chosen_piece([refs[p][0] for p in range(4)], place[1], place[2], q)
        out[0, 0, q * rows : (q + 1) * rows, :] = value.astype(jnp.float32)


def join_rows(pieces, place):
    rows, columns = pieces[0].shape[1:]
    step = columns // 2
    return pl.pallas_call(
        rows_kernel,
        grid_spec=pltpu.PrefetchScalarGridSpec(
            num_scalar_prefetch=1,
            grid=(2, 2),
            in_specs=[pl.BlockSpec((1, rows, step), lambda m, i, at: (m, 0, i))] * 4,
            out_specs=pl.BlockSpec((1, 1, 4 * rows, step), lambda m, i, at: (0, m, 0, i)),
        ),
        out_shape=jax.ShapeDtypeStruct((1, 2, 4 * rows, columns), jnp.float32),
        compiler_params=pltpu.CompilerParams(vmem_limit_bytes=VMEM_LIMIT),
        name="join_rows",
    )(place, *pieces)


def rows_major(values):
    return with_layout_constraint(values, Layout(major_to_minor=(0, 1)))


def together(*values):
    return lax.optimization_barrier(values)


def norm_rows(values):
    center = values - jnp.mean(values, -1, keepdims=True)
    return center * lax.rsqrt(jnp.mean(center * center, -1, keepdims=True) + NORM_EPS)


def modulated(values, shift, scale_up):
    return norm_rows(values) * (1.0 + scale_up) + shift


def gelu_tanh(values):
    return jax.nn.gelu(values, approximate=True)


def dot32(left, right, contract):
    return lax.dot_general(
        left, right, ((contract[0], contract[1]), ((), ())), preferred_element_type=jnp.float32
    )


def product(left, right):
    return dot32(left, right, ((1,), (0,)))


def rows_inner(left, right):
    return dot32(left, right, ((0,), (0,)))


def right_back(left, right):
    return dot32(left, right, ((1,), (1,)))


def swap_r(values):
    count = lax.axis_size("fsdp")
    return lax.ppermute(values, "fsdp", [(at, at ^ 1) for at in range(count)])


def swap_x(values):
    return lax.ppermute(values, "seq", [(at, at ^ 2) for at in range(4)])


def swap_c(values):
    return lax.ppermute(values, "seq", [(at, at ^ 1) for at in range(4)])


CORNERS = [(0, 0), (0, 1), (1, 0), (1, 1)]


def reduce_far(a0, a1, b0, b1):
    return [a0[0], a0[1], b0[0], b0[1], swap_x(a1), swap_r(b1)]


def reduce_last(parts):
    f32, b16 = jnp.float32, jnp.bfloat16
    got_a, got_b = parts[4], parts[5]
    a = [(parts[dr].astype(f32) + got_a[dr].astype(f32)).astype(b16) for dr in range(2)]
    b = [(parts[2 + dx].astype(f32) + got_b[dx].astype(f32)).astype(b16) for dx in range(2)]
    last_a, last_b = swap_r(a[1]), swap_x(b[1])
    return jnp.concatenate(
        [a[0].astype(f32) + last_a.astype(f32), b[0].astype(f32) + last_b.astype(f32)], 1
    )


def shards(
    image_tokens,
    text_tokens,
    conditioning,
    text_lengths,
    mod_weight,
    mod_bias,
    qkv_weight,
    qkv_bias,
    proj_weight,
    proj_bias,
    hidden_weight,
    hidden_bias,
    output_weight,
    output_bias,
    image_cotangent,
    text_cotangent,
):
    f32, b16 = jnp.float32, jnp.bfloat16
    width = image_tokens.shape[2]
    counts = (image_tokens.shape[1], text_tokens.shape[1])
    parts = lax.axis_size("seq")
    owners = lax.axis_size("fsdp")
    line = owners // 2
    head_part = width // (2 * parts)
    heads_here = head_part // HEAD_DIM
    slab = width // owners
    units_slab = output_weight.shape[2]
    units_part = units_slab // parts
    units = units_slab * owners
    units_here = line * units_part
    score_scale = HEAD_DIM ** (-0.5)
    me = lax.axis_index("fsdp")
    s = lax.axis_index("seq")
    r = me % 2
    along = [[z * 2 + q for z in range(line)] for q in range(2)]
    direct_proj = line == parts
    image_rows, text_rows = counts[0] * parts, counts[1] * parts

    def cut(array, start, size, axis):
        return lax.dynamic_slice_in_dim(array, start, size, axis)

    def transpose_owners(values):
        pairs = [
            ((z * 2 + q) * parts + t, (t * 2 + q) * parts + z)
            for z in range(line)
            for q in range(2)
            for t in range(parts)
        ]
        return lax.ppermute(values, ("fsdp", "seq"), pairs)

    def line_gather(rows):
        return lax.all_gather(rows, "fsdp", axis=rows.ndim - 2, tiled=True, axis_index_groups=along)

    def line_reduce(term):
        return lax.psum_scatter(
            term, "fsdp", scatter_dimension=term.ndim - 2, tiled=True, axis_index_groups=along
        )

    def weight_terms(left, right):
        return jnp.stack([rows_inner(left[m], right[m]).astype(b16) for m in range(2)])

    def both_r(values):
        rows = values.reshape(values.shape[:-2] + (2, slab, -1))
        return pick(rows, r, values.ndim - 2), swap_r(pick(rows, 1 - r, values.ndim - 2))

    def by_r(own, other, axis):
        return jnp.where(r == 0, jnp.stack([own, other], axis), jnp.stack([other, own], axis))

    def pick(array, index, axis):
        return lax.dynamic_index_in_dim(array, index, axis, keepdims=False)

    biases = (mod_bias, qkv_bias, proj_bias, hidden_bias, output_bias)
    bias_sizes = [v.shape[2] for v in biases]
    bias_local = jnp.concatenate([v[0].astype(f32) for v in biases], 1)
    padded = -(-slab // 128) * 128
    common = jnp.concatenate([bias_local.reshape(-1), jnp.tile(text_lengths.astype(f32), 128)])
    if (2 * head_part) % 128 == 0 and (2 * units_part) % 128 == 0:
        qkv_own, qkv_other, hid_own, hid_other = pick_parts(
            qkv_weight[0], hidden_weight[0], s, r, head_part, line
        )
    else:
        qkv_view = qkv_weight[0].reshape(2, slab, 3, 2 * parts, head_part)
        qkv_own, qkv_other = [
            pick(qkv_view, s * 2 + at, 3).transpose(1, 0, 2, 3).reshape(slab, 6 * head_part)
            for at in (r, 1 - r)
        ]
        hid_view = pick(hidden_weight[0].reshape(2, slab, line, 2, parts, units_part), s, 4)
        hid_own, hid_other = [
            pick(hid_view, at, 3).reshape(2, slab, units_here) for at in (r, 1 - r)
        ]
    qkv_got = swap_r(qkv_other)
    proj_mine = proj_weight[0]
    if direct_proj:
        chunk = slab // parts
        proj_mine = transpose_owners(cut(proj_weight[0], s * chunk, chunk, 1))
    qkv_mine = by_r(qkv_own, qkv_got, 0).reshape(2 * slab, 6 * head_part)
    hid_got = swap_r(hid_other)
    cond_in, qkv_mine, proj_mine = together(conditioning, qkv_mine, proj_mine)
    send = jnp.concatenate(
        [
            cond_in.reshape(owners, slab),
            jnp.zeros((owners, padded - slab), f32),
            jnp.broadcast_to(common, (owners, common.shape[0])),
        ],
        1,
    )
    small, act_cols, mods = modulation(send[:, None], mod_weight[0], owners, parts)
    small = small[:, 0, padded:]
    lengths = [pick(small[:, -1], me ^ dr, 0) for dr in range(2)]
    bias_all = small[:, :-128].reshape(owners, 2, sum(bias_sizes))
    offsets = [0]
    for size in bias_sizes:
        offsets.append(offsets[-1] + size)
    mod_b, qkv_b, proj_b, hid_b, out_b = [
        bias_all[:, :, offsets[i] : offsets[i + 1]].transpose(1, 0, 2) for i in range(5)
    ]
    group = s * 2 + r
    qkv_b = cut(qkv_b.reshape(2, 2, width), group * head_part, head_part, 2)
    qkv_b = jnp.stack([qkv_b[:, 0], jnp.zeros_like(qkv_b[:, 0]), qkv_b[:, 1]], 1).reshape(
        2, 3 * head_part
    )
    proj_b = proj_b.reshape(2, width)
    out_b = out_b.reshape(2, width)
    hid_b = pick(pick(hid_b.reshape(2, line, 2, parts, units_part), s, 3), r, 2).reshape(
        2, units_here
    )
    mods = mods.reshape(parts, 2, 2, -1).transpose(1, 2, 0, 3).reshape(2, 2, 6 * width)
    mods = mods + mod_b.reshape(2, 6 * width)
    mod_part = mod_bias.shape[2]

    qkv_w = line_gather(qkv_mine)
    qkv_w = [qkv_w[:, m * 3 * head_part : (m + 1) * 3 * head_part] for m in range(2)]
    if direct_proj:
        proj_w = line_gather(proj_mine)
    else:
        proj_all = lax.all_gather(proj_mine, "fsdp", axis=1, tiled=True)
        proj_w = cut(proj_all, group * head_part, head_part, 1)
    mods, image_in, text_in, hid_got = together(mods, image_tokens[0], text_tokens[0], hid_got)
    x_full = [v.reshape(2, -1, width) for v in gather_group(image_in, text_in, 3)]
    hid_w = line_gather(by_r(hid_own, hid_got, 1).reshape(2, 2 * slab, units_here))
    out_w = line_gather(cut(output_weight[0], s * units_part, units_part, 1))

    def mod_at(index, m):
        at = slice(index * width, (index + 1) * width)
        return mods[0, m, None, at], mods[:, m, None, at]

    shift1, scale1, gate1, shift2, scale2, gate2 = [
        [mod_at(i, m) for m in range(2)] for i in range(6)
    ]

    def joined(pieces):
        return [v.reshape(2, -1, v.shape[-1]) for v in pieces]

    def apart(values, m):
        return values.reshape(2, parts, counts[m], -1)

    def flat(values):
        return values.reshape(-1, values.shape[-1])


    hidden1 = [
        flat(modulated(x_full[m].astype(f32), shift1[m][1], scale1[m][1]).astype(b16))
        for m in range(2)
    ]
    qkv = [rows_major((product(hidden1[m], qkv_w[m]) + qkv_b[m]).astype(b16)) for m in range(2)]
    qkv = [v.reshape(2, -1, 3 * head_part) for v in qkv]
    text_slot = jnp.arange(text_rows)
    text_place = ((text_slot // counts[1]) ^ s) * counts[1] + text_slot % counts[1]
    open_text = jnp.stack([(text_place.astype(f32) < n).astype(f32) for n in lengths])
    open_text = jnp.broadcast_to(open_text[:, :, None], (2, text_rows, 128))
    mixed_image, mixed_text, lse_image, lse_text = attention(*qkv, open_text, score_scale)
    attended = [flat(mixed_image), flat(mixed_text)]

    def like(pair, kind):
        return [jax.ShapeDtypeStruct(v.shape, kind) for v in pair]

    own = [image_tokens[0], text_tokens[0]]
    own_up = [image_cotangent[0], text_cotangent[0]]

    def summed(terms, *rest, **options):
        return list(reduce_group(*[apart(terms[m], m) for m in range(2)], *rest, **options))

    vectors = [v for m in range(2) for v in (proj_b[m, None], gate1[m][0], shift2[m][0], scale2[m][0])]
    reduced = summed(
        [product(attended[m], proj_w[m]).astype(b16) for m in range(2)],
        5,
        middle_epilogue,
        own + [jnp.concatenate(vectors, 0)],
        like(own, f32) + like(own, f32) + like(own, b16),
    )
    branch, middle = reduced[:2], reduced[2:4]
    hidden2 = [flat(v) for v in gather_group(*reduced[4:], 6)]

    shapes = [jax.ShapeDtypeStruct((v.shape[0], units_here), f32) for v in hidden2]
    shapes += [jax.ShapeDtypeStruct((v.shape[0], units_here), b16) for v in hidden2]
    extra = hidden2 + [hid_w, hid_b]
    image_up, text_up, extra[0] = together(*own_up, extra[0])
    gathered = gather_group(
        image_up,
        text_up,
        4,
        first_layer_work,
        extra,
        shapes,
        held(extra + shapes) + [pltpu.SemaphoreType.DMA((8,))],
    )
    g_full, before, active = joined(gathered[:2]), gathered[2:4], gathered[4:]
    d_result = [flat((g_full[m].astype(f32) * gate2[m][1]).astype(b16)) for m in range(2)]
    out_t = weight_terms(active, d_result)
    out_g = line_reduce(out_t)
    d_result[0], d_result[1], out_t = together(*d_result, out_t)
    d_before = []
    for m in range(2):
        d_active = right_back(d_result[m], out_w[m])
        d_before.append(jax.vjp(gelu_tanh, before[m])[1](d_active)[0].astype(b16))
    d_hidden2 = [right_back(d_before[m], hid_w[m]).astype(b16) for m in range(2)]

    vectors = [v for m in range(2) for v in (scale2[m][0], gate1[m][0])]
    hid_terms = jax.ShapeDtypeStruct((2, width, units_here), b16)
    reduced = summed(
        d_hidden2,
        7,
        middle_back_epilogue,
        list(middle) + own_up + list(branch) + [jnp.concatenate(vectors, 0)],
        like(own, f32) + like(own, b16) + [jax.ShapeDtypeStruct((8, width), f32)],
        weight_terms_work,
        hidden2 + d_before,
        [hid_terms],
        held(hidden2 + d_before + [hid_terms]) + [pltpu.SemaphoreType.DMA((5,))],
    )
    d_middle, d_branch, sums2, hid_t = reduced[:2], reduced[2:4], reduced[4], reduced[5]
    hid_g = line_reduce(hid_t)
    extra = list(active) + [out_w]
    corner = (4, sum(counts), width)
    gathered = list(gather_group(
        *d_branch,
        8,
        second_layer_work,
        extra,
        [jax.ShapeDtypeStruct((2, sum(counts), width // 2), b16)] * 4,
        held(extra)
        + [pltpu.VMEM((2,) + corner, b16), pltpu.VMEM(corner, b16), pltpu.SemaphoreType.DMA((11,))]
        + [pltpu.SemaphoreType.DMA] * 2,
        micros=90,
    ))
    gathered[0], out_g = together(gathered[0], out_g)
    d_branch_full = [flat(v) for v in gathered[:2]]
    result_near = gathered[2:]
    proj_t = weight_terms(attended, d_branch_full)
    d_attended = [
        rows_major(right_back(d_branch_full[m], proj_w[m]).astype(b16)).reshape(2, -1, head_part)
        for m in range(2)
    ]
    out_far = swap_x(out_g)
    d_attended[0], d_attended[1], proj_t = together(*d_attended, proj_t)
    result_far = reduce_far(*result_near)
    d_qkv = attention_back(*qkv, open_text, lse_image, lse_text, *d_attended, score_scale)
    d_qkv = [flat(v) for v in d_qkv]
    d_qkv[0], d_qkv[1], out_far, *result_far = together(*d_qkv, out_far, *result_far)
    wide = 6 * head_part
    merged = direct_proj and slab % 96 == 0
    if merged:
        qkv_t = stacked_terms(hidden1, d_qkv, proj_t, line)
    else:
        qkv_t = [rows_inner(hidden1[m], d_qkv[m]).astype(b16) for m in range(2)]
        qkv_t = jnp.concatenate(qkv_t, 1)
    both = line_reduce(qkv_t.reshape(-1, wide))
    result_last = reduce_last(result_far)
    d_qkv[0], d_qkv[1], qkv_t, hid_g = together(*d_qkv, qkv_t, hid_g)
    hid_keep, hid_got = both_r(hid_g)
    d_hidden1 = [right_back(d_qkv[m], qkv_w[m]).astype(b16) for m in range(2)]
    d_hidden1[0], d_hidden1[1], result_last, hid_keep = together(
        *d_hidden1, result_last, hid_keep
    )
    hid_far = swap_x(hid_keep)
    reduced = summed(
        d_hidden1,
        9,
        input_back_epilogue,
        own + list(d_middle) + [jnp.concatenate([scale1[m][0] for m in range(2)], 0)],
        like(own, f32) + [jax.ShapeDtypeStruct((8, width), f32)],
        micros=90,
    )
    token_grads, sums1 = [v[None] for v in reduced[:2]], reduced[2]
    sums1, hid_got = together(sums1, hid_got)
    hid_got_far = swap_x(hid_got)
    sums1, result_last, *late = together(sums1, result_last, *d_before, *d_qkv)
    result = [result_last[: counts[0]] + out_b[0], result_last[counts[0] :] + out_b[1]]
    image_out, text_out = [
        (middle[m] + gate2[m][0] * result[m]).astype(b16)[None] for m in range(2)
    ]

    all_rows = []
    for m in range(2):
        columns = row_sums(late[2 + m].astype(f32)).reshape(3, head_part)
        qkv_bt = lax.dynamic_update_slice_in_dim(
            jnp.zeros((2, width), f32), columns[::2], group * head_part, 1
        )
        units_bt = row_sums(late[m].astype(f32)).reshape(line, units_part)
        hid_bt = lax.dynamic_update_slice_in_dim(
            jnp.zeros((line, 2 * units_slab), f32), units_bt, r * units_slab + s * units_part, 1
        )
        up = own_up[m].astype(f32)
        all_rows += [
            sums1[2 * m : 2 * m + 2],
            sums2[4 * m + 2 : 4 * m + 3],
            sums2[4 * m : 4 * m + 2],
            row_sums(up * result[m]),
            qkv_bt,
            sums2[4 * m + 3 : 4 * m + 4],
            hid_bt.reshape(-1, width),
            row_sums((up * gate2[m][0]).astype(b16).astype(f32)),
        ]
    sums = jnp.concatenate(all_rows, 0)
    length = sums.shape[0]
    place = jnp.stack([r, s // 2, s % 2]).astype(jnp.int32)

    def share(own, far=None):
        far = swap_x(own) if far is None else far
        return [own, swap_c(own), far, swap_c(far)]

    out_grad = join_rows(share(out_g, out_far), place)
    hid_parts = share(hid_keep, hid_far) + share(hid_got, hid_got_far)
    hid_grad = join_columns(hid_parts, place, units_part, line, False)
    sums, out_grad, hid_grad = together(sums, out_grad, hid_grad)
    sums = jnp.pad(sums, ((0, -length % 16), (0, 0)))
    qkv_g = both[: 2 * slab].reshape(2, slab, wide)
    proj_g = jnp.zeros((2, 16, 128), b16)
    if merged:
        more, left = both[2 * slab :], wide // 3
        extra = [more[2 * chunk :, i * left : (i + 1) * left] for i in range(3)]
        proj_g = jnp.concatenate([more[: 2 * chunk], jnp.concatenate(extra, 0)], 1)
        proj_g = proj_g.reshape(2, chunk, width)
    sums_all, d_act, qkv_pieces, proj_pieces = finish(
        sums, qkv_g, proj_g, mod_weight[0], owners, merged
    )
    sums_all = sums_all[:, :length].reshape(owners, 2, -1)
    d_mods = sums_all[:, :, : 6 * width]
    bias_sum = jnp.sum(sums_all[:, :, 6 * width :].astype(f32), 0)
    bias_at = [0, 2 * width, 3 * width, 3 * width + units, 4 * width + units]
    bias_grads = [
        cut(bias_sum[:, bias_at[i] : bias_at[i + 1]], me * size, size, 1)[None]
        for i, size in enumerate(bias_sizes[1:])
    ]
    mod_grad_w = jnp.einsum("sd,ste->tde", act_cols, d_mods, preferred_element_type=f32)[None]
    mod_grad_b = jnp.sum(cut(d_mods, me * mod_part, mod_part, 2).astype(f32), 0)[None]
    d_act = d_act[:, 0, :slab].reshape(1, width)
    conditioning_grad = jax.vjp(jax.nn.silu, conditioning)[1](d_act)[0]

    if merged:
        proj_grad = proj_pieces.transpose(1, 0, 2, 3).reshape(1, 2, slab, width).astype(f32)
    else:
        proj_grad = []
        for m in range(2):
            spread = lax.dynamic_update_slice_in_dim(
                jnp.zeros((width, width), b16), proj_t[m], group * head_part, 0
            )
            own = lax.psum_scatter(spread, "fsdp", scatter_dimension=0, tiled=True)
            proj_grad.append(lax.psum(own, "seq").astype(f32))
        proj_grad = jnp.stack(proj_grad)[None]
    qkv_grad = join_natural_columns(qkv_pieces, head_part, 3)
    return (
        image_out,
        text_out,
        token_grads[0],
        token_grads[1],
        conditioning_grad,
        mod_grad_w,
        mod_grad_b,
        qkv_grad,
        bias_grads[0],
        proj_grad,
        bias_grads[1],
        hid_grad,
        bias_grads[2],
        out_grad,
        bias_grads[3],
    )


def solution(mesh):
    tokens = P("fsdp", "seq", None)
    weight = P(None, None, "fsdp", None)
    bias = P(None, None, "fsdp")
    pairs = (weight, bias) * 5
    return jax.shard_map(
        shards,
        mesh=mesh,
        in_specs=(tokens, tokens, P("fsdp", None), P("fsdp")) + pairs + (tokens, tokens),
        out_specs=(tokens, tokens, tokens, tokens, P("fsdp", None)) + pairs,
        check_vma=False,
    )
```

```python
import functools

import jax
import jax.numpy as jnp
from jax import lax
from jax.experimental import pallas as pl
from jax.experimental.layout import Layout, with_layout_constraint
from jax.experimental.pallas import tpu as pltpu
from jax.sharding import PartitionSpec as P

HEAD_DIM = 64
NORM_EPS = 1e-06
MASKED_SCORE = -1e30
VMEM_LIMIT = 60 * 2**20


def mm(left, right):
    return lax.dot_general(left, right, (((1,), (0,)), ((), ())), preferred_element_type=jnp.float32)


def key_scores(key_image, key_text, query_t, open_text, scale):
    image = mm(key_image, query_t) * scale
    text = jnp.where(open_text > 0.0, mm(key_text, query_t) * scale, MASKED_SCORE)
    return image, text


def attention_kernel(part, scale, image_ref, text_ref, open_ref, out_image, out_text, lse_image, lse_text):
    heads = part // HEAD_DIM
    b16 = jnp.bfloat16
    open_text = open_ref[0, :, :1]

    def columns(ref, kind, head):
        return ref[0, :, kind * part + head * HEAD_DIM : kind * part + (head + 1) * HEAD_DIM]

    keys = [(columns(image_ref, 1, h), columns(text_ref, 1, h)) for h in range(heads)]
    values_t = (image_ref[0, :, 2 * part :].T, text_ref[0, :, 2 * part :].T)

    def block(queries, width):
        queries_t = queries.T
        mixed, lse = [], []
        for h in range(heads):
            at = slice(h * HEAD_DIM, (h + 1) * HEAD_DIM)
            image, text = key_scores(*keys[h], queries_t[at], open_text, scale)
            top = jnp.maximum(
                jnp.max(image, 0, keepdims=True), jnp.max(text, 0, keepdims=True)
            )
            image, text = jnp.exp(image - top), jnp.exp(text - top)
            total = jnp.sum(image, 0, keepdims=True) + jnp.sum(text, 0, keepdims=True)
            out_t = mm(values_t[0][at], image.astype(b16)) + mm(values_t[1][at], text.astype(b16))
            mixed.append(out_t / total)
            lse.append(top + jnp.log(total))
        lse.append(jnp.zeros((8 - heads, width), jnp.float32))
        return jnp.concatenate(mixed, 0).T.astype(b16), jnp.concatenate(lse, 0)

    step = 256

    def body(i, carry):
        rows = pl.ds(pl.multiple_of(i * step, step), step)
        mixed, lse = block(image_ref[0, rows, :part], step)
        out_image[0, rows, :] = mixed
        lse_image[0, :, rows] = lse
        return carry

    lax.fori_loop(0, image_ref.shape[1] // step, body, 0)
    mixed, lse = block(text_ref[0, :, :part], text_ref.shape[1])
    out_text[0] = mixed
    lse_text[0] = lse


def attention(image_qkv, text_qkv, open_text, scale):
    two, image_rows, columns = image_qkv.shape
    text_rows, part = text_qkv.shape[1], columns // 3

    def spec(*dims):
        return pl.BlockSpec((1,) + dims, lambda i: (i, 0, 0))

    return pl.pallas_call(
        functools.partial(attention_kernel, part, scale),
        grid=(two,),
        in_specs=[spec(image_rows, columns), spec(text_rows, columns), spec(text_rows, 128)],
        out_specs=[
            spec(image_rows, part),
            spec(text_rows, part),
            spec(8, image_rows),
            spec(8, text_rows),
        ],
        out_shape=[
            jax.ShapeDtypeStruct((two, image_rows, part), jnp.bfloat16),
            jax.ShapeDtypeStruct((two, text_rows, part), jnp.bfloat16),
            jax.ShapeDtypeStruct((two, 8, image_rows), jnp.float32),
            jax.ShapeDtypeStruct((two, 8, text_rows), jnp.float32),
        ],
        compiler_params=pltpu.CompilerParams(vmem_limit_bytes=VMEM_LIMIT),
        cost_estimate=pl.CostEstimate(flops=0, bytes_accessed=90_000_000, transcendentals=0),
        name="attention",
    )(image_qkv, text_qkv, open_text)


def attention_back_kernel(
    part, scale, image_ref, text_ref, open_ref, lse_image, lse_text, up_image, up_text,
    out_image, out_text, d_keys, d_values,
):
    heads = part // HEAD_DIM
    b16 = jnp.bfloat16
    open_text = open_ref[0, :, :1]
    image_rows = image_ref.shape[1]

    def columns(ref, kind, head):
        return ref[0, :, kind * part + head * HEAD_DIM : kind * part + (head + 1) * HEAD_DIM]

    keys = [(columns(image_ref, 1, h), columns(text_ref, 1, h)) for h in range(heads)]
    values = [(columns(image_ref, 2, h), columns(text_ref, 2, h)) for h in range(heads)]
    keys_t = (image_ref[0, :, part : 2 * part].T, text_ref[0, :, part : 2 * part].T)

    def block(queries, ups, lse, first):
        queries_t, ups_t = queries.T, ups.T
        d_queries = []
        for h in range(heads):
            at = slice(h * HEAD_DIM, (h + 1) * HEAD_DIM)
            image, text = key_scores(*keys[h], queries_t[at], open_text, scale)
            row = lse[h : h + 1]
            image, text = jnp.exp(image - row), jnp.exp(text - row)
            up_rows = ups[:, at]
            terms = (mm(image.astype(b16), up_rows), mm(text.astype(b16), up_rows))
            d_image = mm(values[h][0], ups_t[at]) * image
            d_text = mm(values[h][1], ups_t[at]) * text
            row = jnp.sum(d_image, 0, keepdims=True) + jnp.sum(d_text, 0, keepdims=True)
            d_image = (d_image - row * image).astype(b16)
            d_text = (d_text - row * text).astype(b16)
            query_rows = queries[:, at]
            more = (mm(d_image, query_rows), mm(d_text, query_rows))
            d_queries.append((mm(keys_t[0][at], d_image) + mm(keys_t[1][at], d_text)) * scale)
            for ref, (a, b) in ((d_values, terms), (d_keys, more)):
                if first:
                    ref[h, :image_rows] = a
                    ref[h, image_rows:] = b
                else:
                    ref[h, :image_rows] += a
                    ref[h, image_rows:] += b
        return jnp.concatenate(d_queries, 0).T.astype(b16)

    step = 256
    out_text[0, :, :part] = block(text_ref[0, :, :part], up_text[0], lse_text[0], True)

    def body(i, carry):
        rows = pl.ds(pl.multiple_of(i * step, step), step)
        out_image[0, rows, :part] = block(
            image_ref[0, rows, :part], up_image[0, rows, :], lse_image[0, :, rows], False
        )
        return carry

    lax.fori_loop(0, image_rows // step, body, 0)
    for h in range(heads):
        for kind, ref, factor in ((1, d_keys, scale), (2, d_values, 1.0)):
            at = slice(kind * part + h * HEAD_DIM, kind * part + (h + 1) * HEAD_DIM)
            out_image[0, :, at] = (ref[h, :image_rows] * factor).astype(b16)
            out_text[0, :, at] = (ref[h, image_rows:] * factor).astype(b16)


def attention_back(image_qkv, text_qkv, open_text, lse_image, lse_text, up_image, up_text, scale):
    two, image_rows, columns = image_qkv.shape
    text_rows, part = text_qkv.shape[1], columns // 3
    heads = part // HEAD_DIM

    def spec(*dims):
        return pl.BlockSpec((1,) + dims, lambda i: (i, 0, 0))

    return pl.pallas_call(
        functools.partial(attention_back_kernel, part, scale),
        grid=(two,),
        in_specs=[
            spec(image_rows, columns),
            spec(text_rows, columns),
            spec(text_rows, 128),
            spec(8, image_rows),
            spec(8, text_rows),
            spec(image_rows, part),
            spec(text_rows, part),
        ],
        out_specs=[spec(image_rows, columns), spec(text_rows, columns)],
        out_shape=[
            jax.ShapeDtypeStruct(image_qkv.shape, jnp.bfloat16),
            jax.ShapeDtypeStruct(text_qkv.shape, jnp.bfloat16),
        ],
        scratch_shapes=[
            pltpu.VMEM((heads, image_rows + text_rows, HEAD_DIM), jnp.float32),
            pltpu.VMEM((heads, image_rows + text_rows, HEAD_DIM), jnp.float32),
        ],
        compiler_params=pltpu.CompilerParams(vmem_limit_bytes=VMEM_LIMIT),
        cost_estimate=pl.CostEstimate(flops=0, bytes_accessed=200_000_000, transcendentals=0),
        name="attention_back",
    )(image_qkv, text_qkv, open_text, lse_image, lse_text, up_image, up_text)


MESH = pl.DeviceIdType.MESH


def group_peers():
    f, s = lax.axis_index("fsdp"), lax.axis_index("seq")
    return {"r": (f ^ 1, s), "x": (f, s ^ 2), "c": (f, s ^ 1)}


def greet(peers):
    barrier = pltpu.get_barrier_semaphore()
    for peer in peers.values():
        pl.semaphore_signal(barrier, inc=1, device_id=peer, device_id_type=MESH)
    pl.semaphore_wait(barrier, len(peers))


def gather_kernel(work, extra, outs, own_image, own_text, *refs):
    extra_refs, (image, text) = refs[:extra], refs[extra : extra + 2]
    out_refs = refs[extra + 2 : extra + 2 + outs]
    local_sem, send_sem, recv_sem, *scratch = refs[extra + 2 + outs :]
    peers = group_peers()
    begin, run, finish = work(extra_refs, out_refs, scratch, peers)
    begin()
    cut = own_image.shape[1] // 2
    halves = {"a": pl.ds(0, cut), "b": pl.ds(cut, cut), "all": pl.ds(0, 2 * cut)}
    own, full = (own_image, own_text), (image, text)
    greet(peers)
    count = [0]

    def send(peer, source, piece, columns):
        copies = []
        for m in range(2):
            at = own[m].at[:, halves[columns]]
            if source is not None:
                at = full[m].at[source[0], source[1], :, halves[columns]]
            copy = pltpu.make_async_remote_copy(
                src_ref=at,
                dst_ref=full[m].at[piece[0], piece[1], :, halves[columns]],
                send_sem=send_sem.at[count[0]],
                recv_sem=recv_sem.at[count[0]],
                device_id=peers[peer],
                device_id_type=MESH,
            )
            copy.start()
            count[0] += 1
            copies.append(copy)
        return copies

    def landed(copies):
        for copy in copies:
            copy.wait_recv()

    a_r = send("r", None, (1, 0), "a")
    b_x = send("x", None, (0, 2), "b")
    a_x = send("x", None, (0, 2), "a")
    b_r = send("r", None, (1, 0), "b")
    all_c = send("c", None, (0, 1), "all")
    local = []
    for m in range(2):
        copy = pltpu.make_async_copy(own[m], full[m].at[0, 0], local_sem.at[m])
        copy.start()
        local.append(copy)
    landed(a_r)
    a_rx = send("x", (1, 0), (1, 2), "a")
    a_rc = send("c", (1, 0), (1, 1), "a")
    landed(b_x)
    b_xr = send("r", (0, 2), (1, 2), "b")
    b_xc = send("c", (0, 2), (0, 3), "b")
    run()
    landed(a_x)
    a_xc = send("c", (0, 2), (0, 3), "a")
    landed(b_r)
    b_rc = send("c", (1, 0), (1, 1), "b")
    landed(a_rx)
    a_rxc = send("c", (1, 2), (1, 3), "a")
    landed(b_xr)
    b_xrc = send("c", (1, 2), (1, 3), "b")
    for copies in (all_c, a_rc, b_xc, a_xc, b_rc, a_rxc, b_xrc):
        landed(copies)
    for copies in (a_r, b_x, a_x, b_r, all_c, a_rx, a_rc, b_xr, b_xc, a_xc, b_rc, a_rxc, b_xrc):
        for copy in copies:
            copy.wait_send()
    for copy in local:
        copy.wait()
    finish()


def no_work(extra, outs, scratch, peers):
    return (lambda: None,) * 3


def gather_group(
    image, text, collective_id, work=no_work, extra=(), outs=(), scratch=(), micros=35
):
    full = [jax.ShapeDtypeStruct((2, 4) + v.shape, v.dtype) for v in (image, text)]
    anywhere = pl.BlockSpec(memory_space=pl.ANY)
    return pl.pallas_call(
        functools.partial(gather_kernel, work, len(extra), len(outs)),
        in_specs=[anywhere] * (2 + len(extra)),
        out_specs=[anywhere] * (2 + len(outs)),
        out_shape=full + list(outs),
        scratch_shapes=[
            pltpu.SemaphoreType.DMA((2,)),
            pltpu.SemaphoreType.DMA((26,)),
            pltpu.SemaphoreType.DMA((26,)),
        ]
        + list(scratch),
        compiler_params=pltpu.CompilerParams(
            collective_id=collective_id, has_side_effects=True, vmem_limit_bytes=VMEM_LIMIT
        ),
        cost_estimate=pl.CostEstimate(
            flops=0, bytes_accessed=micros * 3_700_000, transcendentals=0
        ),
        name="gather_group",
    )(image, text, *extra)


def copies_of(sources, targets, sems, first):
    return [
        pltpu.make_async_copy(source, target, sems.at[first + i])
        for i, (source, target) in enumerate(zip(sources, targets))
    ]


def start_all(copies):
    for copy in copies:
        copy.start()


def wait_all(copies):
    for copy in copies:
        copy.wait()


def first_layer_work(extra, outs, scratch, peers):
    *held, before_image, before_text, active_image, active_text, sems = scratch
    results = (before_image, before_text, active_image, active_text)
    loads = copies_of(extra, held, sems, 0)
    stores = copies_of(results, outs, sems, 4)
    hidden_image, hidden_text, weight, bias = held

    def layer(rows, m):
        before = mm(rows, weight[m]) + bias[m : m + 1]
        inner = 0.7978845608028654 * (before + 0.044715 * before * before * before)
        return before, (0.5 * before * (1.0 + jnp.tanh(inner))).astype(jnp.bfloat16)

    def run():
        wait_all(loads)

        def body(i, carry):
            rows = pl.ds(pl.multiple_of(i * 256, 256), 256)
            before_image[rows, :], active_image[rows, :] = layer(hidden_image[rows, :], 0)
            return carry

        lax.fori_loop(0, hidden_image.shape[0] // 256, body, 0)
        before_text[...], active_text[...] = layer(hidden_text[...], 1)
        start_all(stores)

    return functools.partial(start_all, loads), run, functools.partial(wait_all, stores)


def second_layer_work(extra, outs, scratch, peers):
    active_image, active_text, weight, terms, got, sems, send_sem, recv_sem = scratch
    f32, b16 = jnp.float32, jnp.bfloat16
    loads = copies_of(extra, scratch[:3], sems, 0)
    pieces = 8
    cut = terms.shape[3] // 2
    first, last = pl.ds(0, cut), pl.ds(cut, cut)
    sources, targets = [], []
    for at in range(2):
        for i in range(2):
            sources += [terms.at[0, 2 * i + at, :, first], terms.at[0, 2 * at + i, :, last]]
            targets += [outs[at].at[i], outs[2 + at].at[i]]
    stores = copies_of(sources, targets, sems, 3)
    image_rows, text_rows = active_image.shape[0] // pieces, active_text.shape[0] // pieces
    swap = pltpu.make_async_remote_copy(
        src_ref=terms.at[1],
        dst_ref=got,
        send_sem=send_sem,
        recv_sem=recv_sem,
        device_id=peers["c"],
        device_id_type=MESH,
    )

    def run():
        wait_all(loads)

        def body(i, carry):
            rows = pl.ds(pl.multiple_of(i * image_rows, image_rows), image_rows)
            product = mm(active_image[rows, :], weight[0]).astype(b16)
            terms[i % 2, i // 2, :image_rows, :] = product
            return carry

        lax.fori_loop(0, pieces, body, 0)
        product = mm(active_text[...], weight[1])
        for i in range(pieces):
            rows = product[i * text_rows : (i + 1) * text_rows].astype(b16)
            terms[i % 2, i // 2, image_rows:, :] = rows
        swap.start()

    def finish():
        swap.wait()
        for i in range(pieces // 2):
            terms[0, i] = (terms[0, i].astype(f32) + got[i].astype(f32)).astype(b16)
        start_all(stores)
        wait_all(stores)

    return functools.partial(start_all, loads), run, finish


def weight_terms_work(extra, outs, scratch, peers):
    left_image, left_text, right_image, right_text, terms, columns_sum, sems = scratch
    loads = copies_of(extra, scratch[:4], sems, 0)
    stores = copies_of([terms, columns_sum], outs, sems, 4)
    block = 256 if terms.shape[1] % 256 == 0 else terms.shape[1]

    def inner(left, right):
        return lax.dot_general(
            left, right, (((0,), (0,)), ((), ())), preferred_element_type=jnp.float32
        ).astype(jnp.bfloat16)

    def run():
        wait_all(loads)

        def body(i, carry):
            columns = pl.ds(pl.multiple_of(i * block, block), block)
            terms[0, columns, :] = inner(left_image[:, columns], right_image[...])
            terms[1, columns, :] = inner(left_text[:, columns], right_text[...])
            return carry

        lax.fori_loop(0, terms.shape[1] // block, body, 0)
        columns_sum[...] = jnp.zeros(columns_sum.shape, jnp.float32)
        columns_sum[0:1] = row_sums(right_image[...].astype(jnp.float32))
        columns_sum[1:2] = row_sums(right_text[...].astype(jnp.float32))
        start_all(stores)

    return functools.partial(start_all, loads), run, functools.partial(wait_all, stores)


def held(arrays):
    return [pltpu.VMEM(v.shape, v.dtype) for v in arrays]


def reduce_kernel(epilogue, extra, outs, work, work_extra, work_outs, image, text, *refs):
    extra_refs, refs = refs[:extra], refs[extra:]
    work_refs, refs = refs[:work_extra], refs[work_extra:]
    out_refs, refs = refs[:outs], refs[outs:]
    work_out_refs, refs = refs[:work_outs], refs[work_outs:]
    (
        mine, near, acc, got_a, got_b, acc_a, acc_b, last_a, last_b, total,
        load_sem, send_sem, recv_sem, *scratch,
    ) = refs
    f32, b16 = jnp.float32, jnp.bfloat16
    peers = group_peers()
    begin, run, finish = work(work_refs, work_out_refs, scratch, peers)
    t_image = image.shape[2]
    cut = image.shape[3] // 2
    spans = (pl.ds(0, t_image), pl.ds(t_image, text.shape[2]))
    sources = (image, text)
    corners = [(1, 1), (0, 1), (1, 0), (0, 0)]
    loads = {}
    for i, (dr, dx) in enumerate(corners):
        loads[dr, dx] = []
        for m in range(2):
            copy = pltpu.make_async_copy(
                sources[m].at[dr, dx * 2], mine.at[dr * 2 + dx, spans[m]], load_sem.at[2 * i + m]
            )
            copy.start()
            loads[dr, dx].append(copy)
    begin()
    greet(peers)
    started = []

    def send(peer, source, target):
        copy = pltpu.make_async_remote_copy(
            src_ref=source,
            dst_ref=target,
            send_sem=send_sem.at[len(started)],
            recv_sem=recv_sem.at[len(started)],
            device_id=peers[peer],
            device_id_type=MESH,
        )
        copy.start()
        started.append(copy)
        return copy

    near_copies = {
        (dr, dx): [
            send("c", sources[m].at[dr, dx * 2 + 1], near.at[dr * 2 + dx, spans[m]])
            for m in range(2)
        ]
        for dr, dx in corners
    }
    a, b = slice(None, cut), slice(cut, None)

    def plus(left, right):
        return (left.astype(f32) + right.astype(f32)).astype(b16)

    far = {}
    for dr, dx in corners:
        at = dr * 2 + dx
        for copy in loads[dr, dx]:
            copy.wait()
        for copy in near_copies[dr, dx]:
            copy.wait_recv()
        acc[at] = plus(mine[at], near[at])
        if dx == 1:
            far["a", dr] = send("x", acc.at[at, :, pl.ds(0, cut)], got_a.at[dr])
        if dr == 1:
            far["b", dx] = send("r", acc.at[at, :, pl.ds(cut, cut)], got_b.at[dx])
    run()
    far["a", 1].wait_recv()
    acc_a[1] = plus(acc[2, :, a], got_a[1])
    to_a = send("r", acc_a.at[1], last_a)
    far["b", 1].wait_recv()
    acc_b[1] = plus(acc[1, :, b], got_b[1])
    to_b = send("x", acc_b.at[1], last_b)
    far["a", 0].wait_recv()
    acc_a[0] = plus(acc[0, :, a], got_a[0])
    far["b", 0].wait_recv()
    acc_b[0] = plus(acc[0, :, b], got_b[0])
    to_a.wait_recv()
    total[:, a] = acc_a[0].astype(f32) + last_a[...].astype(f32)
    to_b.wait_recv()
    total[:, b] = acc_b[0].astype(f32) + last_b[...].astype(f32)
    epilogue(total, t_image, extra_refs, out_refs)
    for copy in started:
        copy.wait_send()
    finish()


def reduce_group(
    image, text, collective_id, epilogue, extra, outs,
    work=no_work, work_extra=(), work_outs=(), scratch=(), micros=40,
):
    anywhere = pl.BlockSpec(memory_space=pl.ANY)
    rows, width = image.shape[2] + text.shape[2], image.shape[3]
    b16 = jnp.bfloat16
    half = (rows, width // 2)
    return pl.pallas_call(
        functools.partial(
            reduce_kernel, epilogue, len(extra), len(outs), work, len(work_extra), len(work_outs)
        ),
        in_specs=[anywhere] * 2
        + [pl.BlockSpec(memory_space=pltpu.VMEM)] * len(extra)
        + [anywhere] * len(work_extra),
        out_specs=[pl.BlockSpec(memory_space=pltpu.VMEM)] * len(outs)
        + [anywhere] * len(work_outs),
        out_shape=list(outs) + list(work_outs),
        scratch_shapes=[
            pltpu.VMEM((4, rows, width), b16),
            pltpu.VMEM((4, rows, width), b16),
            pltpu.VMEM((4, rows, width), b16),
            pltpu.VMEM((2,) + half, b16),
            pltpu.VMEM((2,) + half, b16),
            pltpu.VMEM((2,) + half, b16),
            pltpu.VMEM((2,) + half, b16),
            pltpu.VMEM(half, b16),
            pltpu.VMEM(half, b16),
            pltpu.VMEM((rows, width), jnp.float32),
            pltpu.SemaphoreType.DMA((8,)),
            pltpu.SemaphoreType.DMA((14,)),
            pltpu.SemaphoreType.DMA((14,)),
        ]
        + list(scratch),
        compiler_params=pltpu.CompilerParams(
            collective_id=collective_id, has_side_effects=True, vmem_limit_bytes=VMEM_LIMIT
        ),
        cost_estimate=pl.CostEstimate(
            flops=0, bytes_accessed=micros * 3_700_000, transcendentals=0
        ),
        name="reduce_group",
    )(image, text, *extra, *work_extra)


def row_norm(values):
    center = values - jnp.mean(values, -1, keepdims=True)
    inverse = lax.rsqrt(jnp.mean(center * center, -1, keepdims=True) + NORM_EPS)
    return center * inverse, inverse


def row_sums(values):
    return jnp.sum(values, 0, keepdims=True)


def middle_epilogue(total, t_image, extra, outs):
    vectors = extra[2]
    for m, rows in ((0, slice(None, t_image)), (1, slice(t_image, None))):
        bias, gate, shift, scale = [vectors[4 * m + i : 4 * m + i + 1] for i in range(4)]
        branch = total[rows] + bias
        middle = extra[m][...].astype(jnp.float32) + gate * branch
        normal, _ = row_norm(middle)
        outs[m][...] = branch
        outs[2 + m][...] = middle
        outs[4 + m][...] = (normal * (1.0 + scale) + shift).astype(jnp.bfloat16)


def norm_back(d_hidden, values, scale):
    normal, inverse = row_norm(values)
    e = d_hidden * (1.0 + scale)
    mean = jnp.mean(e, -1, keepdims=True)
    along = jnp.mean(e * normal, -1, keepdims=True)
    return (e - mean - normal * along) * inverse, row_sums(d_hidden), row_sums(d_hidden * normal)


def middle_back_epilogue(total, t_image, extra, outs):
    f32 = jnp.float32
    vectors, sums = extra[6], outs[4]
    for m, rows in ((0, slice(None, t_image)), (1, slice(t_image, None))):
        scale, gate = [vectors[2 * m + i : 2 * m + i + 1] for i in range(2)]
        d_norm, d_shift, d_scale = norm_back(total[rows], extra[m][...], scale)
        d_middle = extra[2 + m][...].astype(f32) + d_norm
        d_branch = (d_middle * gate).astype(jnp.bfloat16)
        outs[m][...] = d_middle
        outs[2 + m][...] = d_branch
        parts = (d_shift, d_scale, row_sums(d_middle * extra[4 + m][...]), row_sums(d_branch.astype(f32)))
        for i, part in enumerate(parts):
            sums[4 * m + i : 4 * m + i + 1] = part


def input_back_epilogue(total, t_image, extra, outs):
    vectors, sums = extra[4], outs[2]
    sums[...] = jnp.zeros(sums.shape, jnp.float32)
    for m, rows in ((0, slice(None, t_image)), (1, slice(t_image, None))):
        d_norm, d_shift, d_scale = norm_back(
            total[rows], extra[m][...].astype(jnp.float32), vectors[m : m + 1]
        )
        outs[m][...] = extra[2 + m][...] + d_norm
        sums[2 * m : 2 * m + 1] = d_shift
        sums[2 * m + 1 : 2 * m + 2] = d_scale


def modulation_kernel(
    owners, parts, slab, send, weight, small_out, act_out, mods_out,
    small, piece, term, got, mods, load_sem, sems,
):
    f, s = lax.axis_index("fsdp"), lax.axis_index("seq")
    quarter = piece.shape[2]
    columns = pl.ds(pl.multiple_of(s * quarter, 128), quarter)
    load = pltpu.make_async_copy(weight.at[:, :, columns], piece, load_sem)
    load.start()
    barrier = pltpu.get_barrier_semaphore()
    for k in range(1, owners):
        pl.semaphore_signal(
            barrier, inc=1, device_id=(lax.rem(f + k, owners), s), device_id_type=MESH
        )
    for q in range(1, parts):
        pl.semaphore_signal(barrier, inc=1, device_id=(f, s ^ q), device_id_type=MESH)
    pl.semaphore_wait(barrier, owners + parts - 2)

    def exchange(source, target, stage):
        copies = []
        for k in range(1, owners):
            peer = lax.rem(f + k, owners)
            copy = pltpu.make_async_remote_copy(
                src_ref=source.at[peer],
                dst_ref=target.at[f],
                send_sem=sems.at[stage, 0, k],
                recv_sem=sems.at[stage, 1, k],
                device_id=(peer, s),
                device_id_type=MESH,
            )
            copy.start()
            copies.append(copy)
        target[f] = source[f]
        for copy in copies:
            copy.wait()

    exchange(send, small, 0)
    small_out[...] = small[...]
    act = jnp.concatenate([small[k, :, :slab] for k in range(owners)], 0)
    act = (act / (1.0 + jnp.exp(-act))).astype(jnp.bfloat16)
    act_out[...] = act
    load.wait()
    for m in range(2):
        full = mm(act, piece[m])
        for k in range(owners):
            for dr in range(2):
                term[k, dr * 2 + m : dr * 2 + m + 1, :] = full[k ^ dr : (k ^ dr) + 1]
    exchange(term, got, 1)
    total = got[0]
    for k in range(1, owners):
        total = total + got[k]
    mods[s] = total
    copies = []
    for q in range(1, parts):
        copy = pltpu.make_async_remote_copy(
            src_ref=mods.at[s],
            dst_ref=mods.at[s],
            send_sem=sems.at[2, 0, q],
            recv_sem=sems.at[2, 1, q],
            device_id=(f, s ^ q),
            device_id_type=MESH,
        )
        copy.start()
        copies.append(copy)
    for copy in copies:
        copy.wait()
    mods_out[...] = mods[...]


def modulation(send, weight, owners, parts):
    slab, columns = weight.shape[1], weight.shape[2]
    quarter = columns // parts
    f32 = jnp.float32
    return pl.pallas_call(
        functools.partial(modulation_kernel, owners, parts, slab),
        in_specs=[
            pl.BlockSpec(memory_space=pltpu.VMEM),
            pl.BlockSpec(memory_space=pl.ANY),
        ],
        out_specs=[pl.BlockSpec(memory_space=pltpu.VMEM)] * 3,
        out_shape=[
            jax.ShapeDtypeStruct(send.shape, f32),
            jax.ShapeDtypeStruct((owners, slab), jnp.bfloat16),
            jax.ShapeDtypeStruct((parts, 4, quarter), f32),
        ],
        scratch_shapes=[
            pltpu.VMEM(send.shape, f32),
            pltpu.VMEM((2, slab, quarter), jnp.bfloat16),
            pltpu.VMEM((owners, 4, quarter), f32),
            pltpu.VMEM((owners, 4, quarter), f32),
            pltpu.VMEM((parts, 4, quarter), f32),
            pltpu.SemaphoreType.DMA,
            pltpu.SemaphoreType.DMA((3, 2, owners)),
        ],
        compiler_params=pltpu.CompilerParams(
            collective_id=1, has_side_effects=True, vmem_limit_bytes=VMEM_LIMIT
        ),
        cost_estimate=pl.CostEstimate(
            flops=4 * owners * slab * quarter, bytes_accessed=60_000_000, transcendentals=0
        ),
        name="modulation",
    )(send, weight)


def finish_kernel(
    owners, slab, sums, both, weight, sums_out, mods_out, act_out, qkv_out, proj_out,
    mine, first, second, rounded, got, act, act_got, held_weight, local_sem, sems, far_sem,
):
    f, s = lax.axis_index("fsdp"), lax.axis_index("seq")
    r, z = f % 2, f // 2
    with_proj = both.shape[0] > 2 * slab
    keep, other = [
        both.at[pl.ds(pl.multiple_of(at * slab, 16), slab)] for at in (r, 1 - r)
    ]
    f32, b16 = jnp.float32, jnp.bfloat16
    load = pltpu.make_async_copy(weight, held_weight, local_sem.at[0])
    load.start()
    peers = {"y": (f ^ 1, s), "x": (f, s ^ 2), "c": (f, s ^ 1)}
    turned = (s * 2 + r, z)
    barrier = pltpu.get_barrier_semaphore()
    for k in range(1, owners):
        pl.semaphore_signal(
            barrier, inc=1, device_id=(lax.rem(f + k, owners), s), device_id_type=MESH
        )
    for peer in ("x", "c"):
        pl.semaphore_signal(barrier, inc=1, device_id=peers[peer], device_id_type=MESH)
    if with_proj:

        @pl.when(z != s)
        def _():
            pl.semaphore_signal(barrier, inc=1, device_id=turned, device_id_type=MESH)
            pl.semaphore_wait(barrier, owners + 2)

        @pl.when(z == s)
        def _():
            pl.semaphore_wait(barrier, owners + 1)

    else:
        pl.semaphore_wait(barrier, owners + 1)

    started = []

    def send(peer, source, target):
        copy = pltpu.make_async_remote_copy(
            src_ref=source,
            dst_ref=target,
            send_sem=sems.at[0, len(started)],
            recv_sem=sems.at[1, len(started)],
            device_id=peers[peer] if isinstance(peer, str) else peer,
            device_id_type=MESH,
        )
        copy.start()
        started.append(copy)
        return copy

    near_sums = send("x", sums, first)
    y_other = send("y", other, qkv_out.at[r, s])
    x_keep = send("x", keep, qkv_out.at[r, s])
    c_keep = send("c", keep, qkv_out.at[r, s])
    own = pltpu.make_async_copy(keep, qkv_out.at[r, s], local_sem.at[1])
    own.start()
    if with_proj:
        proj = both.at[pl.ds(2 * slab, both.shape[0] - 2 * slab)]
        turn = pltpu.make_async_remote_copy(
            src_ref=proj,
            dst_ref=proj_out.at[z],
            send_sem=far_sem.at[0],
            recv_sem=far_sem.at[1],
            device_id=turned,
            device_id_type=MESH,
        )
        stay = pltpu.make_async_copy(proj, proj_out.at[s], far_sem.at[0])

        @pl.when(z != s)
        def _():
            turn.start()

        @pl.when(z == s)
        def _():
            stay.start()

    near_sums.wait_recv()
    mine[...] = sums[...] + first[...]
    send("c", mine, second).wait_recv()
    rounded[...] = (mine[...] + second[...]).astype(b16)
    spread = [
        send((lax.rem(f + k, owners), s), rounded, got.at[f]) for k in range(1, owners)
    ]
    got[f] = rounded[...]
    y_other.wait_recv()
    x_got = send("x", qkv_out.at[1 - r, s], qkv_out.at[1 - r, s])
    last = [c_keep, send("c", qkv_out.at[1 - r, s], qkv_out.at[1 - r, s])]
    x_keep.wait_recv()
    last.append(send("c", qkv_out.at[r, s ^ 2], qkv_out.at[r, s ^ 2]))
    if with_proj:

        @pl.when(z != s)
        def _():
            turn.wait()

        @pl.when(z == s)
        def _():
            stay.wait()

        x_proj = send("x", proj_out.at[s], proj_out.at[s])
        last.append(send("c", proj_out.at[s], proj_out.at[s]))
    for copy in spread:
        copy.wait_recv()
    load.wait()
    everyone = got[...].reshape(owners * sums.shape[0], sums.shape[1])
    rows, width = sums.shape
    per = 14
    total = [None] * owners
    for m in range(2):
        for i in range(6):
            part = lax.dot_general(
                everyone,
                held_weight[m, :, i * width : (i + 1) * width],
                (((1,), (1,)), ((), ())),
                preferred_element_type=f32,
            )
            for k in range(owners):
                at = k * rows + m * per + i
                row = part[at : at + 1]
                total[k] = row if total[k] is None else total[k] + row
    act[...] = jnp.zeros(act.shape, f32)
    for k in range(owners):
        act[k, :, :slab] = total[k]
    act_got[f] = act[f]
    for k in range(1, owners):
        peer = lax.rem(f + k, owners)
        last.append(send((peer, s), act.at[peer], act_got.at[f]))
    sums_out[...] = got[...]
    loose = got[...].astype(f32)
    for m in range(2):
        for i in range(6):
            at = m * per + i
            lines = jnp.concatenate([loose[k, at : at + 1] for k in range(owners)], 0)
            mods_out[m, :, i * width : (i + 1) * width] = lines.astype(b16)
    x_got.wait_recv()
    last.append(send("c", qkv_out.at[1 - r, s ^ 2], qkv_out.at[1 - r, s ^ 2]))
    if with_proj:
        x_proj.wait_recv()
        last.append(send("c", proj_out.at[s ^ 2], proj_out.at[s ^ 2]))
    for copy in last:
        copy.wait_recv()
    act_out[...] = act_got[...]
    own.wait()
    for copy in started:
        copy.wait_send()


def finish(sums, both, weight, owners):
    f32, b16 = jnp.float32, jnp.bfloat16
    slab, wide = weight.shape[1], both.shape[1]
    more = max(both.shape[0] - 2 * slab, 16)
    anywhere = pl.BlockSpec(memory_space=pl.ANY)
    inside = pl.BlockSpec(memory_space=pltpu.VMEM)
    all_sums = (owners,) + sums.shape
    all_act = (owners, 1, -(-slab // 128) * 128)
    count = 2 * owners + 12
    return pl.pallas_call(
        functools.partial(finish_kernel, owners, slab),
        in_specs=[inside, anywhere, anywhere],
        out_specs=[inside, inside, inside, anywhere, anywhere],
        out_shape=[
            jax.ShapeDtypeStruct(all_sums, b16),
            jax.ShapeDtypeStruct((2, owners, weight.shape[2]), b16),
            jax.ShapeDtypeStruct(all_act, f32),
            jax.ShapeDtypeStruct((2, 4, slab, wide), b16),
            jax.ShapeDtypeStruct((4, more, wide), b16),
        ],
        scratch_shapes=[
            pltpu.VMEM(sums.shape, f32),
            pltpu.VMEM(sums.shape, f32),
            pltpu.VMEM(sums.shape, f32),
            pltpu.VMEM(sums.shape, b16),
            pltpu.VMEM(all_sums, b16),
            pltpu.VMEM(all_act, f32),
            pltpu.VMEM(all_act, f32),
            pltpu.VMEM(weight.shape, b16),
            pltpu.SemaphoreType.DMA((2,)),
            pltpu.SemaphoreType.DMA((2, count)),
            pltpu.SemaphoreType.DMA((2,)),
        ],
        compiler_params=pltpu.CompilerParams(
            collective_id=2, has_side_effects=True, vmem_limit_bytes=VMEM_LIMIT
        ),
        cost_estimate=pl.CostEstimate(flops=0, bytes_accessed=130_000_000, transcendentals=0),
        name="finish",
    )(sums, both, weight)


def unfold_kernel(pieces, out):
    more, wide = pieces.shape[1:]
    count, left = more * 3 // 4, wide // 3
    chunk = count // 2
    for q in range(4):
        rest = [pieces[q, count:, i * left : (i + 1) * left] for i in range(3)]
        rest = jnp.concatenate(rest, 0)
        for m in range(2):
            at = slice(m * chunk, (m + 1) * chunk)
            rows = slice(q * chunk, (q + 1) * chunk)
            out[0, m, rows, :wide] = pieces[q, at, :].astype(jnp.float32)
            out[0, m, rows, wide:] = rest[at].astype(jnp.float32)


def unfold_rows(pieces):
    more, wide = pieces.shape[1:]
    return pl.pallas_call(
        unfold_kernel,
        out_shape=jax.ShapeDtypeStruct((1, 2, more * 3 // 2, wide + wide // 3), jnp.float32),
        compiler_params=pltpu.CompilerParams(vmem_limit_bytes=VMEM_LIMIT),
        name="unfold_rows",
    )(pieces)


def front_kernel(part, image, text, vectors, weight, bias, hidden_image, hidden_text, qkv_image, qkv_text):
    b16 = jnp.bfloat16
    line, rows = weight.shape[0], part * 2

    def hidden(values, m):
        shift, scale = vectors[0, 2 * m : 2 * m + 1], vectors[0, 2 * m + 1 : 2 * m + 2]
        normal, _ = row_norm(values.astype(jnp.float32))
        return (normal * (1.0 + scale) + shift).astype(b16)

    def project(values, columns):
        total = None
        for z in range(line):
            term = mm(values[:, z * rows : (z + 1) * rows], weight[z, :rows, columns])
            total = term if total is None else total + term
        return total

    wide = 3 * part
    values = hidden(image[0], 0)
    hidden_image[0] = values
    qkv_image[0] = (project(values, slice(None, wide)) + bias[0:1]).astype(b16)

    @pl.when(pl.program_id(1) == 0)
    def _():
        values = hidden(text[0], 1)
        hidden_text[0] = values
        qkv_text[0] = (project(values, slice(wide, None)) + bias[1:2]).astype(b16)


def front(image, text, vectors, weight, bias, part):
    width = image.shape[2]
    b16 = jnp.bfloat16
    blocks = 2

    def specs(columns):
        return [
            pl.BlockSpec((1, image.shape[1] // blocks, columns), lambda i, j: (i, j, 0)),
            pl.BlockSpec((1, text.shape[1], columns), lambda i, j: (i, 0, 0)),
        ]

    return pl.pallas_call(
        functools.partial(front_kernel, part),
        grid=(2, blocks),
        in_specs=specs(width)
        + [
            pl.BlockSpec((1, 4, width), lambda i, j: (i, 0, 0)),
            pl.BlockSpec(weight.shape, lambda i, j: (0, 0, 0)),
            pl.BlockSpec(bias.shape, lambda i, j: (0, 0)),
        ],
        out_specs=specs(width) + specs(3 * part),
        out_shape=[
            jax.ShapeDtypeStruct(v.shape[:2] + (columns,), b16)
            for columns in (width, 3 * part)
            for v in (image, text)
        ],
        compiler_params=pltpu.CompilerParams(vmem_limit_bytes=VMEM_LIMIT),
        cost_estimate=pl.CostEstimate(flops=0, bytes_accessed=40_000_000, transcendentals=0),
        name="front",
    )(image, text, vectors, weight, bias)


def back_kernel(part, ups_image, ups_text, weight, out_image, out_text):
    line, rows = weight.shape[0], part * 2
    wide = 3 * part

    def back(ups, out, columns):
        for z in range(line):
            out[:, z * rows : (z + 1) * rows] = lax.dot_general(
                ups[...],
                weight[z, :rows, columns],
                (((1,), (1,)), ((), ())),
                preferred_element_type=jnp.float32,
            ).astype(jnp.bfloat16)

    back(ups_image, out_image, slice(None, wide))

    @pl.when(pl.program_id(0) == 0)
    def _():
        back(ups_text, out_text, slice(wide, None))


def back_to_hidden(ups, weight, part, blocks):
    width = weight.shape[0] * 2 * part
    step = ups[0].shape[0] // blocks

    def specs(columns):
        return [
            pl.BlockSpec((step, columns), lambda i: (i, 0)),
            pl.BlockSpec((ups[1].shape[0], columns), lambda i: (0, 0)),
        ]

    return pl.pallas_call(
        functools.partial(back_kernel, part),
        grid=(blocks,),
        in_specs=specs(3 * part) + [pl.BlockSpec(weight.shape, lambda i: (0, 0, 0))],
        out_specs=specs(width),
        out_shape=[jax.ShapeDtypeStruct((v.shape[0], width), jnp.bfloat16) for v in ups],
        compiler_params=pltpu.CompilerParams(vmem_limit_bytes=VMEM_LIMIT),
        cost_estimate=pl.CostEstimate(flops=0, bytes_accessed=25_000_000, transcendentals=0),
        name="back_to_hidden",
    )(*ups, weight)


def feed_back_kernel(
    ups_image, ups_text, before_image, before_text, out_weight, hid_weight,
    d_before_image, d_before_text, d_hidden_image, d_hidden_text,
):
    def back(left, weight):
        return lax.dot_general(
            left, weight, (((1,), (1,)), ((), ())), preferred_element_type=jnp.float32
        )

    def rows(ups, before, m, d_before, d_hidden):
        v = before[...]
        square = v * v
        bend = jnp.tanh(0.7978845608028654 * v * (1.0 + 0.044715 * square))
        slope = 0.5 * (1.0 + bend) + 0.5 * v * (1.0 - bend * bend) * 0.7978845608028654 * (
            1.0 + 0.134145 * square
        )
        d = (back(ups[...], out_weight[m]) * slope).astype(jnp.bfloat16)
        d_before[...] = d
        d_hidden[...] = back(d, hid_weight[m]).astype(jnp.bfloat16)

    rows(ups_image, before_image, 0, d_before_image, d_hidden_image)

    @pl.when(pl.program_id(0) == 0)
    def _():
        rows(ups_text, before_text, 1, d_before_text, d_hidden_text)


def feed_back(ups, before, out_weight, hid_weight, blocks):
    width, units = ups[0].shape[1], before[0].shape[1]
    step = ups[0].shape[0] // blocks

    def specs(columns):
        return [
            pl.BlockSpec((step, columns), lambda i: (i, 0)),
            pl.BlockSpec((ups[1].shape[0], columns), lambda i: (0, 0)),
        ]

    def whole(v):
        return pl.BlockSpec(v.shape, lambda i: (0, 0, 0))

    return pl.pallas_call(
        feed_back_kernel,
        grid=(blocks,),
        in_specs=specs(width) + specs(units) + [whole(out_weight), whole(hid_weight)],
        out_specs=specs(units) + specs(width),
        out_shape=[
            jax.ShapeDtypeStruct((v.shape[0], columns), jnp.bfloat16)
            for columns in (units, width)
            for v in ups
        ],
        compiler_params=pltpu.CompilerParams(vmem_limit_bytes=VMEM_LIMIT),
        cost_estimate=pl.CostEstimate(flops=0, bytes_accessed=60_000_000, transcendentals=0),
        name="feed_back",
    )(*ups, *before, out_weight, hid_weight)


def pair_terms_kernel(left_image, left_text, right_image, right_text, out):
    for m, (left, right) in enumerate(((left_image, right_image), (left_text, right_text))):
        out[m] = lax.dot_general(
            left[...], right[...], (((0,), (0,)), ((), ())), preferred_element_type=jnp.float32
        ).astype(jnp.bfloat16)


def pair_terms(left, right):
    k, c = left[0].shape[1], right[0].shape[1]
    step = 256 if k % 256 == 0 else k
    return pl.pallas_call(
        pair_terms_kernel,
        grid=(k // step,),
        in_specs=[pl.BlockSpec((v.shape[0], step), lambda i: (0, i)) for v in left]
        + [pl.BlockSpec(v.shape, lambda i: (0, 0)) for v in right],
        out_specs=pl.BlockSpec((2, step, c), lambda i: (0, i, 0)),
        out_shape=jax.ShapeDtypeStruct((2, k, c), jnp.bfloat16),
        compiler_params=pltpu.CompilerParams(vmem_limit_bytes=VMEM_LIMIT),
        cost_estimate=pl.CostEstimate(flops=0, bytes_accessed=25_000_000, transcendentals=0),
        name="pair_terms",
    )(*left, *right)


def fold(proj, wide):
    count, left = proj.shape[-2] // 3, wide // 3
    rest = proj[..., wide:]
    extra = [rest[..., i * count : (i + 1) * count, :] for i in range(3)]
    return jnp.concatenate([proj[..., :wide], jnp.concatenate(extra, -1)], -2)


def unfold(rows, count):
    left = rows.shape[-1] // 3
    extra = [rows[..., count:, i * left : (i + 1) * left] for i in range(3)]
    return jnp.concatenate([rows[..., :count, :], jnp.concatenate(extra, -2)], -1)


def pick_kernel(part, line, place, *refs):
    qkv, hid = refs[:3], refs[3 : 3 + 2 * line]
    qkv_own, qkv_other, hid_own, hid_other = refs[3 + 2 * line :]
    high, odd = place[1] == 1, place[2] == 1
    for kind in range(3):
        for m in range(2):
            at = slice((m * 3 + kind) * part, (m * 3 + kind + 1) * part)
            low, up = qkv[kind][m, :, :part], qkv[kind][m, :, part:]
            qkv_own[:, at] = jnp.where(high, up, low)
            qkv_other[:, at] = jnp.where(high, low, up)
    for z in range(line):
        chosen = []
        for q in range(2):
            block = hid[z * 2 + q]
            cut = block.shape[2] // 2
            chosen.append(jnp.where(odd, block[:, :, cut:], block[:, :, :cut]))
        at = slice(z * cut, (z + 1) * cut)
        hid_own[:, :, at] = jnp.where(high, chosen[1], chosen[0])
        hid_other[:, :, at] = jnp.where(high, chosen[0], chosen[1])


def pick_parts(qkv_weight, hidden_weight, s, r, part, line):
    slab, width = qkv_weight.shape[1], qkv_weight.shape[2] // 3
    units = hidden_weight.shape[2] // (2 * line)
    place = jnp.stack([s, r, s % 2]).astype(jnp.int32)
    per_kind = width // (2 * part)

    def qkv_spec(kind):
        return pl.BlockSpec((2, slab, 2 * part), lambda i, at: (0, 0, kind * per_kind + at[0]))

    def hid_spec(f):
        return pl.BlockSpec((2, slab, units // 2), lambda i, at: (0, 0, 2 * f + at[0] // 2))

    shapes = [(slab, 6 * part)] * 2 + [(2, slab, line * units // 4)] * 2
    return pl.pallas_call(
        functools.partial(pick_kernel, part, line),
        grid_spec=pltpu.PrefetchScalarGridSpec(
            num_scalar_prefetch=1,
            grid=(1,),
            in_specs=[qkv_spec(k) for k in range(3)] + [hid_spec(f) for f in range(2 * line)],
            out_specs=[
                pl.BlockSpec(dims, lambda i, at, n=len(dims): (0,) * n) for dims in shapes
            ],
        ),
        out_shape=[jax.ShapeDtypeStruct(dims, jnp.bfloat16) for dims in shapes],
        compiler_params=pltpu.CompilerParams(vmem_limit_bytes=VMEM_LIMIT),
        name="pick_parts",
    )(place, *([qkv_weight] * 3), *([hidden_weight] * (2 * line)))


def chosen_piece(pieces, x, c, q):
    near = [jnp.where(c == q % 2, pieces[2 * dx], pieces[2 * dx + 1]) for dx in range(2)]
    return jnp.where(x == q // 2, near[0], near[1])


def inner(left, right):
    return lax.dot_general(
        left[...], right[...], (((0,), (0,)), ((), ())), preferred_element_type=jnp.float32
    ).astype(jnp.bfloat16)


def stacked_kernel(
    image, text, up_image, up_text, mixed_image, mixed_text, branch_image, branch_text,
    out, sums, proj,
):
    rows, part = image.shape[1], up_image.shape[1]
    wide = 2 * part
    z = pl.program_id(0)

    @pl.when(z == 0)
    def _():
        sums[...] = jnp.zeros(sums.shape, jnp.float32)
        sums[0:1] = row_sums(up_image[...].astype(jnp.float32))
        sums[1:2] = row_sums(up_text[...].astype(jnp.float32))
        proj[0] = inner(mixed_image, branch_image)
        proj[1] = inner(mixed_text, branch_text)

    out[0, :rows, :part] = inner(image, up_image)
    out[0, :rows, part:] = inner(text, up_text)
    chunk = proj.shape[1] // pl.num_programs(0)
    at = pl.ds(pl.multiple_of(z * chunk, 16), chunk)
    more = jnp.concatenate([proj[0, at, :], proj[1, at, :]], 0)
    count = more.shape[0]
    out[0, rows : rows + count, :] = more[:, :wide]
    third, left = count // 3, wide // 3
    for i in range(3):
        out[0, rows + count :, i * left : (i + 1) * left] = more[i * third : (i + 1) * third, wide:]


def stacked_terms(hidden, ups, mixed, branch, line):
    rows, part = hidden[0].shape[1] // line, ups[0].shape[1]
    head_part, width = mixed[0].shape[1], branch[0].shape[1]
    more = 2 * head_part // line * width // (2 * part)
    others = ups + mixed + branch
    return pl.pallas_call(
        stacked_kernel,
        grid=(line,),
        in_specs=[pl.BlockSpec((v.shape[0], rows), lambda z: (0, z)) for v in hidden]
        + [pl.BlockSpec(v.shape, lambda z: (0, 0)) for v in others],
        out_specs=[
            pl.BlockSpec((1, rows + more, 2 * part), lambda z: (z, 0, 0)),
            pl.BlockSpec((8, part), lambda z: (0, 0)),
        ],
        out_shape=[
            jax.ShapeDtypeStruct((line, rows + more, 2 * part), jnp.bfloat16),
            jax.ShapeDtypeStruct((8, part), jnp.float32),
        ],
        scratch_shapes=[pltpu.VMEM((2, head_part, width), jnp.bfloat16)],
        compiler_params=pltpu.CompilerParams(vmem_limit_bytes=VMEM_LIMIT),
        cost_estimate=pl.CostEstimate(flops=0, bytes_accessed=45_000_000, transcendentals=0),
        name="stacked_terms",
    )(*hidden, *others)


def columns_kernel(chunk, kinds, inner_first, place, *refs):
    out = refs[8]
    r, x, c = place[0], place[1], place[2]
    for m in range(out.shape[1]):
        for kind in range(kinds):
            at = slice((m * kinds + kind) * chunk, (m * kinds + kind + 1) * chunk)
            by_dr = [
                [chosen_piece([refs[dr * 4 + p][:, at] for p in range(4)], x, c, q) for q in range(4)]
                for dr in range(2)
            ]
            for q in range(4):
                for natural in range(2):
                    value = jnp.where(r == natural, by_dr[0][q], by_dr[1][q])
                    spot = q * 2 + natural if inner_first else natural * 4 + q
                    start = (kind * 8 + spot) * chunk
                    out[0, m, :, start : start + chunk] = value.astype(jnp.float32)


def natural_columns_kernel(chunk, kinds, pieces, out):
    for m in range(2):
        for kind in range(kinds):
            at = slice((m * kinds + kind) * chunk, (m * kinds + kind + 1) * chunk)
            for q in range(4):
                for p in range(2):
                    start = (kind * 8 + q * 2 + p) * chunk
                    out[0, m, :, start : start + chunk] = pieces[p, q, :, at].astype(jnp.float32)


def join_natural_columns(pieces, chunk, kinds):
    rows, columns = pieces.shape[2], 8 * kinds * chunk
    step = 48 if rows % 48 == 0 else rows
    return pl.pallas_call(
        functools.partial(natural_columns_kernel, chunk, kinds),
        grid=(rows // step,),
        in_specs=[pl.BlockSpec((2, 4, step, pieces.shape[3]), lambda i: (0, 0, i, 0))],
        out_specs=pl.BlockSpec((1, 2, step, columns), lambda i: (0, 0, i, 0)),
        out_shape=jax.ShapeDtypeStruct((1, 2, rows, columns), jnp.float32),
        compiler_params=pltpu.CompilerParams(vmem_limit_bytes=VMEM_LIMIT),
        name="join_natural_columns",
    )(pieces)


def join_columns(pieces, place, chunk, kinds, inner_first):
    rows = pieces[0].shape[-2]
    columns = 8 * kinds * chunk
    step = 64 if rows % 64 == 0 else rows
    if pieces[0].ndim == 3:
        grid = (rows // step, 2)
        piece = pl.BlockSpec((None, step, columns // 8), lambda i, m, at: (m, i, 0))
        out = pl.BlockSpec((1, 1, step, columns), lambda i, m, at: (0, m, i, 0))
    else:
        grid = (rows // step,)
        piece = pl.BlockSpec((step, columns // 4), lambda i, at: (i, 0))
        out = pl.BlockSpec((1, 2, step, columns), lambda i, at: (0, 0, i, 0))
    return pl.pallas_call(
        functools.partial(columns_kernel, chunk, kinds, inner_first),
        grid_spec=pltpu.PrefetchScalarGridSpec(
            num_scalar_prefetch=1, grid=grid, in_specs=[piece] * 8, out_specs=out
        ),
        out_shape=jax.ShapeDtypeStruct((1, 2, rows, columns), jnp.float32),
        compiler_params=pltpu.CompilerParams(vmem_limit_bytes=VMEM_LIMIT),
        name="join_columns",
    )(place, *pieces)


def rows_kernel(place, *refs):
    out = refs[4]
    rows = refs[0].shape[1]
    for q in range(4):
        value = chosen_piece([refs[p][0] for p in range(4)], place[1], place[2], q)
        out[0, 0, q * rows : (q + 1) * rows, :] = value.astype(jnp.float32)


def join_rows(pieces, place):
    rows, columns = pieces[0].shape[1:]
    step = columns // 2
    return pl.pallas_call(
        rows_kernel,
        grid_spec=pltpu.PrefetchScalarGridSpec(
            num_scalar_prefetch=1,
            grid=(2, 2),
            in_specs=[pl.BlockSpec((1, rows, step), lambda m, i, at: (m, 0, i))] * 4,
            out_specs=pl.BlockSpec((1, 1, 4 * rows, step), lambda m, i, at: (0, m, 0, i)),
        ),
        out_shape=jax.ShapeDtypeStruct((1, 2, 4 * rows, columns), jnp.float32),
        compiler_params=pltpu.CompilerParams(vmem_limit_bytes=VMEM_LIMIT),
        name="join_rows",
    )(place, *pieces)


def rows_major(values):
    return with_layout_constraint(values, Layout(major_to_minor=(0, 1)))


def together(*values):
    return lax.optimization_barrier(values)


def norm_rows(values):
    center = values - jnp.mean(values, -1, keepdims=True)
    return center * lax.rsqrt(jnp.mean(center * center, -1, keepdims=True) + NORM_EPS)


def modulated(values, shift, scale_up):
    return norm_rows(values) * (1.0 + scale_up) + shift


def gelu_tanh(values):
    return jax.nn.gelu(values, approximate=True)


def dot32(left, right, contract):
    return lax.dot_general(
        left, right, ((contract[0], contract[1]), ((), ())), preferred_element_type=jnp.float32
    )


def product(left, right):
    return dot32(left, right, ((1,), (0,)))


def rows_inner(left, right):
    return dot32(left, right, ((0,), (0,)))


def right_back(left, right):
    return dot32(left, right, ((1,), (1,)))


def swap_r(values):
    count = lax.axis_size("fsdp")
    return lax.ppermute(values, "fsdp", [(at, at ^ 1) for at in range(count)])


def swap_x(values):
    return lax.ppermute(values, "seq", [(at, at ^ 2) for at in range(4)])


def swap_c(values):
    return lax.ppermute(values, "seq", [(at, at ^ 1) for at in range(4)])


CORNERS = [(0, 0), (0, 1), (1, 0), (1, 1)]


def reduce_far(a0, a1, b0, b1):
    return [a0[0], a0[1], b0[0], b0[1], swap_x(a1), swap_r(b1)]


def reduce_sums(parts):
    f32, b16 = jnp.float32, jnp.bfloat16
    got_a, got_b = parts[4], parts[5]
    a = [(parts[dr].astype(f32) + got_a[dr].astype(f32)).astype(b16) for dr in range(2)]
    b = [(parts[2 + dx].astype(f32) + got_b[dx].astype(f32)).astype(b16) for dx in range(2)]
    return [a[0], b[0], a[1], b[1]]


def reduce_last(a, b, last_a, last_b):
    f32 = jnp.float32
    return jnp.concatenate(
        [a.astype(f32) + last_a.astype(f32), b.astype(f32) + last_b.astype(f32)], 1
    )


def shards(
    image_tokens,
    text_tokens,
    conditioning,
    text_lengths,
    mod_weight,
    mod_bias,
    qkv_weight,
    qkv_bias,
    proj_weight,
    proj_bias,
    hidden_weight,
    hidden_bias,
    output_weight,
    output_bias,
    image_cotangent,
    text_cotangent,
):
    f32, b16 = jnp.float32, jnp.bfloat16
    width = image_tokens.shape[2]
    counts = (image_tokens.shape[1], text_tokens.shape[1])
    parts = lax.axis_size("seq")
    owners = lax.axis_size("fsdp")
    line = owners // 2
    head_part = width // (2 * parts)
    heads_here = head_part // HEAD_DIM
    slab = width // owners
    units_slab = output_weight.shape[2]
    units_part = units_slab // parts
    units = units_slab * owners
    units_here = line * units_part
    score_scale = HEAD_DIM ** (-0.5)
    me = lax.axis_index("fsdp")
    s = lax.axis_index("seq")
    r = me % 2
    along = [[z * 2 + q for z in range(line)] for q in range(2)]
    direct_proj = line == parts
    image_rows, text_rows = counts[0] * parts, counts[1] * parts

    def cut(array, start, size, axis):
        return lax.dynamic_slice_in_dim(array, start, size, axis)

    def transpose_owners(values):
        pairs = [
            ((z * 2 + q) * parts + t, (t * 2 + q) * parts + z)
            for z in range(line)
            for q in range(2)
            for t in range(parts)
        ]
        return lax.ppermute(values, ("fsdp", "seq"), pairs)

    def line_gather(rows):
        return lax.all_gather(rows, "fsdp", axis=rows.ndim - 2, tiled=True, axis_index_groups=along)

    def line_reduce(term):
        return lax.psum_scatter(
            term, "fsdp", scatter_dimension=term.ndim - 2, tiled=True, axis_index_groups=along
        )

    def weight_terms(left, right):
        return jnp.stack([rows_inner(left[m], right[m]).astype(b16) for m in range(2)])

    def both_r(values):
        rows = values.reshape(values.shape[:-2] + (2, slab, -1))
        return pick(rows, r, values.ndim - 2), swap_r(pick(rows, 1 - r, values.ndim - 2))

    def by_r(own, other, axis):
        return jnp.where(r == 0, jnp.stack([own, other], axis), jnp.stack([other, own], axis))

    def pick(array, index, axis):
        return lax.dynamic_index_in_dim(array, index, axis, keepdims=False)

    biases = (mod_bias, qkv_bias, proj_bias, hidden_bias, output_bias)
    bias_sizes = [v.shape[2] for v in biases]
    bias_local = jnp.concatenate([v[0].astype(f32) for v in biases], 1)
    padded = -(-slab // 128) * 128
    common = jnp.concatenate([bias_local.reshape(-1), jnp.tile(text_lengths.astype(f32), 128)])
    if (2 * head_part) % 128 == 0 and (2 * units_part) % 128 == 0:
        qkv_own, qkv_other, hid_own, hid_other = pick_parts(
            qkv_weight[0], hidden_weight[0], s, r, head_part, line
        )
    else:
        qkv_view = qkv_weight[0].reshape(2, slab, 3, 2 * parts, head_part)
        qkv_own, qkv_other = [
            pick(qkv_view, s * 2 + at, 3).transpose(1, 0, 2, 3).reshape(slab, 6 * head_part)
            for at in (r, 1 - r)
        ]
        hid_view = pick(hidden_weight[0].reshape(2, slab, line, 2, parts, units_part), s, 4)
        hid_own, hid_other = [
            pick(hid_view, at, 3).reshape(2, slab, units_here) for at in (r, 1 - r)
        ]
    qkv_got = swap_r(qkv_other)
    proj_mine = proj_weight[0]
    if direct_proj:
        chunk = slab // parts
        proj_mine = transpose_owners(cut(proj_weight[0], s * chunk, chunk, 1))
    wide = 6 * head_part
    merged = direct_proj and slab % 96 == 0 and width - wide == wide // 3
    qkv_mine = by_r(qkv_own, qkv_got, 0).reshape(2 * slab, wide)
    if merged:
        rows = fold(proj_mine.reshape(2 * chunk, width), wide)
        qkv_mine = jnp.concatenate([qkv_mine, rows], 0)
    hid_got = swap_r(hid_other)
    cond_in, qkv_mine = together(conditioning, qkv_mine)
    send = jnp.concatenate(
        [
            cond_in.reshape(owners, slab),
            jnp.zeros((owners, padded - slab), f32),
            jnp.broadcast_to(common, (owners, common.shape[0])),
        ],
        1,
    )
    small, act_cols, mods = modulation(send[:, None], mod_weight[0], owners, parts)
    small = small[:, 0, padded:]
    lengths = [pick(small[:, -1], me ^ dr, 0) for dr in range(2)]
    bias_all = small[:, :-128].reshape(owners, 2, sum(bias_sizes))
    offsets = [0]
    for size in bias_sizes:
        offsets.append(offsets[-1] + size)
    mod_b, qkv_b, proj_b, hid_b, out_b = [
        bias_all[:, :, offsets[i] : offsets[i + 1]].transpose(1, 0, 2) for i in range(5)
    ]
    group = s * 2 + r
    qkv_b = cut(qkv_b.reshape(2, 2, width), group * head_part, head_part, 2)
    qkv_b = jnp.stack([qkv_b[:, 0], jnp.zeros_like(qkv_b[:, 0]), qkv_b[:, 1]], 1).reshape(
        2, 3 * head_part
    )
    proj_b = proj_b.reshape(2, width)
    out_b = out_b.reshape(2, width)
    hid_b = pick(pick(hid_b.reshape(2, line, 2, parts, units_part), s, 3), r, 2).reshape(
        2, units_here
    )
    mods = mods.reshape(parts, 2, 2, -1).transpose(1, 2, 0, 3).reshape(2, 2, 6 * width)
    mods = mods + mod_b.reshape(2, 6 * width)
    mod_part = mod_bias.shape[2]

    front_w = line_gather(qkv_mine).reshape(line, -1, wide)
    qkv_w = front_w[:, : 2 * slab].reshape(width, wide)
    qkv_w = [qkv_w[:, m * 3 * head_part : (m + 1) * 3 * head_part] for m in range(2)]
    if merged:
        proj_w = unfold(front_w[:, 2 * slab :], 2 * chunk).reshape(line, 2, chunk, width)
        proj_w = proj_w.transpose(1, 0, 2, 3).reshape(2, head_part, width)
    elif direct_proj:
        proj_w = line_gather(proj_mine)
    else:
        proj_all = lax.all_gather(proj_mine, "fsdp", axis=1, tiled=True)
        proj_w = cut(proj_all, group * head_part, head_part, 1)
    mods, image_in, text_in, hid_got = together(mods, image_tokens[0], text_tokens[0], hid_got)
    x_full = [v.reshape(2, -1, width) for v in gather_group(image_in, text_in, 3)]
    hid_w = line_gather(by_r(hid_own, hid_got, 1).reshape(2, 2 * slab, units_here))
    out_w = line_gather(cut(output_weight[0], s * units_part, units_part, 1))

    def mod_at(index, m):
        at = slice(index * width, (index + 1) * width)
        return mods[0, m, None, at], mods[:, m, None, at]

    shift1, scale1, gate1, shift2, scale2, gate2 = [
        [mod_at(i, m) for m in range(2)] for i in range(6)
    ]

    def joined(pieces):
        return [v.reshape(2, -1, v.shape[-1]) for v in pieces]

    def apart(values, m):
        return values.reshape(2, parts, counts[m], -1)

    def flat(values):
        return values.reshape(-1, values.shape[-1])


    if merged:
        vectors = jnp.concatenate([v for m in range(2) for v in (shift1[m][1], scale1[m][1])], 1)
        *hidden1, qkv_image, qkv_text = front(*x_full, vectors, front_w, qkv_b, head_part)
        hidden1 = [flat(v) for v in hidden1]
        qkv = [qkv_image, qkv_text]
    else:
        hidden1 = [
            flat(modulated(x_full[m].astype(f32), shift1[m][1], scale1[m][1]).astype(b16))
            for m in range(2)
        ]
        qkv = [
            rows_major((product(hidden1[m], qkv_w[m]) + qkv_b[m]).astype(b16)) for m in range(2)
        ]
        qkv = [v.reshape(2, -1, 3 * head_part) for v in qkv]
    text_slot = jnp.arange(text_rows)
    text_place = ((text_slot // counts[1]) ^ s) * counts[1] + text_slot % counts[1]
    open_text = jnp.stack([(text_place.astype(f32) < n).astype(f32) for n in lengths])
    open_text = jnp.broadcast_to(open_text[:, :, None], (2, text_rows, 128))
    mixed_image, mixed_text, lse_image, lse_text = attention(*qkv, open_text, score_scale)
    attended = [flat(mixed_image), flat(mixed_text)]

    def like(pair, kind):
        return [jax.ShapeDtypeStruct(v.shape, kind) for v in pair]

    own = [image_tokens[0], text_tokens[0]]
    own_up = [image_cotangent[0], text_cotangent[0]]

    def summed(terms, *rest, **options):
        return list(reduce_group(*[apart(terms[m], m) for m in range(2)], *rest, **options))

    vectors = [v for m in range(2) for v in (proj_b[m, None], gate1[m][0], shift2[m][0], scale2[m][0])]
    reduced = summed(
        [product(attended[m], proj_w[m]).astype(b16) for m in range(2)],
        5,
        middle_epilogue,
        own + [jnp.concatenate(vectors, 0)],
        like(own, f32) + like(own, f32) + like(own, b16),
    )
    branch, middle = reduced[:2], reduced[2:4]
    hidden2 = [flat(v) for v in gather_group(*reduced[4:], 6)]

    shapes = [jax.ShapeDtypeStruct((v.shape[0], units_here), f32) for v in hidden2]
    shapes += [jax.ShapeDtypeStruct((v.shape[0], units_here), b16) for v in hidden2]
    extra = hidden2 + [hid_w, hid_b]
    d_own = [(own_up[m].astype(f32) * gate2[m][0]).astype(b16) for m in range(2)]
    image_up, text_up, extra[0] = together(*d_own, extra[0])
    gathered = gather_group(
        image_up,
        text_up,
        4,
        first_layer_work,
        extra,
        shapes,
        held(extra + shapes) + [pltpu.SemaphoreType.DMA((8,))],
    )
    d_result, before, active = [flat(v) for v in gathered[:2]], gathered[2:4], gathered[4:]
    out_t = pair_terms(active, d_result)
    out_g = line_reduce(out_t)
    d_result[0], d_result[1], out_t = together(*d_result, out_t)
    *d_before, d_image, d_text = feed_back(d_result, before, out_w, hid_w, 4)
    d_hidden2 = [d_image, d_text]
    vectors = [v for m in range(2) for v in (scale2[m][0], gate1[m][0])]
    hid_terms = [
        jax.ShapeDtypeStruct((2, width, units_here), b16),
        jax.ShapeDtypeStruct((8, units_here), f32),
    ]
    reduced = summed(
        d_hidden2,
        7,
        middle_back_epilogue,
        list(middle) + own_up + list(branch) + [jnp.concatenate(vectors, 0)],
        like(own, f32) + like(own, b16) + [jax.ShapeDtypeStruct((8, width), f32)],
        weight_terms_work,
        hidden2 + d_before,
        hid_terms,
        held(hidden2 + d_before + hid_terms) + [pltpu.SemaphoreType.DMA((6,))],
    )
    d_middle, d_branch, sums2, hid_t, hid_sums = reduced[:2], reduced[2:4], *reduced[4:]
    hid_g = line_reduce(hid_t)
    extra = list(active) + [out_w]
    corner = (4, sum(counts), width)
    gathered = list(gather_group(
        *d_branch,
        8,
        second_layer_work,
        extra,
        [jax.ShapeDtypeStruct((2, sum(counts), width // 2), b16)] * 4,
        held(extra)
        + [pltpu.VMEM((2,) + corner, b16), pltpu.VMEM(corner, b16), pltpu.SemaphoreType.DMA((11,))]
        + [pltpu.SemaphoreType.DMA] * 2,
        micros=90,
    ))
    gathered[0], out_g = together(gathered[0], out_g)
    d_branch_full = [flat(v) for v in gathered[:2]]
    result_near = gathered[2:]
    d_attended = [
        rows_major(right_back(d_branch_full[m], proj_w[m]).astype(b16)).reshape(2, -1, head_part)
        for m in range(2)
    ]
    out_far = swap_x(out_g)
    result_far = reduce_far(*result_near)
    d_qkv = attention_back(*qkv, open_text, lse_image, lse_text, *d_attended, score_scale)
    d_qkv = [flat(v) for v in d_qkv]
    d_qkv[0], d_qkv[1], out_far, *result_far = together(*d_qkv, out_far, *result_far)
    d_qkv[0], d_qkv[1], *result_sums = together(*d_qkv, *reduce_sums(result_far))
    result_last = [swap_r(result_sums[2]), swap_x(result_sums[3])]
    if merged:
        qkv_t, qkv_sums = stacked_terms(hidden1, d_qkv, attended, d_branch_full, line)
        qkv_t = qkv_t.reshape(-1, wide)
    else:
        qkv_t = [rows_inner(hidden1[m], d_qkv[m]).astype(b16) for m in range(2)]
        qkv_t = jnp.concatenate(qkv_t, 1)
        qkv_sums = jnp.concatenate([row_sums(v.astype(f32)) for v in d_qkv], 0)
    both = line_reduce(qkv_t)
    d_qkv[0], d_qkv[1], qkv_t = together(*d_qkv, qkv_t)
    if merged:
        d_hidden1 = list(back_to_hidden(d_qkv, front_w, head_part, 4))
    else:
        d_hidden1 = [right_back(d_qkv[m], qkv_w[m]).astype(b16) for m in range(2)]
    d_hidden1[0], d_hidden1[1], hid_g, *result_last = together(*d_hidden1, hid_g, *result_last)
    hid_keep, hid_got = both_r(hid_g)
    reduced = summed(
        d_hidden1,
        9,
        input_back_epilogue,
        own + list(d_middle) + [jnp.concatenate([scale1[m][0] for m in range(2)], 0)],
        like(own, f32) + [jax.ShapeDtypeStruct((8, width), f32)],
        micros=90,
    )
    token_grads, sums1 = [v[None] for v in reduced[:2]], reduced[2]
    hid_far = swap_x(hid_keep)
    sums1, hid_got, hid_far = together(sums1, hid_got, hid_far)
    hid_got_far = swap_x(hid_got)
    sums1, *result_last = together(sums1, *result_last)
    result_last = reduce_last(*result_sums[:2], *result_last)
    result = [result_last[: counts[0]] + out_b[0], result_last[counts[0] :] + out_b[1]]
    image_out, text_out = [
        (middle[m] + gate2[m][0] * result[m]).astype(b16)[None] for m in range(2)
    ]

    all_rows = []
    for m in range(2):
        columns = qkv_sums[m].reshape(3, head_part)
        qkv_bt = lax.dynamic_update_slice_in_dim(
            jnp.zeros((2, width), f32), columns[::2], group * head_part, 1
        )
        units_bt = hid_sums[m].reshape(line, units_part)
        hid_bt = lax.dynamic_update_slice_in_dim(
            jnp.zeros((line, 2 * units_slab), f32), units_bt, r * units_slab + s * units_part, 1
        )
        up = own_up[m].astype(f32)
        all_rows += [
            sums1[2 * m : 2 * m + 2],
            sums2[4 * m + 2 : 4 * m + 3],
            sums2[4 * m : 4 * m + 2],
            row_sums(up * result[m]),
            qkv_bt,
            sums2[4 * m + 3 : 4 * m + 4],
            hid_bt.reshape(-1, width),
            row_sums((up * gate2[m][0]).astype(b16).astype(f32)),
        ]
    sums = jnp.concatenate(all_rows, 0)
    length = sums.shape[0]
    place = jnp.stack([r, s // 2, s % 2]).astype(jnp.int32)

    def share(own, far=None):
        far = swap_x(own) if far is None else far
        return [own, swap_c(own), far, swap_c(far)]

    out_grad = join_rows(share(out_g, out_far), place)
    hid_got_far, out_grad = together(hid_got_far, out_grad)
    hid_parts = share(hid_keep, hid_far) + share(hid_got, hid_got_far)
    hid_grad = join_columns(hid_parts, place, units_part, line, False)
    sums, out_grad, hid_grad = together(sums, out_grad, hid_grad)
    sums = jnp.pad(sums, ((0, -length % 16), (0, 0)))
    sums_all, d_mods, d_act, qkv_pieces, proj_pieces = finish(sums, both, mod_weight[0], owners)
    bias_sum = jnp.sum(sums_all[:, :length].astype(f32), 0).reshape(2, 14, width)
    bias_sum = bias_sum[:, 6:].reshape(2, -1)
    bias_at = [0, 2 * width, 3 * width, 3 * width + units, 4 * width + units]
    bias_grads = [
        cut(bias_sum[:, bias_at[i] : bias_at[i + 1]], me * size, size, 1)[None]
        for i, size in enumerate(bias_sizes[1:])
    ]
    mod_grad_w = jnp.einsum("sd,tse->tde", act_cols, d_mods, preferred_element_type=f32)[None]
    mod_grad_b = jnp.sum(cut(d_mods, me * mod_part, mod_part, 2).astype(f32), 1)[None]
    d_act = d_act[:, 0, :slab].reshape(1, width)
    conditioning_grad = jax.vjp(jax.nn.silu, conditioning)[1](d_act)[0]

    if merged:
        proj_grad = unfold_rows(proj_pieces)
    else:
        proj_t = [rows_inner(attended[m], d_branch_full[m]).astype(b16) for m in range(2)]
        proj_grad = []
        for m in range(2):
            spread = lax.dynamic_update_slice_in_dim(
                jnp.zeros((width, width), b16), proj_t[m], group * head_part, 0
            )
            own = lax.psum_scatter(spread, "fsdp", scatter_dimension=0, tiled=True)
            proj_grad.append(lax.psum(own, "seq").astype(f32))
        proj_grad = jnp.stack(proj_grad)[None]
    qkv_grad = join_natural_columns(qkv_pieces, head_part, 3)
    return (
        image_out,
        text_out,
        token_grads[0],
        token_grads[1],
        conditioning_grad,
        mod_grad_w,
        mod_grad_b,
        qkv_grad,
        bias_grads[0],
        proj_grad,
        bias_grads[1],
        hid_grad,
        bias_grads[2],
        out_grad,
        bias_grads[3],
    )


def solution(mesh):
    tokens = P("fsdp", "seq", None)
    weight = P(None, None, "fsdp", None)
    bias = P(None, None, "fsdp")
    pairs = (weight, bias) * 5
    return jax.shard_map(
        shards,
        mesh=mesh,
        in_specs=(tokens, tokens, P("fsdp", None), P("fsdp")) + pairs + (tokens, tokens),
        out_specs=(tokens, tokens, tokens, tokens, P("fsdp", None)) + pairs,
        check_vma=False,
    )
```

```python
import functools

import jax
import jax.numpy as jnp
from jax import lax
from jax.experimental import pallas as pl
from jax.experimental.layout import Layout, with_layout_constraint
from jax.experimental.pallas import tpu as pltpu
from jax.sharding import PartitionSpec as P

HEAD_DIM = 64
NORM_EPS = 1e-06
MASKED_SCORE = -1e30
VMEM_LIMIT = 60 * 2**20


def mm(left, right):
    return lax.dot_general(left, right, (((1,), (0,)), ((), ())), preferred_element_type=jnp.float32)


def key_scores(key_image, key_text, query_t, open_text, scale):
    image = mm(key_image, query_t) * scale
    text = jnp.where(open_text > 0.0, mm(key_text, query_t) * scale, MASKED_SCORE)
    return image, text


def attention_kernel(part, scale, image_ref, text_ref, open_ref, out_image, out_text, lse_image, lse_text):
    heads = part // HEAD_DIM
    b16 = jnp.bfloat16
    open_text = open_ref[0, :, :1]

    def columns(ref, kind, head):
        return ref[0, :, kind * part + head * HEAD_DIM : kind * part + (head + 1) * HEAD_DIM]

    keys = [(columns(image_ref, 1, h), columns(text_ref, 1, h)) for h in range(heads)]
    values_t = (image_ref[0, :, 2 * part :].T, text_ref[0, :, 2 * part :].T)

    def block(queries, width):
        queries_t = queries.T
        mixed, lse = [], []
        for h in range(heads):
            at = slice(h * HEAD_DIM, (h + 1) * HEAD_DIM)
            image, text = key_scores(*keys[h], queries_t[at], open_text, scale)
            top = jnp.maximum(
                jnp.max(image, 0, keepdims=True), jnp.max(text, 0, keepdims=True)
            )
            image, text = jnp.exp(image - top), jnp.exp(text - top)
            total = jnp.sum(image, 0, keepdims=True) + jnp.sum(text, 0, keepdims=True)
            out_t = mm(values_t[0][at], image.astype(b16)) + mm(values_t[1][at], text.astype(b16))
            mixed.append(out_t / total)
            lse.append(top + jnp.log(total))
        lse.append(jnp.zeros((8 - heads, width), jnp.float32))
        return jnp.concatenate(mixed, 0).T.astype(b16), jnp.concatenate(lse, 0)

    step = 256

    def body(i, carry):
        rows = pl.ds(pl.multiple_of(i * step, step), step)
        mixed, lse = block(image_ref[0, rows, :part], step)
        out_image[0, rows, :] = mixed
        lse_image[0, :, rows] = lse
        return carry

    lax.fori_loop(0, image_ref.shape[1] // step, body, 0)
    mixed, lse = block(text_ref[0, :, :part], text_ref.shape[1])
    out_text[0] = mixed
    lse_text[0] = lse


def attention(image_qkv, text_qkv, open_text, scale):
    two, image_rows, columns = image_qkv.shape
    text_rows, part = text_qkv.shape[1], columns // 3

    def spec(*dims):
        return pl.BlockSpec((1,) + dims, lambda i: (i, 0, 0))

    return pl.pallas_call(
        functools.partial(attention_kernel, part, scale),
        grid=(two,),
        in_specs=[spec(image_rows, columns), spec(text_rows, columns), spec(text_rows, 128)],
        out_specs=[
            spec(image_rows, part),
            spec(text_rows, part),
            spec(8, image_rows),
            spec(8, text_rows),
        ],
        out_shape=[
            jax.ShapeDtypeStruct((two, image_rows, part), jnp.bfloat16),
            jax.ShapeDtypeStruct((two, text_rows, part), jnp.bfloat16),
            jax.ShapeDtypeStruct((two, 8, image_rows), jnp.float32),
            jax.ShapeDtypeStruct((two, 8, text_rows), jnp.float32),
        ],
        compiler_params=pltpu.CompilerParams(vmem_limit_bytes=VMEM_LIMIT),
        cost_estimate=pl.CostEstimate(flops=0, bytes_accessed=90_000_000, transcendentals=0),
        name="attention",
    )(image_qkv, text_qkv, open_text)


def attention_back_kernel(
    part, scale, image_ref, text_ref, open_ref, lse_image, lse_text, up_image, up_text,
    out_image, out_text, d_keys, d_values,
):
    heads = part // HEAD_DIM
    b16 = jnp.bfloat16
    open_text = open_ref[0, :, :1]
    image_rows = image_ref.shape[1]

    def columns(ref, kind, head):
        return ref[0, :, kind * part + head * HEAD_DIM : kind * part + (head + 1) * HEAD_DIM]

    keys = [(columns(image_ref, 1, h), columns(text_ref, 1, h)) for h in range(heads)]
    values = [(columns(image_ref, 2, h), columns(text_ref, 2, h)) for h in range(heads)]
    keys_t = (image_ref[0, :, part : 2 * part].T, text_ref[0, :, part : 2 * part].T)

    def block(queries, ups, lse, first):
        queries_t, ups_t = queries.T, ups.T
        d_queries = []
        for h in range(heads):
            at = slice(h * HEAD_DIM, (h + 1) * HEAD_DIM)
            image, text = key_scores(*keys[h], queries_t[at], open_text, scale)
            row = lse[h : h + 1]
            image, text = jnp.exp(image - row), jnp.exp(text - row)
            up_rows = ups[:, at]
            terms = (mm(image.astype(b16), up_rows), mm(text.astype(b16), up_rows))
            d_image = mm(values[h][0], ups_t[at]) * image
            d_text = mm(values[h][1], ups_t[at]) * text
            row = jnp.sum(d_image, 0, keepdims=True) + jnp.sum(d_text, 0, keepdims=True)
            d_image = (d_image - row * image).astype(b16)
            d_text = (d_text - row * text).astype(b16)
            query_rows = queries[:, at]
            more = (mm(d_image, query_rows), mm(d_text, query_rows))
            d_queries.append((mm(keys_t[0][at], d_image) + mm(keys_t[1][at], d_text)) * scale)
            for ref, (a, b) in ((d_values, terms), (d_keys, more)):
                if first:
                    ref[h, :image_rows] = a
                    ref[h, image_rows:] = b
                else:
                    ref[h, :image_rows] += a
                    ref[h, image_rows:] += b
        return jnp.concatenate(d_queries, 0).T.astype(b16)

    step = 256
    out_text[0, :, :part] = block(text_ref[0, :, :part], up_text[0], lse_text[0], True)

    def body(i, carry):
        rows = pl.ds(pl.multiple_of(i * step, step), step)
        out_image[0, rows, :part] = block(
            image_ref[0, rows, :part], up_image[0, rows, :], lse_image[0, :, rows], False
        )
        return carry

    lax.fori_loop(0, image_rows // step, body, 0)
    for h in range(heads):
        for kind, ref, factor in ((1, d_keys, scale), (2, d_values, 1.0)):
            at = slice(kind * part + h * HEAD_DIM, kind * part + (h + 1) * HEAD_DIM)
            out_image[0, :, at] = (ref[h, :image_rows] * factor).astype(b16)
            out_text[0, :, at] = (ref[h, image_rows:] * factor).astype(b16)


def attention_back(image_qkv, text_qkv, open_text, lse_image, lse_text, up_image, up_text, scale):
    two, image_rows, columns = image_qkv.shape
    text_rows, part = text_qkv.shape[1], columns // 3
    heads = part // HEAD_DIM

    def spec(*dims):
        return pl.BlockSpec((1,) + dims, lambda i: (i, 0, 0))

    return pl.pallas_call(
        functools.partial(attention_back_kernel, part, scale),
        grid=(two,),
        in_specs=[
            spec(image_rows, columns),
            spec(text_rows, columns),
            spec(text_rows, 128),
            spec(8, image_rows),
            spec(8, text_rows),
            spec(image_rows, part),
            spec(text_rows, part),
        ],
        out_specs=[spec(image_rows, columns), spec(text_rows, columns)],
        out_shape=[
            jax.ShapeDtypeStruct(image_qkv.shape, jnp.bfloat16),
            jax.ShapeDtypeStruct(text_qkv.shape, jnp.bfloat16),
        ],
        scratch_shapes=[
            pltpu.VMEM((heads, image_rows + text_rows, HEAD_DIM), jnp.float32),
            pltpu.VMEM((heads, image_rows + text_rows, HEAD_DIM), jnp.float32),
        ],
        compiler_params=pltpu.CompilerParams(vmem_limit_bytes=VMEM_LIMIT),
        cost_estimate=pl.CostEstimate(flops=0, bytes_accessed=200_000_000, transcendentals=0),
        name="attention_back",
    )(image_qkv, text_qkv, open_text, lse_image, lse_text, up_image, up_text)


MESH = pl.DeviceIdType.MESH


def group_peers():
    f, s = lax.axis_index("fsdp"), lax.axis_index("seq")
    return {"r": (f ^ 1, s), "x": (f, s ^ 2), "c": (f, s ^ 1)}


def greet(peers):
    barrier = pltpu.get_barrier_semaphore()
    for peer in peers.values():
        pl.semaphore_signal(barrier, inc=1, device_id=peer, device_id_type=MESH)
    pl.semaphore_wait(barrier, len(peers))


def gather_kernel(work, extra, outs, own_image, own_text, *refs):
    extra_refs, (image, text) = refs[:extra], refs[extra : extra + 2]
    out_refs = refs[extra + 2 : extra + 2 + outs]
    local_sem, send_sem, recv_sem, *scratch = refs[extra + 2 + outs :]
    peers = group_peers()
    begin, run, finish = work(extra_refs, out_refs, scratch, peers)
    begin()
    cut = own_image.shape[1] // 2
    halves = {"a": pl.ds(0, cut), "b": pl.ds(cut, cut), "all": pl.ds(0, 2 * cut)}
    own, full = (own_image, own_text), (image, text)
    greet(peers)
    count = [0]

    def send(peer, source, piece, columns):
        copies = []
        for m in range(2):
            at = own[m].at[:, halves[columns]]
            if source is not None:
                at = full[m].at[source[0], source[1], :, halves[columns]]
            copy = pltpu.make_async_remote_copy(
                src_ref=at,
                dst_ref=full[m].at[piece[0], piece[1], :, halves[columns]],
                send_sem=send_sem.at[count[0]],
                recv_sem=recv_sem.at[count[0]],
                device_id=peers[peer],
                device_id_type=MESH,
            )
            copy.start()
            count[0] += 1
            copies.append(copy)
        return copies

    def landed(copies):
        for copy in copies:
            copy.wait_recv()

    a_r = send("r", None, (1, 0), "a")
    b_x = send("x", None, (0, 2), "b")
    a_x = send("x", None, (0, 2), "a")
    b_r = send("r", None, (1, 0), "b")
    all_c = send("c", None, (0, 1), "all")
    local = []
    for m in range(2):
        copy = pltpu.make_async_copy(own[m], full[m].at[0, 0], local_sem.at[m])
        copy.start()
        local.append(copy)
    landed(a_r)
    a_rx = send("x", (1, 0), (1, 2), "a")
    a_rc = send("c", (1, 0), (1, 1), "a")
    landed(b_x)
    b_xr = send("r", (0, 2), (1, 2), "b")
    b_xc = send("c", (0, 2), (0, 3), "b")
    run()
    landed(a_x)
    a_xc = send("c", (0, 2), (0, 3), "a")
    landed(b_r)
    b_rc = send("c", (1, 0), (1, 1), "b")
    landed(a_rx)
    a_rxc = send("c", (1, 2), (1, 3), "a")
    landed(b_xr)
    b_xrc = send("c", (1, 2), (1, 3), "b")
    for copies in (all_c, a_rc, b_xc, a_xc, b_rc, a_rxc, b_xrc):
        landed(copies)
    for copies in (a_r, b_x, a_x, b_r, all_c, a_rx, a_rc, b_xr, b_xc, a_xc, b_rc, a_rxc, b_xrc):
        for copy in copies:
            copy.wait_send()
    for copy in local:
        copy.wait()
    finish()


def no_work(extra, outs, scratch, peers):
    return (lambda: None,) * 3


def gather_group(
    image, text, collective_id, work=no_work, extra=(), outs=(), scratch=(), micros=35
):
    full = [jax.ShapeDtypeStruct((2, 4) + v.shape, v.dtype) for v in (image, text)]
    anywhere = pl.BlockSpec(memory_space=pl.ANY)
    return pl.pallas_call(
        functools.partial(gather_kernel, work, len(extra), len(outs)),
        in_specs=[anywhere] * (2 + len(extra)),
        out_specs=[anywhere] * (2 + len(outs)),
        out_shape=full + list(outs),
        scratch_shapes=[
            pltpu.SemaphoreType.DMA((2,)),
            pltpu.SemaphoreType.DMA((26,)),
            pltpu.SemaphoreType.DMA((26,)),
        ]
        + list(scratch),
        compiler_params=pltpu.CompilerParams(
            collective_id=collective_id, has_side_effects=True, vmem_limit_bytes=VMEM_LIMIT
        ),
        cost_estimate=pl.CostEstimate(
            flops=0, bytes_accessed=micros * 3_700_000, transcendentals=0
        ),
        name="gather_group",
    )(image, text, *extra)


def copies_of(sources, targets, sems, first):
    return [
        pltpu.make_async_copy(source, target, sems.at[first + i])
        for i, (source, target) in enumerate(zip(sources, targets))
    ]


def start_all(copies):
    for copy in copies:
        copy.start()


def wait_all(copies):
    for copy in copies:
        copy.wait()


def first_layer_work(extra, outs, scratch, peers):
    *held, before_image, before_text, active_image, active_text, sems = scratch
    results = (before_image, before_text, active_image, active_text)
    loads = copies_of(extra, held, sems, 0)
    stores = copies_of(results, outs, sems, 4)
    hidden_image, hidden_text, weight, bias = held

    def layer(rows, m):
        before = mm(rows, weight[m]) + bias[m : m + 1]
        inner = 0.7978845608028654 * (before + 0.044715 * before * before * before)
        return before, (0.5 * before * (1.0 + jnp.tanh(inner))).astype(jnp.bfloat16)

    def run():
        wait_all(loads)

        def body(i, carry):
            rows = pl.ds(pl.multiple_of(i * 256, 256), 256)
            before_image[rows, :], active_image[rows, :] = layer(hidden_image[rows, :], 0)
            return carry

        lax.fori_loop(0, hidden_image.shape[0] // 256, body, 0)
        before_text[...], active_text[...] = layer(hidden_text[...], 1)
        start_all(stores)

    return functools.partial(start_all, loads), run, functools.partial(wait_all, stores)


def second_layer_work(extra, outs, scratch, peers):
    active_image, active_text, weight, terms, got, sems, send_sem, recv_sem = scratch
    f32, b16 = jnp.float32, jnp.bfloat16
    loads = copies_of(extra, scratch[:3], sems, 0)
    pieces = 8
    cut = terms.shape[3] // 2
    first, last = pl.ds(0, cut), pl.ds(cut, cut)
    sources, targets = [], []
    for at in range(2):
        for i in range(2):
            sources += [terms.at[0, 2 * i + at, :, first], terms.at[0, 2 * at + i, :, last]]
            targets += [outs[at].at[i], outs[2 + at].at[i]]
    stores = copies_of(sources, targets, sems, 3)
    image_rows, text_rows = active_image.shape[0] // pieces, active_text.shape[0] // pieces
    swap = pltpu.make_async_remote_copy(
        src_ref=terms.at[1],
        dst_ref=got,
        send_sem=send_sem,
        recv_sem=recv_sem,
        device_id=peers["c"],
        device_id_type=MESH,
    )

    def run():
        wait_all(loads)

        def body(i, carry):
            rows = pl.ds(pl.multiple_of(i * image_rows, image_rows), image_rows)
            product = mm(active_image[rows, :], weight[0]).astype(b16)
            terms[i % 2, i // 2, :image_rows, :] = product
            return carry

        lax.fori_loop(0, pieces, body, 0)
        product = mm(active_text[...], weight[1])
        for i in range(pieces):
            rows = product[i * text_rows : (i + 1) * text_rows].astype(b16)
            terms[i % 2, i // 2, image_rows:, :] = rows
        swap.start()

    def finish():
        swap.wait()
        for i in range(pieces // 2):
            terms[0, i] = (terms[0, i].astype(f32) + got[i].astype(f32)).astype(b16)
        start_all(stores)
        wait_all(stores)

    return functools.partial(start_all, loads), run, finish


def weight_terms_work(extra, outs, scratch, peers):
    left_image, left_text, right_image, right_text, terms, columns_sum, sems = scratch
    loads = copies_of(extra, scratch[:4], sems, 0)
    stores = copies_of([terms, columns_sum], outs, sems, 4)
    block = 256 if terms.shape[1] % 256 == 0 else terms.shape[1]

    def inner(left, right):
        return lax.dot_general(
            left, right, (((0,), (0,)), ((), ())), preferred_element_type=jnp.float32
        ).astype(jnp.bfloat16)

    def run():
        wait_all(loads)

        def body(i, carry):
            columns = pl.ds(pl.multiple_of(i * block, block), block)
            terms[0, columns, :] = inner(left_image[:, columns], right_image[...])
            terms[1, columns, :] = inner(left_text[:, columns], right_text[...])
            return carry

        lax.fori_loop(0, terms.shape[1] // block, body, 0)
        columns_sum[...] = jnp.zeros(columns_sum.shape, jnp.float32)
        columns_sum[0:1] = row_sums(right_image[...].astype(jnp.float32))
        columns_sum[1:2] = row_sums(right_text[...].astype(jnp.float32))
        start_all(stores)

    return functools.partial(start_all, loads), run, functools.partial(wait_all, stores)


def held(arrays):
    return [pltpu.VMEM(v.shape, v.dtype) for v in arrays]


def reduce_kernel(epilogue, extra, outs, work, work_extra, work_outs, image, text, *refs):
    extra_refs, refs = refs[:extra], refs[extra:]
    work_refs, refs = refs[:work_extra], refs[work_extra:]
    out_refs, refs = refs[:outs], refs[outs:]
    work_out_refs, refs = refs[:work_outs], refs[work_outs:]
    (
        mine, near, acc, got_a, got_b, acc_a, acc_b, last_a, last_b, total,
        load_sem, send_sem, recv_sem, *scratch,
    ) = refs
    f32, b16 = jnp.float32, jnp.bfloat16
    peers = group_peers()
    begin, run, finish = work(work_refs, work_out_refs, scratch, peers)
    t_image = image.shape[2]
    cut = image.shape[3] // 2
    spans = (pl.ds(0, t_image), pl.ds(t_image, text.shape[2]))
    sources = (image, text)
    corners = [(1, 1), (0, 1), (1, 0), (0, 0)]
    loads = {}
    for i, (dr, dx) in enumerate(corners):
        loads[dr, dx] = []
        for m in range(2):
            copy = pltpu.make_async_copy(
                sources[m].at[dr, dx * 2], mine.at[dr * 2 + dx, spans[m]], load_sem.at[2 * i + m]
            )
            copy.start()
            loads[dr, dx].append(copy)
    begin()
    greet(peers)
    started = []

    def send(peer, source, target):
        copy = pltpu.make_async_remote_copy(
            src_ref=source,
            dst_ref=target,
            send_sem=send_sem.at[len(started)],
            recv_sem=recv_sem.at[len(started)],
            device_id=peers[peer],
            device_id_type=MESH,
        )
        copy.start()
        started.append(copy)
        return copy

    near_copies = {
        (dr, dx): [
            send("c", sources[m].at[dr, dx * 2 + 1], near.at[dr * 2 + dx, spans[m]])
            for m in range(2)
        ]
        for dr, dx in corners
    }
    a, b = slice(None, cut), slice(cut, None)

    def plus(left, right):
        return (left.astype(f32) + right.astype(f32)).astype(b16)

    far = {}
    for dr, dx in corners:
        at = dr * 2 + dx
        for copy in loads[dr, dx]:
            copy.wait()
        for copy in near_copies[dr, dx]:
            copy.wait_recv()
        acc[at] = plus(mine[at], near[at])
        if dx == 1:
            far["a", dr] = send("x", acc.at[at, :, pl.ds(0, cut)], got_a.at[dr])
        if dr == 1:
            far["b", dx] = send("r", acc.at[at, :, pl.ds(cut, cut)], got_b.at[dx])
    run()
    far["a", 1].wait_recv()
    acc_a[1] = plus(acc[2, :, a], got_a[1])
    to_a = send("r", acc_a.at[1], last_a)
    far["b", 1].wait_recv()
    acc_b[1] = plus(acc[1, :, b], got_b[1])
    to_b = send("x", acc_b.at[1], last_b)
    far["a", 0].wait_recv()
    acc_a[0] = plus(acc[0, :, a], got_a[0])
    far["b", 0].wait_recv()
    acc_b[0] = plus(acc[0, :, b], got_b[0])
    to_a.wait_recv()
    total[:, a] = acc_a[0].astype(f32) + last_a[...].astype(f32)
    to_b.wait_recv()
    total[:, b] = acc_b[0].astype(f32) + last_b[...].astype(f32)
    epilogue(total, t_image, extra_refs, out_refs)
    for copy in started:
        copy.wait_send()
    finish()


def reduce_group(
    image, text, collective_id, epilogue, extra, outs,
    work=no_work, work_extra=(), work_outs=(), scratch=(), micros=40,
):
    anywhere = pl.BlockSpec(memory_space=pl.ANY)
    rows, width = image.shape[2] + text.shape[2], image.shape[3]
    b16 = jnp.bfloat16
    half = (rows, width // 2)
    return pl.pallas_call(
        functools.partial(
            reduce_kernel, epilogue, len(extra), len(outs), work, len(work_extra), len(work_outs)
        ),
        in_specs=[anywhere] * 2
        + [pl.BlockSpec(memory_space=pltpu.VMEM)] * len(extra)
        + [anywhere] * len(work_extra),
        out_specs=[pl.BlockSpec(memory_space=pltpu.VMEM)] * len(outs)
        + [anywhere] * len(work_outs),
        out_shape=list(outs) + list(work_outs),
        scratch_shapes=[
            pltpu.VMEM((4, rows, width), b16),
            pltpu.VMEM((4, rows, width), b16),
            pltpu.VMEM((4, rows, width), b16),
            pltpu.VMEM((2,) + half, b16),
            pltpu.VMEM((2,) + half, b16),
            pltpu.VMEM((2,) + half, b16),
            pltpu.VMEM((2,) + half, b16),
            pltpu.VMEM(half, b16),
            pltpu.VMEM(half, b16),
            pltpu.VMEM((rows, width), jnp.float32),
            pltpu.SemaphoreType.DMA((8,)),
            pltpu.SemaphoreType.DMA((14,)),
            pltpu.SemaphoreType.DMA((14,)),
        ]
        + list(scratch),
        compiler_params=pltpu.CompilerParams(
            collective_id=collective_id, has_side_effects=True, vmem_limit_bytes=VMEM_LIMIT
        ),
        cost_estimate=pl.CostEstimate(
            flops=0, bytes_accessed=micros * 3_700_000, transcendentals=0
        ),
        name="reduce_group",
    )(image, text, *extra, *work_extra)


def row_norm(values):
    center = values - jnp.mean(values, -1, keepdims=True)
    inverse = lax.rsqrt(jnp.mean(center * center, -1, keepdims=True) + NORM_EPS)
    return center * inverse, inverse


def row_sums(values):
    return jnp.sum(values, 0, keepdims=True)


def middle_epilogue(total, t_image, extra, outs):
    vectors = extra[2]
    for m, rows in ((0, slice(None, t_image)), (1, slice(t_image, None))):
        bias, gate, shift, scale = [vectors[4 * m + i : 4 * m + i + 1] for i in range(4)]
        branch = total[rows] + bias
        middle = extra[m][...].astype(jnp.float32) + gate * branch
        normal, _ = row_norm(middle)
        outs[m][...] = branch
        outs[2 + m][...] = middle
        outs[4 + m][...] = (normal * (1.0 + scale) + shift).astype(jnp.bfloat16)


def norm_back(d_hidden, values, scale):
    normal, inverse = row_norm(values)
    e = d_hidden * (1.0 + scale)
    mean = jnp.mean(e, -1, keepdims=True)
    along = jnp.mean(e * normal, -1, keepdims=True)
    return (e - mean - normal * along) * inverse, row_sums(d_hidden), row_sums(d_hidden * normal)


def middle_back_epilogue(total, t_image, extra, outs):
    f32 = jnp.float32
    vectors, sums = extra[6], outs[4]
    for m, rows in ((0, slice(None, t_image)), (1, slice(t_image, None))):
        scale, gate = [vectors[2 * m + i : 2 * m + i + 1] for i in range(2)]
        d_norm, d_shift, d_scale = norm_back(total[rows], extra[m][...], scale)
        d_middle = extra[2 + m][...].astype(f32) + d_norm
        d_branch = (d_middle * gate).astype(jnp.bfloat16)
        outs[m][...] = d_middle
        outs[2 + m][...] = d_branch
        parts = (d_shift, d_scale, row_sums(d_middle * extra[4 + m][...]), row_sums(d_branch.astype(f32)))
        for i, part in enumerate(parts):
            sums[4 * m + i : 4 * m + i + 1] = part


def input_back_epilogue(total, t_image, extra, outs):
    vectors, sums = extra[4], outs[2]
    sums[...] = jnp.zeros(sums.shape, jnp.float32)
    for m, rows in ((0, slice(None, t_image)), (1, slice(t_image, None))):
        d_norm, d_shift, d_scale = norm_back(
            total[rows], extra[m][...].astype(jnp.float32), vectors[m : m + 1]
        )
        outs[m][...] = extra[2 + m][...] + d_norm
        sums[2 * m : 2 * m + 1] = d_shift
        sums[2 * m + 1 : 2 * m + 2] = d_scale


def modulation_kernel(
    owners, parts, slab, send, weight, small_out, act_out, mods_out,
    small, piece, term, got, mods, others, load_sem, sems,
):
    f, s = lax.axis_index("fsdp"), lax.axis_index("seq")
    quarter = piece.shape[2]
    columns = pl.ds(pl.multiple_of(s * quarter, 128), quarter)
    load = pltpu.make_async_copy(weight.at[:, :, columns], piece, load_sem)
    load.start()
    barrier = pltpu.get_barrier_semaphore()
    for k in range(1, owners):
        pl.semaphore_signal(
            barrier, inc=1, device_id=(lax.rem(f + k, owners), s), device_id_type=MESH
        )
    for q in range(1, parts):
        pl.semaphore_signal(barrier, inc=1, device_id=(f, s ^ q), device_id_type=MESH)
    pl.semaphore_wait(barrier, owners + parts - 2)

    def exchange(source, target, stage):
        copies = []
        for k in range(1, owners):
            peer = lax.rem(f + k, owners)
            copy = pltpu.make_async_remote_copy(
                src_ref=source.at[peer],
                dst_ref=target.at[f],
                send_sem=sems.at[stage, 0, k],
                recv_sem=sems.at[stage, 1, k],
                device_id=(peer, s),
                device_id_type=MESH,
            )
            copy.start()
            copies.append(copy)
        target[f] = source[f]
        for copy in copies:
            copy.wait()

    exchange(send, small.at[s % 2], 0)
    swap = pltpu.make_async_remote_copy(
        src_ref=small.at[s % 2],
        dst_ref=small.at[s % 2],
        send_sem=sems.at[0, 0, 0],
        recv_sem=sems.at[0, 1, 0],
        device_id=(f, s ^ 1),
        device_id_type=MESH,
    )
    swap.start()
    act = jnp.concatenate([small[s % 2, k, :, :slab] for k in range(owners)], 0)
    act = (act / (1.0 + jnp.exp(-act))).astype(jnp.bfloat16)
    act_out[...] = act
    load.wait()
    for m in range(2):
        full = mm(act, piece[m])
        for k in range(owners):
            term[k, m : m + 1, :] = full[k : k + 1]
    exchange(term, got, 1)
    total = got[0]
    for k in range(1, owners):
        total = total + got[k]
    mods[s] = total
    copies = []
    for q in range(1, parts):
        copy = pltpu.make_async_remote_copy(
            src_ref=mods.at[s],
            dst_ref=mods.at[s],
            send_sem=sems.at[2, 0, q],
            recv_sem=sems.at[2, 1, q],
            device_id=(f, s ^ q),
            device_id_type=MESH,
        )
        copy.start()
        copies.append(copy)
    for copy in copies:
        copy.wait()
    pair = pltpu.make_async_remote_copy(
        src_ref=mods,
        dst_ref=others,
        send_sem=sems.at[3, 0, 0],
        recv_sem=sems.at[3, 1, 0],
        device_id=(f ^ 1, s),
        device_id_type=MESH,
    )
    pair.start()
    mods_out[:, 0:2, :] = mods[...]
    pair.wait()
    mods_out[:, 2:4, :] = others[...]
    swap.wait()
    small_out[...] = small[...]


def modulation(send, weight, owners, parts):
    slab, columns = weight.shape[1], weight.shape[2]
    quarter = columns // parts
    f32 = jnp.float32
    return pl.pallas_call(
        functools.partial(modulation_kernel, owners, parts, slab),
        in_specs=[
            pl.BlockSpec(memory_space=pltpu.VMEM),
            pl.BlockSpec(memory_space=pl.ANY),
        ],
        out_specs=[pl.BlockSpec(memory_space=pltpu.VMEM)] * 3,
        out_shape=[
            jax.ShapeDtypeStruct((2,) + send.shape, f32),
            jax.ShapeDtypeStruct((owners, slab), jnp.bfloat16),
            jax.ShapeDtypeStruct((parts, 4, quarter), f32),
        ],
        scratch_shapes=[
            pltpu.VMEM((2,) + send.shape, f32),
            pltpu.VMEM((2, slab, quarter), jnp.bfloat16),
            pltpu.VMEM((owners, 2, quarter), f32),
            pltpu.VMEM((owners, 2, quarter), f32),
            pltpu.VMEM((parts, 2, quarter), f32),
            pltpu.VMEM((parts, 2, quarter), f32),
            pltpu.SemaphoreType.DMA,
            pltpu.SemaphoreType.DMA((4, 2, owners)),
        ],
        compiler_params=pltpu.CompilerParams(
            collective_id=1, has_side_effects=True, vmem_limit_bytes=VMEM_LIMIT
        ),
        cost_estimate=pl.CostEstimate(
            flops=4 * owners * slab * quarter, bytes_accessed=60_000_000, transcendentals=0
        ),
        name="modulation",
    )(send, weight)


def finish_kernel(
    owners, slab, sums, both, weight, sums_out, mods_out, act_out, qkv_out, proj_out,
    mine, first, second, rounded, got, act, act_got, held_weight, local_sem, sems, far_sem,
):
    f, s = lax.axis_index("fsdp"), lax.axis_index("seq")
    r, z = f % 2, f // 2
    with_proj = both.shape[0] > 2 * slab
    keep, other = [
        both.at[pl.ds(pl.multiple_of(at * slab, 16), slab)] for at in (r, 1 - r)
    ]
    f32, b16 = jnp.float32, jnp.bfloat16
    load = pltpu.make_async_copy(weight, held_weight, local_sem.at[0])
    load.start()
    peers = {"y": (f ^ 1, s), "x": (f, s ^ 2), "c": (f, s ^ 1)}
    turned = (s * 2 + r, z)
    barrier = pltpu.get_barrier_semaphore()
    for k in range(1, owners):
        pl.semaphore_signal(
            barrier, inc=1, device_id=(lax.rem(f + k, owners), s), device_id_type=MESH
        )
    for peer in ("x", "c"):
        pl.semaphore_signal(barrier, inc=1, device_id=peers[peer], device_id_type=MESH)
    if with_proj:

        @pl.when(z != s)
        def _():
            pl.semaphore_signal(barrier, inc=1, device_id=turned, device_id_type=MESH)
            pl.semaphore_wait(barrier, owners + 2)

        @pl.when(z == s)
        def _():
            pl.semaphore_wait(barrier, owners + 1)

    else:
        pl.semaphore_wait(barrier, owners + 1)

    started = []

    def send(peer, source, target):
        copy = pltpu.make_async_remote_copy(
            src_ref=source,
            dst_ref=target,
            send_sem=sems.at[0, len(started)],
            recv_sem=sems.at[1, len(started)],
            device_id=peers[peer] if isinstance(peer, str) else peer,
            device_id_type=MESH,
        )
        copy.start()
        started.append(copy)
        return copy

    near_sums = send("x", sums, first)
    y_other = send("y", other, qkv_out.at[r, s])
    x_keep = send("x", keep, qkv_out.at[r, s])
    c_keep = send("c", keep, qkv_out.at[r, s])
    own = pltpu.make_async_copy(keep, qkv_out.at[r, s], local_sem.at[1])
    own.start()
    if with_proj:
        proj = both.at[pl.ds(2 * slab, both.shape[0] - 2 * slab)]
        turn = pltpu.make_async_remote_copy(
            src_ref=proj,
            dst_ref=proj_out.at[z],
            send_sem=far_sem.at[0],
            recv_sem=far_sem.at[1],
            device_id=turned,
            device_id_type=MESH,
        )
        stay = pltpu.make_async_copy(proj, proj_out.at[s], far_sem.at[0])

        @pl.when(z != s)
        def _():
            turn.start()

        @pl.when(z == s)
        def _():
            stay.start()

    near_sums.wait_recv()
    mine[...] = sums[...] + first[...]
    send("c", mine, second).wait_recv()
    rounded[...] = (mine[...] + second[...]).astype(b16)
    half = sums.shape[0] // 2
    mine_rows = pl.ds(pl.multiple_of(s % 2 * half, 16), half)
    spread = [
        send((lax.rem(f + k, owners), s), rounded.at[mine_rows], got.at[f, mine_rows])
        for k in range(1, owners)
    ]
    got[f, mine_rows, :] = rounded[mine_rows, :]
    y_other.wait_recv()
    x_got = send("x", qkv_out.at[1 - r, s], qkv_out.at[1 - r, s])
    last = [c_keep, send("c", qkv_out.at[1 - r, s], qkv_out.at[1 - r, s])]
    x_keep.wait_recv()
    last.append(send("c", qkv_out.at[r, s ^ 2], qkv_out.at[r, s ^ 2]))
    if with_proj:

        @pl.when(z != s)
        def _():
            turn.wait()

        @pl.when(z == s)
        def _():
            stay.wait()

        x_proj = send("x", proj_out.at[s], proj_out.at[s])
        last.append(send("c", proj_out.at[s], proj_out.at[s]))
    for copy in spread:
        copy.wait_recv()
    send("c", got.at[:, mine_rows], got.at[:, mine_rows]).wait_recv()
    load.wait()
    everyone = got[...].reshape(owners * sums.shape[0], sums.shape[1])
    rows, width = sums.shape
    per = 14
    total = [None] * owners
    for m in range(2):
        for i in range(6):
            part = lax.dot_general(
                everyone,
                held_weight[m, :, i * width : (i + 1) * width],
                (((1,), (1,)), ((), ())),
                preferred_element_type=f32,
            )
            for k in range(owners):
                at = k * rows + m * per + i
                row = part[at : at + 1]
                total[k] = row if total[k] is None else total[k] + row
    act[...] = jnp.zeros(act.shape, f32)
    for k in range(owners):
        act[k, :, :slab] = total[k]
    act_got[f] = act[f]
    for k in range(1, owners):
        peer = lax.rem(f + k, owners)
        last.append(send((peer, s), act.at[peer], act_got.at[f]))
    sums_out[...] = got[...]
    loose = got[...].astype(f32)
    for m in range(2):
        for i in range(6):
            at = m * per + i
            lines = jnp.concatenate([loose[k, at : at + 1] for k in range(owners)], 0)
            mods_out[m, :, i * width : (i + 1) * width] = lines.astype(b16)
    x_got.wait_recv()
    last.append(send("c", qkv_out.at[1 - r, s ^ 2], qkv_out.at[1 - r, s ^ 2]))
    if with_proj:
        x_proj.wait_recv()
        last.append(send("c", proj_out.at[s ^ 2], proj_out.at[s ^ 2]))
    for copy in last:
        copy.wait_recv()
    act_out[...] = act_got[...]
    own.wait()
    for copy in started:
        copy.wait_send()


def finish(sums, both, weight, owners):
    f32, b16 = jnp.float32, jnp.bfloat16
    slab, wide = weight.shape[1], both.shape[1]
    more = max(both.shape[0] - 2 * slab, 16)
    anywhere = pl.BlockSpec(memory_space=pl.ANY)
    inside = pl.BlockSpec(memory_space=pltpu.VMEM)
    all_sums = (owners,) + sums.shape
    all_act = (owners, 1, -(-slab // 128) * 128)
    count = 2 * owners + 12
    return pl.pallas_call(
        functools.partial(finish_kernel, owners, slab),
        in_specs=[inside, anywhere, anywhere],
        out_specs=[inside, inside, inside, anywhere, anywhere],
        out_shape=[
            jax.ShapeDtypeStruct(all_sums, b16),
            jax.ShapeDtypeStruct((2, owners, weight.shape[2]), b16),
            jax.ShapeDtypeStruct(all_act, f32),
            jax.ShapeDtypeStruct((2, 4, slab, wide), b16),
            jax.ShapeDtypeStruct((4, more, wide), b16),
        ],
        scratch_shapes=[
            pltpu.VMEM(sums.shape, f32),
            pltpu.VMEM(sums.shape, f32),
            pltpu.VMEM(sums.shape, f32),
            pltpu.VMEM(sums.shape, b16),
            pltpu.VMEM(all_sums, b16),
            pltpu.VMEM(all_act, f32),
            pltpu.VMEM(all_act, f32),
            pltpu.VMEM(weight.shape, b16),
            pltpu.SemaphoreType.DMA((2,)),
            pltpu.SemaphoreType.DMA((2, count)),
            pltpu.SemaphoreType.DMA((2,)),
        ],
        compiler_params=pltpu.CompilerParams(
            collective_id=2, has_side_effects=True, vmem_limit_bytes=VMEM_LIMIT
        ),
        cost_estimate=pl.CostEstimate(flops=0, bytes_accessed=130_000_000, transcendentals=0),
        name="finish",
    )(sums, both, weight)


def unfold_kernel(pieces, out):
    more, wide = pieces.shape[1:]
    count, left = more * 3 // 4, wide // 3
    chunk = count // 2
    for q in range(4):
        rest = [pieces[q, count:, i * left : (i + 1) * left] for i in range(3)]
        rest = jnp.concatenate(rest, 0)
        for m in range(2):
            at = slice(m * chunk, (m + 1) * chunk)
            rows = slice(q * chunk, (q + 1) * chunk)
            out[0, m, rows, :wide] = pieces[q, at, :].astype(jnp.float32)
            out[0, m, rows, wide:] = rest[at].astype(jnp.float32)


def unfold_rows(pieces):
    more, wide = pieces.shape[1:]
    return pl.pallas_call(
        unfold_kernel,
        out_shape=jax.ShapeDtypeStruct((1, 2, more * 3 // 2, wide + wide // 3), jnp.float32),
        compiler_params=pltpu.CompilerParams(vmem_limit_bytes=VMEM_LIMIT),
        name="unfold_rows",
    )(pieces)


def norm_kernel(image, text, vectors, hidden_image, hidden_text):
    def hidden(values, m):
        shift, scale = vectors[0, 2 * m : 2 * m + 1], vectors[0, 2 * m + 1 : 2 * m + 2]
        normal, _ = row_norm(values.astype(jnp.float32))
        return (normal * (1.0 + scale) + shift).astype(jnp.bfloat16)

    hidden_image[0] = hidden(image[0], 0)

    @pl.when(pl.program_id(1) == 0)
    def _():
        hidden_text[0] = hidden(text[0], 1)


def project_kernel(part, image, text, weight, bias, out_image, out_text):
    line, rows = weight.shape[0], part * 2
    wide = 3 * part

    def project(values, columns, m):
        total = bias[m : m + 1]
        for z in range(line):
            total = total + mm(values[0, :, z * rows : (z + 1) * rows], weight[z, :rows, columns])
        return total.astype(jnp.bfloat16)

    out_image[0] = project(image, slice(None, wide), 0)

    @pl.when(pl.program_id(1) == 0)
    def _():
        out_text[0] = project(text, slice(wide, None), 1)


def front_specs(image, text, blocks, columns):
    return [
        pl.BlockSpec((1, image.shape[1] // blocks, columns), lambda i, j: (i, j, 0)),
        pl.BlockSpec((1, text.shape[1], columns), lambda i, j: (i, 0, 0)),
    ]


def front_norm(image, text, vectors):
    width = image.shape[2]
    return pl.pallas_call(
        norm_kernel,
        grid=(2, 4),
        in_specs=front_specs(image, text, 4, width)
        + [pl.BlockSpec((1, 4, width), lambda i, j: (i, 0, 0))],
        out_specs=front_specs(image, text, 4, width),
        out_shape=[jax.ShapeDtypeStruct(v.shape, jnp.bfloat16) for v in (image, text)],
        compiler_params=pltpu.CompilerParams(vmem_limit_bytes=VMEM_LIMIT),
        cost_estimate=pl.CostEstimate(flops=0, bytes_accessed=25_000_000, transcendentals=0),
        name="front_norm",
    )(image, text, vectors)


def front_project(image, text, weight, bias, part):
    return pl.pallas_call(
        functools.partial(project_kernel, part),
        grid=(2, 2),
        in_specs=front_specs(image, text, 2, image.shape[2])
        + [
            pl.BlockSpec(weight.shape, lambda i, j: (0, 0, 0)),
            pl.BlockSpec(bias.shape, lambda i, j: (0, 0)),
        ],
        out_specs=front_specs(image, text, 2, 3 * part),
        out_shape=[
            jax.ShapeDtypeStruct(v.shape[:2] + (3 * part,), jnp.bfloat16) for v in (image, text)
        ],
        compiler_params=pltpu.CompilerParams(vmem_limit_bytes=VMEM_LIMIT),
        cost_estimate=pl.CostEstimate(flops=0, bytes_accessed=35_000_000, transcendentals=0),
        name="front_project",
    )(image, text, weight, bias)


def back_kernel(part, ups_image, ups_text, weight, out_image, out_text):
    line, rows = weight.shape[0], part * 2
    wide = 3 * part

    def back(ups, out, columns):
        for z in range(line):
            out[:, z * rows : (z + 1) * rows] = lax.dot_general(
                ups[...],
                weight[z, :rows, columns],
                (((1,), (1,)), ((), ())),
                preferred_element_type=jnp.float32,
            ).astype(jnp.bfloat16)

    back(ups_image, out_image, slice(None, wide))

    @pl.when(pl.program_id(0) == 0)
    def _():
        back(ups_text, out_text, slice(wide, None))


def back_to_hidden(ups, weight, part, blocks):
    width = weight.shape[0] * 2 * part
    step = ups[0].shape[0] // blocks

    def specs(columns):
        return [
            pl.BlockSpec((step, columns), lambda i: (i, 0)),
            pl.BlockSpec((ups[1].shape[0], columns), lambda i: (0, 0)),
        ]

    return pl.pallas_call(
        functools.partial(back_kernel, part),
        grid=(blocks,),
        in_specs=specs(3 * part) + [pl.BlockSpec(weight.shape, lambda i: (0, 0, 0))],
        out_specs=specs(width),
        out_shape=[jax.ShapeDtypeStruct((v.shape[0], width), jnp.bfloat16) for v in ups],
        compiler_params=pltpu.CompilerParams(vmem_limit_bytes=VMEM_LIMIT),
        cost_estimate=pl.CostEstimate(flops=0, bytes_accessed=25_000_000, transcendentals=0),
        name="back_to_hidden",
    )(*ups, weight)


def feed_back_kernel(
    ups_image, ups_text, before_image, before_text, out_weight, hid_weight,
    d_before_image, d_before_text, d_hidden_image, d_hidden_text,
):
    def back(left, weight):
        return lax.dot_general(
            left, weight, (((1,), (1,)), ((), ())), preferred_element_type=jnp.float32
        )

    def rows(ups, before, m, d_before, d_hidden):
        v = before[...]
        square = v * v
        bend = jnp.tanh(0.7978845608028654 * v * (1.0 + 0.044715 * square))
        slope = 0.5 * (1.0 + bend) + 0.5 * v * (1.0 - bend * bend) * 0.7978845608028654 * (
            1.0 + 0.134145 * square
        )
        d = (back(ups[...], out_weight[m]) * slope).astype(jnp.bfloat16)
        d_before[...] = d
        d_hidden[...] = back(d, hid_weight[m]).astype(jnp.bfloat16)

    rows(ups_image, before_image, 0, d_before_image, d_hidden_image)

    @pl.when(pl.program_id(0) == 0)
    def _():
        rows(ups_text, before_text, 1, d_before_text, d_hidden_text)


def feed_back(ups, before, out_weight, hid_weight, blocks):
    width, units = ups[0].shape[1], before[0].shape[1]
    step = ups[0].shape[0] // blocks

    def specs(columns):
        return [
            pl.BlockSpec((step, columns), lambda i: (i, 0)),
            pl.BlockSpec((ups[1].shape[0], columns), lambda i: (0, 0)),
        ]

    def whole(v):
        return pl.BlockSpec(v.shape, lambda i: (0, 0, 0))

    return pl.pallas_call(
        feed_back_kernel,
        grid=(blocks,),
        in_specs=specs(width) + specs(units) + [whole(out_weight), whole(hid_weight)],
        out_specs=specs(units) + specs(width),
        out_shape=[
            jax.ShapeDtypeStruct((v.shape[0], columns), jnp.bfloat16)
            for columns in (units, width)
            for v in ups
        ],
        compiler_params=pltpu.CompilerParams(vmem_limit_bytes=VMEM_LIMIT),
        cost_estimate=pl.CostEstimate(flops=0, bytes_accessed=60_000_000, transcendentals=0),
        name="feed_back",
    )(*ups, *before, out_weight, hid_weight)


def pair_terms_kernel(left_image, left_text, right_image, right_text, out):
    for m, (left, right) in enumerate(((left_image, right_image), (left_text, right_text))):
        out[m] = lax.dot_general(
            left[...], right[...], (((0,), (0,)), ((), ())), preferred_element_type=jnp.float32
        ).astype(jnp.bfloat16)


def pair_terms(left, right):
    k, c = left[0].shape[1], right[0].shape[1]
    step = 256 if k % 256 == 0 else k
    return pl.pallas_call(
        pair_terms_kernel,
        grid=(k // step,),
        in_specs=[pl.BlockSpec((v.shape[0], step), lambda i: (0, i)) for v in left]
        + [pl.BlockSpec(v.shape, lambda i: (0, 0)) for v in right],
        out_specs=pl.BlockSpec((2, step, c), lambda i: (0, i, 0)),
        out_shape=jax.ShapeDtypeStruct((2, k, c), jnp.bfloat16),
        compiler_params=pltpu.CompilerParams(vmem_limit_bytes=VMEM_LIMIT),
        cost_estimate=pl.CostEstimate(flops=0, bytes_accessed=25_000_000, transcendentals=0),
        name="pair_terms",
    )(*left, *right)


def fold(proj, wide):
    count, left = proj.shape[-2] // 3, wide // 3
    rest = proj[..., wide:]
    extra = [rest[..., i * count : (i + 1) * count, :] for i in range(3)]
    return jnp.concatenate([proj[..., :wide], jnp.concatenate(extra, -1)], -2)


def unfold(rows, count):
    left = rows.shape[-1] // 3
    extra = [rows[..., count:, i * left : (i + 1) * left] for i in range(3)]
    return jnp.concatenate([rows[..., :count, :], jnp.concatenate(extra, -2)], -1)


def pick_qkv_kernel(part, place, *refs):
    own, other = refs[3:]
    high = place[1] == 1
    for kind in range(3):
        for m in range(2):
            at = slice((m * 3 + kind) * part, (m * 3 + kind + 1) * part)
            low, up = refs[kind][m, :, :part], refs[kind][m, :, part:]
            own[:, at] = jnp.where(high, up, low)
            other[:, at] = jnp.where(high, low, up)


def pick_qkv(weight, place, part):
    slab, width = weight.shape[1], weight.shape[2] // 3
    per_kind = width // (2 * part)

    def spec(kind):
        return pl.BlockSpec((2, slab, 2 * part), lambda i, at: (0, 0, kind * per_kind + at[0]))

    shape = (slab, 6 * part)
    return pl.pallas_call(
        functools.partial(pick_qkv_kernel, part),
        grid_spec=pltpu.PrefetchScalarGridSpec(
            num_scalar_prefetch=1,
            grid=(1,),
            in_specs=[spec(k) for k in range(3)],
            out_specs=[pl.BlockSpec(shape, lambda i, at: (0, 0))] * 2,
        ),
        out_shape=[jax.ShapeDtypeStruct(shape, jnp.bfloat16)] * 2,
        compiler_params=pltpu.CompilerParams(vmem_limit_bytes=VMEM_LIMIT),
        name="pick_qkv",
    )(place, *([weight] * 3))


def pick_hid_kernel(line, place, *refs):
    own, other = refs[2 * line :]
    high, odd = place[1] == 1, place[2] == 1
    for z in range(line):
        chosen = []
        for q in range(2):
            block = refs[z * 2 + q]
            cut = block.shape[2] // 2
            chosen.append(jnp.where(odd, block[:, :, cut:], block[:, :, :cut]))
        at = slice(z * cut, (z + 1) * cut)
        own[:, :, at] = jnp.where(high, chosen[1], chosen[0])
        other[:, :, at] = jnp.where(high, chosen[0], chosen[1])


def pick_hid(weight, place, line):
    slab, units = weight.shape[1], weight.shape[2] // (2 * line)

    def spec(f):
        return pl.BlockSpec((2, slab, units // 2), lambda i, at: (0, 0, 2 * f + at[0] // 2))

    shape = (2, slab, line * units // 4)
    return pl.pallas_call(
        functools.partial(pick_hid_kernel, line),
        grid_spec=pltpu.PrefetchScalarGridSpec(
            num_scalar_prefetch=1,
            grid=(1,),
            in_specs=[spec(f) for f in range(2 * line)],
            out_specs=[pl.BlockSpec(shape, lambda i, at: (0, 0, 0))] * 2,
        ),
        out_shape=[jax.ShapeDtypeStruct(shape, jnp.bfloat16)] * 2,
        compiler_params=pltpu.CompilerParams(vmem_limit_bytes=VMEM_LIMIT),
        name="pick_hid",
    )(place, *([weight] * (2 * line)))


def chosen_piece(pieces, x, c, q):
    near = [jnp.where(c == q % 2, pieces[2 * dx], pieces[2 * dx + 1]) for dx in range(2)]
    return jnp.where(x == q // 2, near[0], near[1])


def inner(left, right):
    return lax.dot_general(
        left[...], right[...], (((0,), (0,)), ((), ())), preferred_element_type=jnp.float32
    ).astype(jnp.bfloat16)


def stacked_kernel(
    image, text, up_image, up_text, mixed_image, mixed_text, branch_image, branch_text,
    out, sums, proj,
):
    rows, part = image.shape[1], up_image.shape[1]
    wide = 2 * part
    z = pl.program_id(0)

    @pl.when(z == 0)
    def _():
        sums[...] = jnp.zeros(sums.shape, jnp.float32)
        sums[0:1] = row_sums(up_image[...].astype(jnp.float32))
        sums[1:2] = row_sums(up_text[...].astype(jnp.float32))
        proj[0] = inner(mixed_image, branch_image)
        proj[1] = inner(mixed_text, branch_text)

    out[0, :rows, :part] = inner(image, up_image)
    out[0, :rows, part:] = inner(text, up_text)
    chunk = proj.shape[1] // pl.num_programs(0)
    at = pl.ds(pl.multiple_of(z * chunk, 16), chunk)
    more = jnp.concatenate([proj[0, at, :], proj[1, at, :]], 0)
    count = more.shape[0]
    out[0, rows : rows + count, :] = more[:, :wide]
    third, left = count // 3, wide // 3
    for i in range(3):
        out[0, rows + count :, i * left : (i + 1) * left] = more[i * third : (i + 1) * third, wide:]


def stacked_terms(hidden, ups, mixed, branch, line):
    rows, part = hidden[0].shape[1] // line, ups[0].shape[1]
    head_part, width = mixed[0].shape[1], branch[0].shape[1]
    more = 2 * head_part // line * width // (2 * part)
    others = ups + mixed + branch
    return pl.pallas_call(
        stacked_kernel,
        grid=(line,),
        in_specs=[pl.BlockSpec((v.shape[0], rows), lambda z: (0, z)) for v in hidden]
        + [pl.BlockSpec(v.shape, lambda z: (0, 0)) for v in others],
        out_specs=[
            pl.BlockSpec((1, rows + more, 2 * part), lambda z: (z, 0, 0)),
            pl.BlockSpec((8, part), lambda z: (0, 0)),
        ],
        out_shape=[
            jax.ShapeDtypeStruct((line, rows + more, 2 * part), jnp.bfloat16),
            jax.ShapeDtypeStruct((8, part), jnp.float32),
        ],
        scratch_shapes=[pltpu.VMEM((2, head_part, width), jnp.bfloat16)],
        compiler_params=pltpu.CompilerParams(vmem_limit_bytes=VMEM_LIMIT),
        cost_estimate=pl.CostEstimate(flops=0, bytes_accessed=45_000_000, transcendentals=0),
        name="stacked_terms",
    )(*hidden, *others)


def columns_kernel(chunk, kinds, inner_first, place, *refs):
    out = refs[8]
    r, x, c = place[0], place[1], place[2]
    for m in range(out.shape[1]):
        for kind in range(kinds):
            at = slice((m * kinds + kind) * chunk, (m * kinds + kind + 1) * chunk)
            by_dr = [
                [chosen_piece([refs[dr * 4 + p][:, at] for p in range(4)], x, c, q) for q in range(4)]
                for dr in range(2)
            ]
            for q in range(4):
                for natural in range(2):
                    value = jnp.where(r == natural, by_dr[0][q], by_dr[1][q])
                    spot = q * 2 + natural if inner_first else natural * 4 + q
                    start = (kind * 8 + spot) * chunk
                    out[0, m, :, start : start + chunk] = value.astype(jnp.float32)


def natural_columns_kernel(chunk, kinds, pieces, out):
    for m in range(2):
        for kind in range(kinds):
            at = slice((m * kinds + kind) * chunk, (m * kinds + kind + 1) * chunk)
            for q in range(4):
                for p in range(2):
                    start = (kind * 8 + q * 2 + p) * chunk
                    out[0, m, :, start : start + chunk] = pieces[p, q, :, at].astype(jnp.float32)


def join_natural_columns(pieces, chunk, kinds):
    rows, columns = pieces.shape[2], 8 * kinds * chunk
    step = 48 if rows % 48 == 0 else rows
    return pl.pallas_call(
        functools.partial(natural_columns_kernel, chunk, kinds),
        grid=(rows // step,),
        in_specs=[pl.BlockSpec((2, 4, step, pieces.shape[3]), lambda i: (0, 0, i, 0))],
        out_specs=pl.BlockSpec((1, 2, step, columns), lambda i: (0, 0, i, 0)),
        out_shape=jax.ShapeDtypeStruct((1, 2, rows, columns), jnp.float32),
        compiler_params=pltpu.CompilerParams(vmem_limit_bytes=VMEM_LIMIT),
        name="join_natural_columns",
    )(pieces)


def join_columns(pieces, place, chunk, kinds, inner_first):
    rows = pieces[0].shape[-2]
    columns = 8 * kinds * chunk
    step = 64 if rows % 64 == 0 else rows
    if pieces[0].ndim == 3:
        grid = (rows // step, 2)
        piece = pl.BlockSpec((None, step, columns // 8), lambda i, m, at: (m, i, 0))
        out = pl.BlockSpec((1, 1, step, columns), lambda i, m, at: (0, m, i, 0))
    else:
        grid = (rows // step,)
        piece = pl.BlockSpec((step, columns // 4), lambda i, at: (i, 0))
        out = pl.BlockSpec((1, 2, step, columns), lambda i, at: (0, 0, i, 0))
    return pl.pallas_call(
        functools.partial(columns_kernel, chunk, kinds, inner_first),
        grid_spec=pltpu.PrefetchScalarGridSpec(
            num_scalar_prefetch=1, grid=grid, in_specs=[piece] * 8, out_specs=out
        ),
        out_shape=jax.ShapeDtypeStruct((1, 2, rows, columns), jnp.float32),
        compiler_params=pltpu.CompilerParams(vmem_limit_bytes=VMEM_LIMIT),
        name="join_columns",
    )(place, *pieces)


def rows_kernel(place, *refs):
    out = refs[4]
    rows = refs[0].shape[1]
    for q in range(4):
        value = chosen_piece([refs[p][0] for p in range(4)], place[1], place[2], q)
        out[0, 0, q * rows : (q + 1) * rows, :] = value.astype(jnp.float32)


def join_rows(pieces, place):
    rows, columns = pieces[0].shape[1:]
    step = columns // 2
    return pl.pallas_call(
        rows_kernel,
        grid_spec=pltpu.PrefetchScalarGridSpec(
            num_scalar_prefetch=1,
            grid=(2, 2),
            in_specs=[pl.BlockSpec((1, rows, step), lambda m, i, at: (m, 0, i))] * 4,
            out_specs=pl.BlockSpec((1, 1, 4 * rows, step), lambda m, i, at: (0, m, 0, i)),
        ),
        out_shape=jax.ShapeDtypeStruct((1, 2, 4 * rows, columns), jnp.float32),
        compiler_params=pltpu.CompilerParams(vmem_limit_bytes=VMEM_LIMIT),
        name="join_rows",
    )(place, *pieces)


def rows_major(values):
    return with_layout_constraint(values, Layout(major_to_minor=(0, 1)))


def together(*values):
    return lax.optimization_barrier(values)


def norm_rows(values):
    center = values - jnp.mean(values, -1, keepdims=True)
    return center * lax.rsqrt(jnp.mean(center * center, -1, keepdims=True) + NORM_EPS)


def modulated(values, shift, scale_up):
    return norm_rows(values) * (1.0 + scale_up) + shift


def gelu_tanh(values):
    return jax.nn.gelu(values, approximate=True)


def dot32(left, right, contract):
    return lax.dot_general(
        left, right, ((contract[0], contract[1]), ((), ())), preferred_element_type=jnp.float32
    )


def product(left, right):
    return dot32(left, right, ((1,), (0,)))


def rows_inner(left, right):
    return dot32(left, right, ((0,), (0,)))


def right_back(left, right):
    return dot32(left, right, ((1,), (1,)))


def swap_r(values):
    count = lax.axis_size("fsdp")
    return lax.ppermute(values, "fsdp", [(at, at ^ 1) for at in range(count)])


def swap_x(values):
    return lax.ppermute(values, "seq", [(at, at ^ 2) for at in range(4)])


def swap_c(values):
    return lax.ppermute(values, "seq", [(at, at ^ 1) for at in range(4)])


CORNERS = [(0, 0), (0, 1), (1, 0), (1, 1)]


def reduce_far(a0, a1, b0, b1):
    return [a0[0], a0[1], b0[0], b0[1], swap_x(a1), swap_r(b1)]


def reduce_sums(parts):
    f32, b16 = jnp.float32, jnp.bfloat16
    got_a, got_b = parts[4], parts[5]
    a = [(parts[dr].astype(f32) + got_a[dr].astype(f32)).astype(b16) for dr in range(2)]
    b = [(parts[2 + dx].astype(f32) + got_b[dx].astype(f32)).astype(b16) for dx in range(2)]
    return [a[0], b[0], a[1], b[1]]


def reduce_last(a, b, last_a, last_b):
    f32 = jnp.float32
    return jnp.concatenate(
        [a.astype(f32) + last_a.astype(f32), b.astype(f32) + last_b.astype(f32)], 1
    )


def shards(
    image_tokens,
    text_tokens,
    conditioning,
    text_lengths,
    mod_weight,
    mod_bias,
    qkv_weight,
    qkv_bias,
    proj_weight,
    proj_bias,
    hidden_weight,
    hidden_bias,
    output_weight,
    output_bias,
    image_cotangent,
    text_cotangent,
):
    f32, b16 = jnp.float32, jnp.bfloat16
    width = image_tokens.shape[2]
    counts = (image_tokens.shape[1], text_tokens.shape[1])
    parts = lax.axis_size("seq")
    owners = lax.axis_size("fsdp")
    line = owners // 2
    head_part = width // (2 * parts)
    heads_here = head_part // HEAD_DIM
    slab = width // owners
    units_slab = output_weight.shape[2]
    units_part = units_slab // parts
    units = units_slab * owners
    units_here = line * units_part
    score_scale = HEAD_DIM ** (-0.5)
    me = lax.axis_index("fsdp")
    s = lax.axis_index("seq")
    r = me % 2
    along = [[z * 2 + q for z in range(line)] for q in range(2)]
    direct_proj = line == parts
    image_rows, text_rows = counts[0] * parts, counts[1] * parts

    def cut(array, start, size, axis):
        return lax.dynamic_slice_in_dim(array, start, size, axis)

    def transpose_owners(values):
        pairs = [
            ((z * 2 + q) * parts + t, (t * 2 + q) * parts + z)
            for z in range(line)
            for q in range(2)
            for t in range(parts)
        ]
        return lax.ppermute(values, ("fsdp", "seq"), pairs)

    def line_gather(rows):
        return lax.all_gather(rows, "fsdp", axis=rows.ndim - 2, tiled=True, axis_index_groups=along)

    def line_reduce(term):
        return lax.psum_scatter(
            term, "fsdp", scatter_dimension=term.ndim - 2, tiled=True, axis_index_groups=along
        )

    def weight_terms(left, right):
        return jnp.stack([rows_inner(left[m], right[m]).astype(b16) for m in range(2)])

    def both_r(values):
        rows = values.reshape(values.shape[:-2] + (2, slab, -1))
        return pick(rows, r, values.ndim - 2), swap_r(pick(rows, 1 - r, values.ndim - 2))

    def by_r(own, other, axis):
        return jnp.where(r == 0, jnp.stack([own, other], axis), jnp.stack([other, own], axis))

    def pick(array, index, axis):
        return lax.dynamic_index_in_dim(array, index, axis, keepdims=False)

    biases = (mod_bias, qkv_bias, proj_bias, hidden_bias, output_bias)
    bias_sizes = [v.shape[2] for v in biases]
    bias_local = jnp.concatenate([v[0].astype(f32) for v in biases], 1)
    padded = -(-slab // 128) * 128
    common = jnp.concatenate([bias_local.reshape(-1), jnp.tile(text_lengths.astype(f32), 128)])
    common = jnp.pad(common, (0, -common.shape[0] % 256))
    half = common.shape[0] // 2
    common = cut(common, s % 2 * half, half, 0)
    spot = jnp.stack([s, r, s % 2]).astype(jnp.int32)
    aligned = (2 * head_part) % 128 == 0 and (2 * units_part) % 128 == 0
    if aligned:
        qkv_own, qkv_other = pick_qkv(qkv_weight[0], spot, head_part)
    else:
        qkv_view = qkv_weight[0].reshape(2, slab, 3, 2 * parts, head_part)
        qkv_own, qkv_other = [
            pick(qkv_view, s * 2 + at, 3).transpose(1, 0, 2, 3).reshape(slab, 6 * head_part)
            for at in (r, 1 - r)
        ]
    qkv_got = swap_r(qkv_other)
    proj_mine = proj_weight[0]
    if direct_proj:
        chunk = slab // parts
        proj_mine = transpose_owners(cut(proj_weight[0], s * chunk, chunk, 1))
    wide = 6 * head_part
    merged = direct_proj and slab % 96 == 0 and width - wide == wide // 3
    qkv_mine = by_r(qkv_own, qkv_got, 0).reshape(2 * slab, wide)
    if merged:
        rows = fold(proj_mine.reshape(2 * chunk, width), wide)
        qkv_mine = jnp.concatenate([qkv_mine, rows], 0)
    cond_in, qkv_mine = together(conditioning, qkv_mine)
    send = jnp.concatenate(
        [
            cond_in.reshape(owners, slab),
            jnp.zeros((owners, padded - slab), f32),
            jnp.broadcast_to(common, (owners, common.shape[0])),
        ],
        1,
    )
    small, act_cols, mods = modulation(send[:, None], mod_weight[0], owners, parts)
    small = small[:, :, 0, padded:].transpose(1, 0, 2).reshape(owners, -1)
    biases_end = 2 * sum(bias_sizes)
    lengths = [pick(small[:, biases_end], me ^ dr, 0) for dr in range(2)]
    bias_all = small[:, :biases_end].reshape(owners, 2, sum(bias_sizes))
    offsets = [0]
    for size in bias_sizes:
        offsets.append(offsets[-1] + size)
    mod_b, qkv_b, proj_b, hid_b, out_b = [
        bias_all[:, :, offsets[i] : offsets[i + 1]].transpose(1, 0, 2) for i in range(5)
    ]
    group = s * 2 + r
    qkv_b = cut(qkv_b.reshape(2, 2, width), group * head_part, head_part, 2)
    qkv_b = jnp.stack([qkv_b[:, 0], jnp.zeros_like(qkv_b[:, 0]), qkv_b[:, 1]], 1).reshape(
        2, 3 * head_part
    )
    proj_b = proj_b.reshape(2, width)
    out_b = out_b.reshape(2, width)
    hid_b = pick(pick(hid_b.reshape(2, line, 2, parts, units_part), s, 3), r, 2).reshape(
        2, units_here
    )
    mods = mods.reshape(parts, 2, 2, -1).transpose(1, 2, 0, 3).reshape(2, 2, 6 * width)
    mods = mods + mod_b.reshape(2, 6 * width)
    mod_part = mod_bias.shape[2]

    front_w = line_gather(qkv_mine).reshape(line, -1, wide)
    qkv_w = front_w[:, : 2 * slab].reshape(width, wide)
    qkv_w = [qkv_w[:, m * 3 * head_part : (m + 1) * 3 * head_part] for m in range(2)]
    if merged:
        proj_w = unfold(front_w[:, 2 * slab :], 2 * chunk).reshape(line, 2, chunk, width)
        proj_w = proj_w.transpose(1, 0, 2, 3).reshape(2, head_part, width)
    elif direct_proj:
        proj_w = line_gather(proj_mine)
    else:
        proj_all = lax.all_gather(proj_mine, "fsdp", axis=1, tiled=True)
        proj_w = cut(proj_all, group * head_part, head_part, 1)
    mods, image_in, text_in = together(mods, image_tokens[0], text_tokens[0])
    x_full = [v.reshape(2, -1, width) for v in gather_group(image_in, text_in, 3)]
    x_full[0], hid_spot = together(x_full[0], spot)
    if aligned:
        hid_own, hid_other = pick_hid(hidden_weight[0], hid_spot, line)
    else:
        hid_view = pick(hidden_weight[0].reshape(2, slab, line, 2, parts, units_part), s, 4)
        hid_own, hid_other = [
            pick(hid_view, at, 3).reshape(2, slab, units_here) for at in (r, 1 - r)
        ]
    hid_got = swap_r(hid_other)

    def mod_at(index, m):
        at = slice(index * width, (index + 1) * width)
        return mods[0, m, None, at], mods[:, m, None, at]

    shift1, scale1, gate1, shift2, scale2, gate2 = [
        [mod_at(i, m) for m in range(2)] for i in range(6)
    ]

    def joined(pieces):
        return [v.reshape(2, -1, v.shape[-1]) for v in pieces]

    def apart(values, m):
        return values.reshape(2, parts, counts[m], -1)

    def flat(values):
        return values.reshape(-1, values.shape[-1])


    if merged:
        vectors = jnp.concatenate([v for m in range(2) for v in (shift1[m][1], scale1[m][1])], 1)
        hidden1 = list(front_norm(*x_full, vectors))
        hidden1[0], hid_got = together(hidden1[0], hid_got)
        front_w, hidden1[0] = together(front_w, hidden1[0])
        qkv = list(front_project(*hidden1, front_w, qkv_b, head_part))
        hidden1 = [flat(v) for v in hidden1]
    else:
        hidden1 = [
            flat(modulated(x_full[m].astype(f32), shift1[m][1], scale1[m][1]).astype(b16))
            for m in range(2)
        ]
        qkv = [
            rows_major((product(hidden1[m], qkv_w[m]) + qkv_b[m]).astype(b16)) for m in range(2)
        ]
        qkv = [v.reshape(2, -1, 3 * head_part) for v in qkv]
    hid_w = line_gather(by_r(hid_own, hid_got, 1).reshape(2, 2 * slab, units_here))
    out_w = line_gather(cut(output_weight[0], s * units_part, units_part, 1))
    text_slot = jnp.arange(text_rows)
    text_place = ((text_slot // counts[1]) ^ s) * counts[1] + text_slot % counts[1]
    open_text = jnp.stack([(text_place.astype(f32) < n).astype(f32) for n in lengths])
    open_text = jnp.broadcast_to(open_text[:, :, None], (2, text_rows, 128))
    mixed_image, mixed_text, lse_image, lse_text = attention(*qkv, open_text, score_scale)
    attended = [flat(mixed_image), flat(mixed_text)]

    def like(pair, kind):
        return [jax.ShapeDtypeStruct(v.shape, kind) for v in pair]

    own = [image_tokens[0], text_tokens[0]]
    own_up = [image_cotangent[0], text_cotangent[0]]

    def summed(terms, *rest, **options):
        return list(reduce_group(*[apart(terms[m], m) for m in range(2)], *rest, **options))

    vectors = [v for m in range(2) for v in (proj_b[m, None], gate1[m][0], shift2[m][0], scale2[m][0])]
    reduced = summed(
        [product(attended[m], proj_w[m]).astype(b16) for m in range(2)],
        5,
        middle_epilogue,
        own + [jnp.concatenate(vectors, 0)],
        like(own, f32) + like(own, f32) + like(own, b16),
    )
    branch, middle = reduced[:2], reduced[2:4]
    hidden2 = [flat(v) for v in gather_group(*reduced[4:], 6)]

    shapes = [jax.ShapeDtypeStruct((v.shape[0], units_here), f32) for v in hidden2]
    shapes += [jax.ShapeDtypeStruct((v.shape[0], units_here), b16) for v in hidden2]
    extra = hidden2 + [hid_w, hid_b]
    d_own = [(own_up[m].astype(f32) * gate2[m][0]).astype(b16) for m in range(2)]
    image_up, text_up, extra[0] = together(*d_own, extra[0])
    gathered = gather_group(
        image_up,
        text_up,
        4,
        first_layer_work,
        extra,
        shapes,
        held(extra + shapes) + [pltpu.SemaphoreType.DMA((8,))],
    )
    d_result, before, active = [flat(v) for v in gathered[:2]], gathered[2:4], gathered[4:]
    out_t = pair_terms(active, d_result)
    out_g = line_reduce(out_t)
    d_result[0], d_result[1], out_t = together(*d_result, out_t)
    *d_before, d_image, d_text = feed_back(d_result, before, out_w, hid_w, 4)
    d_hidden2 = [d_image, d_text]
    vectors = [v for m in range(2) for v in (scale2[m][0], gate1[m][0])]
    hid_terms = [
        jax.ShapeDtypeStruct((2, width, units_here), b16),
        jax.ShapeDtypeStruct((8, units_here), f32),
    ]
    reduced = summed(
        d_hidden2,
        7,
        middle_back_epilogue,
        list(middle) + own_up + list(branch) + [jnp.concatenate(vectors, 0)],
        like(own, f32) + like(own, b16) + [jax.ShapeDtypeStruct((8, width), f32)],
        weight_terms_work,
        hidden2 + d_before,
        hid_terms,
        held(hidden2 + d_before + hid_terms) + [pltpu.SemaphoreType.DMA((6,))],
    )
    d_middle, d_branch, sums2, hid_t, hid_sums = reduced[:2], reduced[2:4], *reduced[4:]
    hid_g = line_reduce(hid_t)
    extra = list(active) + [out_w]
    corner = (4, sum(counts), width)
    gathered = list(gather_group(
        *d_branch,
        8,
        second_layer_work,
        extra,
        [jax.ShapeDtypeStruct((2, sum(counts), width // 2), b16)] * 4,
        held(extra)
        + [pltpu.VMEM((2,) + corner, b16), pltpu.VMEM(corner, b16), pltpu.SemaphoreType.DMA((11,))]
        + [pltpu.SemaphoreType.DMA] * 2,
        micros=90,
    ))
    gathered[0], out_g = together(gathered[0], out_g)
    d_branch_full = [flat(v) for v in gathered[:2]]
    result_near = gathered[2:]
    d_attended = [
        rows_major(right_back(d_branch_full[m], proj_w[m]).astype(b16)).reshape(2, -1, head_part)
        for m in range(2)
    ]
    out_far = swap_x(out_g)
    result_far = reduce_far(*result_near)
    d_qkv = attention_back(*qkv, open_text, lse_image, lse_text, *d_attended, score_scale)
    d_qkv = [flat(v) for v in d_qkv]
    d_qkv[0], d_qkv[1], out_far, *result_far = together(*d_qkv, out_far, *result_far)
    d_qkv[0], d_qkv[1], *result_sums = together(*d_qkv, *reduce_sums(result_far))
    result_last = [swap_r(result_sums[2]), swap_x(result_sums[3])]
    if merged:
        qkv_t, qkv_sums = stacked_terms(hidden1, d_qkv, attended, d_branch_full, line)
        qkv_t = qkv_t.reshape(-1, wide)
    else:
        qkv_t = [rows_inner(hidden1[m], d_qkv[m]).astype(b16) for m in range(2)]
        qkv_t = jnp.concatenate(qkv_t, 1)
        qkv_sums = jnp.concatenate([row_sums(v.astype(f32)) for v in d_qkv], 0)
    both = line_reduce(qkv_t)
    d_qkv[0], d_qkv[1], qkv_t = together(*d_qkv, qkv_t)
    if merged:
        d_hidden1 = list(back_to_hidden(d_qkv, front_w, head_part, 4))
    else:
        d_hidden1 = [right_back(d_qkv[m], qkv_w[m]).astype(b16) for m in range(2)]
    d_hidden1[0], d_hidden1[1], hid_g, *result_last = together(*d_hidden1, hid_g, *result_last)
    hid_keep, hid_got = both_r(hid_g)
    reduced = summed(
        d_hidden1,
        9,
        input_back_epilogue,
        own + list(d_middle) + [jnp.concatenate([scale1[m][0] for m in range(2)], 0)],
        like(own, f32) + [jax.ShapeDtypeStruct((8, width), f32)],
        micros=90,
    )
    token_grads, sums1 = [v[None] for v in reduced[:2]], reduced[2]
    hid_far = swap_x(hid_keep)
    sums1, hid_got, hid_far = together(sums1, hid_got, hid_far)
    hid_got_far = swap_x(hid_got)
    sums1, *result_last = together(sums1, *result_last)
    result_last = reduce_last(*result_sums[:2], *result_last)
    result = [result_last[: counts[0]] + out_b[0], result_last[counts[0] :] + out_b[1]]
    image_out, text_out = [
        (middle[m] + gate2[m][0] * result[m]).astype(b16)[None] for m in range(2)
    ]

    all_rows = []
    for m in range(2):
        columns = qkv_sums[m].reshape(3, head_part)
        qkv_bt = lax.dynamic_update_slice_in_dim(
            jnp.zeros((2, width), f32), columns[::2], group * head_part, 1
        )
        units_bt = hid_sums[m].reshape(line, units_part)
        hid_bt = lax.dynamic_update_slice_in_dim(
            jnp.zeros((line, 2 * units_slab), f32), units_bt, r * units_slab + s * units_part, 1
        )
        up = own_up[m].astype(f32)
        all_rows += [
            sums1[2 * m : 2 * m + 2],
            sums2[4 * m + 2 : 4 * m + 3],
            sums2[4 * m : 4 * m + 2],
            row_sums(up * result[m]),
            qkv_bt,
            sums2[4 * m + 3 : 4 * m + 4],
            hid_bt.reshape(-1, width),
            row_sums((up * gate2[m][0]).astype(b16).astype(f32)),
        ]
    sums = jnp.concatenate(all_rows, 0)
    length = sums.shape[0]
    place = jnp.stack([r, s // 2, s % 2]).astype(jnp.int32)

    def share(own, far=None):
        far = swap_x(own) if far is None else far
        return [own, swap_c(own), far, swap_c(far)]

    out_grad = join_rows(share(out_g, out_far), place)
    hid_got_far, out_grad = together(hid_got_far, out_grad)
    hid_parts = share(hid_keep, hid_far) + share(hid_got, hid_got_far)
    hid_grad = join_columns(hid_parts, place, units_part, line, False)
    sums, out_grad, hid_grad = together(sums, out_grad, hid_grad)
    sums = jnp.pad(sums, ((0, -length % 16), (0, 0)))
    sums_all, d_mods, d_act, qkv_pieces, proj_pieces = finish(sums, both, mod_weight[0], owners)
    bias_sum = jnp.sum(sums_all[:, :length].astype(f32), 0).reshape(2, 14, width)
    bias_sum = bias_sum[:, 6:].reshape(2, -1)
    bias_at = [0, 2 * width, 3 * width, 3 * width + units, 4 * width + units]
    bias_grads = [
        cut(bias_sum[:, bias_at[i] : bias_at[i + 1]], me * size, size, 1)[None]
        for i, size in enumerate(bias_sizes[1:])
    ]
    mod_grad_w = jnp.einsum("sd,tse->tde", act_cols, d_mods, preferred_element_type=f32)[None]
    mod_grad_b = jnp.sum(cut(d_mods, me * mod_part, mod_part, 2).astype(f32), 1)[None]
    d_act = d_act[:, 0, :slab].reshape(1, width)
    conditioning_grad = jax.vjp(jax.nn.silu, conditioning)[1](d_act)[0]

    if merged:
        proj_grad = unfold_rows(proj_pieces)
    else:
        proj_t = [rows_inner(attended[m], d_branch_full[m]).astype(b16) for m in range(2)]
        proj_grad = []
        for m in range(2):
            spread = lax.dynamic_update_slice_in_dim(
                jnp.zeros((width, width), b16), proj_t[m], group * head_part, 0
            )
            own = lax.psum_scatter(spread, "fsdp", scatter_dimension=0, tiled=True)
            proj_grad.append(lax.psum(own, "seq").astype(f32))
        proj_grad = jnp.stack(proj_grad)[None]
    qkv_grad = join_natural_columns(qkv_pieces, head_part, 3)
    return (
        image_out,
        text_out,
        token_grads[0],
        token_grads[1],
        conditioning_grad,
        mod_grad_w,
        mod_grad_b,
        qkv_grad,
        bias_grads[0],
        proj_grad,
        bias_grads[1],
        hid_grad,
        bias_grads[2],
        out_grad,
        bias_grads[3],
    )


def solution(mesh):
    tokens = P("fsdp", "seq", None)
    weight = P(None, None, "fsdp", None)
    bias = P(None, None, "fsdp")
    pairs = (weight, bias) * 5
    return jax.shard_map(
        shards,
        mesh=mesh,
        in_specs=(tokens, tokens, P("fsdp", None), P("fsdp")) + pairs + (tokens, tokens),
        out_specs=(tokens, tokens, tokens, tokens, P("fsdp", None)) + pairs,
        check_vma=False,
    )
```

```python
import functools

import jax
import jax.numpy as jnp
from jax import lax
from jax.experimental import pallas as pl
from jax.experimental.layout import Layout, with_layout_constraint
from jax.experimental.pallas import tpu as pltpu
from jax.sharding import PartitionSpec as P

HEAD_DIM = 64
NORM_EPS = 1e-06
MASKED_SCORE = -1e30
VMEM_LIMIT = 60 * 2**20


def mm(left, right):
    return lax.dot_general(left, right, (((1,), (0,)), ((), ())), preferred_element_type=jnp.float32)


def key_scores(key_image, key_text, query_t, open_text, scale):
    image = mm(key_image, query_t) * scale
    text = jnp.where(open_text > 0.0, mm(key_text, query_t) * scale, MASKED_SCORE)
    return image, text


def attention_kernel(part, scale, image_ref, text_ref, open_ref, out_image, out_text, lse_image, lse_text):
    heads = part // HEAD_DIM
    b16 = jnp.bfloat16
    open_text = open_ref[0, :, :1]

    def columns(ref, kind, head):
        return ref[0, :, kind * part + head * HEAD_DIM : kind * part + (head + 1) * HEAD_DIM]

    keys = [(columns(image_ref, 1, h), columns(text_ref, 1, h)) for h in range(heads)]
    values_t = (image_ref[0, :, 2 * part :].T, text_ref[0, :, 2 * part :].T)

    def block(queries, width):
        queries_t = queries.T
        mixed, lse = [], []
        for h in range(heads):
            at = slice(h * HEAD_DIM, (h + 1) * HEAD_DIM)
            image, text = key_scores(*keys[h], queries_t[at], open_text, scale)
            top = jnp.maximum(
                jnp.max(image, 0, keepdims=True), jnp.max(text, 0, keepdims=True)
            )
            image, text = jnp.exp(image - top), jnp.exp(text - top)
            total = jnp.sum(image, 0, keepdims=True) + jnp.sum(text, 0, keepdims=True)
            out_t = mm(values_t[0][at], image.astype(b16)) + mm(values_t[1][at], text.astype(b16))
            mixed.append(out_t / total)
            lse.append(top + jnp.log(total))
        lse.append(jnp.zeros((8 - heads, width), jnp.float32))
        return jnp.concatenate(mixed, 0).T.astype(b16), jnp.concatenate(lse, 0)

    step = 256

    def body(i, carry):
        rows = pl.ds(pl.multiple_of(i * step, step), step)
        mixed, lse = block(image_ref[0, rows, :part], step)
        out_image[0, rows, :] = mixed
        lse_image[0, :, rows] = lse
        return carry

    lax.fori_loop(0, image_ref.shape[1] // step, body, 0)
    mixed, lse = block(text_ref[0, :, :part], text_ref.shape[1])
    out_text[0] = mixed
    lse_text[0] = lse


def attention(image_qkv, text_qkv, open_text, scale):
    two, image_rows, columns = image_qkv.shape
    text_rows, part = text_qkv.shape[1], columns // 3

    def spec(*dims):
        return pl.BlockSpec((1,) + dims, lambda i: (i, 0, 0))

    return pl.pallas_call(
        functools.partial(attention_kernel, part, scale),
        grid=(two,),
        in_specs=[spec(image_rows, columns), spec(text_rows, columns), spec(text_rows, 128)],
        out_specs=[
            spec(image_rows, part),
            spec(text_rows, part),
            spec(8, image_rows),
            spec(8, text_rows),
        ],
        out_shape=[
            jax.ShapeDtypeStruct((two, image_rows, part), jnp.bfloat16),
            jax.ShapeDtypeStruct((two, text_rows, part), jnp.bfloat16),
            jax.ShapeDtypeStruct((two, 8, image_rows), jnp.float32),
            jax.ShapeDtypeStruct((two, 8, text_rows), jnp.float32),
        ],
        compiler_params=pltpu.CompilerParams(vmem_limit_bytes=VMEM_LIMIT),
        cost_estimate=pl.CostEstimate(flops=0, bytes_accessed=90_000_000, transcendentals=0),
        name="attention",
    )(image_qkv, text_qkv, open_text)


def attention_back_kernel(
    part, scale, image_ref, text_ref, open_ref, lse_image, lse_text, up_image, up_text,
    out_image, out_text, d_keys, d_values,
):
    heads = part // HEAD_DIM
    b16 = jnp.bfloat16
    open_text = open_ref[0, :, :1]
    image_rows = image_ref.shape[1]

    def columns(ref, kind, head):
        return ref[0, :, kind * part + head * HEAD_DIM : kind * part + (head + 1) * HEAD_DIM]

    keys = [(columns(image_ref, 1, h), columns(text_ref, 1, h)) for h in range(heads)]
    values = [(columns(image_ref, 2, h), columns(text_ref, 2, h)) for h in range(heads)]
    keys_t = (image_ref[0, :, part : 2 * part].T, text_ref[0, :, part : 2 * part].T)

    def block(queries, ups, lse, first):
        queries_t, ups_t = queries.T, ups.T
        d_queries = []
        for h in range(heads):
            at = slice(h * HEAD_DIM, (h + 1) * HEAD_DIM)
            image, text = key_scores(*keys[h], queries_t[at], open_text, scale)
            row = lse[h : h + 1]
            image, text = jnp.exp(image - row), jnp.exp(text - row)
            up_rows = ups[:, at]
            terms = (mm(image.astype(b16), up_rows), mm(text.astype(b16), up_rows))
            d_image = mm(values[h][0], ups_t[at]) * image
            d_text = mm(values[h][1], ups_t[at]) * text
            row = jnp.sum(d_image, 0, keepdims=True) + jnp.sum(d_text, 0, keepdims=True)
            d_image = (d_image - row * image).astype(b16)
            d_text = (d_text - row * text).astype(b16)
            query_rows = queries[:, at]
            more = (mm(d_image, query_rows), mm(d_text, query_rows))
            d_queries.append((mm(keys_t[0][at], d_image) + mm(keys_t[1][at], d_text)) * scale)
            for ref, (a, b) in ((d_values, terms), (d_keys, more)):
                if first:
                    ref[h, :image_rows] = a
                    ref[h, image_rows:] = b
                else:
                    ref[h, :image_rows] += a
                    ref[h, image_rows:] += b
        return jnp.concatenate(d_queries, 0).T.astype(b16)

    step = 256
    out_text[0, :, :part] = block(text_ref[0, :, :part], up_text[0], lse_text[0], True)

    def body(i, carry):
        rows = pl.ds(pl.multiple_of(i * step, step), step)
        out_image[0, rows, :part] = block(
            image_ref[0, rows, :part], up_image[0, rows, :], lse_image[0, :, rows], False
        )
        return carry

    lax.fori_loop(0, image_rows // step, body, 0)
    for h in range(heads):
        for kind, ref, factor in ((1, d_keys, scale), (2, d_values, 1.0)):
            at = slice(kind * part + h * HEAD_DIM, kind * part + (h + 1) * HEAD_DIM)
            out_image[0, :, at] = (ref[h, :image_rows] * factor).astype(b16)
            out_text[0, :, at] = (ref[h, image_rows:] * factor).astype(b16)


def attention_back(image_qkv, text_qkv, open_text, lse_image, lse_text, up_image, up_text, scale):
    two, image_rows, columns = image_qkv.shape
    text_rows, part = text_qkv.shape[1], columns // 3
    heads = part // HEAD_DIM

    def spec(*dims):
        return pl.BlockSpec((1,) + dims, lambda i: (i, 0, 0))

    return pl.pallas_call(
        functools.partial(attention_back_kernel, part, scale),
        grid=(two,),
        in_specs=[
            spec(image_rows, columns),
            spec(text_rows, columns),
            spec(text_rows, 128),
            spec(8, image_rows),
            spec(8, text_rows),
            spec(image_rows, part),
            spec(text_rows, part),
        ],
        out_specs=[spec(image_rows, columns), spec(text_rows, columns)],
        out_shape=[
            jax.ShapeDtypeStruct(image_qkv.shape, jnp.bfloat16),
            jax.ShapeDtypeStruct(text_qkv.shape, jnp.bfloat16),
        ],
        scratch_shapes=[
            pltpu.VMEM((heads, image_rows + text_rows, HEAD_DIM), jnp.float32),
            pltpu.VMEM((heads, image_rows + text_rows, HEAD_DIM), jnp.float32),
        ],
        compiler_params=pltpu.CompilerParams(vmem_limit_bytes=VMEM_LIMIT),
        cost_estimate=pl.CostEstimate(flops=0, bytes_accessed=200_000_000, transcendentals=0),
        name="attention_back",
    )(image_qkv, text_qkv, open_text, lse_image, lse_text, up_image, up_text)


MESH = pl.DeviceIdType.MESH


def group_peers():
    f, s = lax.axis_index("fsdp"), lax.axis_index("seq")
    return {"r": (f ^ 1, s), "x": (f, s ^ 2), "c": (f, s ^ 1)}


def greet(peers):
    barrier = pltpu.get_barrier_semaphore()
    for peer in peers.values():
        pl.semaphore_signal(barrier, inc=1, device_id=peer, device_id_type=MESH)
    pl.semaphore_wait(barrier, len(peers))


def gather_kernel(work, extra, outs, own_image, own_text, *refs):
    extra_refs, (image, text) = refs[:extra], refs[extra : extra + 2]
    out_refs = refs[extra + 2 : extra + 2 + outs]
    local_sem, send_sem, recv_sem, *scratch = refs[extra + 2 + outs :]
    peers = group_peers()
    begin, run, finish = work(extra_refs, out_refs, scratch, peers)
    begin()
    cut = own_image.shape[1] // 2
    halves = {"a": pl.ds(0, cut), "b": pl.ds(cut, cut), "all": pl.ds(0, 2 * cut)}
    own, full = (own_image, own_text), (image, text)
    greet(peers)
    count = [0]

    def send(peer, source, piece, columns):
        copies = []
        for m in range(2):
            at = own[m].at[:, halves[columns]]
            if source is not None:
                at = full[m].at[source[0], source[1], :, halves[columns]]
            copy = pltpu.make_async_remote_copy(
                src_ref=at,
                dst_ref=full[m].at[piece[0], piece[1], :, halves[columns]],
                send_sem=send_sem.at[count[0]],
                recv_sem=recv_sem.at[count[0]],
                device_id=peers[peer],
                device_id_type=MESH,
            )
            copy.start()
            count[0] += 1
            copies.append(copy)
        return copies

    def landed(copies):
        for copy in copies:
            copy.wait_recv()

    a_r = send("r", None, (1, 0), "a")
    b_x = send("x", None, (0, 2), "b")
    a_x = send("x", None, (0, 2), "a")
    b_r = send("r", None, (1, 0), "b")
    all_c = send("c", None, (0, 1), "all")
    local = []
    for m in range(2):
        copy = pltpu.make_async_copy(own[m], full[m].at[0, 0], local_sem.at[m])
        copy.start()
        local.append(copy)
    landed(a_r)
    a_rx = send("x", (1, 0), (1, 2), "a")
    a_rc = send("c", (1, 0), (1, 1), "a")
    landed(b_x)
    b_xr = send("r", (0, 2), (1, 2), "b")
    b_xc = send("c", (0, 2), (0, 3), "b")
    run()
    landed(a_x)
    a_xc = send("c", (0, 2), (0, 3), "a")
    landed(b_r)
    b_rc = send("c", (1, 0), (1, 1), "b")
    landed(a_rx)
    a_rxc = send("c", (1, 2), (1, 3), "a")
    landed(b_xr)
    b_xrc = send("c", (1, 2), (1, 3), "b")
    for copies in (all_c, a_rc, b_xc, a_xc, b_rc, a_rxc, b_xrc):
        landed(copies)
    for copies in (a_r, b_x, a_x, b_r, all_c, a_rx, a_rc, b_xr, b_xc, a_xc, b_rc, a_rxc, b_xrc):
        for copy in copies:
            copy.wait_send()
    for copy in local:
        copy.wait()
    finish()


def no_work(extra, outs, scratch, peers):
    return (lambda: None,) * 3


def gather_group(
    image, text, collective_id, work=no_work, extra=(), outs=(), scratch=(), micros=35
):
    full = [jax.ShapeDtypeStruct((2, 4) + v.shape, v.dtype) for v in (image, text)]
    anywhere = pl.BlockSpec(memory_space=pl.ANY)
    return pl.pallas_call(
        functools.partial(gather_kernel, work, len(extra), len(outs)),
        in_specs=[anywhere] * (2 + len(extra)),
        out_specs=[anywhere] * (2 + len(outs)),
        out_shape=full + list(outs),
        scratch_shapes=[
            pltpu.SemaphoreType.DMA((2,)),
            pltpu.SemaphoreType.DMA((26,)),
            pltpu.SemaphoreType.DMA((26,)),
        ]
        + list(scratch),
        compiler_params=pltpu.CompilerParams(
            collective_id=collective_id, has_side_effects=True, vmem_limit_bytes=VMEM_LIMIT
        ),
        cost_estimate=pl.CostEstimate(
            flops=0, bytes_accessed=micros * 3_700_000, transcendentals=0
        ),
        name="gather_group",
    )(image, text, *extra)


def copies_of(sources, targets, sems, first):
    return [
        pltpu.make_async_copy(source, target, sems.at[first + i])
        for i, (source, target) in enumerate(zip(sources, targets))
    ]


def start_all(copies):
    for copy in copies:
        copy.start()


def wait_all(copies):
    for copy in copies:
        copy.wait()


def first_layer_work(extra, outs, scratch, peers):
    *held, before_image, before_text, active_image, active_text, sems = scratch
    results = (before_image, before_text, active_image, active_text)
    loads = copies_of(extra, held, sems, 0)
    stores = copies_of(results, outs, sems, 4)
    hidden_image, hidden_text, weight, bias = held

    def layer(rows, m):
        before = mm(rows, weight[m]) + bias[m : m + 1]
        inner = 0.7978845608028654 * (before + 0.044715 * before * before * before)
        return before, (0.5 * before * (1.0 + jnp.tanh(inner))).astype(jnp.bfloat16)

    def run():
        wait_all(loads)

        def body(i, carry):
            rows = pl.ds(pl.multiple_of(i * 256, 256), 256)
            before_image[rows, :], active_image[rows, :] = layer(hidden_image[rows, :], 0)
            return carry

        lax.fori_loop(0, hidden_image.shape[0] // 256, body, 0)
        before_text[...], active_text[...] = layer(hidden_text[...], 1)
        start_all(stores)

    return functools.partial(start_all, loads), run, functools.partial(wait_all, stores)


def second_layer_work(extra, outs, scratch, peers):
    active_image, active_text, weight, terms, got, sems, send_sem, recv_sem = scratch
    f32, b16 = jnp.float32, jnp.bfloat16
    loads = copies_of(extra, scratch[:3], sems, 0)
    pieces = 8
    cut = terms.shape[3] // 2
    first, last = pl.ds(0, cut), pl.ds(cut, cut)
    sources, targets = [], []
    for at in range(2):
        for i in range(2):
            sources += [terms.at[0, 2 * i + at, :, first], terms.at[0, 2 * at + i, :, last]]
            targets += [outs[at].at[i], outs[2 + at].at[i]]
    stores = copies_of(sources, targets, sems, 3)
    image_rows, text_rows = active_image.shape[0] // pieces, active_text.shape[0] // pieces
    swap = pltpu.make_async_remote_copy(
        src_ref=terms.at[1],
        dst_ref=got,
        send_sem=send_sem,
        recv_sem=recv_sem,
        device_id=peers["c"],
        device_id_type=MESH,
    )

    def run():
        wait_all(loads)

        def body(i, carry):
            rows = pl.ds(pl.multiple_of(i * image_rows, image_rows), image_rows)
            product = mm(active_image[rows, :], weight[0]).astype(b16)
            terms[i % 2, i // 2, :image_rows, :] = product
            return carry

        lax.fori_loop(0, pieces, body, 0)
        product = mm(active_text[...], weight[1])
        for i in range(pieces):
            rows = product[i * text_rows : (i + 1) * text_rows].astype(b16)
            terms[i % 2, i // 2, image_rows:, :] = rows
        swap.start()

    def finish():
        swap.wait()
        for i in range(pieces // 2):
            terms[0, i] = (terms[0, i].astype(f32) + got[i].astype(f32)).astype(b16)
        start_all(stores)
        wait_all(stores)

    return functools.partial(start_all, loads), run, finish


def weight_terms_work(extra, outs, scratch, peers):
    left_image, left_text, right_image, right_text, terms, columns_sum, sems = scratch
    loads = copies_of(extra, scratch[:4], sems, 0)
    stores = copies_of([terms, columns_sum], outs, sems, 4)
    block = 256 if terms.shape[1] % 256 == 0 else terms.shape[1]

    def inner(left, right):
        return lax.dot_general(
            left, right, (((0,), (0,)), ((), ())), preferred_element_type=jnp.float32
        ).astype(jnp.bfloat16)

    def run():
        wait_all(loads)

        def body(i, carry):
            columns = pl.ds(pl.multiple_of(i * block, block), block)
            terms[0, columns, :] = inner(left_image[:, columns], right_image[...])
            terms[1, columns, :] = inner(left_text[:, columns], right_text[...])
            return carry

        lax.fori_loop(0, terms.shape[1] // block, body, 0)
        columns_sum[...] = jnp.zeros(columns_sum.shape, jnp.float32)
        columns_sum[0:1] = row_sums(right_image[...].astype(jnp.float32))
        columns_sum[1:2] = row_sums(right_text[...].astype(jnp.float32))
        start_all(stores)

    return functools.partial(start_all, loads), run, functools.partial(wait_all, stores)


def held(arrays):
    return [pltpu.VMEM(v.shape, v.dtype) for v in arrays]


def reduce_kernel(epilogue, extra, outs, work, work_extra, work_outs, image, text, *refs):
    extra_refs, refs = refs[:extra], refs[extra:]
    work_refs, refs = refs[:work_extra], refs[work_extra:]
    out_refs, refs = refs[:outs], refs[outs:]
    work_out_refs, refs = refs[:work_outs], refs[work_outs:]
    (
        mine, near, acc, got_a, got_b, acc_a, acc_b, last_a, last_b, total,
        load_sem, send_sem, recv_sem, *scratch,
    ) = refs
    f32, b16 = jnp.float32, jnp.bfloat16
    peers = group_peers()
    begin, run, finish = work(work_refs, work_out_refs, scratch, peers)
    t_image = image.shape[2]
    cut = image.shape[3] // 2
    spans = (pl.ds(0, t_image), pl.ds(t_image, text.shape[2]))
    sources = (image, text)
    corners = [(1, 1), (0, 1), (1, 0), (0, 0)]
    loads = {}
    for i, (dr, dx) in enumerate(corners):
        loads[dr, dx] = []
        for m in range(2):
            copy = pltpu.make_async_copy(
                sources[m].at[dr, dx * 2], mine.at[dr * 2 + dx, spans[m]], load_sem.at[2 * i + m]
            )
            copy.start()
            loads[dr, dx].append(copy)
    begin()
    greet(peers)
    started = []

    def send(peer, source, target):
        copy = pltpu.make_async_remote_copy(
            src_ref=source,
            dst_ref=target,
            send_sem=send_sem.at[len(started)],
            recv_sem=recv_sem.at[len(started)],
            device_id=peers[peer],
            device_id_type=MESH,
        )
        copy.start()
        started.append(copy)
        return copy

    near_copies = {
        (dr, dx): [
            send("c", sources[m].at[dr, dx * 2 + 1], near.at[dr * 2 + dx, spans[m]])
            for m in range(2)
        ]
        for dr, dx in corners
    }
    a, b = slice(None, cut), slice(cut, None)

    def plus(left, right):
        return (left.astype(f32) + right.astype(f32)).astype(b16)

    far = {}
    for dr, dx in corners:
        at = dr * 2 + dx
        for copy in loads[dr, dx]:
            copy.wait()
        for copy in near_copies[dr, dx]:
            copy.wait_recv()
        acc[at] = plus(mine[at], near[at])
        if dx == 1:
            far["a", dr] = send("x", acc.at[at, :, pl.ds(0, cut)], got_a.at[dr])
        if dr == 1:
            far["b", dx] = send("r", acc.at[at, :, pl.ds(cut, cut)], got_b.at[dx])
    run()
    far["a", 1].wait_recv()
    acc_a[1] = plus(acc[2, :, a], got_a[1])
    to_a = send("r", acc_a.at[1], last_a)
    far["b", 1].wait_recv()
    acc_b[1] = plus(acc[1, :, b], got_b[1])
    to_b = send("x", acc_b.at[1], last_b)
    far["a", 0].wait_recv()
    acc_a[0] = plus(acc[0, :, a], got_a[0])
    far["b", 0].wait_recv()
    acc_b[0] = plus(acc[0, :, b], got_b[0])
    to_a.wait_recv()
    total[:, a] = acc_a[0].astype(f32) + last_a[...].astype(f32)
    to_b.wait_recv()
    total[:, b] = acc_b[0].astype(f32) + last_b[...].astype(f32)
    epilogue(total, t_image, extra_refs, out_refs)
    for copy in started:
        copy.wait_send()
    finish()


def reduce_group(
    image, text, collective_id, epilogue, extra, outs,
    work=no_work, work_extra=(), work_outs=(), scratch=(), micros=40,
):
    anywhere = pl.BlockSpec(memory_space=pl.ANY)
    rows, width = image.shape[2] + text.shape[2], image.shape[3]
    b16 = jnp.bfloat16
    half = (rows, width // 2)
    return pl.pallas_call(
        functools.partial(
            reduce_kernel, epilogue, len(extra), len(outs), work, len(work_extra), len(work_outs)
        ),
        in_specs=[anywhere] * 2
        + [pl.BlockSpec(memory_space=pltpu.VMEM)] * len(extra)
        + [anywhere] * len(work_extra),
        out_specs=[pl.BlockSpec(memory_space=pltpu.VMEM)] * len(outs)
        + [anywhere] * len(work_outs),
        out_shape=list(outs) + list(work_outs),
        scratch_shapes=[
            pltpu.VMEM((4, rows, width), b16),
            pltpu.VMEM((4, rows, width), b16),
            pltpu.VMEM((4, rows, width), b16),
            pltpu.VMEM((2,) + half, b16),
            pltpu.VMEM((2,) + half, b16),
            pltpu.VMEM((2,) + half, b16),
            pltpu.VMEM((2,) + half, b16),
            pltpu.VMEM(half, b16),
            pltpu.VMEM(half, b16),
            pltpu.VMEM((rows, width), jnp.float32),
            pltpu.SemaphoreType.DMA((8,)),
            pltpu.SemaphoreType.DMA((14,)),
            pltpu.SemaphoreType.DMA((14,)),
        ]
        + list(scratch),
        compiler_params=pltpu.CompilerParams(
            collective_id=collective_id, has_side_effects=True, vmem_limit_bytes=VMEM_LIMIT
        ),
        cost_estimate=pl.CostEstimate(
            flops=0, bytes_accessed=micros * 3_700_000, transcendentals=0
        ),
        name="reduce_group",
    )(image, text, *extra, *work_extra)


def row_norm(values):
    center = values - jnp.mean(values, -1, keepdims=True)
    inverse = lax.rsqrt(jnp.mean(center * center, -1, keepdims=True) + NORM_EPS)
    return center * inverse, inverse


def row_sums(values):
    return jnp.sum(values, 0, keepdims=True)


def middle_epilogue(total, t_image, extra, outs):
    vectors = extra[2]
    for m, rows in ((0, slice(None, t_image)), (1, slice(t_image, None))):
        bias, gate, shift, scale = [vectors[4 * m + i : 4 * m + i + 1] for i in range(4)]
        branch = total[rows] + bias
        middle = extra[m][...].astype(jnp.float32) + gate * branch
        normal, _ = row_norm(middle)
        outs[m][...] = branch
        outs[2 + m][...] = middle
        outs[4 + m][...] = (normal * (1.0 + scale) + shift).astype(jnp.bfloat16)


def norm_back(d_hidden, values, scale):
    normal, inverse = row_norm(values)
    e = d_hidden * (1.0 + scale)
    mean = jnp.mean(e, -1, keepdims=True)
    along = jnp.mean(e * normal, -1, keepdims=True)
    return (e - mean - normal * along) * inverse, row_sums(d_hidden), row_sums(d_hidden * normal)


def middle_back_epilogue(total, t_image, extra, outs):
    f32 = jnp.float32
    vectors, sums = extra[6], outs[4]
    for m, rows in ((0, slice(None, t_image)), (1, slice(t_image, None))):
        scale, gate = [vectors[2 * m + i : 2 * m + i + 1] for i in range(2)]
        d_norm, d_shift, d_scale = norm_back(total[rows], extra[m][...], scale)
        d_middle = extra[2 + m][...].astype(f32) + d_norm
        d_branch = (d_middle * gate).astype(jnp.bfloat16)
        outs[m][...] = d_middle
        outs[2 + m][...] = d_branch
        parts = (d_shift, d_scale, row_sums(d_middle * extra[4 + m][...]), row_sums(d_branch.astype(f32)))
        for i, part in enumerate(parts):
            sums[4 * m + i : 4 * m + i + 1] = part


def input_back_epilogue(total, t_image, extra, outs):
    vectors, sums = extra[4], outs[2]
    sums[...] = jnp.zeros(sums.shape, jnp.float32)
    for m, rows in ((0, slice(None, t_image)), (1, slice(t_image, None))):
        d_norm, d_shift, d_scale = norm_back(
            total[rows], extra[m][...].astype(jnp.float32), vectors[m : m + 1]
        )
        outs[m][...] = extra[2 + m][...] + d_norm
        sums[2 * m : 2 * m + 1] = d_shift
        sums[2 * m + 1 : 2 * m + 2] = d_scale


def modulation_kernel(
    owners, parts, slab, send, weight, small_out, act_out, mods_out,
    small, piece, term, got, mods, others, load_sem, sems,
):
    f, s = lax.axis_index("fsdp"), lax.axis_index("seq")
    quarter = piece.shape[2]
    columns = pl.ds(pl.multiple_of(s * quarter, 128), quarter)
    load = pltpu.make_async_copy(weight.at[:, :, columns], piece, load_sem)
    load.start()
    barrier = pltpu.get_barrier_semaphore()
    for k in range(1, owners):
        pl.semaphore_signal(
            barrier, inc=1, device_id=(lax.rem(f + k, owners), s), device_id_type=MESH
        )
    for q in range(1, parts):
        pl.semaphore_signal(barrier, inc=1, device_id=(f, s ^ q), device_id_type=MESH)
    pl.semaphore_wait(barrier, owners + parts - 2)

    def exchange(source, target, stage):
        copies = []
        for k in range(1, owners):
            peer = lax.rem(f + k, owners)
            copy = pltpu.make_async_remote_copy(
                src_ref=source.at[peer],
                dst_ref=target.at[f],
                send_sem=sems.at[stage, 0, k],
                recv_sem=sems.at[stage, 1, k],
                device_id=(peer, s),
                device_id_type=MESH,
            )
            copy.start()
            copies.append(copy)
        target[f] = source[f]
        for copy in copies:
            copy.wait()

    exchange(send, small.at[s % 2], 0)
    swap = pltpu.make_async_remote_copy(
        src_ref=small.at[s % 2],
        dst_ref=small.at[s % 2],
        send_sem=sems.at[0, 0, 0],
        recv_sem=sems.at[0, 1, 0],
        device_id=(f, s ^ 1),
        device_id_type=MESH,
    )
    swap.start()
    act = jnp.concatenate([small[s % 2, k, :, :slab] for k in range(owners)], 0)
    act = (act / (1.0 + jnp.exp(-act))).astype(jnp.bfloat16)
    act_out[...] = act
    load.wait()
    for m in range(2):
        full = mm(act, piece[m])
        for k in range(owners):
            term[k, m : m + 1, :] = full[k : k + 1]
    exchange(term, got, 1)
    total = got[0]
    for k in range(1, owners):
        total = total + got[k]
    mods[s] = total
    copies = []
    for q in range(1, parts):
        copy = pltpu.make_async_remote_copy(
            src_ref=mods.at[s],
            dst_ref=mods.at[s],
            send_sem=sems.at[2, 0, q],
            recv_sem=sems.at[2, 1, q],
            device_id=(f, s ^ q),
            device_id_type=MESH,
        )
        copy.start()
        copies.append(copy)
    for copy in copies:
        copy.wait()
    pair = pltpu.make_async_remote_copy(
        src_ref=mods,
        dst_ref=others,
        send_sem=sems.at[3, 0, 0],
        recv_sem=sems.at[3, 1, 0],
        device_id=(f ^ 1, s),
        device_id_type=MESH,
    )
    pair.start()
    mods_out[:, 0:2, :] = mods[...]
    pair.wait()
    mods_out[:, 2:4, :] = others[...]
    swap.wait()
    small_out[...] = small[...]


def modulation(send, weight, owners, parts):
    slab, columns = weight.shape[1], weight.shape[2]
    quarter = columns // parts
    f32 = jnp.float32
    return pl.pallas_call(
        functools.partial(modulation_kernel, owners, parts, slab),
        in_specs=[
            pl.BlockSpec(memory_space=pltpu.VMEM),
            pl.BlockSpec(memory_space=pl.ANY),
        ],
        out_specs=[pl.BlockSpec(memory_space=pltpu.VMEM)] * 3,
        out_shape=[
            jax.ShapeDtypeStruct((2,) + send.shape, f32),
            jax.ShapeDtypeStruct((owners, slab), jnp.bfloat16),
            jax.ShapeDtypeStruct((parts, 4, quarter), f32),
        ],
        scratch_shapes=[
            pltpu.VMEM((2,) + send.shape, f32),
            pltpu.VMEM((2, slab, quarter), jnp.bfloat16),
            pltpu.VMEM((owners, 2, quarter), f32),
            pltpu.VMEM((owners, 2, quarter), f32),
            pltpu.VMEM((parts, 2, quarter), f32),
            pltpu.VMEM((parts, 2, quarter), f32),
            pltpu.SemaphoreType.DMA,
            pltpu.SemaphoreType.DMA((4, 2, owners)),
        ],
        compiler_params=pltpu.CompilerParams(
            collective_id=1, has_side_effects=True, vmem_limit_bytes=VMEM_LIMIT
        ),
        cost_estimate=pl.CostEstimate(
            flops=4 * owners * slab * quarter, bytes_accessed=60_000_000, transcendentals=0
        ),
        name="modulation",
    )(send, weight)


def finish_kernel(
    owners, slab, sums, both, weight, sums_out, mods_out, act_out, qkv_out, proj_out,
    mine, first, second, rounded, got, act, act_got, held_weight, local_sem, sems, far_sem,
):
    f, s = lax.axis_index("fsdp"), lax.axis_index("seq")
    r, z = f % 2, f // 2
    with_proj = both.shape[0] > 2 * slab
    keep, other = [
        both.at[pl.ds(pl.multiple_of(at * slab, 16), slab)] for at in (r, 1 - r)
    ]
    f32, b16 = jnp.float32, jnp.bfloat16
    load = pltpu.make_async_copy(weight, held_weight, local_sem.at[0])
    load.start()
    peers = {"y": (f ^ 1, s), "x": (f, s ^ 2), "c": (f, s ^ 1)}
    turned = (s * 2 + r, z)
    barrier = pltpu.get_barrier_semaphore()
    for k in range(1, owners):
        pl.semaphore_signal(
            barrier, inc=1, device_id=(lax.rem(f + k, owners), s), device_id_type=MESH
        )
    for peer in ("x", "c"):
        pl.semaphore_signal(barrier, inc=1, device_id=peers[peer], device_id_type=MESH)
    if with_proj:

        @pl.when(z != s)
        def _():
            pl.semaphore_signal(barrier, inc=1, device_id=turned, device_id_type=MESH)
            pl.semaphore_wait(barrier, owners + 2)

        @pl.when(z == s)
        def _():
            pl.semaphore_wait(barrier, owners + 1)

    else:
        pl.semaphore_wait(barrier, owners + 1)

    started = []

    def send(peer, source, target):
        copy = pltpu.make_async_remote_copy(
            src_ref=source,
            dst_ref=target,
            send_sem=sems.at[0, len(started)],
            recv_sem=sems.at[1, len(started)],
            device_id=peers[peer] if isinstance(peer, str) else peer,
            device_id_type=MESH,
        )
        copy.start()
        started.append(copy)
        return copy

    near_sums = send("c", sums, first)
    y_other = send("y", other, qkv_out.at[r, s])
    c_keep = send("c", keep, qkv_out.at[r, s])
    own = pltpu.make_async_copy(keep, qkv_out.at[r, s], local_sem.at[1])
    own.start()
    if with_proj:
        proj = both.at[pl.ds(2 * slab, both.shape[0] - 2 * slab)]
        turn = pltpu.make_async_remote_copy(
            src_ref=proj,
            dst_ref=proj_out.at[z],
            send_sem=far_sem.at[0],
            recv_sem=far_sem.at[1],
            device_id=turned,
            device_id_type=MESH,
        )
        stay = pltpu.make_async_copy(proj, proj_out.at[s], far_sem.at[0])

        @pl.when(z != s)
        def _():
            turn.start()

        @pl.when(z == s)
        def _():
            stay.start()

    half = sums.shape[0] // 2
    mine_rows = pl.ds(pl.multiple_of(s % 2 * half, 16), half)
    near_sums.wait_recv()
    mine[...] = sums[...] + first[...]
    far_sums = send("x", mine.at[mine_rows], second.at[mine_rows])
    x_keep = send("x", keep, qkv_out.at[r, s])
    far_sums.wait_recv()
    rounded[mine_rows, :] = (mine[mine_rows, :] + second[mine_rows, :]).astype(b16)
    spread = [
        send((lax.rem(f + k, owners), s), rounded.at[mine_rows], got.at[f, mine_rows])
        for k in range(1, owners)
    ]
    got[f, mine_rows, :] = rounded[mine_rows, :]
    y_other.wait_recv()
    x_got = send("x", qkv_out.at[1 - r, s], qkv_out.at[1 - r, s])
    last = [c_keep, send("c", qkv_out.at[1 - r, s], qkv_out.at[1 - r, s])]
    x_keep.wait_recv()
    last.append(send("c", qkv_out.at[r, s ^ 2], qkv_out.at[r, s ^ 2]))
    if with_proj:

        @pl.when(z != s)
        def _():
            turn.wait()

        @pl.when(z == s)
        def _():
            stay.wait()

        x_proj = send("x", proj_out.at[s], proj_out.at[s])
        last.append(send("c", proj_out.at[s], proj_out.at[s]))
    for copy in spread:
        copy.wait_recv()
    send("c", got.at[:, mine_rows], got.at[:, mine_rows]).wait_recv()
    load.wait()
    everyone = got[...].reshape(owners * sums.shape[0], sums.shape[1])
    rows, width = sums.shape
    per = 14
    total = [None] * owners
    for m in range(2):
        for i in range(6):
            part = lax.dot_general(
                everyone,
                held_weight[m, :, i * width : (i + 1) * width],
                (((1,), (1,)), ((), ())),
                preferred_element_type=f32,
            )
            for k in range(owners):
                at = k * rows + m * per + i
                row = part[at : at + 1]
                total[k] = row if total[k] is None else total[k] + row
    act[...] = jnp.zeros(act.shape, f32)
    for k in range(owners):
        act[k, :, :slab] = total[k]
    act_got[f] = act[f]
    for k in range(1, owners):
        peer = lax.rem(f + k, owners)
        last.append(send((peer, s), act.at[peer], act_got.at[f]))
    sums_out[...] = got[...]
    loose = got[...].astype(f32)
    for m in range(2):
        for i in range(6):
            at = m * per + i
            lines = jnp.concatenate([loose[k, at : at + 1] for k in range(owners)], 0)
            mods_out[m, :, i * width : (i + 1) * width] = lines.astype(b16)
    x_got.wait_recv()
    last.append(send("c", qkv_out.at[1 - r, s ^ 2], qkv_out.at[1 - r, s ^ 2]))
    if with_proj:
        x_proj.wait_recv()
        last.append(send("c", proj_out.at[s ^ 2], proj_out.at[s ^ 2]))
    for copy in last:
        copy.wait_recv()
    act_out[...] = act_got[...]
    own.wait()
    for copy in started:
        copy.wait_send()


def finish(sums, both, weight, owners):
    f32, b16 = jnp.float32, jnp.bfloat16
    slab, wide = weight.shape[1], both.shape[1]
    more = max(both.shape[0] - 2 * slab, 16)
    anywhere = pl.BlockSpec(memory_space=pl.ANY)
    inside = pl.BlockSpec(memory_space=pltpu.VMEM)
    all_sums = (owners,) + sums.shape
    all_act = (owners, 1, -(-slab // 128) * 128)
    count = 2 * owners + 12
    return pl.pallas_call(
        functools.partial(finish_kernel, owners, slab),
        in_specs=[inside, anywhere, anywhere],
        out_specs=[inside, inside, inside, anywhere, anywhere],
        out_shape=[
            jax.ShapeDtypeStruct(all_sums, b16),
            jax.ShapeDtypeStruct((2, owners, weight.shape[2]), b16),
            jax.ShapeDtypeStruct(all_act, f32),
            jax.ShapeDtypeStruct((2, 4, slab, wide), b16),
            jax.ShapeDtypeStruct((4, more, wide), b16),
        ],
        scratch_shapes=[
            pltpu.VMEM(sums.shape, f32),
            pltpu.VMEM(sums.shape, f32),
            pltpu.VMEM(sums.shape, f32),
            pltpu.VMEM(sums.shape, b16),
            pltpu.VMEM(all_sums, b16),
            pltpu.VMEM(all_act, f32),
            pltpu.VMEM(all_act, f32),
            pltpu.VMEM(weight.shape, b16),
            pltpu.SemaphoreType.DMA((2,)),
            pltpu.SemaphoreType.DMA((2, count)),
            pltpu.SemaphoreType.DMA((2,)),
        ],
        compiler_params=pltpu.CompilerParams(
            collective_id=2, has_side_effects=True, vmem_limit_bytes=VMEM_LIMIT
        ),
        cost_estimate=pl.CostEstimate(flops=0, bytes_accessed=130_000_000, transcendentals=0),
        name="finish",
    )(sums, both, weight)


def unfold_kernel(pieces, out):
    more, wide = pieces.shape[1:]
    count, left = more * 3 // 4, wide // 3
    chunk = count // 2
    for q in range(4):
        rest = [pieces[q, count:, i * left : (i + 1) * left] for i in range(3)]
        rest = jnp.concatenate(rest, 0)
        for m in range(2):
            at = slice(m * chunk, (m + 1) * chunk)
            rows = slice(q * chunk, (q + 1) * chunk)
            out[0, m, rows, :wide] = pieces[q, at, :].astype(jnp.float32)
            out[0, m, rows, wide:] = rest[at].astype(jnp.float32)


def unfold_rows(pieces):
    more, wide = pieces.shape[1:]
    return pl.pallas_call(
        unfold_kernel,
        out_shape=jax.ShapeDtypeStruct((1, 2, more * 3 // 2, wide + wide // 3), jnp.float32),
        compiler_params=pltpu.CompilerParams(vmem_limit_bytes=VMEM_LIMIT),
        name="unfold_rows",
    )(pieces)


def norm_kernel(image, text, vectors, hidden_image, hidden_text):
    def hidden(values, m):
        shift, scale = vectors[0, 2 * m : 2 * m + 1], vectors[0, 2 * m + 1 : 2 * m + 2]
        normal, _ = row_norm(values.astype(jnp.float32))
        return (normal * (1.0 + scale) + shift).astype(jnp.bfloat16)

    hidden_image[0] = hidden(image[0], 0)

    @pl.when(pl.program_id(1) == 0)
    def _():
        hidden_text[0] = hidden(text[0], 1)


def project_kernel(part, image, text, weight, bias, out_image, out_text):
    line, rows = weight.shape[0], part * 2
    wide = 3 * part

    def project(values, columns, m):
        total = bias[m : m + 1]
        for z in range(line):
            total = total + mm(values[0, :, z * rows : (z + 1) * rows], weight[z, :rows, columns])
        return total.astype(jnp.bfloat16)

    out_image[0] = project(image, slice(None, wide), 0)

    @pl.when(pl.program_id(1) == 0)
    def _():
        out_text[0] = project(text, slice(wide, None), 1)


def front_specs(image, text, blocks, columns):
    return [
        pl.BlockSpec((1, image.shape[1] // blocks, columns), lambda i, j: (i, j, 0)),
        pl.BlockSpec((1, text.shape[1], columns), lambda i, j: (i, 0, 0)),
    ]


def front_norm(image, text, vectors):
    width = image.shape[2]
    return pl.pallas_call(
        norm_kernel,
        grid=(2, 4),
        in_specs=front_specs(image, text, 4, width)
        + [pl.BlockSpec((1, 4, width), lambda i, j: (i, 0, 0))],
        out_specs=front_specs(image, text, 4, width),
        out_shape=[jax.ShapeDtypeStruct(v.shape, jnp.bfloat16) for v in (image, text)],
        compiler_params=pltpu.CompilerParams(vmem_limit_bytes=VMEM_LIMIT),
        cost_estimate=pl.CostEstimate(flops=0, bytes_accessed=25_000_000, transcendentals=0),
        name="front_norm",
    )(image, text, vectors)


def front_project(image, text, weight, bias, part):
    return pl.pallas_call(
        functools.partial(project_kernel, part),
        grid=(2, 2),
        in_specs=front_specs(image, text, 2, image.shape[2])
        + [
            pl.BlockSpec(weight.shape, lambda i, j: (0, 0, 0)),
            pl.BlockSpec(bias.shape, lambda i, j: (0, 0)),
        ],
        out_specs=front_specs(image, text, 2, 3 * part),
        out_shape=[
            jax.ShapeDtypeStruct(v.shape[:2] + (3 * part,), jnp.bfloat16) for v in (image, text)
        ],
        compiler_params=pltpu.CompilerParams(vmem_limit_bytes=VMEM_LIMIT),
        cost_estimate=pl.CostEstimate(flops=0, bytes_accessed=35_000_000, transcendentals=0),
        name="front_project",
    )(image, text, weight, bias)


def back_kernel(part, ups_image, ups_text, weight, out_image, out_text):
    line, rows = weight.shape[0], part * 2
    wide = 3 * part

    def back(ups, out, columns):
        for z in range(line):
            out[:, z * rows : (z + 1) * rows] = lax.dot_general(
                ups[...],
                weight[z, :rows, columns],
                (((1,), (1,)), ((), ())),
                preferred_element_type=jnp.float32,
            ).astype(jnp.bfloat16)

    back(ups_image, out_image, slice(None, wide))

    @pl.when(pl.program_id(0) == 0)
    def _():
        back(ups_text, out_text, slice(wide, None))


def back_to_hidden(ups, weight, part, blocks):
    width = weight.shape[0] * 2 * part
    step = ups[0].shape[0] // blocks

    def specs(columns):
        return [
            pl.BlockSpec((step, columns), lambda i: (i, 0)),
            pl.BlockSpec((ups[1].shape[0], columns), lambda i: (0, 0)),
        ]

    return pl.pallas_call(
        functools.partial(back_kernel, part),
        grid=(blocks,),
        in_specs=specs(3 * part) + [pl.BlockSpec(weight.shape, lambda i: (0, 0, 0))],
        out_specs=specs(width),
        out_shape=[jax.ShapeDtypeStruct((v.shape[0], width), jnp.bfloat16) for v in ups],
        compiler_params=pltpu.CompilerParams(vmem_limit_bytes=VMEM_LIMIT),
        cost_estimate=pl.CostEstimate(flops=0, bytes_accessed=25_000_000, transcendentals=0),
        name="back_to_hidden",
    )(*ups, weight)


def feed_back_kernel(
    ups_image, ups_text, before_image, before_text, out_weight, hid_weight,
    d_before_image, d_before_text, d_hidden_image, d_hidden_text,
):
    def back(left, weight):
        return lax.dot_general(
            left, weight, (((1,), (1,)), ((), ())), preferred_element_type=jnp.float32
        )

    def rows(ups, before, m, d_before, d_hidden):
        v = before[...]
        square = v * v
        bend = jnp.tanh(0.7978845608028654 * v * (1.0 + 0.044715 * square))
        slope = 0.5 * (1.0 + bend) + 0.5 * v * (1.0 - bend * bend) * 0.7978845608028654 * (
            1.0 + 0.134145 * square
        )
        d = (back(ups[...], out_weight[m]) * slope).astype(jnp.bfloat16)
        d_before[...] = d
        d_hidden[...] = back(d, hid_weight[m]).astype(jnp.bfloat16)

    rows(ups_image, before_image, 0, d_before_image, d_hidden_image)

    @pl.when(pl.program_id(0) == 0)
    def _():
        rows(ups_text, before_text, 1, d_before_text, d_hidden_text)


def feed_back(ups, before, out_weight, hid_weight, blocks):
    width, units = ups[0].shape[1], before[0].shape[1]
    step = ups[0].shape[0] // blocks

    def specs(columns):
        return [
            pl.BlockSpec((step, columns), lambda i: (i, 0)),
            pl.BlockSpec((ups[1].shape[0], columns), lambda i: (0, 0)),
        ]

    def whole(v):
        return pl.BlockSpec(v.shape, lambda i: (0, 0, 0))

    return pl.pallas_call(
        feed_back_kernel,
        grid=(blocks,),
        in_specs=specs(width) + specs(units) + [whole(out_weight), whole(hid_weight)],
        out_specs=specs(units) + specs(width),
        out_shape=[
            jax.ShapeDtypeStruct((v.shape[0], columns), jnp.bfloat16)
            for columns in (units, width)
            for v in ups
        ],
        compiler_params=pltpu.CompilerParams(vmem_limit_bytes=VMEM_LIMIT),
        cost_estimate=pl.CostEstimate(flops=0, bytes_accessed=60_000_000, transcendentals=0),
        name="feed_back",
    )(*ups, *before, out_weight, hid_weight)


def pair_terms_kernel(left_image, left_text, right_image, right_text, out):
    for m, (left, right) in enumerate(((left_image, right_image), (left_text, right_text))):
        out[m] = lax.dot_general(
            left[...], right[...], (((0,), (0,)), ((), ())), preferred_element_type=jnp.float32
        ).astype(jnp.bfloat16)


def pair_terms(left, right):
    k, c = left[0].shape[1], right[0].shape[1]
    step = 256 if k % 256 == 0 else k
    return pl.pallas_call(
        pair_terms_kernel,
        grid=(k // step,),
        in_specs=[pl.BlockSpec((v.shape[0], step), lambda i: (0, i)) for v in left]
        + [pl.BlockSpec(v.shape, lambda i: (0, 0)) for v in right],
        out_specs=pl.BlockSpec((2, step, c), lambda i: (0, i, 0)),
        out_shape=jax.ShapeDtypeStruct((2, k, c), jnp.bfloat16),
        compiler_params=pltpu.CompilerParams(vmem_limit_bytes=VMEM_LIMIT),
        cost_estimate=pl.CostEstimate(flops=0, bytes_accessed=25_000_000, transcendentals=0),
        name="pair_terms",
    )(*left, *right)


def fold(proj, wide):
    count, left = proj.shape[-2] // 3, wide // 3
    rest = proj[..., wide:]
    extra = [rest[..., i * count : (i + 1) * count, :] for i in range(3)]
    return jnp.concatenate([proj[..., :wide], jnp.concatenate(extra, -1)], -2)


def unfold(rows, count):
    left = rows.shape[-1] // 3
    extra = [rows[..., count:, i * left : (i + 1) * left] for i in range(3)]
    return jnp.concatenate([rows[..., :count, :], jnp.concatenate(extra, -2)], -1)


def pick_qkv_kernel(part, place, *refs):
    own, other = refs[3:]
    high = place[1] == 1
    for kind in range(3):
        for m in range(2):
            at = slice((m * 3 + kind) * part, (m * 3 + kind + 1) * part)
            low, up = refs[kind][m, :, :part], refs[kind][m, :, part:]
            own[:, at] = jnp.where(high, up, low)
            other[:, at] = jnp.where(high, low, up)


def pick_qkv(weight, place, part):
    slab, width = weight.shape[1], weight.shape[2] // 3
    per_kind = width // (2 * part)

    def spec(kind):
        return pl.BlockSpec((2, slab, 2 * part), lambda i, at: (0, 0, kind * per_kind + at[0]))

    shape = (slab, 6 * part)
    return pl.pallas_call(
        functools.partial(pick_qkv_kernel, part),
        grid_spec=pltpu.PrefetchScalarGridSpec(
            num_scalar_prefetch=1,
            grid=(1,),
            in_specs=[spec(k) for k in range(3)],
            out_specs=[pl.BlockSpec(shape, lambda i, at: (0, 0))] * 2,
        ),
        out_shape=[jax.ShapeDtypeStruct(shape, jnp.bfloat16)] * 2,
        compiler_params=pltpu.CompilerParams(vmem_limit_bytes=VMEM_LIMIT),
        name="pick_qkv",
    )(place, *([weight] * 3))


def pick_hid_kernel(line, place, *refs):
    own, other = refs[2 * line :]
    high, odd = place[1] == 1, place[2] == 1
    for z in range(line):
        chosen = []
        for q in range(2):
            block = refs[z * 2 + q]
            cut = block.shape[2] // 2
            chosen.append(jnp.where(odd, block[:, :, cut:], block[:, :, :cut]))
        at = slice(z * cut, (z + 1) * cut)
        own[:, :, at] = jnp.where(high, chosen[1], chosen[0])
        other[:, :, at] = jnp.where(high, chosen[0], chosen[1])


def pick_hid(weight, place, line):
    slab, units = weight.shape[1], weight.shape[2] // (2 * line)

    def spec(f):
        return pl.BlockSpec((2, slab, units // 2), lambda i, at: (0, 0, 2 * f + at[0] // 2))

    shape = (2, slab, line * units // 4)
    return pl.pallas_call(
        functools.partial(pick_hid_kernel, line),
        grid_spec=pltpu.PrefetchScalarGridSpec(
            num_scalar_prefetch=1,
            grid=(1,),
            in_specs=[spec(f) for f in range(2 * line)],
            out_specs=[pl.BlockSpec(shape, lambda i, at: (0, 0, 0))] * 2,
        ),
        out_shape=[jax.ShapeDtypeStruct(shape, jnp.bfloat16)] * 2,
        compiler_params=pltpu.CompilerParams(vmem_limit_bytes=VMEM_LIMIT),
        name="pick_hid",
    )(place, *([weight] * (2 * line)))


def chosen_piece(pieces, x, c, q):
    near = [jnp.where(c == q % 2, pieces[2 * dx], pieces[2 * dx + 1]) for dx in range(2)]
    return jnp.where(x == q // 2, near[0], near[1])


def inner(left, right):
    return lax.dot_general(
        left[...], right[...], (((0,), (0,)), ((), ())), preferred_element_type=jnp.float32
    ).astype(jnp.bfloat16)


def stacked_kernel(
    image, text, up_image, up_text, mixed_image, mixed_text, branch_image, branch_text,
    out, sums, proj,
):
    rows, part = image.shape[1], up_image.shape[1]
    wide = 2 * part
    z = pl.program_id(0)

    @pl.when(z == 0)
    def _():
        sums[...] = jnp.zeros(sums.shape, jnp.float32)
        sums[0:1] = row_sums(up_image[...].astype(jnp.float32))
        sums[1:2] = row_sums(up_text[...].astype(jnp.float32))
        proj[0] = inner(mixed_image, branch_image)
        proj[1] = inner(mixed_text, branch_text)

    out[0, :rows, :part] = inner(image, up_image)
    out[0, :rows, part:] = inner(text, up_text)
    chunk = proj.shape[1] // pl.num_programs(0)
    at = pl.ds(pl.multiple_of(z * chunk, 16), chunk)
    more = jnp.concatenate([proj[0, at, :], proj[1, at, :]], 0)
    count = more.shape[0]
    out[0, rows : rows + count, :] = more[:, :wide]
    third, left = count // 3, wide // 3
    for i in range(3):
        out[0, rows + count :, i * left : (i + 1) * left] = more[i * third : (i + 1) * third, wide:]


def stacked_terms(hidden, ups, mixed, branch, line):
    rows, part = hidden[0].shape[1] // line, ups[0].shape[1]
    head_part, width = mixed[0].shape[1], branch[0].shape[1]
    more = 2 * head_part // line * width // (2 * part)
    others = ups + mixed + branch
    return pl.pallas_call(
        stacked_kernel,
        grid=(line,),
        in_specs=[pl.BlockSpec((v.shape[0], rows), lambda z: (0, z)) for v in hidden]
        + [pl.BlockSpec(v.shape, lambda z: (0, 0)) for v in others],
        out_specs=[
            pl.BlockSpec((1, rows + more, 2 * part), lambda z: (z, 0, 0)),
            pl.BlockSpec((8, part), lambda z: (0, 0)),
        ],
        out_shape=[
            jax.ShapeDtypeStruct((line, rows + more, 2 * part), jnp.bfloat16),
            jax.ShapeDtypeStruct((8, part), jnp.float32),
        ],
        scratch_shapes=[pltpu.VMEM((2, head_part, width), jnp.bfloat16)],
        compiler_params=pltpu.CompilerParams(vmem_limit_bytes=VMEM_LIMIT),
        cost_estimate=pl.CostEstimate(flops=0, bytes_accessed=45_000_000, transcendentals=0),
        name="stacked_terms",
    )(*hidden, *others)


def columns_kernel(chunk, kinds, inner_first, place, *refs):
    out = refs[8]
    r, x, c = place[0], place[1], place[2]
    for m in range(out.shape[1]):
        for kind in range(kinds):
            at = slice((m * kinds + kind) * chunk, (m * kinds + kind + 1) * chunk)
            by_dr = [
                [chosen_piece([refs[dr * 4 + p][:, at] for p in range(4)], x, c, q) for q in range(4)]
                for dr in range(2)
            ]
            for q in range(4):
                for natural in range(2):
                    value = jnp.where(r == natural, by_dr[0][q], by_dr[1][q])
                    spot = q * 2 + natural if inner_first else natural * 4 + q
                    start = (kind * 8 + spot) * chunk
                    out[0, m, :, start : start + chunk] = value.astype(jnp.float32)


def natural_columns_kernel(chunk, kinds, pieces, out):
    for m in range(2):
        for kind in range(kinds):
            at = slice((m * kinds + kind) * chunk, (m * kinds + kind + 1) * chunk)
            for q in range(4):
                for p in range(2):
                    start = (kind * 8 + q * 2 + p) * chunk
                    out[0, m, :, start : start + chunk] = pieces[p, q, :, at].astype(jnp.float32)


def join_natural_columns(pieces, chunk, kinds):
    rows, columns = pieces.shape[2], 8 * kinds * chunk
    step = 48 if rows % 48 == 0 else rows
    return pl.pallas_call(
        functools.partial(natural_columns_kernel, chunk, kinds),
        grid=(rows // step,),
        in_specs=[pl.BlockSpec((2, 4, step, pieces.shape[3]), lambda i: (0, 0, i, 0))],
        out_specs=pl.BlockSpec((1, 2, step, columns), lambda i: (0, 0, i, 0)),
        out_shape=jax.ShapeDtypeStruct((1, 2, rows, columns), jnp.float32),
        compiler_params=pltpu.CompilerParams(vmem_limit_bytes=VMEM_LIMIT),
        name="join_natural_columns",
    )(pieces)


def join_columns(pieces, place, chunk, kinds, inner_first):
    rows = pieces[0].shape[-2]
    columns = 8 * kinds * chunk
    step = 64 if rows % 64 == 0 else rows
    if pieces[0].ndim == 3:
        grid = (rows // step, 2)
        piece = pl.BlockSpec((None, step, columns // 8), lambda i, m, at: (m, i, 0))
        out = pl.BlockSpec((1, 1, step, columns), lambda i, m, at: (0, m, i, 0))
    else:
        grid = (rows // step,)
        piece = pl.BlockSpec((step, columns // 4), lambda i, at: (i, 0))
        out = pl.BlockSpec((1, 2, step, columns), lambda i, at: (0, 0, i, 0))
    return pl.pallas_call(
        functools.partial(columns_kernel, chunk, kinds, inner_first),
        grid_spec=pltpu.PrefetchScalarGridSpec(
            num_scalar_prefetch=1, grid=grid, in_specs=[piece] * 8, out_specs=out
        ),
        out_shape=jax.ShapeDtypeStruct((1, 2, rows, columns), jnp.float32),
        compiler_params=pltpu.CompilerParams(vmem_limit_bytes=VMEM_LIMIT),
        name="join_columns",
    )(place, *pieces)


def rows_kernel(place, *refs):
    out = refs[4]
    rows = refs[0].shape[1]
    for q in range(4):
        value = chosen_piece([refs[p][0] for p in range(4)], place[1], place[2], q)
        out[0, 0, q * rows : (q + 1) * rows, :] = value.astype(jnp.float32)


def join_rows(pieces, place):
    rows, columns = pieces[0].shape[1:]
    step = columns // 2
    return pl.pallas_call(
        rows_kernel,
        grid_spec=pltpu.PrefetchScalarGridSpec(
            num_scalar_prefetch=1,
            grid=(2, 2),
            in_specs=[pl.BlockSpec((1, rows, step), lambda m, i, at: (m, 0, i))] * 4,
            out_specs=pl.BlockSpec((1, 1, 4 * rows, step), lambda m, i, at: (0, m, 0, i)),
        ),
        out_shape=jax.ShapeDtypeStruct((1, 2, 4 * rows, columns), jnp.float32),
        compiler_params=pltpu.CompilerParams(vmem_limit_bytes=VMEM_LIMIT),
        name="join_rows",
    )(place, *pieces)


def rows_major(values):
    return with_layout_constraint(values, Layout(major_to_minor=(0, 1)))


def together(*values):
    return lax.optimization_barrier(values)


def norm_rows(values):
    center = values - jnp.mean(values, -1, keepdims=True)
    return center * lax.rsqrt(jnp.mean(center * center, -1, keepdims=True) + NORM_EPS)


def modulated(values, shift, scale_up):
    return norm_rows(values) * (1.0 + scale_up) + shift


def gelu_tanh(values):
    return jax.nn.gelu(values, approximate=True)


def dot32(left, right, contract):
    return lax.dot_general(
        left, right, ((contract[0], contract[1]), ((), ())), preferred_element_type=jnp.float32
    )


def product(left, right):
    return dot32(left, right, ((1,), (0,)))


def rows_inner(left, right):
    return dot32(left, right, ((0,), (0,)))


def right_back(left, right):
    return dot32(left, right, ((1,), (1,)))


def swap_r(values):
    count = lax.axis_size("fsdp")
    return lax.ppermute(values, "fsdp", [(at, at ^ 1) for at in range(count)])


def swap_x(values):
    return lax.ppermute(values, "seq", [(at, at ^ 2) for at in range(4)])


def swap_c(values):
    return lax.ppermute(values, "seq", [(at, at ^ 1) for at in range(4)])


CORNERS = [(0, 0), (0, 1), (1, 0), (1, 1)]


def reduce_far(a0, a1, b0, b1):
    return [a0[0], a0[1], b0[0], b0[1], swap_x(a1), swap_r(b1)]


def reduce_sums(parts):
    f32, b16 = jnp.float32, jnp.bfloat16
    got_a, got_b = parts[4], parts[5]
    a = [(parts[dr].astype(f32) + got_a[dr].astype(f32)).astype(b16) for dr in range(2)]
    b = [(parts[2 + dx].astype(f32) + got_b[dx].astype(f32)).astype(b16) for dx in range(2)]
    return [a[0], b[0], a[1], b[1]]


def reduce_last(a, b, last_a, last_b):
    f32 = jnp.float32
    return jnp.concatenate(
        [a.astype(f32) + last_a.astype(f32), b.astype(f32) + last_b.astype(f32)], 1
    )


def shards(
    image_tokens,
    text_tokens,
    conditioning,
    text_lengths,
    mod_weight,
    mod_bias,
    qkv_weight,
    qkv_bias,
    proj_weight,
    proj_bias,
    hidden_weight,
    hidden_bias,
    output_weight,
    output_bias,
    image_cotangent,
    text_cotangent,
):
    f32, b16 = jnp.float32, jnp.bfloat16
    width = image_tokens.shape[2]
    counts = (image_tokens.shape[1], text_tokens.shape[1])
    parts = lax.axis_size("seq")
    owners = lax.axis_size("fsdp")
    line = owners // 2
    head_part = width // (2 * parts)
    heads_here = head_part // HEAD_DIM
    slab = width // owners
    units_slab = output_weight.shape[2]
    units_part = units_slab // parts
    units = units_slab * owners
    units_here = line * units_part
    score_scale = HEAD_DIM ** (-0.5)
    me = lax.axis_index("fsdp")
    s = lax.axis_index("seq")
    r = me % 2
    along = [[z * 2 + q for z in range(line)] for q in range(2)]
    direct_proj = line == parts
    image_rows, text_rows = counts[0] * parts, counts[1] * parts

    def cut(array, start, size, axis):
        return lax.dynamic_slice_in_dim(array, start, size, axis)

    def transpose_owners(values):
        pairs = [
            ((z * 2 + q) * parts + t, (t * 2 + q) * parts + z)
            for z in range(line)
            for q in range(2)
            for t in range(parts)
        ]
        return lax.ppermute(values, ("fsdp", "seq"), pairs)

    def line_gather(rows):
        return lax.all_gather(rows, "fsdp", axis=rows.ndim - 2, tiled=True, axis_index_groups=along)

    def line_reduce(term):
        return lax.psum_scatter(
            term, "fsdp", scatter_dimension=term.ndim - 2, tiled=True, axis_index_groups=along
        )

    def weight_terms(left, right):
        return jnp.stack([rows_inner(left[m], right[m]).astype(b16) for m in range(2)])

    def both_r(values):
        rows = values.reshape(values.shape[:-2] + (2, slab, -1))
        return pick(rows, r, values.ndim - 2), swap_r(pick(rows, 1 - r, values.ndim - 2))

    def by_r(own, other, axis):
        return jnp.where(r == 0, jnp.stack([own, other], axis), jnp.stack([other, own], axis))

    def pick(array, index, axis):
        return lax.dynamic_index_in_dim(array, index, axis, keepdims=False)

    biases = (mod_bias, qkv_bias, proj_bias, hidden_bias, output_bias)
    bias_sizes = [v.shape[2] for v in biases]
    bias_local = jnp.concatenate([v[0].astype(f32) for v in biases], 1)
    padded = -(-slab // 128) * 128
    common = jnp.concatenate([bias_local.reshape(-1), jnp.tile(text_lengths.astype(f32), 128)])
    common = jnp.pad(common, (0, -common.shape[0] % 256))
    half = common.shape[0] // 2
    common = cut(common, s % 2 * half, half, 0)
    spot = jnp.stack([s, r, s % 2]).astype(jnp.int32)
    aligned = (2 * head_part) % 128 == 0 and (2 * units_part) % 128 == 0
    if aligned:
        qkv_own, qkv_other = pick_qkv(qkv_weight[0], spot, head_part)
    else:
        qkv_view = qkv_weight[0].reshape(2, slab, 3, 2 * parts, head_part)
        qkv_own, qkv_other = [
            pick(qkv_view, s * 2 + at, 3).transpose(1, 0, 2, 3).reshape(slab, 6 * head_part)
            for at in (r, 1 - r)
        ]
    qkv_got = swap_r(qkv_other)
    proj_mine = proj_weight[0]
    if direct_proj:
        chunk = slab // parts
        proj_mine = transpose_owners(cut(proj_weight[0], s * chunk, chunk, 1))
    wide = 6 * head_part
    merged = direct_proj and slab % 96 == 0 and width - wide == wide // 3
    qkv_mine = by_r(qkv_own, qkv_got, 0).reshape(2 * slab, wide)
    if merged:
        rows = fold(proj_mine.reshape(2 * chunk, width), wide)
        qkv_mine = jnp.concatenate([qkv_mine, rows], 0)
    cond_in, qkv_mine = together(conditioning, qkv_mine)
    send = jnp.concatenate(
        [
            cond_in.reshape(owners, slab),
            jnp.zeros((owners, padded - slab), f32),
            jnp.broadcast_to(common, (owners, common.shape[0])),
        ],
        1,
    )
    small, act_cols, mods = modulation(send[:, None], mod_weight[0], owners, parts)
    small = small[:, :, 0, padded:].transpose(1, 0, 2).reshape(owners, -1)
    biases_end = 2 * sum(bias_sizes)
    lengths = [pick(small[:, biases_end], me ^ dr, 0) for dr in range(2)]
    bias_all = small[:, :biases_end].reshape(owners, 2, sum(bias_sizes))
    offsets = [0]
    for size in bias_sizes:
        offsets.append(offsets[-1] + size)
    mod_b, qkv_b, proj_b, hid_b, out_b = [
        bias_all[:, :, offsets[i] : offsets[i + 1]].transpose(1, 0, 2) for i in range(5)
    ]
    group = s * 2 + r
    qkv_b = cut(qkv_b.reshape(2, 2, width), group * head_part, head_part, 2)
    qkv_b = jnp.stack([qkv_b[:, 0], jnp.zeros_like(qkv_b[:, 0]), qkv_b[:, 1]], 1).reshape(
        2, 3 * head_part
    )
    proj_b = proj_b.reshape(2, width)
    out_b = out_b.reshape(2, width)
    hid_b = pick(pick(hid_b.reshape(2, line, 2, parts, units_part), s, 3), r, 2).reshape(
        2, units_here
    )
    mods = mods.reshape(parts, 2, 2, -1).transpose(1, 2, 0, 3).reshape(2, 2, 6 * width)
    mods = mods + mod_b.reshape(2, 6 * width)
    mod_part = mod_bias.shape[2]

    front_w = line_gather(qkv_mine).reshape(line, -1, wide)
    qkv_w = front_w[:, : 2 * slab].reshape(width, wide)
    qkv_w = [qkv_w[:, m * 3 * head_part : (m + 1) * 3 * head_part] for m in range(2)]
    if merged:
        proj_w = unfold(front_w[:, 2 * slab :], 2 * chunk).reshape(line, 2, chunk, width)
        proj_w = proj_w.transpose(1, 0, 2, 3).reshape(2, head_part, width)
    elif direct_proj:
        proj_w = line_gather(proj_mine)
    else:
        proj_all = lax.all_gather(proj_mine, "fsdp", axis=1, tiled=True)
        proj_w = cut(proj_all, group * head_part, head_part, 1)
    mods, image_in, text_in = together(mods, image_tokens[0], text_tokens[0])
    x_full = [v.reshape(2, -1, width) for v in gather_group(image_in, text_in, 3)]
    x_full[0], hid_spot = together(x_full[0], spot)
    if aligned:
        hid_own, hid_other = pick_hid(hidden_weight[0], hid_spot, line)
    else:
        hid_view = pick(hidden_weight[0].reshape(2, slab, line, 2, parts, units_part), s, 4)
        hid_own, hid_other = [
            pick(hid_view, at, 3).reshape(2, slab, units_here) for at in (r, 1 - r)
        ]
    hid_got = swap_r(hid_other)

    def mod_at(index, m):
        at = slice(index * width, (index + 1) * width)
        return mods[0, m, None, at], mods[:, m, None, at]

    shift1, scale1, gate1, shift2, scale2, gate2 = [
        [mod_at(i, m) for m in range(2)] for i in range(6)
    ]

    def joined(pieces):
        return [v.reshape(2, -1, v.shape[-1]) for v in pieces]

    def apart(values, m):
        return values.reshape(2, parts, counts[m], -1)

    def flat(values):
        return values.reshape(-1, values.shape[-1])


    if merged:
        vectors = jnp.concatenate([v for m in range(2) for v in (shift1[m][1], scale1[m][1])], 1)
        hidden1 = list(front_norm(*x_full, vectors))
        hidden1[0], hid_got = together(hidden1[0], hid_got)
        front_w, hidden1[0] = together(front_w, hidden1[0])
        qkv = list(front_project(*hidden1, front_w, qkv_b, head_part))
        hidden1 = [flat(v) for v in hidden1]
    else:
        hidden1 = [
            flat(modulated(x_full[m].astype(f32), shift1[m][1], scale1[m][1]).astype(b16))
            for m in range(2)
        ]
        qkv = [
            rows_major((product(hidden1[m], qkv_w[m]) + qkv_b[m]).astype(b16)) for m in range(2)
        ]
        qkv = [v.reshape(2, -1, 3 * head_part) for v in qkv]
    hid_w = line_gather(by_r(hid_own, hid_got, 1).reshape(2, 2 * slab, units_here))
    out_w = line_gather(cut(output_weight[0], s * units_part, units_part, 1))
    text_slot = jnp.arange(text_rows)
    text_place = ((text_slot // counts[1]) ^ s) * counts[1] + text_slot % counts[1]
    open_text = jnp.stack([(text_place.astype(f32) < n).astype(f32) for n in lengths])
    open_text = jnp.broadcast_to(open_text[:, :, None], (2, text_rows, 128))
    mixed_image, mixed_text, lse_image, lse_text = attention(*qkv, open_text, score_scale)
    attended = [flat(mixed_image), flat(mixed_text)]

    def like(pair, kind):
        return [jax.ShapeDtypeStruct(v.shape, kind) for v in pair]

    own = [image_tokens[0], text_tokens[0]]
    own_up = [image_cotangent[0], text_cotangent[0]]

    def summed(terms, *rest, **options):
        return list(reduce_group(*[apart(terms[m], m) for m in range(2)], *rest, **options))

    vectors = [v for m in range(2) for v in (proj_b[m, None], gate1[m][0], shift2[m][0], scale2[m][0])]
    reduced = summed(
        [product(attended[m], proj_w[m]).astype(b16) for m in range(2)],
        5,
        middle_epilogue,
        own + [jnp.concatenate(vectors, 0)],
        like(own, f32) + like(own, f32) + like(own, b16),
    )
    branch, middle = reduced[:2], reduced[2:4]
    hidden2 = [flat(v) for v in gather_group(*reduced[4:], 6)]

    shapes = [jax.ShapeDtypeStruct((v.shape[0], units_here), f32) for v in hidden2]
    shapes += [jax.ShapeDtypeStruct((v.shape[0], units_here), b16) for v in hidden2]
    extra = hidden2 + [hid_w, hid_b]
    d_own = [(own_up[m].astype(f32) * gate2[m][0]).astype(b16) for m in range(2)]
    image_up, text_up, extra[0] = together(*d_own, extra[0])
    gathered = gather_group(
        image_up,
        text_up,
        4,
        first_layer_work,
        extra,
        shapes,
        held(extra + shapes) + [pltpu.SemaphoreType.DMA((8,))],
    )
    d_result, before, active = [flat(v) for v in gathered[:2]], gathered[2:4], gathered[4:]
    out_t = pair_terms(active, d_result)
    out_g = line_reduce(out_t)
    d_result[0], d_result[1], out_t = together(*d_result, out_t)
    *d_before, d_image, d_text = feed_back(d_result, before, out_w, hid_w, 4)
    d_hidden2 = [d_image, d_text]
    vectors = [v for m in range(2) for v in (scale2[m][0], gate1[m][0])]
    hid_terms = [
        jax.ShapeDtypeStruct((2, width, units_here), b16),
        jax.ShapeDtypeStruct((8, units_here), f32),
    ]
    reduced = summed(
        d_hidden2,
        7,
        middle_back_epilogue,
        list(middle) + own_up + list(branch) + [jnp.concatenate(vectors, 0)],
        like(own, f32) + like(own, b16) + [jax.ShapeDtypeStruct((8, width), f32)],
        weight_terms_work,
        hidden2 + d_before,
        hid_terms,
        held(hidden2 + d_before + hid_terms) + [pltpu.SemaphoreType.DMA((6,))],
    )
    d_middle, d_branch, sums2, hid_t, hid_sums = reduced[:2], reduced[2:4], *reduced[4:]
    hid_g = line_reduce(hid_t)
    extra = list(active) + [out_w]
    corner = (4, sum(counts), width)
    gathered = list(gather_group(
        *d_branch,
        8,
        second_layer_work,
        extra,
        [jax.ShapeDtypeStruct((2, sum(counts), width // 2), b16)] * 4,
        held(extra)
        + [pltpu.VMEM((2,) + corner, b16), pltpu.VMEM(corner, b16), pltpu.SemaphoreType.DMA((11,))]
        + [pltpu.SemaphoreType.DMA] * 2,
        micros=90,
    ))
    gathered[0], out_g = together(gathered[0], out_g)
    d_branch_full = [flat(v) for v in gathered[:2]]
    result_near = gathered[2:]
    d_attended = [
        rows_major(right_back(d_branch_full[m], proj_w[m]).astype(b16)).reshape(2, -1, head_part)
        for m in range(2)
    ]
    out_far = swap_x(out_g)
    result_far = reduce_far(*result_near)
    d_qkv = attention_back(*qkv, open_text, lse_image, lse_text, *d_attended, score_scale)
    d_qkv = [flat(v) for v in d_qkv]
    d_qkv[0], d_qkv[1], out_far, *result_far = together(*d_qkv, out_far, *result_far)
    d_qkv[0], d_qkv[1], *result_sums = together(*d_qkv, *reduce_sums(result_far))
    result_last = [swap_r(result_sums[2]), swap_x(result_sums[3])]
    if merged:
        qkv_t, qkv_sums = stacked_terms(hidden1, d_qkv, attended, d_branch_full, line)
        qkv_t = qkv_t.reshape(-1, wide)
    else:
        qkv_t = [rows_inner(hidden1[m], d_qkv[m]).astype(b16) for m in range(2)]
        qkv_t = jnp.concatenate(qkv_t, 1)
        qkv_sums = jnp.concatenate([row_sums(v.astype(f32)) for v in d_qkv], 0)
    both = line_reduce(qkv_t)
    d_qkv[0], d_qkv[1], qkv_t = together(*d_qkv, qkv_t)
    if merged:
        d_hidden1 = list(back_to_hidden(d_qkv, front_w, head_part, 4))
    else:
        d_hidden1 = [right_back(d_qkv[m], qkv_w[m]).astype(b16) for m in range(2)]
    d_hidden1[0], d_hidden1[1], hid_g, *result_last = together(*d_hidden1, hid_g, *result_last)
    hid_keep, hid_got = both_r(hid_g)
    reduced = summed(
        d_hidden1,
        9,
        input_back_epilogue,
        own + list(d_middle) + [jnp.concatenate([scale1[m][0] for m in range(2)], 0)],
        like(own, f32) + [jax.ShapeDtypeStruct((8, width), f32)],
        micros=90,
    )
    token_grads, sums1 = [v[None] for v in reduced[:2]], reduced[2]
    hid_far = swap_x(hid_keep)
    sums1, hid_got, hid_far = together(sums1, hid_got, hid_far)
    hid_got_far = swap_x(hid_got)
    sums1, *result_last = together(sums1, *result_last)
    result_last = reduce_last(*result_sums[:2], *result_last)
    result = [result_last[: counts[0]] + out_b[0], result_last[counts[0] :] + out_b[1]]
    image_out, text_out = [
        (middle[m] + gate2[m][0] * result[m]).astype(b16)[None] for m in range(2)
    ]

    all_rows = []
    for m in range(2):
        columns = qkv_sums[m].reshape(3, head_part)
        qkv_bt = lax.dynamic_update_slice_in_dim(
            jnp.zeros((2, width), f32), columns[::2], group * head_part, 1
        )
        units_bt = hid_sums[m].reshape(line, units_part)
        hid_bt = lax.dynamic_update_slice_in_dim(
            jnp.zeros((line, 2 * units_slab), f32), units_bt, r * units_slab + s * units_part, 1
        )
        up = own_up[m].astype(f32)
        all_rows += [
            sums1[2 * m : 2 * m + 2],
            sums2[4 * m + 2 : 4 * m + 3],
            sums2[4 * m : 4 * m + 2],
            row_sums(up * result[m]),
            qkv_bt,
            sums2[4 * m + 3 : 4 * m + 4],
            hid_bt.reshape(-1, width),
            row_sums((up * gate2[m][0]).astype(b16).astype(f32)),
        ]
    sums = jnp.concatenate(all_rows, 0)
    length = sums.shape[0]
    place = jnp.stack([r, s // 2, s % 2]).astype(jnp.int32)

    def share(own, far=None):
        far = swap_x(own) if far is None else far
        return [own, swap_c(own), far, swap_c(far)]

    out_grad = join_rows(share(out_g, out_far), place)
    hid_got_far, out_grad = together(hid_got_far, out_grad)
    hid_parts = share(hid_keep, hid_far) + share(hid_got, hid_got_far)
    hid_grad = join_columns(hid_parts, place, units_part, line, False)
    sums, out_grad, hid_grad = together(sums, out_grad, hid_grad)
    sums = jnp.pad(sums, ((0, -length % 16), (0, 0)))
    sums_all, d_mods, d_act, qkv_pieces, proj_pieces = finish(sums, both, mod_weight[0], owners)
    bias_sum = jnp.sum(sums_all[:, :length].astype(f32), 0).reshape(2, 14, width)
    bias_sum = bias_sum[:, 6:].reshape(2, -1)
    bias_at = [0, 2 * width, 3 * width, 3 * width + units, 4 * width + units]
    bias_grads = [
        cut(bias_sum[:, bias_at[i] : bias_at[i + 1]], me * size, size, 1)[None]
        for i, size in enumerate(bias_sizes[1:])
    ]
    mod_grad_w = jnp.einsum("sd,tse->tde", act_cols, d_mods, preferred_element_type=f32)[None]
    mod_grad_b = jnp.sum(cut(d_mods, me * mod_part, mod_part, 2).astype(f32), 1)[None]
    d_act = d_act[:, 0, :slab].reshape(1, width)
    conditioning_grad = jax.vjp(jax.nn.silu, conditioning)[1](d_act)[0]

    if merged:
        proj_grad = unfold_rows(proj_pieces)
    else:
        proj_t = [rows_inner(attended[m], d_branch_full[m]).astype(b16) for m in range(2)]
        proj_grad = []
        for m in range(2):
            spread = lax.dynamic_update_slice_in_dim(
                jnp.zeros((width, width), b16), proj_t[m], group * head_part, 0
            )
            own = lax.psum_scatter(spread, "fsdp", scatter_dimension=0, tiled=True)
            proj_grad.append(lax.psum(own, "seq").astype(f32))
        proj_grad = jnp.stack(proj_grad)[None]
    qkv_grad = join_natural_columns(qkv_pieces, head_part, 3)
    return (
        image_out,
        text_out,
        token_grads[0],
        token_grads[1],
        conditioning_grad,
        mod_grad_w,
        mod_grad_b,
        qkv_grad,
        bias_grads[0],
        proj_grad,
        bias_grads[1],
        hid_grad,
        bias_grads[2],
        out_grad,
        bias_grads[3],
    )


def solution(mesh):
    tokens = P("fsdp", "seq", None)
    weight = P(None, None, "fsdp", None)
    bias = P(None, None, "fsdp")
    pairs = (weight, bias) * 5
    return jax.shard_map(
        shards,
        mesh=mesh,
        in_specs=(tokens, tokens, P("fsdp", None), P("fsdp")) + pairs + (tokens, tokens),
        out_specs=(tokens, tokens, tokens, tokens, P("fsdp", None)) + pairs,
        check_vma=False,
    )
```
